32 devices in a mesh: probe: 2 (over y), space: 16 (over z, x, core).
Axes of the slice: x: 2, y: 2, z: 4, core: 2. Of those that a mesh axis runs over, the one named last changes fastest.
Arguments:
- probe_dirs: float32 [8, 16, 256], P('probe', 'space'), may hold values from -6 to 6
- log_param: float32 [16, 256], P('space'), may hold values from -1 to 1
- background: float32 [128, 32, 512], P('space'), may hold values from 0.3 to 1.5
- site_class: int32 [128, 32, 512], P('space'), may hold values from 0 to 3
- trap_density: float32 [4], replicated, may hold values from 0.2 to 1
Outputs:
- q_basis: float32 [8, 16, 256], P('probe', 'space')
- lower_factor: float32 [8, 8], replicated
The draws below stay inside these ranges and needn't reach their ends.
All inputs are finite; a program needn't handle non-finite values.
Results may differ from the reference program's by a relative error of at most 0.0003.
Values sent between devices are 32-bit elements; how exact they have to be, the bound alone decides.
No kernel may reach another device: no remote copies, remote signals or barrier semaphores. Data moves between devices by JAX's collectives and lax.ppermute only.
A program may use at most 64 MiB of HBM per device.

```python
import math
import jax
import jax.numpy as jnp
from jax import lax

PX = 64
PY = 4
REF = 8
NCLASS = 4
STEPS = 4
PROBES = 8
PZ = 16
PCELLS = 256
NZ = 128
NFY = 32
NFX = 512
NCOARSE = 4096


def draw_probe_dirs(key, part):
    group_count = max(1, PROBES // 4)
    key_base = jax.random.fold_in(key, 101)
    key_noise = jax.random.fold_in(key, 202)
    key_gain = jax.random.fold_in(key, 303)
    bases = jnp.clip(jax.random.normal(key_base, (group_count, PZ, PCELLS), jnp.float32), -4.0, 4.0)
    noise = jnp.clip(jax.random.normal(key_noise, (PROBES, PZ, PCELLS), jnp.float32), -4.0, 4.0)
    spread = 1.0 / 128.0
    gains = jnp.exp(jax.random.uniform(key_gain, (PROBES,), jnp.float32, -0.35, 0.35))
    member = jnp.arange(PROBES, dtype=jnp.int32) % group_count
    chosen = bases[member]
    return chosen * gains[:, None, None] + spread * noise


def set_ends(values, own_key, smallest, high):
    dims = values.shape
    place = [jax.random.randint(jax.random.fold_in(own_key, axis), (), 0, dims[axis]) for axis in range(len(dims))]
    values = values.at[tuple(place)].set(smallest)
    longest = dims.index(max(dims))
    place[longest] = (place[longest] + 1) % dims[longest]
    return values.at[tuple(place)].set(high)


def shard_levels(key, dims, split, low, high):
    level, own = 1.0, jax.random.fold_in(key, 6)
    for axis_at, blocks in split:
        steps = jnp.exp(jax.random.uniform(jax.random.fold_in(own, axis_at), (blocks,), jnp.float32, low / len(split), high / len(split)))
        level = level * jnp.repeat(steps, dims[axis_at] // blocks).reshape([-1 if axis == axis_at else 1 for axis in range(len(dims))])
    return level


def setup_inputs(seed: int = 0) -> dict:
    key_of = jax.random.split(jax.random.key(seed), 6)
    return {
        "probe_dirs": draw_probe_dirs(jax.random.fold_in(key_of[5], 71), 0),
        "log_param": jnp.clip(jax.random.uniform(key_of[1], (PZ, PCELLS), jnp.float32, -1.0, 1.0) * shard_levels(key_of[1], (PZ, PCELLS), ((0, 16),), -0.4, 0.0), -1.0, 1.0),
        "background": jnp.clip(0.3 + 1.2 * jax.random.uniform(key_of[2], (NZ, NFY, NFX), jnp.float32) ** shard_levels(key_of[2], (NZ, NFY, NFX), ((0, 16),), -0.2, 0.2), 0.3, 1.5),
        "site_class": set_ends(jax.random.randint(key_of[3], (NZ, NFY, NFX), 0, NCLASS), jax.random.fold_in(key_of[3], 1), 0, NCLASS - 1).astype(jnp.int32),
        "trap_density": jnp.clip(jnp.exp(jax.random.uniform(key_of[4], (NCLASS,), jnp.float32, math.log(0.2), math.log(1.0))), 0.2, 1.0),
    }


TIME_STEP = 0.12

def lower_solve(factor, rows):
    return lax.linalg.triangular_solve(factor, rows, left_side=True, lower=True)

def prolong(coarse):
    leading = coarse.shape[:-2]
    planes = coarse.shape[-2]
    coarse_grid = coarse.reshape(leading + (planes, PY, PX))
    expanded = jnp.broadcast_to(coarse_grid[..., :, None, :, None, :, None], leading + (planes, REF, PY, REF, PX, REF))
    return expanded.reshape(leading + (planes * REF, PY * REF, PX * REF))

def restrict(finegrid):
    planes = finegrid.shape[0] // REF
    shaped = finegrid.reshape((planes, REF, PY, REF, PX, REF))
    return jnp.sum(shaped, axis=(1, 3, 5)).reshape((planes, PY * PX))

def stencil(padded, current, trap_rate):
    up_down = padded[2:, :, :] + padded[:-2, :, :]
    flat_pad = jnp.pad(current, ((0, 0), (1, 1), (1, 1)))
    lateral = flat_pad[:, 2:, 1:-1] + flat_pad[:, :-2, 1:-1] + flat_pad[:, 1:-1, 2:] + flat_pad[:, 1:-1, :-2]
    return current + TIME_STEP * (up_down + lateral - 6.0 * current - trap_rate * current)

def advance(current, trap_rate):
    padded = jnp.pad(current, ((1, 1), (0, 0), (0, 0)))
    return stencil(padded, current, trap_rate)

def reference(probe_dirs, log_param, background, site_class, trap_density):
    trap_rate = trap_density[site_class] * jnp.exp(prolong(log_param))
    source = -TIME_STEP * trap_rate * background

    def hessian_column(direction):
        tangent = source * prolong(direction)
        for step_index in range(STEPS - 1):
            tangent = advance(tangent, trap_rate)
        adjoint = tangent
        summed = adjoint
        for step_index in range(STEPS - 1):
            adjoint = advance(adjoint, trap_rate)
            summed = summed + adjoint
        return restrict(source * summed)
    images = lax.map(hessian_column, probe_dirs)
    rows = images.reshape((PROBES, NCOARSE))
    highest = lax.Precision.HIGHEST
    gram_one = jnp.dot(rows.astype(jnp.float32), rows.T.astype(jnp.float32), precision=highest, preferred_element_type=jnp.float32) / NCOARSE
    factor_one = jnp.linalg.cholesky(gram_one)
    basis_one = lower_solve(factor_one, rows)
    gram_two = jnp.dot(basis_one.astype(jnp.float32), basis_one.T.astype(jnp.float32), precision=highest, preferred_element_type=jnp.float32) / NCOARSE
    factor_two = jnp.linalg.cholesky(gram_two)
    q_rows = lower_solve(factor_two, basis_one)
    lower_factor = jnp.dot(factor_one.astype(jnp.float32), factor_two.astype(jnp.float32), precision=highest, preferred_element_type=jnp.float32)
    return (q_rows.reshape((PROBES, PZ, PCELLS)), lower_factor)
```

```python
import functools

import jax
import jax.numpy as jnp
from jax import lax
from jax.experimental import pallas as pl
from jax.experimental.pallas import tpu as pltpu
from jax.sharding import PartitionSpec as P

PX = 64
PY = 4
REF = 8
STEP = 0.12
HALO = 3
LANES = 128
HIGHEST = lax.Precision.HIGHEST


def dot_nn(a, b):
    return lax.dot_general(
        a, b, (((1,), (0,)), ((), ())), precision=HIGHEST, preferred_element_type=jnp.float32
    )


def dot_nt(a, b):
    return lax.dot_general(
        a, b, (((1,), (1,)), ((), ())), precision=HIGHEST, preferred_element_type=jnp.float32
    )


def image_kernel(
    probes, edge, density, background, sites, low, high, own, out, coef, src, field, wide, sums
):
    planes, rows, columns = background.shape
    chunks = columns // LANES
    tiles = rows // 8
    height = rows + 8
    total = planes + 2 * HALO
    first_own, last_own = HALO, HALO + planes - 1
    base_b = total
    zero_plane = 2 * total - 2
    has_low, has_high = edge[0], edge[1]
    lane = lax.broadcasted_iota(jnp.int32, (8, LANES), 1)
    at_first, at_last = lane == 0, lane == LANES - 1
    nothing = jnp.zeros((8, LANES), jnp.float32)

    def block(p, k):
        return 8 + height * (p * chunks + k)

    def clear(plane, carry):
        for b in range(probes * chunks + 1):
            field[plane, pl.ds(height * b, 8), :] = nothing
        return carry

    lax.fori_loop(0, zero_plane, clear, 0)
    for r in range(field.shape[1] // 8):
        field[zero_plane, pl.ds(8 * r, 8), :] = nothing

    coarse = jnp.concatenate(
        [low[2 * HALO * rows :, : PX * PY], own[...], high[2 * HALO * rows :, : PX * PY]], axis=0
    )
    row_at = lax.broadcasted_iota(jnp.int32, coarse.shape, 0) % 8
    coarse = jnp.where(row_at == probes, jnp.exp(coarse), coarse)
    cell = lax.broadcasted_iota(jnp.int32, (PX, columns), 0)
    spread = (lax.broadcasted_iota(jnp.int32, (PX, columns), 1) // REF == cell).astype(jnp.float32)
    for y in range(PY):
        wide[y] = dot_nn(coarse[:, y * PX : (y + 1) * PX], spread)

    def coefficients(plane, part, bg_at, site_at):
        for j in range(tiles):
            for k in range(chunks):
                bg, site = bg_at(j, k), site_at(j, k)
                trap = jnp.full((8, LANES), density[density.shape[0] - 1])
                for n in range(density.shape[0] - 2, -1, -1):
                    trap = jnp.where(site == n, density[n], trap)
                at = pl.ds(k * LANES, LANES)
                trap = trap * wide[j, pl.ds(8 * part + probes, 1), at]
                s = -STEP * trap * bg
                coef[plane, k, pl.ds(8 * j, 8), :] = (1.0 / STEP - 6.0) - trap
                src[plane, k, pl.ds(8 * j, 8), :] = s
                for p in range(probes):
                    field[plane, pl.ds(block(p, k) + 8 * j, 8), :] = (
                        s * wide[j, pl.ds(8 * part + p, 1), at]
                    )

    def from_halo(ref, z):
        def bg_at(j, k):
            return ref[pl.ds(z * rows + 8 * j, 8), pl.ds(k * LANES, LANES)]

        def site_at(j, k):
            return ref[pl.ds((HALO + z) * rows + 8 * j, 8), pl.ds(k * LANES, LANES)]

        return bg_at, site_at

    def from_own(z):
        def bg_at(j, k):
            return background[z, pl.ds(8 * j, 8), pl.ds(k * LANES, LANES)]

        def site_at(j, k):
            return sites[z, pl.ds(8 * j, 8), pl.ds(k * LANES, LANES)]

        return bg_at, site_at

    def own_plane(z, carry):
        coefficients(HALO + z, 1, *from_own(z))
        return carry

    lax.fori_loop(0, planes, own_plane, 0)
    for z in range(HALO):
        coefficients(z, 0, *from_halo(low, z))
        coefficients(last_own + 1 + z, 2, *from_halo(high, z))

    def stencil(z, center, down, up, emit, extra):
        for j in range(tiles):
            weights = [coef[z, k, pl.ds(8 * j, 8), :] for k in range(chunks)]
            for p in range(probes):
                values = [
                    field[center, pl.ds(block(p, k) + 8 * j, 8), :] for k in range(chunks)
                ]
                forward = [pltpu.roll(v, 1, 1) for v in values]
                backward = [pltpu.roll(v, LANES - 1, 1) for v in values]
                for k in range(chunks):
                    at = block(p, k) + 8 * j
                    left = jnp.where(at_first, forward[k - 1] if k else 0.0, forward[k])
                    right = jnp.where(
                        at_last, backward[k + 1] if k + 1 < chunks else 0.0, backward[k]
                    )
                    beside = field[center, pl.ds(at - 1, 8), :] + field[center, pl.ds(at + 1, 8), :]
                    above = field[down, pl.ds(at, 8), :] + field[up, pl.ds(at, 8), :]
                    weight = weights[k] + extra if extra else weights[k]
                    result = ((left + right) + (beside + above)) + weight * values[k]
                    emit(z, p, j, k, at, result)

    def in_a(z):
        return z

    def in_b(z):
        return base_b - 1 + z

    def pick(flag, one, other):
        return jnp.where(flag, one, other)

    def step(start, stop, index, to, extra=0.0):
        def body(z, carry):
            def emit(z, p, j, k, at, result):
                field[to(z), pl.ds(at, 8), :] = result

            stencil(z, index(z), index(z - 1), index(z + 1), emit, extra)
            return carry

        lax.fori_loop(start, stop, body, 0)

    def bound_low(z):
        return jnp.where(has_low == 0, first_own, z)

    def bound_high(z):
        return jnp.where(has_high == 0, last_own + 1, z)

    def outside(z):
        return ((z < first_own) & (has_low == 0)) | ((z > last_own) & (has_high == 0))

    def one(z):
        return pick(outside(z), zero_plane, in_b(z))

    def two(z):
        return pick(outside(z), zero_plane, in_a(z))

    step(bound_low(1), bound_high(total - 1), in_a, in_b)
    step(bound_low(2), bound_high(total - 2), one, in_a)
    step(bound_low(3), bound_high(total - 3), two, in_b)

    def tangent(z):
        return pick((z < first_own) | (z > last_own), zero_plane, in_b(z))

    step(first_own, last_own + 1, tangent, in_a, 1.0 / STEP)

    def widened(z):
        inside = (z >= first_own) & (z <= last_own)
        near_low = (z == first_own - 1) & (has_low != 0)
        near_high = (z == last_own + 1) & (has_high != 0)
        return pick(
            inside,
            in_a(z),
            pick(near_low, in_b(first_own), pick(near_high, in_b(last_own), zero_plane)),
        )

    free = [0, 1, 2] + [total - 3, total - 2, total - 1]
    free += [base_b, base_b + 1, base_b + total - 4, base_b + total - 3]

    def in_free(z):
        at = z - (first_own - 1)
        place = jnp.int32(free[0])
        for n in range(1, planes + 2):
            place = jnp.where(at == n, free[n], place)
        return place

    step(bound_low(first_own - 1), bound_high(last_own + 2), widened, in_free)

    def middle(z):
        kept = (z >= first_own - 1) & (z <= last_own + 1)
        near_low = z == first_own - 2
        near_high = z == last_own + 2
        place = pick(
            kept,
            in_free(z),
            pick(
                near_low,
                widened(first_own - 1),
                pick(near_high, widened(last_own + 1), zero_plane),
            ),
        )
        return pick(outside(z), zero_plane, place)

    sums[...] = jnp.zeros(sums.shape, jnp.float32)

    def last(part):
        def body(z, carry):
            kept = widened(z)

            def emit(z, p, j, k, at, result):
                s = src[z, k, pl.ds(8 * j, 8), :]
                result = result + (1.0 / STEP**2) * field[kept, pl.ds(at, 8), :]
                place = ((part * PY + j) * probes + p) * 8
                sums[pl.ds(place, 8), pl.ds(k * LANES, LANES)] += s * result

            stencil(z, middle(z), middle(z - 1), middle(z + 1), emit, 0.0)
            return carry

        return body

    lax.fori_loop(1, first_own, last(0), 0)
    lax.fori_loop(first_own, last_own + 1, last(1), 0)
    lax.fori_loop(last_own + 1, total - 1, last(2), 0)
    for part, z, near in ((0, 0, first_own - 2), (2, total - 1, last_own + 2)):
        plane = middle(near)
        for j in range(tiles):
            for p in range(probes):
                for k in range(chunks):
                    place = ((part * PY + j) * probes + p) * 8
                    sums[pl.ds(place, 8), pl.ds(k * LANES, LANES)] += (
                        src[z, k, pl.ds(8 * j, 8), :] * field[plane, pl.ds(block(p, k) + 8 * j, 8), :]
                    )

    count = 3 * PY * probes
    added = jnp.sum(sums[...].reshape(count, 8, columns), axis=1) * STEP**6
    cell = lax.broadcasted_iota(jnp.int32, (PX, columns), 0)
    gather = (lax.broadcasted_iota(jnp.int32, (PX, columns), 1) // REF == cell).astype(jnp.float32)
    images = dot_nt(added, gather)
    for part in range(3):
        for y in range(PY):
            at = (part * PY + y) * probes
            out[part, :, pl.ds(y * PX, PX)] = images[at : at + probes, :]


def eliminate(gram):
    count = gram.shape[0]
    rows = lax.broadcasted_iota(jnp.int32, (count, count), 0)
    columns = lax.broadcasted_iota(jnp.int32, (count, count), 1)
    inverse = jnp.where(rows == columns, 1.0, 0.0)
    for j in range(count - 1):
        scale = 1.0 / gram[j : j + 1, j : j + 1]
        ratio = jnp.where(rows > j, gram[:, j : j + 1] * scale, 0.0)
        gram = gram - ratio * gram[j : j + 1, :]
        inverse = inverse - ratio * inverse[j : j + 1, :]
    diagonal = jnp.sum(jnp.where(rows == columns, gram, 0.0), axis=1, keepdims=True)
    scale = 1.0 / jnp.sqrt(diagonal)
    upper = jnp.where(columns >= rows, gram, 0.0) * scale
    return upper, inverse * scale


def factor_kernel(place, parts, q_out, lower_out, rows_ref, q_ref):
    groups, slabs, _, probes, cells = parts.shape
    count = groups * probes
    for g in range(groups):

        def gather(slab, carry):
            before = jnp.maximum(slab - 1, 0)
            after = jnp.minimum(slab + 1, slabs - 1)
            image = parts[g, slab, 1]
            image = image + jnp.where(slab > 0, parts[g, before, 2], 0.0)
            image = image + jnp.where(slab < slabs - 1, parts[g, after, 0], 0.0)
            at = pl.multiple_of(slab * cells, cells)
            rows_ref[pl.ds(g * probes, probes), pl.ds(at, cells)] = image
            return carry

        lax.fori_loop(0, slabs, gather, 0, unroll=True if slabs <= 16 else 8)
    total = slabs * cells
    rows = rows_ref[...]
    upper_one, inverse_one = eliminate(dot_nt(rows, rows) / total)
    basis = dot_nn(inverse_one, rows)
    rows_ref[...] = basis
    upper_two, inverse_two = eliminate(dot_nt(basis, basis) / total)
    mine = rows_ref[:, pl.ds(pl.multiple_of(place[1] * cells, cells), cells)]
    q_ref[...] = dot_nn(inverse_two, mine)
    for g in range(groups):

        @pl.when(place[0] == g)
        def _():
            q_out[:, 0, :] = q_ref[pl.ds(g * probes, probes), :]

    r = lax.broadcasted_iota(jnp.int32, (count, count), 0)
    c = lax.broadcasted_iota(jnp.int32, (count, count), 1)
    lower_one = dot_nt(jnp.where(r == c, 1.0, 0.0), upper_one)
    lower_out[...] = dot_nt(lower_one, upper_two)


def shards(probe_dirs, log_param, background, site_class, trap_density):
    probes = probe_dirs.shape[0]
    cells = probe_dirs.shape[2]
    planes, rows, columns = background.shape
    slabs = lax.axis_size("space")
    groups = lax.axis_size("probe")
    at_space = lax.axis_index("space")
    vmem = pl.BlockSpec(memory_space=pltpu.VMEM)
    smem = pl.BlockSpec(memory_space=pltpu.SMEM)

    coarse = jnp.concatenate(
        [probe_dirs[:, 0], log_param, jnp.zeros((7 - probes, cells), jnp.float32)], axis=0
    )
    tail = jnp.pad(coarse, ((0, 0), (0, columns - cells)))

    def packet(z):
        return jnp.concatenate(
            [
                background[z : z + HALO].reshape(HALO * rows, columns),
                site_class[z : z + HALO].reshape(HALO * rows, columns).astype(jnp.float32),
                tail,
            ],
            axis=0,
        )

    up = [(i, i + 1) for i in range(slabs - 1)]
    down = [(j, i) for i, j in up]
    high = lax.ppermute(packet(0), "space", down)
    low = lax.ppermute(packet(planes - HALO), "space", up)
    edge = jnp.stack([at_space > 0, at_space < slabs - 1]).astype(jnp.int32)

    total = planes + 2 * HALO
    chunks = columns // LANES
    field_rows = (rows + 8) * probes * chunks + 8
    images = pl.pallas_call(
        functools.partial(image_kernel, probes),
        out_shape=jax.ShapeDtypeStruct((3, probes, cells), jnp.float32),
        in_specs=[smem, smem] + [vmem] * 5,
        out_specs=vmem,
        scratch_shapes=[
            pltpu.VMEM((total, chunks, rows, LANES), jnp.float32),
            pltpu.VMEM((total, chunks, rows, LANES), jnp.float32),
            pltpu.VMEM((2 * total - 1, field_rows, LANES), jnp.float32),
            pltpu.VMEM((PY, 24, columns), jnp.float32),
            pltpu.VMEM((3 * PY * probes * 8, columns), jnp.float32),
        ],
        compiler_params=pltpu.CompilerParams(vmem_limit_bytes=48 * 2**20),
        name="images",
    )(edge, trap_density, background, site_class, low, high, coarse)

    every = lax.all_gather(images, ("probe", "space"), axis=0, tiled=False)
    every = every.reshape((groups, slabs, 3, probes, cells))
    place = jnp.stack([lax.axis_index("probe"), at_space]).astype(jnp.int32)
    return pl.pallas_call(
        factor_kernel,
        out_shape=(
            jax.ShapeDtypeStruct((probes, 1, cells), jnp.float32),
            jax.ShapeDtypeStruct((groups * probes, groups * probes), jnp.float32),
        ),
        in_specs=[smem, vmem],
        out_specs=(vmem, vmem),
        scratch_shapes=[
            pltpu.VMEM((groups * probes, slabs * cells), jnp.float32),
            pltpu.VMEM((groups * probes, cells), jnp.float32),
        ],
        compiler_params=pltpu.CompilerParams(vmem_limit_bytes=48 * 2**20),
        name="factor",
    )(place, every)


def solution(mesh):
    placed = (
        P("probe", "space", None),
        P("space", None),
        P("space", None, None),
        P("space", None, None),
        P(),
    )
    return jax.shard_map(
        shards,
        mesh=mesh,
        in_specs=placed,
        out_specs=(P("probe", "space", None), P()),
        check_vma=False,
    )
```

```python
import functools

import jax
import jax.numpy as jnp
from jax import lax
from jax.experimental import pallas as pl
from jax.experimental.pallas import tpu as pltpu
from jax.sharding import PartitionSpec as P

PX = 64
PY = 4
REF = 8
STEP = 0.12
HALO = 3
LANES = 128
HIGHEST = lax.Precision.HIGHEST


def dot_nn(a, b):
    return lax.dot_general(
        a, b, (((1,), (0,)), ((), ())), precision=HIGHEST, preferred_element_type=jnp.float32
    )


def dot_nt(a, b):
    return lax.dot_general(
        a, b, (((1,), (1,)), ((), ())), precision=HIGHEST, preferred_element_type=jnp.float32
    )


def parts_of(x):
    first = x.astype(jnp.bfloat16)
    rest = x - first.astype(jnp.float32)
    second = rest.astype(jnp.bfloat16)
    third = (rest - second.astype(jnp.float32)).astype(jnp.bfloat16)
    return first, second, third


def bf16_dot(a, b):
    return jnp.dot(a, b, preferred_element_type=jnp.float32)


def interleave(values, order, split, kept):
    parts = parts_of(values) if split else (values.astype(jnp.bfloat16),)
    for k in range(kept.shape[0]):
        columns = order[:, k * LANES : (k + 1) * LANES]
        kept[k] = sum(bf16_dot(part, columns) for part in parts)


def cell_matrix(chunks):
    half = REF // chunks
    cell = lax.broadcasted_iota(jnp.int32, (PX * PY, LANES), 0) % PX
    lane = lax.broadcasted_iota(jnp.int32, (PX * PY, LANES), 1) // half
    return jnp.where(cell == lane, 1.0, 0.0).astype(jnp.float32)


def own_cells(folds):
    half = REF // folds
    sublane = lax.broadcasted_iota(jnp.int32, (8, PX * PY), 0) // half
    return lax.broadcasted_iota(jnp.int32, (8, PX * PY), 1) // PX == sublane


def prolonged(coarse, folds, chunks):
    mask = own_cells(folds)
    rows = [jnp.where(mask, coarse[n : n + 1, :], 0.0) for n in range(coarse.shape[0])]
    return dot_nn(jnp.concatenate(rows, axis=0), cell_matrix(chunks))


def coefficients(density, scale, background, sites, z, rows, folds, chunks, store):
    for r in range(folds):
        for k in range(chunks):
            at = pl.ds(z * rows + r, 8, stride=folds)
            bg, site = background[k, at, :], sites[k, at, :]
            trap = jnp.full((8, LANES), density[density.shape[0] - 1])
            for n in range(density.shape[0] - 2, -1, -1):
                trap = jnp.where(site == float(n), density[n], trap)
            trap = trap * scale
            store(r * chunks + k, (1.0 / STEP - 6.0) - trap, -STEP * trap * bg)


def prepare_kernel(probes, density, background, sites, coarse, coef, src, order, bg, site):
    planes, rows, columns = background.shape
    chunks, folds = columns // LANES, rows // 8
    x = lax.broadcasted_iota(jnp.int32, (columns, columns), 0)
    place = lax.broadcasted_iota(jnp.int32, (columns, columns), 1)
    wanted = chunks * (place % LANES) + place // LANES
    order[...] = jnp.where(x == wanted, 1.0, 0.0).astype(jnp.bfloat16)
    scale = prolonged(jnp.exp(coarse[probes : probes + 1, :]), folds, chunks)
    interleave(background[...].reshape(planes * rows, columns), order, True, bg)
    interleave(
        sites[...].reshape(planes * rows, columns).astype(jnp.float32), order, False, site
    )

    def plane(z, carry):
        def store(at, c, s):
            coef[z, at] = c
            src[z, at] = s

        coefficients(density, scale, bg, site, z, rows, folds, chunks, store)
        return carry

    lax.fori_loop(0, planes, plane, 0)


def image_kernel(
    probes, rows, edge, density, own_coef, own_src, order, low, high, own, out,
    coef, src, field, bg, site, sems,
):
    planes = own_coef.shape[0]
    columns = order.shape[0]
    chunks, folds = columns // LANES, rows // 8
    tiles = chunks * folds
    total = planes + 2 * HALO
    first_own, last_own = HALO, HALO + planes - 1
    base_b = total
    zero_plane = 2 * total - 2
    has_low, has_high = edge[0], edge[1]
    lane = lax.broadcasted_iota(jnp.int32, (8, LANES), 1)
    sublane = lax.broadcasted_iota(jnp.int32, (8, LANES), 0)
    nothing = jnp.zeros((8, LANES), jnp.float32)

    copies = [
        pltpu.make_async_copy(own_coef, coef.at[pl.ds(HALO, planes)], sems.at[0]),
        pltpu.make_async_copy(own_src, src.at[pl.ds(HALO, planes)], sems.at[1]),
    ]
    for copy in copies:
        copy.start()
    for p in range(probes):
        for t in range(tiles):
            field[zero_plane, p, t] = nothing

    rows_of = [low[2 * HALO * rows :, : PX * PY], own[...], high[2 * HALO * rows :, : PX * PY]]
    coarse = jnp.concatenate(
        [
            jnp.where(lax.broadcasted_iota(jnp.int32, x.shape, 0) == probes, jnp.exp(x), x)[
                : probes + 1
            ]
            for x in rows_of
        ],
        axis=0,
    )
    wide = prolonged(coarse, folds, chunks)

    def spread(part, n):
        at = (part * (probes + 1) + n) * 8
        return wide[at : at + 8, :]

    for side, packet in enumerate((low, high)):
        at = pl.ds(side * HALO * rows, HALO * rows)
        interleave(packet[pl.ds(0, HALO * rows), :], order, True, bg.at[:, at, :])
        interleave(packet[pl.ds(HALO * rows, HALO * rows), :], order, False, site.at[:, at, :])

    for side, part, first in ((0, 0, 0), (1, 2, last_own + 1)):
        for z in range(HALO):

            def store(at, c, s):
                coef[first + z, at] = c
                src[first + z, at] = s
                for p in range(probes):
                    field[first + z, p, at] = s * spread(part, p)

            coefficients(
                density, spread(part, probes), bg, site, side * HALO + z, rows, folds, chunks, store
            )
    for copy in copies:
        copy.wait()

    def own_start(z, carry):
        for t in range(tiles):
            s = src[z, t]
            for p in range(probes):
                field[z, p, t] = s * spread(1, p)
        return carry

    lax.fori_loop(first_own, last_own + 1, own_start, 0)

    def stencil(z, center, down, up, emit, extra):
        for p in range(probes):
            value = [[field[center, p, r * chunks + k] for k in range(chunks)] for r in range(folds)]
            for r in range(folds):
                for k in range(chunks):
                    t = r * chunks + k
                    if k:
                        left = value[r][k - 1]
                    else:
                        left = jnp.where(lane == 0, 0.0, pltpu.roll(value[r][chunks - 1], 1, 1))
                    if k + 1 < chunks:
                        right = value[r][k + 1]
                    else:
                        right = jnp.where(
                            lane == LANES - 1, 0.0, pltpu.roll(value[r][0], LANES - 1, 1)
                        )
                    if r:
                        before = value[r - 1][k]
                    else:
                        before = jnp.where(sublane == 0, 0.0, pltpu.roll(value[folds - 1][k], 1, 0))
                    if r + 1 < folds:
                        after = value[r + 1][k]
                    else:
                        after = jnp.where(sublane == 7, 0.0, pltpu.roll(value[0][k], 7, 0))
                    weight = coef[z, t]
                    if extra:
                        weight = weight + extra
                    above = field[down, p, t] + field[up, p, t]
                    sides = (left + right) + (before + after)
                    emit(z, p, t, (sides + above) + weight * value[r][k])

    def in_a(z):
        return z

    def in_b(z):
        return base_b - 1 + z

    def pick(flag, one, other):
        return jnp.where(flag, one, other)

    def step(start, stop, index, to, extra=0.0):
        def body(z, carry):
            def emit(z, p, t, result):
                field[to(z), p, t] = result

            stencil(z, index(z), index(z - 1), index(z + 1), emit, extra)
            return carry

        lax.fori_loop(start, stop, body, 0)

    def bound_low(z):
        return jnp.where(has_low == 0, first_own, z)

    def bound_high(z):
        return jnp.where(has_high == 0, last_own + 1, z)

    def outside(z):
        return ((z < first_own) & (has_low == 0)) | ((z > last_own) & (has_high == 0))

    def one(z):
        return pick(outside(z), zero_plane, in_b(z))

    def two(z):
        return pick(outside(z), zero_plane, in_a(z))

    step(bound_low(1), bound_high(total - 1), in_a, in_b)
    step(bound_low(2), bound_high(total - 2), one, in_a)
    step(bound_low(3), bound_high(total - 3), two, in_b)

    def tangent(z):
        return pick((z < first_own) | (z > last_own), zero_plane, in_b(z))

    step(first_own, last_own + 1, tangent, in_a, 1.0 / STEP)

    def widened(z):
        inside = (z >= first_own) & (z <= last_own)
        near_low = (z == first_own - 1) & (has_low != 0)
        near_high = (z == last_own + 1) & (has_high != 0)
        return pick(
            inside,
            in_a(z),
            pick(near_low, in_b(first_own), pick(near_high, in_b(last_own), zero_plane)),
        )

    free = [0, 1, 2] + [total - 3, total - 2, total - 1]
    free += [base_b, base_b + 1, base_b + total - 4, base_b + total - 3]

    def in_free(z):
        at = z - (first_own - 1)
        place = jnp.int32(free[0])
        for n in range(1, planes + 2):
            place = jnp.where(at == n, free[n], place)
        return place

    step(bound_low(first_own - 1), bound_high(last_own + 2), widened, in_free)

    def middle(z):
        kept = (z >= first_own - 1) & (z <= last_own + 1)
        near_low = z == first_own - 2
        near_high = z == last_own + 2
        place = pick(
            kept,
            in_free(z),
            pick(
                near_low,
                widened(first_own - 1),
                pick(near_high, widened(last_own + 1), zero_plane),
            ),
        )
        return pick(outside(z), zero_plane, place)

    def last(z, carry):
        kept = widened(z)
        sums = [[c] for c in carry]

        def emit(z, p, t, result):
            result = result + (1.0 / STEP**2) * field[kept, p, t]
            sums[p].append(src[z, t] * result)

        stencil(z, middle(z), middle(z - 1), middle(z + 1), emit, 0.0)
        return tuple(sum(terms[1:], terms[0]) for terms in sums)

    def outer(z, near):
        sums = []
        for p in range(probes):
            plane = middle(near)
            sums.append(sum(src[z, t] * field[plane, p, t] for t in range(tiles)))
        return tuple(sums)

    empty = (nothing,) * probes
    below = lax.fori_loop(1, first_own, last, outer(0, first_own - 2))
    inside = lax.fori_loop(first_own, last_own + 1, last, empty)
    above = lax.fori_loop(last_own + 1, total - 1, last, outer(total - 1, last_own + 2))

    added = jnp.concatenate(below + inside + above, axis=0) * STEP**6
    images = dot_nt(added, cell_matrix(chunks))
    mask = own_cells(folds)
    copies_out = out.shape[0]
    for part in range(3):
        image = jnp.concatenate(
            [
                jnp.sum(
                    jnp.where(mask, images[8 * (part * probes + p) :][:8], 0.0),
                    axis=0,
                    keepdims=True,
                )
                for p in range(probes)
            ],
            axis=0,
        )

        for n in range(min(copies_out, 32)):
            out[n, part] = image

        if copies_out > 32:

            def more(n, carry):
                out[n, part] = image
                return carry

            lax.fori_loop(32, copies_out, more, 0)


def eliminate(gram):
    count = gram.shape[0]
    rows = lax.broadcasted_iota(jnp.int32, (count, count), 0)
    columns = lax.broadcasted_iota(jnp.int32, (count, count), 1)
    inverse = jnp.where(rows == columns, 1.0, 0.0)
    for j in range(count - 1):
        scale = 1.0 / gram[j : j + 1, j : j + 1]
        ratio = jnp.where(rows > j, gram[:, j : j + 1] * scale, 0.0)
        gram = gram - ratio * gram[j : j + 1, :]
        inverse = inverse - ratio * inverse[j : j + 1, :]
    diagonal = jnp.sum(jnp.where(rows == columns, gram, 0.0), axis=1, keepdims=True)
    scale = 1.0 / jnp.sqrt(diagonal)
    upper = jnp.where(columns >= rows, gram, 0.0) * scale
    return upper, inverse * scale


def factor_kernel(place, parts, q_out, lower_out, rows_ref, q_ref):
    groups, slabs, _, probes, cells = parts.shape
    count = groups * probes
    for g in range(groups):

        def gather(slab, carry):
            before = jnp.maximum(slab - 1, 0)
            after = jnp.minimum(slab + 1, slabs - 1)
            image = parts[g, slab, 1]
            image = image + jnp.where(slab > 0, parts[g, before, 2], 0.0)
            image = image + jnp.where(slab < slabs - 1, parts[g, after, 0], 0.0)
            at = pl.multiple_of(slab * cells, cells)
            rows_ref[pl.ds(g * probes, probes), pl.ds(at, cells)] = image
            return carry

        lax.fori_loop(0, slabs, gather, 0, unroll=True if slabs <= 16 else 8)
    total = slabs * cells
    rows = rows_ref[...]
    upper_one, inverse_one = eliminate(dot_nt(rows, rows) / total)
    basis = dot_nn(inverse_one, rows)
    rows_ref[...] = basis
    upper_two, inverse_two = eliminate(dot_nt(basis, basis) / total)
    mine = rows_ref[:, pl.ds(pl.multiple_of(place[1] * cells, cells), cells)]
    q_ref[...] = dot_nn(inverse_two, mine)
    for g in range(groups):

        @pl.when(place[0] == g)
        def _():
            q_out[:, 0, :] = q_ref[pl.ds(g * probes, probes), :]

    r = lax.broadcasted_iota(jnp.int32, (count, count), 0)
    c = lax.broadcasted_iota(jnp.int32, (count, count), 1)
    lower_one = dot_nt(jnp.where(r == c, 1.0, 0.0), upper_one)
    lower_out[...] = dot_nt(lower_one, upper_two)


def shards(probe_dirs, log_param, background, site_class, trap_density):
    probes = probe_dirs.shape[0]
    cells = probe_dirs.shape[2]
    planes, rows, columns = background.shape
    slabs = lax.axis_size("space")
    groups = lax.axis_size("probe")
    at_space = lax.axis_index("space")
    vmem = pl.BlockSpec(memory_space=pltpu.VMEM)
    smem = pl.BlockSpec(memory_space=pltpu.SMEM)
    hbm = pl.BlockSpec(memory_space=pl.ANY)

    coarse = jnp.concatenate(
        [probe_dirs[:, 0], log_param, jnp.zeros((7 - probes, cells), jnp.float32)], axis=0
    )
    tail = jnp.pad(coarse, ((0, 0), (0, columns - cells)))

    def packet(z):
        return jnp.concatenate(
            [
                background[z : z + HALO].reshape(HALO * rows, columns),
                site_class[z : z + HALO].reshape(HALO * rows, columns).astype(jnp.float32),
                tail,
            ],
            axis=0,
        )

    up = [(i, i + 1) for i in range(slabs - 1)]
    down = [(j, i) for i, j in up]
    high = lax.ppermute(packet(0), "space", down)
    low = lax.ppermute(packet(planes - HALO), "space", up)
    edge = jnp.stack([at_space > 0, at_space < slabs - 1]).astype(jnp.int32)

    total = planes + 2 * HALO
    chunks, folds = columns // LANES, rows // 8
    tiles = chunks * folds
    own_shape = jax.ShapeDtypeStruct((planes, tiles, 8, LANES), jnp.float32)
    own_coef, own_src, order = pl.pallas_call(
        functools.partial(prepare_kernel, probes),
        out_shape=(
            own_shape,
            own_shape,
            jax.ShapeDtypeStruct((columns, columns), jnp.bfloat16),
        ),
        in_specs=[smem, vmem, vmem, vmem],
        out_specs=(vmem, vmem, vmem),
        scratch_shapes=[
            pltpu.VMEM((chunks, planes * rows, LANES), jnp.float32),
            pltpu.VMEM((chunks, planes * rows, LANES), jnp.float32),
        ],
        compiler_params=pltpu.CompilerParams(vmem_limit_bytes=32 * 2**20),
        cost_estimate=pl.CostEstimate(flops=10**9, bytes_accessed=2**22, transcendentals=256),
        name="prepare",
    )(trap_density, background, site_class, coarse)

    images = pl.pallas_call(
        functools.partial(image_kernel, probes, rows),
        out_shape=jax.ShapeDtypeStruct((groups * slabs, 3, probes, cells), jnp.float32),
        in_specs=[smem, smem, hbm, hbm] + [vmem] * 4,
        out_specs=vmem,
        scratch_shapes=[
            pltpu.VMEM((total, tiles, 8, LANES), jnp.float32),
            pltpu.VMEM((total, tiles, 8, LANES), jnp.float32),
            pltpu.VMEM((2 * total - 1, probes, tiles, 8, LANES), jnp.float32),
            pltpu.VMEM((chunks, 2 * HALO * rows, LANES), jnp.float32),
            pltpu.VMEM((chunks, 2 * HALO * rows, LANES), jnp.float32),
            pltpu.SemaphoreType.DMA((2,)),
        ],
        compiler_params=pltpu.CompilerParams(vmem_limit_bytes=48 * 2**20),
        name="images",
    )(edge, trap_density, own_coef, own_src, order, low, high, coarse)

    every = lax.all_to_all(images, ("probe", "space"), split_axis=0, concat_axis=0, tiled=True)
    every = every.reshape((groups, slabs, 3, probes, cells))
    place = jnp.stack([lax.axis_index("probe"), at_space]).astype(jnp.int32)
    return pl.pallas_call(
        factor_kernel,
        out_shape=(
            jax.ShapeDtypeStruct((probes, 1, cells), jnp.float32),
            jax.ShapeDtypeStruct((groups * probes, groups * probes), jnp.float32),
        ),
        in_specs=[smem, vmem],
        out_specs=(vmem, vmem),
        scratch_shapes=[
            pltpu.VMEM((groups * probes, slabs * cells), jnp.float32),
            pltpu.VMEM((groups * probes, cells), jnp.float32),
        ],
        compiler_params=pltpu.CompilerParams(vmem_limit_bytes=48 * 2**20),
        name="factor",
    )(place, every)


def solution(mesh):
    placed = (
        P("probe", "space", None),
        P("space", None),
        P("space", None, None),
        P("space", None, None),
        P(),
    )
    return jax.shard_map(
        shards,
        mesh=mesh,
        in_specs=placed,
        out_specs=(P("probe", "space", None), P()),
        check_vma=False,
    )
```

```python
import functools

import jax
import jax.numpy as jnp
from jax import lax
from jax.experimental import pallas as pl
from jax.experimental.pallas import tpu as pltpu
from jax.sharding import PartitionSpec as P

PX = 64
PY = 4
REF = 8
STEP = 0.12
HALO = 3
LANES = 128
HIGHEST = lax.Precision.HIGHEST


def dot_nn(a, b):
    return lax.dot_general(
        a, b, (((1,), (0,)), ((), ())), precision=HIGHEST, preferred_element_type=jnp.float32
    )


def dot_nt(a, b):
    return lax.dot_general(
        a, b, (((1,), (1,)), ((), ())), precision=HIGHEST, preferred_element_type=jnp.float32
    )


def parts_of(x):
    first = x.astype(jnp.bfloat16)
    rest = x - first.astype(jnp.float32)
    second = rest.astype(jnp.bfloat16)
    third = (rest - second.astype(jnp.float32)).astype(jnp.bfloat16)
    return first, second, third


def bf16_dot(a, b):
    return jnp.dot(a, b, preferred_element_type=jnp.float32)


def interleave(values, order, split, kept):
    parts = parts_of(values) if split else (values.astype(jnp.bfloat16),)
    for k in range(kept.shape[0]):
        columns = order[:, k * LANES : (k + 1) * LANES]
        kept[k] = sum(bf16_dot(part, columns) for part in parts)


def cell_matrix(chunks):
    half = REF // chunks
    cell = lax.broadcasted_iota(jnp.int32, (PX * PY, LANES), 0) % PX
    lane = lax.broadcasted_iota(jnp.int32, (PX * PY, LANES), 1) // half
    return jnp.where(cell == lane, 1.0, 0.0).astype(jnp.float32)


def own_cells(folds):
    half = REF // folds
    sublane = lax.broadcasted_iota(jnp.int32, (8, PX * PY), 0) // half
    return lax.broadcasted_iota(jnp.int32, (8, PX * PY), 1) // PX == sublane


def prolonged(coarse, folds, chunks):
    mask = own_cells(folds)
    rows = [jnp.where(mask, coarse[n : n + 1, :], 0.0) for n in range(coarse.shape[0])]
    return dot_nn(jnp.concatenate(rows, axis=0), cell_matrix(chunks))


def prepare_kernel(
    density, background_in, sites_in, log_param_in, dirs_in,
    coef, src, wide, packet, background, sites, log_param, dirs, order, bg, site, sems,
):
    pairs = [
        (background_in, background),
        (sites_in, sites),
        (log_param_in, log_param),
        (dirs_in, dirs),
    ]
    copies = [pltpu.make_async_copy(a, b, sems.at[n]) for n, (a, b) in enumerate(pairs)]
    for copy in copies:
        copy.start()
    planes, rows, columns = background.shape
    probes = dirs.shape[0]
    chunks, folds = columns // LANES, rows // 8
    tiles = chunks * folds
    x = lax.broadcasted_iota(jnp.int32, (columns, columns), 0)
    place = lax.broadcasted_iota(jnp.int32, (columns, columns), 1)
    wanted = chunks * (place % LANES) + place // LANES
    order[...] = jnp.where(x == wanted, 1.0, 0.0).astype(jnp.bfloat16)
    copies[2].wait()
    copies[3].wait()
    coarse = [dirs[p] for p in range(probes)] + [jnp.exp(log_param[...])]
    spread = prolonged(jnp.concatenate(coarse, axis=0), folds, chunks)
    for p in range(probes):
        wide[p] = spread[8 * p : 8 * p + 8, :]
        packet[p] = spread[8 * p : 8 * p + 8, :]
    scale = spread[8 * probes :, :]
    copies[0].wait()
    interleave(background[...].reshape(planes * rows, columns), order, True, bg)
    copies[1].wait()
    interleave(
        sites[...].reshape(planes * rows, columns).astype(jnp.float32), order, False, site
    )
    for z in range(planes):
        for r in range(folds):
            for k in range(chunks):
                at = pl.ds(z * rows + r, 8, stride=folds)
                t = r * chunks + k
                trap = jnp.full((8, LANES), density[density.shape[0] - 1])
                for n in range(density.shape[0] - 2, -1, -1):
                    trap = jnp.where(site[k, at, :] == float(n), density[n], trap)
                trap = trap * scale
                weight = (1.0 / STEP - 6.0) - trap
                source = -STEP * trap * bg[k, at, :]
                coef[z * tiles + t] = weight
                src[z * tiles + t] = source
                if z < 2 * HALO:
                    packet[probes + z * tiles + t] = source
                if z < 2 * HALO - 1:
                    packet[probes + (2 * HALO + z) * tiles + t] = weight


def image_kernel(
    chunks, folds, edge, own_coef, own_src, wide, packet, out, coef, src, even, odd, sems
):
    tiles = chunks * folds
    planes = own_coef.shape[0] // tiles
    probes = wide.shape[0]
    total = planes + 2 * HALO
    zero_plane = total
    no_low, no_high = edge[0] == 0, edge[1] == 0
    lane = lax.broadcasted_iota(jnp.int32, (8, LANES), 1)
    sublane = lax.broadcasted_iota(jnp.int32, (8, LANES), 0)
    nothing = jnp.zeros((8, LANES), jnp.float32)

    far, near = 2 * HALO * tiles, (2 * HALO - 1) * tiles
    copies = [
        (own_src, src.at[pl.ds(0, planes * tiles)]),
        (own_coef, coef.at[pl.ds(0, planes * tiles)]),
        (packet.at[pl.ds(probes, far)], src.at[pl.ds(planes * tiles, far)]),
        (packet.at[pl.ds(probes + far, near)], coef.at[pl.ds(planes * tiles, near)]),
    ]
    copies = [pltpu.make_async_copy(a, b, sems.at[n]) for n, (a, b) in enumerate(copies)]
    for copy in copies:
        copy.start()
    for p in range(probes):
        for t in range(tiles):
            even[zero_plane, p, t] = nothing
            odd[zero_plane, p, t] = nothing
    for copy in copies:
        copy.wait()

    def start(spread):
        def body(z, carry):
            for t in range(tiles):
                s = src[z * tiles + t]
                for p in range(probes):
                    even[z, p, t] = s * spread[p]
            return carry

        return body

    lax.fori_loop(0, planes, start(wide), 0)
    lax.fori_loop(planes, total, start(packet), 0)

    def stencil(ref, z, down, up, emit, extra):
        for p in range(probes):
            value = [[ref[z, p, r * chunks + k] for k in range(chunks)] for r in range(folds)]
            for r in range(folds):
                for k in range(chunks):
                    t = r * chunks + k
                    if k:
                        left = value[r][k - 1]
                    else:
                        left = jnp.where(lane == 0, 0.0, pltpu.roll(value[r][chunks - 1], 1, 1))
                    if k + 1 < chunks:
                        right = value[r][k + 1]
                    else:
                        right = jnp.where(
                            lane == LANES - 1, 0.0, pltpu.roll(value[r][0], LANES - 1, 1)
                        )
                    if r:
                        before = value[r - 1][k]
                    else:
                        before = jnp.where(sublane == 0, 0.0, pltpu.roll(value[folds - 1][k], 1, 0))
                    if r + 1 < folds:
                        after = value[r + 1][k]
                    else:
                        after = jnp.where(sublane == 7, 0.0, pltpu.roll(value[0][k], 7, 0))
                    weight = coef[z * tiles + t]
                    if extra:
                        weight = weight + extra
                    above = ref[down, p, t] + ref[up, p, t]
                    sides = (left + right) + (before + after)
                    emit(z, p, t, (sides + above) + weight * value[r][k])

    def low(z):
        return jnp.where(no_low, 0, z)

    def high(z):
        return jnp.where(no_high, planes, z)

    def beside(z, valid):
        first, stop = valid
        down = jnp.where(z > first, z - 1, zero_plane)
        up = jnp.where(z + 1 < stop, z + 1, zero_plane)
        return down, up

    def step(ref, to, valid, wanted, extra=0.0):
        def body(z, carry):
            def emit(z, p, t, result):
                to[z, p, t] = result

            stencil(ref, z, *beside(z, valid), emit, extra)
            return carry

        lax.fori_loop(*wanted, body, 0)

    def widen(ref, to, valid):
        first, stop = valid

        @pl.when(jnp.logical_not(no_low))
        def _():
            for p in range(probes):
                for t in range(tiles):
                    to[first - 1, p, t] = ref[first, p, t]

        @pl.when(jnp.logical_not(no_high))
        def _():
            for p in range(probes):
                for t in range(tiles):
                    to[stop, p, t] = ref[stop - 1, p, t]

    all_planes = (0, high(total))
    by_one = (low(1), high(total - 1))
    by_two = (low(2), high(total - 2))
    mine = (low(HALO), high(total - HALO))

    step(even, odd, all_planes, by_one)
    step(odd, even, by_one, by_two)
    step(even, odd, by_two, mine)
    step(odd, even, mine, mine, 1.0 / STEP)
    widen(odd, even, mine)
    step(even, odd, by_two, by_two)
    widen(even, odd, by_two)

    def last(z, carry):
        first, stop = by_two
        kept = jnp.where((z >= first) & (z < stop), z, zero_plane)
        sums = [[c] for c in carry]

        def emit(z, p, t, result):
            result = result + (1.0 / STEP**2) * even[kept, p, t]
            sums[p].append(src[z * tiles + t] * result)

        stencil(odd, z, *beside(z, by_one), emit, 0.0)
        return tuple(sum(terms[1:], terms[0]) for terms in sums)

    def outer(z, near, there):
        at = jnp.where(there, near, zero_plane)
        return tuple(
            sum(src[z * tiles + t] * odd[at, p, t] for t in range(tiles)) for p in range(probes)
        )

    first, stop = by_one
    inside = outer(0, 1, jnp.logical_not(no_low))
    inside = lax.fori_loop(first, planes, last, inside)
    above = outer(total - 1, total - 2, jnp.logical_not(no_high))
    above = lax.fori_loop(planes, stop, last, above)

    added = jnp.concatenate(inside + above, axis=0) * STEP**6
    images = dot_nt(added, cell_matrix(chunks))
    mask = own_cells(folds)
    for part in range(2):
        image = jnp.concatenate(
            [
                jnp.sum(
                    jnp.where(mask, images[8 * (part * probes + p) :][:8], 0.0),
                    axis=0,
                    keepdims=True,
                )
                for p in range(probes)
            ],
            axis=0,
        )

        def send(n, carry):
            out[n, part] = image
            return carry

        lax.fori_loop(0, out.shape[0], send, 0, unroll=8)


def eliminate(gram):
    count = gram.shape[0]
    rows = lax.broadcasted_iota(jnp.int32, (count, count), 0)
    columns = lax.broadcasted_iota(jnp.int32, (count, count), 1)
    inverse = jnp.where(rows == columns, 1.0, 0.0)
    for j in range(count - 1):
        scale = 1.0 / gram[j : j + 1, j : j + 1]
        ratio = jnp.where(rows > j, gram[:, j : j + 1] * scale, 0.0)
        gram = gram - ratio * gram[j : j + 1, :]
        inverse = inverse - ratio * inverse[j : j + 1, :]
    diagonal = jnp.sum(jnp.where(rows == columns, gram, 0.0), axis=1, keepdims=True)
    scale = 1.0 / jnp.sqrt(diagonal)
    upper = jnp.where(columns >= rows, gram, 0.0) * scale
    return upper, inverse * scale


def factor_kernel(place, parts, q_out, lower_out, rows_ref, q_ref):
    groups, slabs, _, probes, cells = parts.shape
    count = groups * probes
    for g in range(groups):

        def gather(slab, carry):
            before = jnp.maximum(slab - 1, 0)
            image = parts[g, slab, 0] + jnp.where(slab > 0, parts[g, before, 1], 0.0)
            at = pl.multiple_of(slab * cells, cells)
            rows_ref[pl.ds(g * probes, probes), pl.ds(at, cells)] = image
            return carry

        lax.fori_loop(0, slabs, gather, 0, unroll=True if slabs <= 16 else 8)
    total = slabs * cells
    rows = rows_ref[...]
    upper_one, inverse_one = eliminate(dot_nt(rows, rows) / total)
    basis = dot_nn(inverse_one, rows)
    rows_ref[...] = basis
    upper_two, inverse_two = eliminate(dot_nt(basis, basis) / total)
    mine = rows_ref[:, pl.ds(pl.multiple_of(place[1] * cells, cells), cells)]
    q_ref[...] = dot_nn(inverse_two, mine)
    for g in range(groups):

        @pl.when(place[0] == g)
        def _():
            q_out[:, 0, :] = q_ref[pl.ds(g * probes, probes), :]

    r = lax.broadcasted_iota(jnp.int32, (count, count), 0)
    c = lax.broadcasted_iota(jnp.int32, (count, count), 1)
    lower_one = dot_nt(jnp.where(r == c, 1.0, 0.0), upper_one)
    lower_out[...] = dot_nt(lower_one, upper_two)


def shards(probe_dirs, log_param, background, site_class, trap_density):
    probes = probe_dirs.shape[0]
    cells = probe_dirs.shape[2]
    planes, rows, columns = background.shape
    slabs = lax.axis_size("space")
    groups = lax.axis_size("probe")
    at_space = lax.axis_index("space")
    vmem = pl.BlockSpec(memory_space=pltpu.VMEM)
    smem = pl.BlockSpec(memory_space=pltpu.SMEM)
    hbm = pl.BlockSpec(memory_space=pltpu.HBM)
    anywhere = pl.BlockSpec(memory_space=pl.ANY)

    total = planes + 2 * HALO
    tiles = rows * columns // (8 * LANES)
    tile = (8, LANES)
    own_shape = jax.ShapeDtypeStruct((planes * tiles,) + tile, jnp.float32)
    packet_shape = jax.ShapeDtypeStruct((probes + (4 * HALO - 1) * tiles,) + tile, jnp.float32)
    row_scratch = pltpu.VMEM((columns // LANES, planes * rows, LANES), jnp.float32)
    own_coef, own_src, wide, packet = pl.pallas_call(
        prepare_kernel,
        out_shape=(
            own_shape,
            own_shape,
            jax.ShapeDtypeStruct((probes,) + tile, jnp.float32),
            packet_shape,
        ),
        in_specs=[smem, hbm, hbm, hbm, hbm],
        out_specs=(vmem,) * 4,
        scratch_shapes=[
            pltpu.VMEM(background.shape, jnp.float32),
            pltpu.VMEM(site_class.shape, jnp.int32),
            pltpu.VMEM(log_param.shape, jnp.float32),
            pltpu.VMEM(probe_dirs.shape, jnp.float32),
            pltpu.VMEM((columns, columns), jnp.bfloat16),
            row_scratch,
            row_scratch,
            pltpu.SemaphoreType.DMA((4,)),
        ],
        compiler_params=pltpu.CompilerParams(vmem_limit_bytes=48 * 2**20),
        name="prepare",
    )(trap_density, background, site_class, log_param, probe_dirs)

    down = [(i + 1, i) for i in range(slabs - 1)]
    next_packet = lax.ppermute(packet, "space", down)
    edge = jnp.stack([at_space > 0, at_space < slabs - 1]).astype(jnp.int32)
    field = pltpu.VMEM((total + 1, probes, tiles) + tile, jnp.float32)
    images = pl.pallas_call(
        functools.partial(image_kernel, columns // LANES, rows // 8),
        out_shape=jax.ShapeDtypeStruct((groups * slabs, 2, probes, cells), jnp.float32),
        in_specs=[smem, anywhere, anywhere, vmem, vmem],
        out_specs=vmem,
        scratch_shapes=[
            pltpu.VMEM((total * tiles,) + tile, jnp.float32),
            pltpu.VMEM((total * tiles,) + tile, jnp.float32),
            field,
            field,
            pltpu.SemaphoreType.DMA((4,)),
        ],
        compiler_params=pltpu.CompilerParams(vmem_limit_bytes=48 * 2**20),
        name="images",
    )(edge, own_coef, own_src, wide, next_packet)

    every = lax.all_to_all(images, ("probe", "space"), split_axis=0, concat_axis=0, tiled=True)
    every = every.reshape((groups, slabs, 2, probes, cells))
    place = jnp.stack([lax.axis_index("probe"), at_space]).astype(jnp.int32)
    return pl.pallas_call(
        factor_kernel,
        out_shape=(
            jax.ShapeDtypeStruct((probes, 1, cells), jnp.float32),
            jax.ShapeDtypeStruct((groups * probes, groups * probes), jnp.float32),
        ),
        in_specs=[smem, vmem],
        out_specs=(vmem, vmem),
        scratch_shapes=[
            pltpu.VMEM((groups * probes, slabs * cells), jnp.float32),
            pltpu.VMEM((groups * probes, cells), jnp.float32),
        ],
        compiler_params=pltpu.CompilerParams(vmem_limit_bytes=48 * 2**20),
        name="factor",
    )(place, every)


def solution(mesh):
    placed = (
        P("probe", "space", None),
        P("space", None),
        P("space", None, None),
        P("space", None, None),
        P(),
    )
    return jax.shard_map(
        shards,
        mesh=mesh,
        in_specs=placed,
        out_specs=(P("probe", "space", None), P()),
        check_vma=False,
    )
```

```python
import functools

import jax
import jax.numpy as jnp
from jax import lax
from jax.experimental import pallas as pl
from jax.experimental.pallas import tpu as pltpu
from jax.sharding import PartitionSpec as P

PX = 64
PY = 4
REF = 8
STEP = 0.12
HALO = 3
LANES = 128
HIGHEST = lax.Precision.HIGHEST


def dot_nn(a, b):
    return lax.dot_general(
        a, b, (((1,), (0,)), ((), ())), precision=HIGHEST, preferred_element_type=jnp.float32
    )


def dot_nt(a, b):
    return lax.dot_general(
        a, b, (((1,), (1,)), ((), ())), precision=HIGHEST, preferred_element_type=jnp.float32
    )


def parts_of(x):
    first = x.astype(jnp.bfloat16)
    rest = x - first.astype(jnp.float32)
    second = rest.astype(jnp.bfloat16)
    third = (rest - second.astype(jnp.float32)).astype(jnp.bfloat16)
    return first, second, third


def bf16_dot(a, b):
    return jnp.dot(a, b, preferred_element_type=jnp.float32)


def interleave(values, order, split, kept):
    parts = parts_of(values) if split else (values.astype(jnp.bfloat16),)
    for k in range(kept.shape[0]):
        columns = order[:, k * LANES : (k + 1) * LANES]
        kept[k] = sum(bf16_dot(part, columns) for part in parts)


def cell_matrix(chunks):
    half = REF // chunks
    cell = lax.broadcasted_iota(jnp.int32, (PX * PY, LANES), 0) % PX
    lane = lax.broadcasted_iota(jnp.int32, (PX * PY, LANES), 1) // half
    return jnp.where(cell == lane, 1.0, 0.0).astype(jnp.float32)


def own_cells(folds):
    half = REF // folds
    sublane = lax.broadcasted_iota(jnp.int32, (8, PX * PY), 0) // half
    return lax.broadcasted_iota(jnp.int32, (8, PX * PY), 1) // PX == sublane


def prolonged(coarse, folds, chunks):
    mask = own_cells(folds)
    rows = [jnp.where(mask, coarse[n : n + 1, :], 0.0) for n in range(coarse.shape[0])]
    return dot_nn(jnp.concatenate(rows, axis=0), cell_matrix(chunks))


def prepare_kernel(
    density, background_in, sites_in, log_param_in, dirs_in,
    coef, src, wide, packet, background, sites, log_param, dirs, order, bg, site, sems,
):
    pairs = [
        (background_in, background),
        (sites_in, sites),
        (log_param_in, log_param),
        (dirs_in, dirs),
    ]
    copies = [pltpu.make_async_copy(a, b, sems.at[n]) for n, (a, b) in enumerate(pairs)]
    for copy in copies:
        copy.start()
    planes, rows, columns = background.shape
    probes = dirs.shape[0]
    chunks, folds = columns // LANES, rows // 8
    tiles = chunks * folds
    x = lax.broadcasted_iota(jnp.int32, (columns, columns), 0)
    place = lax.broadcasted_iota(jnp.int32, (columns, columns), 1)
    wanted = chunks * (place % LANES) + place // LANES
    order[...] = jnp.where(x == wanted, 1.0, 0.0).astype(jnp.bfloat16)
    copies[2].wait()
    copies[3].wait()
    coarse = [dirs[p] for p in range(probes)] + [jnp.exp(log_param[...])]
    spread = prolonged(jnp.concatenate(coarse, axis=0), folds, chunks)
    for p in range(probes):
        wide[p] = spread[8 * p : 8 * p + 8, :]
        packet[p] = spread[8 * p : 8 * p + 8, :]
    scale = spread[8 * probes :, :]
    copies[0].wait()
    interleave(background[...].reshape(planes * rows, columns), order, True, bg)
    copies[1].wait()
    interleave(
        sites[...].reshape(planes * rows, columns).astype(jnp.float32), order, False, site
    )
    for z in range(planes):
        for r in range(folds):
            for k in range(chunks):
                at = pl.ds(z * rows + r, 8, stride=folds)
                t = r * chunks + k
                trap = jnp.full((8, LANES), density[density.shape[0] - 1])
                for n in range(density.shape[0] - 2, -1, -1):
                    trap = jnp.where(site[k, at, :] == float(n), density[n], trap)
                trap = trap * scale
                weight = (1.0 / STEP - 6.0) - trap
                source = -STEP * trap * bg[k, at, :]
                coef[z * tiles + t] = weight
                src[z * tiles + t] = source
                if z < 2 * HALO:
                    packet[probes + z * tiles + t] = source
                if z < 2 * HALO - 1:
                    packet[probes + (2 * HALO + z) * tiles + t] = weight


def image_kernel(
    chunks, folds, edge, own_coef, own_src, own_wide, packet, out,
    coef, src, wide, even, odd, sems,
):
    tiles = chunks * folds
    planes = own_coef.shape[0] // tiles
    probes = own_wide.shape[0]
    total = planes + 2 * HALO
    zero_plane = total
    no_low, no_high = edge[0] == 0, edge[1] == 0
    lane = lax.broadcasted_iota(jnp.int32, (8, LANES), 1)
    sublane = lax.broadcasted_iota(jnp.int32, (8, LANES), 0)
    nothing = jnp.zeros((8, LANES), jnp.float32)

    far, near = 2 * HALO * tiles, (2 * HALO - 1) * tiles
    copies = [
        (own_src, src.at[pl.ds(0, planes * tiles)]),
        (own_coef, coef.at[pl.ds(0, planes * tiles)]),
        (own_wide, wide.at[pl.ds(0, probes)]),
        (packet.at[pl.ds(0, probes)], wide.at[pl.ds(probes, probes)]),
        (packet.at[pl.ds(probes, far)], src.at[pl.ds(planes * tiles, far)]),
        (packet.at[pl.ds(probes + far, near)], coef.at[pl.ds(planes * tiles, near)]),
    ]
    copies = [pltpu.make_async_copy(a, b, sems.at[n]) for n, (a, b) in enumerate(copies)]
    for copy in copies:
        copy.start()
    for t in range(tiles):
        src[zero_plane * tiles + t] = nothing
        coef[(total - 1) * tiles + t] = nothing
        for p in range(probes):
            even[zero_plane, p, t] = nothing
            odd[zero_plane, p, t] = nothing
    for copy in copies:
        copy.wait()

    def from_left(x):
        return jnp.where(lane == 0, 0.0, pltpu.roll(x, 1, 1))

    def from_right(x):
        return jnp.where(lane == LANES - 1, 0.0, pltpu.roll(x, LANES - 1, 1))

    def from_before(x):
        return jnp.where(sublane == 0, 0.0, pltpu.roll(x, 1, 0))

    def from_after(x):
        return jnp.where(sublane == 7, 0.0, pltpu.roll(x, 7, 0))

    def low(z):
        return jnp.where(no_low, 0, z)

    def high(z):
        return jnp.where(no_high, planes, z)

    def first_step(part, other):
        own = [wide[part * probes + p] for p in range(probes)]
        shifted = [[f(x) for x in own] for f in (from_left, from_right, from_before, from_after)]
        beyond = [wide[(1 - part) * probes + p] for p in range(probes)] if other else []

        def body(z, carry):
            down = jnp.where(z > 0, z - 1, zero_plane) * tiles
            up = (z + 1) * tiles
            s = [[src[z * tiles + r * chunks + k] for k in range(chunks)] for r in range(folds)]
            for r in range(folds):
                for k in range(chunks):
                    t = r * chunks + k
                    total = coef[z * tiles + t] * s[r][k]
                    outer = []
                    for there, value, turn, kind in (
                        (k > 0, s[r][k - 1], (1, 1), 0),
                        (k + 1 < chunks, s[r][(k + 1) % chunks], (LANES - 1, 1), 1),
                        (r > 0, s[r - 1][k], (1, 0), 2),
                        (r + 1 < folds, s[(r + 1) % folds][k], (7, 0), 3),
                    ):
                        if there:
                            total = total + value
                        else:
                            outer.append((pltpu.roll(value, *turn), shifted[kind]))
                    for name, value in (("down", src[down + t]), ("up", src[up + t])):
                        if name == other:
                            outer.append((value, beyond))
                        else:
                            total = total + value
                    for p in range(probes):
                        result = total * own[p]
                        for value, factor in outer:
                            result = result + value * factor[p]
                        odd[z, p, t] = result
            return carry

        return body

    def stencil(ref, valid, z, emit, extra):
        first, stop = valid

        def at(z):
            return jnp.where((z >= first) & (z < stop), z, zero_plane)

        down, here, there, up = at(z - 1), at(z), at(z + 1), at(z + 2)
        for p in range(probes):
            pair = [[ref[plane, p, t] for t in range(tiles)] for plane in (here, there)]
            for r in range(folds):
                for k in range(chunks):
                    t = r * chunks + k
                    for n, value in enumerate(pair):
                        left = value[t - 1] if k else from_left(value[t + chunks - 1])
                        right = value[t + 1] if k + 1 < chunks else from_right(value[t + 1 - chunks])
                        before = value[t - chunks] if r else from_before(value[t + tiles - chunks])
                        after = (
                            value[t + chunks] if r + 1 < folds else from_after(value[t + chunks - tiles])
                        )
                        above = pair[1 - n][t] + (ref[up, p, t] if n else ref[down, p, t])
                        weight = coef[(z + n) * tiles + t]
                        if extra:
                            weight = weight + extra
                        sides = (left + right) + (before + after)
                        emit(z + n, p, t, (sides + above) + weight * value[t])

    def step(ref, to, valid, wanted, extra=0.0):
        start, stop = wanted

        def body(n, carry):
            def emit(z, p, t, result):
                to[z, p, t] = result

            stencil(ref, valid, jnp.minimum(start + 2 * n, stop - 2), emit, extra)
            return carry

        lax.fori_loop(0, (stop - start + 1) // 2, body, 0)

    def widen(ref, to, valid):
        first, stop = valid

        @pl.when(jnp.logical_not(no_low))
        def _():
            for p in range(probes):
                for t in range(tiles):
                    to[first - 1, p, t] = ref[first, p, t]

        @pl.when(jnp.logical_not(no_high))
        def _():
            for p in range(probes):
                for t in range(tiles):
                    to[stop, p, t] = ref[stop - 1, p, t]

    by_one = (low(1), high(total - 1))
    by_two = (low(2), high(total - 2))
    mine = (low(HALO), high(total - HALO))

    lax.fori_loop(low(1), planes - 1, first_step(0, None), 0)
    first_step(0, "up")(planes - 1, 0)

    @pl.when(jnp.logical_not(no_high))
    def _():
        first_step(1, "down")(planes, 0)
        lax.fori_loop(planes + 1, total - 1, first_step(1, None), 0)

    step(odd, even, by_one, by_two)
    step(even, odd, by_two, mine)
    step(odd, even, mine, mine, 1.0 / STEP)
    widen(odd, even, mine)
    step(even, odd, by_two, by_two)
    widen(even, odd, by_two)

    def last(start):
        def body(n, carry):
            z = start + 2 * n
            first, stop = by_two
            sums = [[c] for c in carry]

            def emit(z, p, t, result):
                kept = jnp.where((z >= first) & (z < stop), z, zero_plane)
                result = result + (1.0 / STEP**2) * even[kept, p, t]
                sums[p].append(src[z * tiles + t] * result)

            stencil(odd, by_one, z, emit, 0.0)
            return tuple(sum(terms[1:], terms[0]) for terms in sums)

        return body

    empty = (nothing,) * probes
    inside = lax.fori_loop(0, planes // 2, last(0), empty)
    above = lax.fori_loop(0, jnp.where(no_high, 0, HALO), last(planes), empty)

    added = jnp.concatenate(inside + above, axis=0) * STEP**6
    images = dot_nt(added, cell_matrix(chunks))
    mask = own_cells(folds)
    for part in range(2):
        image = jnp.concatenate(
            [
                jnp.sum(
                    jnp.where(mask, images[8 * (part * probes + p) :][:8], 0.0),
                    axis=0,
                    keepdims=True,
                )
                for p in range(probes)
            ],
            axis=0,
        )

        def send(n, carry):
            out[n, part] = image
            return carry

        lax.fori_loop(0, out.shape[0], send, 0, unroll=8)


def eliminate(gram):
    count = gram.shape[0]
    rows = lax.broadcasted_iota(jnp.int32, (count, count), 0)
    columns = lax.broadcasted_iota(jnp.int32, (count, count), 1)
    inverse = jnp.where(rows == columns, 1.0, 0.0)
    for j in range(count - 1):
        scale = 1.0 / gram[j : j + 1, j : j + 1]
        ratio = jnp.where(rows > j, gram[:, j : j + 1] * scale, 0.0)
        gram = gram - ratio * gram[j : j + 1, :]
        inverse = inverse - ratio * inverse[j : j + 1, :]
    diagonal = jnp.sum(jnp.where(rows == columns, gram, 0.0), axis=1, keepdims=True)
    scale = 1.0 / jnp.sqrt(diagonal)
    upper = jnp.where(columns >= rows, gram, 0.0) * scale
    return upper, inverse * scale


def factor_kernel(place, parts, q_out, lower_out, rows_ref, q_ref):
    groups, slabs, _, probes, cells = parts.shape
    count = groups * probes
    for g in range(groups):

        def gather(slab, carry):
            before = jnp.maximum(slab - 1, 0)
            image = parts[g, slab, 0] + jnp.where(slab > 0, parts[g, before, 1], 0.0)
            at = pl.multiple_of(slab * cells, cells)
            rows_ref[pl.ds(g * probes, probes), pl.ds(at, cells)] = image
            return carry

        lax.fori_loop(0, slabs, gather, 0, unroll=True if slabs <= 16 else 8)
    total = slabs * cells
    rows = rows_ref[...]
    upper_one, inverse_one = eliminate(dot_nt(rows, rows) / total)
    basis = dot_nn(inverse_one, rows)
    rows_ref[...] = basis
    upper_two, inverse_two = eliminate(dot_nt(basis, basis) / total)
    mine = rows_ref[:, pl.ds(pl.multiple_of(place[1] * cells, cells), cells)]
    q_ref[...] = dot_nn(inverse_two, mine)
    for g in range(groups):

        @pl.when(place[0] == g)
        def _():
            q_out[:, 0, :] = q_ref[pl.ds(g * probes, probes), :]

    r = lax.broadcasted_iota(jnp.int32, (count, count), 0)
    c = lax.broadcasted_iota(jnp.int32, (count, count), 1)
    lower_one = dot_nt(jnp.where(r == c, 1.0, 0.0), upper_one)
    lower_out[...] = dot_nt(lower_one, upper_two)


def shards(probe_dirs, log_param, background, site_class, trap_density):
    probes = probe_dirs.shape[0]
    cells = probe_dirs.shape[2]
    planes, rows, columns = background.shape
    slabs = lax.axis_size("space")
    groups = lax.axis_size("probe")
    at_space = lax.axis_index("space")
    vmem = pl.BlockSpec(memory_space=pltpu.VMEM)
    smem = pl.BlockSpec(memory_space=pltpu.SMEM)
    hbm = pl.BlockSpec(memory_space=pltpu.HBM)
    anywhere = pl.BlockSpec(memory_space=pl.ANY)

    total = planes + 2 * HALO
    tiles = rows * columns // (8 * LANES)
    tile = (8, LANES)
    own_shape = jax.ShapeDtypeStruct((planes * tiles,) + tile, jnp.float32)
    packet_shape = jax.ShapeDtypeStruct((probes + (4 * HALO - 1) * tiles,) + tile, jnp.float32)
    row_scratch = pltpu.VMEM((columns // LANES, planes * rows, LANES), jnp.float32)
    own_coef, own_src, wide, packet = pl.pallas_call(
        prepare_kernel,
        out_shape=(
            own_shape,
            own_shape,
            jax.ShapeDtypeStruct((probes,) + tile, jnp.float32),
            packet_shape,
        ),
        in_specs=[smem, hbm, hbm, hbm, hbm],
        out_specs=(vmem,) * 4,
        scratch_shapes=[
            pltpu.VMEM(background.shape, jnp.float32),
            pltpu.VMEM(site_class.shape, jnp.int32),
            pltpu.VMEM(log_param.shape, jnp.float32),
            pltpu.VMEM(probe_dirs.shape, jnp.float32),
            pltpu.VMEM((columns, columns), jnp.bfloat16),
            row_scratch,
            row_scratch,
            pltpu.SemaphoreType.DMA((4,)),
        ],
        compiler_params=pltpu.CompilerParams(vmem_limit_bytes=62 * 2**20),
        name="prepare",
    )(trap_density, background, site_class, log_param, probe_dirs)

    down = [(i + 1, i) for i in range(slabs - 1)]
    next_packet = lax.ppermute(packet, "space", down)
    edge = jnp.stack([at_space > 0, at_space < slabs - 1]).astype(jnp.int32)
    field = pltpu.VMEM((total + 1, probes, tiles) + tile, jnp.float32)
    images = pl.pallas_call(
        functools.partial(image_kernel, columns // LANES, rows // 8),
        out_shape=jax.ShapeDtypeStruct((groups * slabs, 2, probes, cells), jnp.float32),
        in_specs=[smem] + [anywhere] * 4,
        out_specs=vmem,
        scratch_shapes=[
            pltpu.VMEM((total * tiles,) + tile, jnp.float32),
            pltpu.VMEM(((total + 1) * tiles,) + tile, jnp.float32),
            pltpu.VMEM((2 * probes,) + tile, jnp.float32),
            field,
            field,
            pltpu.SemaphoreType.DMA((6,)),
        ],
        compiler_params=pltpu.CompilerParams(vmem_limit_bytes=48 * 2**20),
        name="images",
    )(edge, own_coef, own_src, wide, next_packet)

    every = lax.all_to_all(images, ("probe", "space"), split_axis=0, concat_axis=0, tiled=True)
    every = every.reshape((groups, slabs, 2, probes, cells))
    place = jnp.stack([lax.axis_index("probe"), at_space]).astype(jnp.int32)
    return pl.pallas_call(
        factor_kernel,
        out_shape=(
            jax.ShapeDtypeStruct((probes, 1, cells), jnp.float32),
            jax.ShapeDtypeStruct((groups * probes, groups * probes), jnp.float32),
        ),
        in_specs=[smem, vmem],
        out_specs=(vmem, vmem),
        scratch_shapes=[
            pltpu.VMEM((groups * probes, slabs * cells), jnp.float32),
            pltpu.VMEM((groups * probes, cells), jnp.float32),
        ],
        compiler_params=pltpu.CompilerParams(vmem_limit_bytes=48 * 2**20),
        name="factor",
    )(place, every)


def solution(mesh):
    placed = (
        P("probe", "space", None),
        P("space", None),
        P("space", None, None),
        P("space", None, None),
        P(),
    )
    return jax.shard_map(
        shards,
        mesh=mesh,
        in_specs=placed,
        out_specs=(P("probe", "space", None), P()),
        check_vma=False,
    )
```

```python
import functools

import jax
import jax.numpy as jnp
from jax import lax
from jax.experimental import pallas as pl
from jax.experimental.pallas import tpu as pltpu
from jax.sharding import PartitionSpec as P

PX = 64
PY = 4
REF = 8
STEP = 0.12
HALO = 3
LANES = 128
HIGHEST = lax.Precision.HIGHEST


def dot_nn(a, b):
    return lax.dot_general(
        a, b, (((1,), (0,)), ((), ())), precision=HIGHEST, preferred_element_type=jnp.float32
    )


def dot_nt(a, b):
    return lax.dot_general(
        a, b, (((1,), (1,)), ((), ())), precision=HIGHEST, preferred_element_type=jnp.float32
    )


def parts_of(x):
    first = x.astype(jnp.bfloat16)
    rest = x - first.astype(jnp.float32)
    second = rest.astype(jnp.bfloat16)
    third = (rest - second.astype(jnp.float32)).astype(jnp.bfloat16)
    return first, second, third


def bf16_dot(a, b):
    return jnp.dot(a, b, preferred_element_type=jnp.float32)


def interleave(values, order, split, kept):
    parts = parts_of(values) if split else (values.astype(jnp.bfloat16),)
    for k in range(kept.shape[0]):
        columns = order[:, k * LANES : (k + 1) * LANES]
        kept[k] = sum(bf16_dot(part, columns) for part in parts)


def cell_matrix(chunks):
    half = REF // chunks
    cell = lax.broadcasted_iota(jnp.int32, (PX * PY, LANES), 0) % PX
    lane = lax.broadcasted_iota(jnp.int32, (PX * PY, LANES), 1) // half
    return jnp.where(cell == lane, 1.0, 0.0).astype(jnp.float32)


def own_cells(folds):
    half = REF // folds
    sublane = lax.broadcasted_iota(jnp.int32, (8, PX * PY), 0) // half
    return lax.broadcasted_iota(jnp.int32, (8, PX * PY), 1) // PX == sublane


def prolonged(coarse, folds, chunks):
    mask = own_cells(folds)
    rows = [jnp.where(mask, coarse[n : n + 1, :], 0.0) for n in range(coarse.shape[0])]
    return dot_nn(jnp.concatenate(rows, axis=0), cell_matrix(chunks))


def cell_order(columns, chunks):
    x = lax.broadcasted_iota(jnp.int32, (columns, columns), 0)
    place = lax.broadcasted_iota(jnp.int32, (columns, columns), 1)
    wanted = chunks * (place % LANES) + place // LANES
    return jnp.where(x == wanted, 1.0, 0.0).astype(jnp.bfloat16)


def spread_cells(dirs, log_param, folds, chunks):
    probes = dirs.shape[0]
    coarse = [dirs[p] for p in range(probes)] + [jnp.exp(log_param[...])]
    spread = prolonged(jnp.concatenate(coarse, axis=0), folds, chunks)
    return [spread[8 * n : 8 * n + 8, :] for n in range(probes + 1)]


def weights_and_sources(density, scale, background, sites, planes, order, bg, site, store):
    first, count = planes
    rows, columns = background.shape[1:]
    chunks, folds = columns // LANES, rows // 8
    at = pl.ds(first, count)
    cells = (count * rows, columns)
    interleave(background[at].reshape(cells), order, True, bg.at[:, pl.ds(0, count * rows)])
    interleave(
        sites[at].reshape(cells).astype(jnp.float32),
        order,
        False,
        site.at[:, pl.ds(0, count * rows)],
    )
    for z in range(count):
        for r in range(folds):
            for k in range(chunks):
                row = pl.ds(z * rows + r, 8, stride=folds)
                kind = site[k, row, :]
                trap = jnp.full((8, LANES), density[density.shape[0] - 1])
                for n in range(density.shape[0] - 2, -1, -1):
                    trap = jnp.where(kind == float(n), density[n], trap)
                trap = trap * scale
                weight = (1.0 / STEP - 6.0) - trap
                store(first + z, r * chunks + k, weight, -STEP * trap * bg[k, row, :])


def packet_kernel(
    density, background_in, sites_in, log_param_in, dirs_in, packet,
    background, sites, log_param, dirs, order, bg, site, made, sems, out_sems,
):
    rows, columns = background.shape[1:]
    chunks, folds = columns // LANES, rows // 8
    tiles = chunks * folds
    probes = dirs.shape[0]
    halves = [(0, HALO), (HALO, HALO)]
    copies = [(log_param_in, log_param), (dirs_in, dirs)]
    for first, count in halves:
        at = pl.ds(first, count)
        copies += [(background_in.at[at], background.at[at]), (sites_in.at[at], sites.at[at])]
    copies = [pltpu.make_async_copy(a, b, sems.at[n]) for n, (a, b) in enumerate(copies)]
    for copy in copies:
        copy.start()
    order[...] = cell_order(columns, chunks)
    copies[0].wait()
    copies[1].wait()
    spread = spread_cells(dirs, log_param, folds, chunks)
    for p in range(probes):
        made[p] = spread[p]

    def store(z, t, weight, source):
        made[probes + z * tiles + t] = source
        if z < 2 * HALO - 1:
            made[probes + (2 * HALO + z) * tiles + t] = weight

    first_weight = probes + 2 * HALO * tiles
    ranges = [
        [(0, probes + HALO * tiles), (first_weight, HALO * tiles)],
        [(probes + HALO * tiles, HALO * tiles), (first_weight + HALO * tiles, (HALO - 1) * tiles)],
    ]
    sent = []
    for n, half in enumerate(halves):
        copies[2 + 2 * n].wait()
        copies[3 + 2 * n].wait()
        weights_and_sources(
            density, spread[probes], background, sites, half, order, bg, site, store
        )
        for start, length in ranges[n]:
            at = pl.ds(start, length)
            copy = pltpu.make_async_copy(made.at[at], packet.at[at], out_sems.at[len(sent)])
            copy.start()
            sent.append(copy)
    for copy in sent:
        copy.wait()


class Steps:
    def __init__(self, chunks, folds, probes, zero_plane, coef, src):
        self.chunks, self.folds, self.tiles = chunks, folds, chunks * folds
        self.probes, self.zero_plane = probes, zero_plane
        self.coef, self.src = coef, src
        self.lane = lax.broadcasted_iota(jnp.int32, (8, LANES), 1)
        self.sublane = lax.broadcasted_iota(jnp.int32, (8, LANES), 0)

    def clear(self, *fields):
        nothing = jnp.zeros((8, LANES), jnp.float32)
        for t in range(self.tiles):
            for field in fields:
                for p in range(self.probes):
                    field[self.zero_plane, p, t] = nothing

    def from_left(self, x):
        return jnp.where(self.lane == 0, 0.0, pltpu.roll(x, 1, 1))

    def from_right(self, x):
        return jnp.where(self.lane == LANES - 1, 0.0, pltpu.roll(x, LANES - 1, 1))

    def from_before(self, x):
        return jnp.where(self.sublane == 0, 0.0, pltpu.roll(x, 1, 0))

    def from_after(self, x):
        return jnp.where(self.sublane == 7, 0.0, pltpu.roll(x, 7, 0))

    def first(self, own, to, other=None, beyond=()):
        chunks, folds, tiles = self.chunks, self.folds, self.tiles
        src, coef = self.src, self.coef
        turns = (self.from_left, self.from_right, self.from_before, self.from_after)
        shifted = [[f(x) for x in own] for f in turns]

        def body(z, carry):
            down = jnp.where(z > 0, z - 1, self.zero_plane) * tiles
            up = (z + 1) * tiles
            s = [[src[z * tiles + r * chunks + k] for k in range(chunks)] for r in range(folds)]
            for r in range(folds):
                for k in range(chunks):
                    t = r * chunks + k
                    same = coef[z * tiles + t] * s[r][k]
                    outer = []
                    for there, value, turn, kind in (
                        (k > 0, s[r][k - 1], (1, 1), 0),
                        (k + 1 < chunks, s[r][(k + 1) % chunks], (LANES - 1, 1), 1),
                        (r > 0, s[r - 1][k], (1, 0), 2),
                        (r + 1 < folds, s[(r + 1) % folds][k], (7, 0), 3),
                    ):
                        if there:
                            same = same + value
                        else:
                            outer.append((pltpu.roll(value, *turn), shifted[kind]))
                    for name, value in (("down", src[down + t]), ("up", src[up + t])):
                        if name == other:
                            outer.append((value, beyond))
                        else:
                            same = same + value
                    for p in range(self.probes):
                        result = same * own[p]
                        for value, factor in outer:
                            result = result + value * factor[p]
                        to[z, p, t] = result
            return carry

        return body

    def stencil(self, ref, valid, z, emit, extra):
        chunks, folds, tiles = self.chunks, self.folds, self.tiles
        first, stop = valid

        def at(z):
            return jnp.where((z >= first) & (z < stop), z, self.zero_plane)

        down, here, there, up = at(z - 1), at(z), at(z + 1), at(z + 2)
        for p in range(self.probes):
            pair = [[ref[plane, p, t] for t in range(tiles)] for plane in (here, there)]
            for r in range(folds):
                for k in range(chunks):
                    t = r * chunks + k
                    for n, value in enumerate(pair):
                        left = value[t - 1] if k else self.from_left(value[t + chunks - 1])
                        if k + 1 < chunks:
                            right = value[t + 1]
                        else:
                            right = self.from_right(value[t + 1 - chunks])
                        if r:
                            before = value[t - chunks]
                        else:
                            before = self.from_before(value[t + tiles - chunks])
                        if r + 1 < folds:
                            after = value[t + chunks]
                        else:
                            after = self.from_after(value[t + chunks - tiles])
                        above = pair[1 - n][t] + (ref[up, p, t] if n else ref[down, p, t])
                        weight = self.coef[(z + n) * tiles + t]
                        if extra:
                            weight = weight + extra
                        sides = (left + right) + (before + after)
                        emit(z + n, p, t, (sides + above) + weight * value[t])

    def step(self, ref, to, valid, wanted, extra=0.0):
        start, stop = wanted

        def body(n, carry):
            def emit(z, p, t, result):
                to[z, p, t] = result

            self.stencil(ref, valid, jnp.minimum(start + 2 * n, stop - 2), emit, extra)
            return carry

        lax.fori_loop(0, (stop - start + 1) // 2, body, 0)

    def widen(self, ref, to, valid, at_low, at_high):
        first, stop = valid

        def move(a, b):
            for p in range(self.probes):
                for t in range(self.tiles):
                    to[b, p, t] = ref[a, p, t]

        pl.when(at_low)(lambda: move(first, first - 1))
        pl.when(at_high)(lambda: move(stop - 1, stop))

    def images(self, odd, even, by_one, by_two, start, pairs, carry):
        first, stop = by_two

        def body(n, carry):
            z = start + 2 * n
            sums = [[c] for c in carry]

            def emit(z, p, t, result):
                kept = jnp.where((z >= first) & (z < stop), z, self.zero_plane)
                result = result + (1.0 / STEP**2) * even[kept, p, t]
                sums[p].append(self.src[z * self.tiles + t] * result)

            self.stencil(odd, by_one, z, emit, 0.0)
            return tuple(sum(terms[1:], terms[0]) for terms in sums)

        return lax.fori_loop(0, pairs, body, carry)

    def after_tangent(self, odd, even, mine, at_low, at_high):
        first, stop = mine
        by_two = (jnp.where(at_low, first - 1, first), jnp.where(at_high, stop + 1, stop))
        by_one = (jnp.where(at_low, first - 2, first), jnp.where(at_high, stop + 2, stop))
        self.step(odd, even, mine, mine, 1.0 / STEP)
        self.widen(odd, even, mine, at_low, at_high)
        self.step(even, odd, by_two, by_two)
        self.widen(even, odd, by_two, at_low, at_high)
        return by_one, by_two


def inner_kernel(
    edge, density, background_in, sites_in, log_param_in, dirs_in,
    coef, src, wide, kept, sums,
    background, sites, log_param, dirs, order, bg, site, even, odd, sems,
):
    planes, rows, columns = background.shape
    chunks, folds = columns // LANES, rows // 8
    tiles = chunks * folds
    probes = dirs.shape[0]
    copies = [
        (log_param_in, log_param),
        (dirs_in, dirs),
        (background_in, background),
        (sites_in, sites),
    ]
    copies = [pltpu.make_async_copy(a, b, sems.at[n]) for n, (a, b) in enumerate(copies)]
    for copy in copies:
        copy.start()
    steps = Steps(chunks, folds, probes, planes, coef, src)
    steps.clear(even, odd)
    nothing = jnp.zeros((8, LANES), jnp.float32)
    for t in range(tiles):
        src[planes * tiles + t] = nothing
    order[...] = cell_order(columns, chunks)
    for copy in copies:
        copy.wait()
    spread = spread_cells(dirs, log_param, folds, chunks)
    for p in range(probes):
        wide[p] = spread[p]

    def store(z, t, weight, source):
        coef[z * tiles + t] = weight
        src[z * tiles + t] = source

    weights_and_sources(
        density, spread[probes], background, sites, (0, planes), order, bg, site, store
    )
    at_low = edge[0] != 0

    def low(z):
        return jnp.where(at_low, z, 0)

    last = planes - HALO
    lax.fori_loop(low(1), last + 2, steps.first(spread[:probes], odd), 0)
    steps.step(odd, even, (low(1), last + 2), (low(2), last + 1))
    for n, (ref, z) in enumerate(((odd, last), (odd, last + 1), (even, last - 1), (even, last))):
        for p in range(probes):
            for t in range(tiles):
                kept[n, p, t] = ref[z, p, t]
    mine = (low(HALO), last)
    steps.step(even, odd, (low(2), last + 1), mine)
    by_one, by_two = steps.after_tangent(odd, even, mine, at_low, True)
    empty = (nothing,) * probes
    result = steps.images(odd, even, by_one, by_two, 0, planes // 2, empty)
    for p in range(probes):
        sums[p] = result[p]


def outer_kernel(
    chunks, folds, edge, own_coef, own_src, own_wide, kept, own_sums, packet, out,
    coef, src, wide, sums, even, odd, sems,
):
    tiles = chunks * folds
    probes = own_wide.shape[0]
    total = even.shape[0] - 1
    planes = total - 2 * HALO
    steps = Steps(chunks, folds, probes, total, coef, src)
    far, near = 2 * HALO * tiles, (2 * HALO - 1) * tiles
    last = planes - HALO
    unused = (last - HALO) * tiles
    own = pl.ds(unused, planes * tiles - unused)
    copies = [
        (own_src.at[own], src.at[own]),
        (own_coef.at[own], coef.at[own]),
        (own_wide, wide.at[pl.ds(0, probes)]),
        (packet.at[pl.ds(0, probes)], wide.at[pl.ds(probes, probes)]),
        (packet.at[pl.ds(probes, far)], src.at[pl.ds(planes * tiles, far)]),
        (packet.at[pl.ds(probes + far, near)], coef.at[pl.ds(planes * tiles, near)]),
        (kept.at[pl.ds(0, 2)], odd.at[pl.ds(last, 2)]),
        (kept.at[pl.ds(2, 2)], even.at[pl.ds(last - 1, 2)]),
        (own_sums, sums),
    ]
    copies = [pltpu.make_async_copy(a, b, sems.at[n]) for n, (a, b) in enumerate(copies)]
    for copy in copies:
        copy.start()
    steps.clear(even, odd)
    nothing = jnp.zeros((8, LANES), jnp.float32)
    for t in range(tiles):
        coef[(total - 1) * tiles + t] = nothing
    for copy in copies:
        copy.wait()

    at_high = edge[1] != 0

    def high(z):
        return jnp.where(at_high, z, planes)

    mine = [wide[p] for p in range(probes)]
    beyond = [wide[probes + p] for p in range(probes)]
    steps.first(mine, odd, "up", beyond)(planes - 1, 0)

    @pl.when(at_high)
    def _():
        steps.first(beyond, odd, "down", mine)(planes, 0)
        lax.fori_loop(planes + 1, total - 1, steps.first(beyond, odd), 0)

    steps.step(odd, even, (last, high(total - 1)), (last + 1, high(total - 2)))
    mine = (last, high(total - HALO))
    steps.step(even, odd, (last - 1, high(total - 2)), mine)
    by_one, by_two = steps.after_tangent(odd, even, mine, True, at_high)
    inside = tuple(sums[p] for p in range(probes))
    start = last - HALO
    inside = steps.images(odd, even, by_one, by_two, start, HALO, inside)
    empty = (nothing,) * probes
    above = steps.images(odd, even, by_one, by_two, planes, jnp.where(at_high, HALO, 0), empty)

    added = jnp.concatenate(inside + above, axis=0) * STEP**6
    images = dot_nt(added, cell_matrix(chunks))
    mask = own_cells(folds)
    for part in range(2):
        image = jnp.concatenate(
            [
                jnp.sum(
                    jnp.where(mask, images[8 * (part * probes + p) :][:8], 0.0),
                    axis=0,
                    keepdims=True,
                )
                for p in range(probes)
            ],
            axis=0,
        )

        def send(n, carry):
            out[n, part] = image
            return carry

        lax.fori_loop(0, out.shape[0], send, 0, unroll=8)


def eliminate(gram):
    count = gram.shape[0]
    rows = lax.broadcasted_iota(jnp.int32, (count, count), 0)
    columns = lax.broadcasted_iota(jnp.int32, (count, count), 1)
    inverse = jnp.where(rows == columns, 1.0, 0.0)
    for j in range(count - 1):
        scale = 1.0 / gram[j : j + 1, j : j + 1]
        ratio = jnp.where(rows > j, gram[:, j : j + 1] * scale, 0.0)
        gram = gram - ratio * gram[j : j + 1, :]
        inverse = inverse - ratio * inverse[j : j + 1, :]
    diagonal = jnp.sum(jnp.where(rows == columns, gram, 0.0), axis=1, keepdims=True)
    scale = 1.0 / jnp.sqrt(diagonal)
    upper = jnp.where(columns >= rows, gram, 0.0) * scale
    return upper, inverse * scale


def factor_kernel(place, parts, q_out, lower_out, rows_ref, q_ref):
    groups, slabs, _, probes, cells = parts.shape
    count = groups * probes
    for g in range(groups):

        def gather(slab, carry):
            before = jnp.maximum(slab - 1, 0)
            image = parts[g, slab, 0] + jnp.where(slab > 0, parts[g, before, 1], 0.0)
            at = pl.multiple_of(slab * cells, cells)
            rows_ref[pl.ds(g * probes, probes), pl.ds(at, cells)] = image
            return carry

        lax.fori_loop(0, slabs, gather, 0, unroll=True if slabs <= 16 else 8)
    total = slabs * cells
    rows = rows_ref[...]
    upper_one, inverse_one = eliminate(dot_nt(rows, rows) / total)
    basis = dot_nn(inverse_one, rows)
    rows_ref[...] = basis
    upper_two, inverse_two = eliminate(dot_nt(basis, basis) / total)
    mine = rows_ref[:, pl.ds(pl.multiple_of(place[1] * cells, cells), cells)]
    q_ref[...] = dot_nn(inverse_two, mine)
    for g in range(groups):

        @pl.when(place[0] == g)
        def _():
            q_out[:, 0, :] = q_ref[pl.ds(g * probes, probes), :]

    r = lax.broadcasted_iota(jnp.int32, (count, count), 0)
    c = lax.broadcasted_iota(jnp.int32, (count, count), 1)
    lower_one = dot_nt(jnp.where(r == c, 1.0, 0.0), upper_one)
    lower_out[...] = dot_nt(lower_one, upper_two)


def shards(probe_dirs, log_param, background, site_class, trap_density):
    probes = probe_dirs.shape[0]
    cells = probe_dirs.shape[2]
    planes, rows, columns = background.shape
    slabs = lax.axis_size("space")
    groups = lax.axis_size("probe")
    at_space = lax.axis_index("space")
    vmem = pl.BlockSpec(memory_space=pltpu.VMEM)
    smem = pl.BlockSpec(memory_space=pltpu.SMEM)
    anywhere = pl.BlockSpec(memory_space=pl.ANY)
    params = pltpu.CompilerParams(vmem_limit_bytes=62 * 2**20)

    chunks, folds = columns // LANES, rows // 8
    tiles = chunks * folds
    total = planes + 2 * HALO
    tile = (8, LANES)

    def shape(*dims):
        return jax.ShapeDtypeStruct(dims + tile, jnp.float32)

    def scratch(*dims):
        return pltpu.VMEM(dims + tile, jnp.float32)

    def copies(count):
        return pltpu.SemaphoreType.DMA((count,))

    def inputs(held):
        return [
            pltpu.VMEM((held, rows, columns), jnp.float32),
            pltpu.VMEM((held, rows, columns), jnp.int32),
            pltpu.VMEM(log_param.shape, jnp.float32),
            pltpu.VMEM(probe_dirs.shape, jnp.float32),
            pltpu.VMEM((columns, columns), jnp.bfloat16),
        ]

    def rows_of(held):
        return pltpu.VMEM((chunks, held * rows, LANES), jnp.float32)

    size = probes + (4 * HALO - 1) * tiles
    packet = pl.pallas_call(
        packet_kernel,
        out_shape=shape(size),
        in_specs=[smem] + [anywhere] * 4,
        out_specs=anywhere,
        scratch_shapes=inputs(2 * HALO)
        + [rows_of(HALO), rows_of(HALO), scratch(size), copies(6), copies(4)],
        compiler_params=params,
        name="packet",
    )(trap_density, background, site_class, log_param, probe_dirs)

    down = [(i + 1, i) for i in range(slabs - 1)]
    next_packet = lax.ppermute(packet, "space", down)
    edge = jnp.stack([at_space > 0, at_space < slabs - 1]).astype(jnp.int32)
    own_coef, own_src, wide, kept, sums = pl.pallas_call(
        inner_kernel,
        out_shape=(
            shape(planes * tiles),
            shape((planes + 1) * tiles),
            shape(probes),
            shape(4, probes, tiles),
            shape(probes),
        ),
        in_specs=[smem, smem] + [anywhere] * 4,
        out_specs=(vmem,) * 5,
        scratch_shapes=inputs(planes)
        + [rows_of(planes), rows_of(planes)]
        + [scratch(planes + 1, probes, tiles)] * 2
        + [copies(4)],
        compiler_params=pltpu.CompilerParams(vmem_limit_bytes=28 * 2**20),
        cost_estimate=pl.CostEstimate(flops=10**9, bytes_accessed=2**24, transcendentals=256),
        name="inner",
    )(edge, trap_density, background, site_class, log_param, probe_dirs)

    images = pl.pallas_call(
        functools.partial(outer_kernel, chunks, folds),
        out_shape=jax.ShapeDtypeStruct((groups * slabs, 2, probes, cells), jnp.float32),
        in_specs=[smem] + [anywhere] * 6,
        out_specs=vmem,
        scratch_shapes=[
            scratch(total * tiles),
            scratch(total * tiles),
            scratch(2 * probes),
            scratch(probes),
            scratch(total + 1, probes, tiles),
            scratch(total + 1, probes, tiles),
            copies(9),
        ],
        compiler_params=pltpu.CompilerParams(vmem_limit_bytes=28 * 2**20),
        name="outer",
    )(edge, own_coef, own_src, wide, kept, sums, next_packet)

    every = lax.all_to_all(images, ("probe", "space"), split_axis=0, concat_axis=0, tiled=True)
    every = every.reshape((groups, slabs, 2, probes, cells))
    place = jnp.stack([lax.axis_index("probe"), at_space]).astype(jnp.int32)
    return pl.pallas_call(
        factor_kernel,
        out_shape=(
            jax.ShapeDtypeStruct((probes, 1, cells), jnp.float32),
            jax.ShapeDtypeStruct((groups * probes, groups * probes), jnp.float32),
        ),
        in_specs=[smem, vmem],
        out_specs=(vmem, vmem),
        scratch_shapes=[
            pltpu.VMEM((groups * probes, slabs * cells), jnp.float32),
            pltpu.VMEM((groups * probes, cells), jnp.float32),
        ],
        compiler_params=pltpu.CompilerParams(vmem_limit_bytes=48 * 2**20),
        name="factor",
    )(place, every)


def solution(mesh):
    placed = (
        P("probe", "space", None),
        P("space", None),
        P("space", None, None),
        P("space", None, None),
        P(),
    )
    return jax.shard_map(
        shards,
        mesh=mesh,
        in_specs=placed,
        out_specs=(P("probe", "space", None), P()),
        check_vma=False,
    )
```

```python
import functools

import jax
import jax.numpy as jnp
from jax import lax
from jax.experimental import pallas as pl
from jax.experimental.pallas import tpu as pltpu
from jax.sharding import PartitionSpec as P

PX = 64
PY = 4
REF = 8
STEP = 0.12
HALO = 3
LANES = 128
HIGHEST = lax.Precision.HIGHEST


def dot_nn(a, b):
    return lax.dot_general(
        a, b, (((1,), (0,)), ((), ())), precision=HIGHEST, preferred_element_type=jnp.float32
    )


def dot_nt(a, b):
    return lax.dot_general(
        a, b, (((1,), (1,)), ((), ())), precision=HIGHEST, preferred_element_type=jnp.float32
    )


def parts_of(x):
    first = x.astype(jnp.bfloat16)
    rest = x - first.astype(jnp.float32)
    second = rest.astype(jnp.bfloat16)
    third = (rest - second.astype(jnp.float32)).astype(jnp.bfloat16)
    return first, second, third


def bf16_dot(a, b):
    return jnp.dot(a, b, preferred_element_type=jnp.float32)


def interleave(values, order, split, kept):
    parts = parts_of(values) if split else (values.astype(jnp.bfloat16),)
    for k in range(kept.shape[0]):
        columns = order[:, k * LANES : (k + 1) * LANES]
        kept[k] = sum(bf16_dot(part, columns) for part in parts)


def cell_matrix(chunks):
    half = REF // chunks
    cell = lax.broadcasted_iota(jnp.int32, (PX * PY, LANES), 0) % PX
    lane = lax.broadcasted_iota(jnp.int32, (PX * PY, LANES), 1) // half
    return jnp.where(cell == lane, 1.0, 0.0).astype(jnp.float32)


def own_cells(folds):
    half = REF // folds
    sublane = lax.broadcasted_iota(jnp.int32, (8, PX * PY), 0) // half
    return lax.broadcasted_iota(jnp.int32, (8, PX * PY), 1) // PX == sublane


def prolonged(coarse, folds, chunks):
    mask = own_cells(folds)
    rows = [jnp.where(mask, coarse[n : n + 1, :], 0.0) for n in range(coarse.shape[0])]
    return dot_nn(jnp.concatenate(rows, axis=0), cell_matrix(chunks))


def cell_order(columns, chunks):
    x = lax.broadcasted_iota(jnp.int32, (columns, columns), 0)
    place = lax.broadcasted_iota(jnp.int32, (columns, columns), 1)
    wanted = chunks * (place % LANES) + place // LANES
    return jnp.where(x == wanted, 1.0, 0.0).astype(jnp.bfloat16)


def spread_cells(dirs, log_param, folds, chunks):
    probes = dirs.shape[0]
    coarse = [dirs[p] for p in range(probes)] + [jnp.exp(log_param[...])]
    spread = prolonged(jnp.concatenate(coarse, axis=0), folds, chunks)
    return [spread[8 * n : 8 * n + 8, :] for n in range(probes + 1)]


def weights_and_sources(density, scale, background, sites, planes, order, bg, site, store):
    first, count = planes
    rows, columns = background.shape[1:]
    chunks, folds = columns // LANES, rows // 8
    at = pl.ds(first, count)
    cells = (count * rows, columns)
    interleave(background[at].reshape(cells), order, True, bg.at[:, pl.ds(0, count * rows)])
    interleave(
        sites[at].reshape(cells).astype(jnp.float32),
        order,
        False,
        site.at[:, pl.ds(0, count * rows)],
    )
    for z in range(count):
        for r in range(folds):
            for k in range(chunks):
                row = pl.ds(z * rows + r, 8, stride=folds)
                kind = site[k, row, :]
                trap = jnp.full((8, LANES), density[density.shape[0] - 1])
                for n in range(density.shape[0] - 2, -1, -1):
                    trap = jnp.where(kind == float(n), density[n], trap)
                trap = trap * scale
                weight = (1.0 / STEP - 6.0) - trap
                store(first + z, r * chunks + k, weight, -STEP * trap * bg[k, row, :])


def packet_kernel(
    first, weights, density, background_in, sites_in, log_param_in, dirs_in, packet,
    background, sites, log_param, dirs, order, bg, site, made, sems,
):
    count, rows, columns = background.shape
    chunks, folds = columns // LANES, rows // 8
    tiles = chunks * folds
    probes = dirs.shape[0]
    at = pl.ds(first, count)
    copies = [
        (log_param_in, log_param),
        (dirs_in, dirs),
        (background_in.at[at], background),
        (sites_in.at[at], sites),
    ]
    copies = [pltpu.make_async_copy(a, b, sems.at[n]) for n, (a, b) in enumerate(copies)]
    for copy in copies:
        copy.start()
    order[...] = cell_order(columns, chunks)
    copies[0].wait()
    copies[1].wait()
    spread = spread_cells(dirs, log_param, folds, chunks)
    for p in range(probes):
        made[p] = spread[p]

    def store(z, t, weight, source):
        made[probes + z * tiles + t] = source
        if z < weights:
            made[probes + (count + z) * tiles + t] = weight

    copies[2].wait()
    copies[3].wait()
    weights_and_sources(
        density, spread[probes], background, sites, (0, count), order, bg, site, store
    )
    sent = pltpu.make_async_copy(made, packet, sems.at[4])
    sent.start()
    sent.wait()


class Steps:
    def __init__(self, chunks, folds, probes, zero_plane, coef, src):
        self.chunks, self.folds, self.tiles = chunks, folds, chunks * folds
        self.probes, self.zero_plane = probes, zero_plane
        self.coef, self.src = coef, src
        self.lane = lax.broadcasted_iota(jnp.int32, (8, LANES), 1)
        self.sublane = lax.broadcasted_iota(jnp.int32, (8, LANES), 0)

    def clear(self, *fields):
        nothing = jnp.zeros((8, LANES), jnp.float32)
        for t in range(self.tiles):
            for field in fields:
                for p in range(self.probes):
                    field[self.zero_plane, p, t] = nothing

    def from_left(self, x):
        return jnp.where(self.lane == 0, 0.0, pltpu.roll(x, 1, 1))

    def from_right(self, x):
        return jnp.where(self.lane == LANES - 1, 0.0, pltpu.roll(x, LANES - 1, 1))

    def from_before(self, x):
        return jnp.where(self.sublane == 0, 0.0, pltpu.roll(x, 1, 0))

    def from_after(self, x):
        return jnp.where(self.sublane == 7, 0.0, pltpu.roll(x, 7, 0))

    def first(self, own, to, other=None, beyond=()):
        chunks, folds, tiles = self.chunks, self.folds, self.tiles
        src, coef = self.src, self.coef
        turns = (self.from_left, self.from_right, self.from_before, self.from_after)
        shifted = [[f(x) for x in own] for f in turns]

        def body(z, carry):
            down = jnp.where(z > 0, z - 1, self.zero_plane) * tiles
            up = (z + 1) * tiles
            s = [[src[z * tiles + r * chunks + k] for k in range(chunks)] for r in range(folds)]
            for r in range(folds):
                for k in range(chunks):
                    t = r * chunks + k
                    same = coef[z * tiles + t] * s[r][k]
                    outer = []
                    for there, value, turn, kind in (
                        (k > 0, s[r][k - 1], (1, 1), 0),
                        (k + 1 < chunks, s[r][(k + 1) % chunks], (LANES - 1, 1), 1),
                        (r > 0, s[r - 1][k], (1, 0), 2),
                        (r + 1 < folds, s[(r + 1) % folds][k], (7, 0), 3),
                    ):
                        if there:
                            same = same + value
                        else:
                            outer.append((pltpu.roll(value, *turn), shifted[kind]))
                    for name, value in (("down", src[down + t]), ("up", src[up + t])):
                        if name == other:
                            outer.append((value, beyond))
                        else:
                            same = same + value
                    for p in range(self.probes):
                        result = same * own[p]
                        for value, factor in outer:
                            result = result + value * factor[p]
                        to[z, p, t] = result
            return carry

        return body

    def stencil(self, ref, valid, z, emit, extra):
        chunks, folds, tiles = self.chunks, self.folds, self.tiles
        first, stop = valid

        def at(z):
            return jnp.where((z >= first) & (z < stop), z, self.zero_plane)

        down, here, there, up = at(z - 1), at(z), at(z + 1), at(z + 2)
        for p in range(self.probes):
            pair = [[ref[plane, p, t] for t in range(tiles)] for plane in (here, there)]
            for r in range(folds):
                for k in range(chunks):
                    t = r * chunks + k
                    for n, value in enumerate(pair):
                        left = value[t - 1] if k else self.from_left(value[t + chunks - 1])
                        if k + 1 < chunks:
                            right = value[t + 1]
                        else:
                            right = self.from_right(value[t + 1 - chunks])
                        if r:
                            before = value[t - chunks]
                        else:
                            before = self.from_before(value[t + tiles - chunks])
                        if r + 1 < folds:
                            after = value[t + chunks]
                        else:
                            after = self.from_after(value[t + chunks - tiles])
                        above = pair[1 - n][t] + (ref[up, p, t] if n else ref[down, p, t])
                        weight = self.coef[(z + n) * tiles + t]
                        if extra:
                            weight = weight + extra
                        sides = (left + right) + (before + after)
                        emit(z + n, p, t, (sides + above) + weight * value[t])

    def step(self, ref, to, valid, wanted, extra=0.0):
        start, stop = wanted

        def body(n, carry):
            def emit(z, p, t, result):
                to[z, p, t] = result

            self.stencil(ref, valid, jnp.minimum(start + 2 * n, stop - 2), emit, extra)
            return carry

        lax.fori_loop(0, (stop - start + 1) // 2, body, 0)

    def widen(self, ref, to, valid, at_low, at_high):
        first, stop = valid

        def move(a, b):
            for p in range(self.probes):
                for t in range(self.tiles):
                    to[b, p, t] = ref[a, p, t]

        pl.when(at_low)(lambda: move(first, first - 1))
        pl.when(at_high)(lambda: move(stop - 1, stop))

    def images(self, m, u, by_one, by_two, span, carry, other=None):
        chunks, folds, tiles = self.chunks, self.folds, self.tiles
        src = self.src

        def at(z, valid):
            return jnp.where((z >= valid[0]) & (z < valid[1]), z, self.zero_plane)

        def body(z, carry):
            carry = [list(c) for c in carry]
            down = jnp.where(z > 0, z - 1, self.zero_plane) * tiles
            up = (z + 1) * tiles
            here, kept = at(z, by_one), at(z, by_two)
            s = [src[z * tiles + t] for t in range(tiles)]
            for t in range(tiles):
                r, k = t // chunks, t % chunks
                same = self.coef[z * tiles + t] * s[t]
                moved = []
                if k:
                    same = same + s[t - 1]
                else:
                    moved.append((2, self.from_left(s[t + chunks - 1])))
                if k + 1 < chunks:
                    same = same + s[t + 1]
                else:
                    moved.append((1, self.from_right(s[t + 1 - chunks])))
                if r:
                    same = same + s[t - chunks]
                else:
                    moved.append((4, self.from_before(s[t + tiles - chunks])))
                if r + 1 < folds:
                    same = same + s[t + chunks]
                else:
                    moved.append((3, self.from_after(s[t + chunks - tiles])))
                for name, value in (("down", src[down + t]), ("up", src[up + t])):
                    if name == other:
                        moved.append((5, value))
                    else:
                        same = same + value
                scaled = s[t] * (1.0 / STEP**2)
                for p in range(self.probes):
                    value = m[here, p, t]
                    carry[p][0] = carry[p][0] + (same * value + scaled * u[kept, p, t])
                    for n, factor in moved:
                        carry[p][n] = carry[p][n] + factor * value
            return tuple(tuple(c) for c in carry)

        if isinstance(span, int):
            return body(span, carry)
        return lax.fori_loop(*span, body, carry)

    def empty_sums(self):
        nothing = jnp.zeros((8, LANES), jnp.float32)
        return ((nothing,) * 6,) * self.probes

    def moved_sums(self, sums):
        return [
            c[0]
            + (self.from_left(c[1]) + self.from_right(c[2]))
            + (self.from_before(c[3]) + self.from_after(c[4]))
            for c in sums
        ]

    def after_tangent(self, odd, even, mine, at_low, at_high):
        first, stop = mine
        by_two = (jnp.where(at_low, first - 1, first), jnp.where(at_high, stop + 1, stop))
        by_one = (jnp.where(at_low, first - 2, first), jnp.where(at_high, stop + 2, stop))
        self.step(odd, even, mine, mine, 1.0 / STEP)
        self.widen(odd, even, mine, at_low, at_high)
        self.step(even, odd, by_two, by_two)
        self.widen(even, odd, by_two, at_low, at_high)
        return by_one, by_two


def inner_kernel(
    edge, density, background_in, sites_in, log_param_in, dirs_in,
    coef, src, wide, kept, sums,
    background, sites, log_param, dirs, order, bg, site, even, odd, sems,
):
    planes, rows, columns = background.shape
    chunks, folds = columns // LANES, rows // 8
    tiles = chunks * folds
    probes = dirs.shape[0]
    copies = [
        (log_param_in, log_param),
        (dirs_in, dirs),
        (background_in, background),
        (sites_in, sites),
    ]
    copies = [pltpu.make_async_copy(a, b, sems.at[n]) for n, (a, b) in enumerate(copies)]
    for copy in copies:
        copy.start()
    steps = Steps(chunks, folds, probes, planes, coef, src)
    steps.clear(even, odd)
    nothing = jnp.zeros((8, LANES), jnp.float32)
    for t in range(tiles):
        src[planes * tiles + t] = nothing
    order[...] = cell_order(columns, chunks)
    for copy in copies:
        copy.wait()
    spread = spread_cells(dirs, log_param, folds, chunks)
    for p in range(probes):
        wide[p] = spread[p]

    def store(z, t, weight, source):
        coef[z * tiles + t] = weight
        src[z * tiles + t] = source

    weights_and_sources(
        density, spread[probes], background, sites, (0, planes), order, bg, site, store
    )
    at_low = edge[0] != 0

    def low(z):
        return jnp.where(at_low, z, 0)

    last = planes - HALO
    lax.fori_loop(low(1), last + 2, steps.first(spread[:probes], odd), 0)
    steps.step(odd, even, (low(1), last + 2), (low(2), last + 1))
    for n, (ref, z) in enumerate(((odd, last), (odd, last + 1), (even, last - 1), (even, last))):
        for p in range(probes):
            for t in range(tiles):
                kept[n, p, t] = ref[z, p, t]
    mine = (low(HALO), last)
    steps.step(even, odd, (low(2), last + 1), mine)
    by_one, by_two = steps.after_tangent(odd, even, mine, at_low, True)
    result = steps.moved_sums(steps.images(odd, even, by_one, by_two, by_one, steps.empty_sums()))
    for p in range(probes):
        sums[p] = result[p]


def outer_kernel(
    chunks, folds, edge, own_coef, own_src, own_wide, kept, own_sums, near, far, out,
    coef, src, wide, sums, even, odd, sems,
):
    tiles = chunks * folds
    probes = own_wide.shape[0]
    total = even.shape[0] - 1
    planes = total - 2 * HALO
    steps = Steps(chunks, folds, probes, total, coef, src)
    half = HALO * tiles
    last = planes - HALO
    unused = (last - HALO) * tiles
    own = pl.ds(unused, planes * tiles - unused)
    copies = [
        (near.at[pl.ds(0, probes)], wide.at[pl.ds(probes, probes)]),
        (near.at[pl.ds(probes, half)], src.at[pl.ds(planes * tiles, half)]),
        (near.at[pl.ds(probes + half, half)], coef.at[pl.ds(planes * tiles, half)]),
        (own_wide, wide.at[pl.ds(0, probes)]),
        (own_src.at[own], src.at[own]),
        (own_coef.at[own], coef.at[own]),
        (far.at[pl.ds(probes, half)], src.at[pl.ds(planes * tiles + half, half)]),
        (
            far.at[pl.ds(probes + half, half - tiles)],
            coef.at[pl.ds(planes * tiles + half, half - tiles)],
        ),
        (kept.at[pl.ds(0, 2)], odd.at[pl.ds(last, 2)]),
        (kept.at[pl.ds(2, 2)], even.at[pl.ds(last - 1, 2)]),
        (own_sums, sums),
    ]
    copies = [pltpu.make_async_copy(a, b, sems.at[n]) for n, (a, b) in enumerate(copies)]
    for copy in copies:
        copy.start()
    steps.clear(even, odd)
    for copy in copies[:8]:
        copy.wait()

    at_high = edge[1] != 0

    def high(z):
        return jnp.where(at_high, z, planes)

    mine = [wide[p] for p in range(probes)]
    beyond = [wide[probes + p] for p in range(probes)]
    steps.first(mine, odd, "up", beyond)(planes - 1, 0)

    @pl.when(at_high)
    def _():
        steps.first(beyond, odd, "down", mine)(planes, 0)
        lax.fori_loop(planes + 1, total - 1, steps.first(beyond, odd), 0)

    for copy in copies[8:]:
        copy.wait()
    steps.step(odd, even, (last, high(total - 1)), (last + 1, high(total - 2)))
    mine = (last, high(total - HALO))
    steps.step(even, odd, (last - 1, high(total - 2)), mine)
    by_one, by_two = steps.after_tangent(odd, even, mine, True, at_high)
    start, stop = by_one
    empty = steps.empty_sums()
    inside = steps.images(odd, even, by_one, by_two, (start, planes - 1), empty)
    inside = steps.images(odd, even, by_one, by_two, planes - 1, inside, "up")
    above = [list(c) for c in empty]
    for p in range(probes):
        above[p][0] = inside[p][5]
    above = steps.images(odd, even, by_one, by_two, (planes + 1, stop), tuple(tuple(c) for c in above))
    above = steps.images(odd, even, by_one, by_two, planes, above, "down")
    inside = [x + sums[p] + above[p][5] for p, x in enumerate(steps.moved_sums(inside))]
    above = steps.moved_sums(above)

    added = jnp.concatenate(inside + above, axis=0) * STEP**6
    images = dot_nt(added, cell_matrix(chunks))
    mask = own_cells(folds)
    for part in range(2):
        image = jnp.concatenate(
            [
                jnp.sum(
                    jnp.where(mask, images[8 * (part * probes + p) :][:8], 0.0),
                    axis=0,
                    keepdims=True,
                )
                for p in range(probes)
            ],
            axis=0,
        )

        def send(n, carry):
            out[n, part] = image
            return carry

        lax.fori_loop(0, out.shape[0], send, 0, unroll=8)


def eliminate(gram):
    count = gram.shape[0]
    rows = lax.broadcasted_iota(jnp.int32, (count, count), 0)
    columns = lax.broadcasted_iota(jnp.int32, (count, count), 1)
    inverse = jnp.where(rows == columns, 1.0, 0.0)
    for j in range(count - 1):
        across = jnp.broadcast_to(gram[:, j : j + 1], (count, count))
        turned = 1.0 / across
        ratio = jnp.where(rows > j, across, 0.0)
        gram_row, inverse_row = (gram * turned)[j : j + 1, :], (inverse * turned)[j : j + 1, :]
        gram = gram - ratio * gram_row
        inverse = inverse - ratio * inverse_row
    diagonal = jnp.sum(jnp.where(rows == columns, gram, 0.0), axis=1, keepdims=True)
    scale = 1.0 / jnp.sqrt(diagonal)
    upper = jnp.where(columns >= rows, gram, 0.0) * scale
    return upper, inverse * scale


def float_parts(x):
    first = x.astype(jnp.bfloat16).astype(jnp.float32)
    rest = x - first
    second = rest.astype(jnp.bfloat16).astype(jnp.float32)
    return first, second, rest - second


def gram_of(parts, count):
    stacked = jnp.concatenate(list(parts) + [jnp.zeros_like(parts[0])], axis=0)
    stacked = stacked.astype(jnp.bfloat16)
    every = lax.dot_general(
        stacked, stacked, (((1,), (1,)), ((), ())), preferred_element_type=jnp.float32
    )
    tall = every[:count] + (every[count : 2 * count] + every[2 * count : 3 * count])
    return tall[:, :count] + (tall[:, count : 2 * count] + tall[:, 2 * count : 3 * count])


def times(a, parts):
    first, second, third = float_parts(a)
    left = jnp.concatenate([first, second, third, first, second, first], axis=1)
    right = jnp.concatenate([parts[0]] * 3 + [parts[1]] * 2 + [parts[2]], axis=0)
    return bf16_dot(left.astype(jnp.bfloat16), right.astype(jnp.bfloat16))


def factor_kernel(place, parts, q_out, lower_out, rows_ref, q_ref):
    groups, slabs, _, probes, cells = parts.shape
    count = groups * probes
    for g in range(groups):

        def gather(slab, carry):
            before = jnp.maximum(slab - 1, 0)
            image = parts[g, slab, 0] + jnp.where(slab > 0, parts[g, before, 1], 0.0)
            at = pl.multiple_of(slab * cells, cells)
            rows_ref[pl.ds(g * probes, probes), pl.ds(at, cells)] = image
            return carry

        lax.fori_loop(0, slabs, gather, 0, unroll=True if slabs <= 16 else 8)
    total = slabs * cells
    rows = rows_ref[...]
    parts_one = float_parts(rows)
    upper_one, inverse_one = eliminate(gram_of(parts_one, count) / total)
    basis = times(inverse_one, parts_one)
    rows_ref[...] = basis
    upper_two, inverse_two = eliminate(gram_of(float_parts(basis), count) / total)
    mine = rows_ref[:, pl.ds(pl.multiple_of(place[1] * cells, cells), cells)]
    q_ref[...] = dot_nn(inverse_two, mine)
    for g in range(groups):

        @pl.when(place[0] == g)
        def _():
            q_out[:, 0, :] = q_ref[pl.ds(g * probes, probes), :]

    r = lax.broadcasted_iota(jnp.int32, (count, count), 0)
    c = lax.broadcasted_iota(jnp.int32, (count, count), 1)
    lower_one = dot_nt(jnp.where(r == c, 1.0, 0.0), upper_one)
    lower_out[...] = dot_nt(lower_one, upper_two)


def shards(probe_dirs, log_param, background, site_class, trap_density):
    probes = probe_dirs.shape[0]
    cells = probe_dirs.shape[2]
    planes, rows, columns = background.shape
    slabs = lax.axis_size("space")
    groups = lax.axis_size("probe")
    at_space = lax.axis_index("space")
    vmem = pl.BlockSpec(memory_space=pltpu.VMEM)
    smem = pl.BlockSpec(memory_space=pltpu.SMEM)
    anywhere = pl.BlockSpec(memory_space=pl.ANY)
    params = pltpu.CompilerParams(vmem_limit_bytes=62 * 2**20)

    chunks, folds = columns // LANES, rows // 8
    tiles = chunks * folds
    total = planes + 2 * HALO
    tile = (8, LANES)

    def shape(*dims):
        return jax.ShapeDtypeStruct(dims + tile, jnp.float32)

    def scratch(*dims):
        return pltpu.VMEM(dims + tile, jnp.float32)

    def copies(count):
        return pltpu.SemaphoreType.DMA((count,))

    def inputs(held):
        return [
            pltpu.VMEM((held, rows, columns), jnp.float32),
            pltpu.VMEM((held, rows, columns), jnp.int32),
            pltpu.VMEM(log_param.shape, jnp.float32),
            pltpu.VMEM(probe_dirs.shape, jnp.float32),
            pltpu.VMEM((columns, columns), jnp.bfloat16),
        ]

    def rows_of(held):
        return pltpu.VMEM((chunks, held * rows, LANES), jnp.float32)

    down = [(i + 1, i) for i in range(slabs - 1)]

    def send(first, weights):
        size = probes + (HALO + weights) * tiles
        packet = pl.pallas_call(
            functools.partial(packet_kernel, first, weights),
            out_shape=shape(size),
            in_specs=[smem] + [anywhere] * 4,
            out_specs=anywhere,
            scratch_shapes=inputs(HALO)
            + [rows_of(HALO), rows_of(HALO), scratch(size), copies(5)],
            compiler_params=params,
            cost_estimate=pl.CostEstimate(flops=10**8, bytes_accessed=2**22, transcendentals=256),
            name="packet" + str(first),
        )(trap_density, background, site_class, log_param, probe_dirs)
        return lax.ppermute(packet, "space", down)

    near = send(0, HALO)
    far = send(HALO, HALO - 1)
    edge = jnp.stack([at_space > 0, at_space < slabs - 1]).astype(jnp.int32)
    own_coef, own_src, wide, kept, sums = pl.pallas_call(
        inner_kernel,
        out_shape=(
            shape(planes * tiles),
            shape((planes + 1) * tiles),
            shape(probes),
            shape(4, probes, tiles),
            shape(probes),
        ),
        in_specs=[smem, smem] + [anywhere] * 4,
        out_specs=(vmem,) * 5,
        scratch_shapes=inputs(planes)
        + [rows_of(planes), rows_of(planes)]
        + [scratch(planes + 1, probes, tiles)] * 2
        + [copies(4)],
        compiler_params=pltpu.CompilerParams(vmem_limit_bytes=28 * 2**20),
        cost_estimate=pl.CostEstimate(flops=10**9, bytes_accessed=2**24, transcendentals=256),
        name="inner",
    )(edge, trap_density, background, site_class, log_param, probe_dirs)

    images = pl.pallas_call(
        functools.partial(outer_kernel, chunks, folds),
        out_shape=jax.ShapeDtypeStruct((groups * slabs, 2, probes, cells), jnp.float32),
        in_specs=[smem] + [anywhere] * 7,
        out_specs=vmem,
        scratch_shapes=[
            scratch(total * tiles),
            scratch(total * tiles),
            scratch(2 * probes),
            scratch(probes),
            scratch(total + 1, probes, tiles),
            scratch(total + 1, probes, tiles),
            copies(11),
        ],
        compiler_params=pltpu.CompilerParams(vmem_limit_bytes=28 * 2**20),
        name="outer",
    )(edge, own_coef, own_src, wide, kept, sums, near, far)

    every = lax.all_to_all(images, ("probe", "space"), split_axis=0, concat_axis=0, tiled=True)
    every = every.reshape((groups, slabs, 2, probes, cells))
    place = jnp.stack([lax.axis_index("probe"), at_space]).astype(jnp.int32)
    return pl.pallas_call(
        factor_kernel,
        out_shape=(
            jax.ShapeDtypeStruct((probes, 1, cells), jnp.float32),
            jax.ShapeDtypeStruct((groups * probes, groups * probes), jnp.float32),
        ),
        in_specs=[smem, vmem],
        out_specs=(vmem, vmem),
        scratch_shapes=[
            pltpu.VMEM((groups * probes, slabs * cells), jnp.float32),
            pltpu.VMEM((groups * probes, cells), jnp.float32),
        ],
        compiler_params=pltpu.CompilerParams(vmem_limit_bytes=48 * 2**20),
        name="factor",
    )(place, every)


def solution(mesh):
    placed = (
        P("probe", "space", None),
        P("space", None),
        P("space", None, None),
        P("space", None, None),
        P(),
    )
    return jax.shard_map(
        shards,
        mesh=mesh,
        in_specs=placed,
        out_specs=(P("probe", "space", None), P()),
        check_vma=False,
    )
```

```python
import functools

import jax
import jax.numpy as jnp
from jax import lax
from jax.experimental import pallas as pl
from jax.experimental.pallas import tpu as pltpu
from jax.sharding import PartitionSpec as P

PX = 64
PY = 4
REF = 8
STEP = 0.12
HALO = 3
LANES = 128
HIGHEST = lax.Precision.HIGHEST


def dot_nn(a, b):
    return lax.dot_general(
        a, b, (((1,), (0,)), ((), ())), precision=HIGHEST, preferred_element_type=jnp.float32
    )


def dot_nt(a, b):
    return lax.dot_general(
        a, b, (((1,), (1,)), ((), ())), precision=HIGHEST, preferred_element_type=jnp.float32
    )


def parts_of(x):
    first = x.astype(jnp.bfloat16)
    rest = x - first.astype(jnp.float32)
    second = rest.astype(jnp.bfloat16)
    third = (rest - second.astype(jnp.float32)).astype(jnp.bfloat16)
    return first, second, third


def bf16_dot(a, b):
    return jnp.dot(a, b, preferred_element_type=jnp.float32)


def interleave(values, order, split, kept):
    parts = parts_of(values) if split else (values.astype(jnp.bfloat16),)
    for k in range(kept.shape[0]):
        columns = order[:, k * LANES : (k + 1) * LANES]
        kept[k] = sum(bf16_dot(part, columns) for part in parts)


def cell_matrix(chunks):
    half = REF // chunks
    cell = lax.broadcasted_iota(jnp.int32, (PX * PY, LANES), 0) % PX
    lane = lax.broadcasted_iota(jnp.int32, (PX * PY, LANES), 1) // half
    return jnp.where(cell == lane, 1.0, 0.0).astype(jnp.float32)


def own_cells(folds):
    half = REF // folds
    sublane = lax.broadcasted_iota(jnp.int32, (8, PX * PY), 0) // half
    return lax.broadcasted_iota(jnp.int32, (8, PX * PY), 1) // PX == sublane


def prolonged(coarse, folds, chunks):
    mask = own_cells(folds)
    rows = [jnp.where(mask, coarse[n : n + 1, :], 0.0) for n in range(coarse.shape[0])]
    return dot_nn(jnp.concatenate(rows, axis=0), cell_matrix(chunks))


def cell_order(columns, chunks):
    x = lax.broadcasted_iota(jnp.int32, (columns, columns), 0)
    place = lax.broadcasted_iota(jnp.int32, (columns, columns), 1)
    wanted = chunks * (place % LANES) + place // LANES
    return jnp.where(x == wanted, 1.0, 0.0).astype(jnp.bfloat16)


def spread_cells(dirs, log_param, folds, chunks):
    probes = dirs.shape[0]
    coarse = [dirs[p] for p in range(probes)] + [jnp.exp(log_param[...])]
    spread = prolonged(jnp.concatenate(coarse, axis=0), folds, chunks)
    return [spread[8 * n : 8 * n + 8, :] for n in range(probes + 1)]


def weights_and_sources(density, scale, background, sites, planes, order, bg, site, store):
    first, count = planes
    rows, columns = background.shape[1:]
    chunks, folds = columns // LANES, rows // 8
    at = pl.ds(first, count)
    cells = (count * rows, columns)
    interleave(background[at].reshape(cells), order, True, bg.at[:, pl.ds(0, count * rows)])
    interleave(
        sites[at].reshape(cells).astype(jnp.float32),
        order,
        False,
        site.at[:, pl.ds(0, count * rows)],
    )
    for z in range(count):
        for r in range(folds):
            for k in range(chunks):
                row = pl.ds(z * rows + r, 8, stride=folds)
                kind = site[k, row, :]
                trap = jnp.full((8, LANES), density[density.shape[0] - 1])
                for n in range(density.shape[0] - 2, -1, -1):
                    trap = jnp.where(kind == float(n), density[n], trap)
                trap = trap * scale
                weight = (1.0 / STEP - 6.0) - trap
                store(first + z, r * chunks + k, weight, -STEP * trap * bg[k, row, :])


def packet_kernel(
    density, background_in, sites_in, log_param_in, dirs_in, packet,
    background, sites, log_param, dirs, order, bg, site, made, sems, out_sems,
):
    rows, columns = background.shape[1:]
    chunks, folds = columns // LANES, rows // 8
    tiles = chunks * folds
    probes = dirs.shape[0]
    halves = [(0, HALO), (HALO, HALO)]
    copies = [(log_param_in, log_param), (dirs_in, dirs)]
    for first, count in halves:
        at = pl.ds(first, count)
        copies += [(background_in.at[at], background.at[at]), (sites_in.at[at], sites.at[at])]
    copies = [pltpu.make_async_copy(a, b, sems.at[n]) for n, (a, b) in enumerate(copies)]
    for copy in copies:
        copy.start()
    order[...] = cell_order(columns, chunks)
    copies[0].wait()
    copies[1].wait()
    spread = spread_cells(dirs, log_param, folds, chunks)
    for p in range(probes):
        made[p] = spread[p]

    def store(z, t, weight, source):
        made[probes + z * tiles + t] = source
        if z < 2 * HALO - 1:
            made[probes + (2 * HALO + z) * tiles + t] = weight

    first_weight = probes + 2 * HALO * tiles
    ranges = [
        [(0, probes + HALO * tiles), (first_weight, HALO * tiles)],
        [(probes + HALO * tiles, HALO * tiles), (first_weight + HALO * tiles, (HALO - 1) * tiles)],
    ]
    sent = []
    for n, half in enumerate(halves):
        copies[2 + 2 * n].wait()
        copies[3 + 2 * n].wait()
        weights_and_sources(
            density, spread[probes], background, sites, half, order, bg, site, store
        )
        for start, length in ranges[n]:
            at = pl.ds(start, length)
            copy = pltpu.make_async_copy(made.at[at], packet.at[at], out_sems.at[len(sent)])
            copy.start()
            sent.append(copy)
    for copy in sent:
        copy.wait()


class Steps:
    def __init__(self, chunks, folds, probes, zero_plane, coef, src):
        self.chunks, self.folds, self.tiles = chunks, folds, chunks * folds
        self.probes, self.zero_plane = probes, zero_plane
        self.coef, self.src = coef, src
        self.lane = lax.broadcasted_iota(jnp.int32, (8, LANES), 1)
        self.sublane = lax.broadcasted_iota(jnp.int32, (8, LANES), 0)

    def clear(self, *fields):
        nothing = jnp.zeros((8, LANES), jnp.float32)
        for t in range(self.tiles):
            for field in fields:
                for p in range(self.probes):
                    field[self.zero_plane, p, t] = nothing

    def from_left(self, x):
        return jnp.where(self.lane == 0, 0.0, pltpu.roll(x, 1, 1))

    def from_right(self, x):
        return jnp.where(self.lane == LANES - 1, 0.0, pltpu.roll(x, LANES - 1, 1))

    def from_before(self, x):
        return jnp.where(self.sublane == 0, 0.0, pltpu.roll(x, 1, 0))

    def from_after(self, x):
        return jnp.where(self.sublane == 7, 0.0, pltpu.roll(x, 7, 0))

    def first(self, own, to, other=None, beyond=()):
        chunks, folds, tiles = self.chunks, self.folds, self.tiles
        src, coef = self.src, self.coef
        turns = (self.from_left, self.from_right, self.from_before, self.from_after)
        shifted = [[f(x) for x in own] for f in turns]

        def body(z, carry):
            down = jnp.where(z > 0, z - 1, self.zero_plane) * tiles
            up = (z + 1) * tiles
            s = [[src[z * tiles + r * chunks + k] for k in range(chunks)] for r in range(folds)]
            for r in range(folds):
                for k in range(chunks):
                    t = r * chunks + k
                    same = coef[z * tiles + t] * s[r][k]
                    outer = []
                    for there, value, turn, kind in (
                        (k > 0, s[r][k - 1], (1, 1), 0),
                        (k + 1 < chunks, s[r][(k + 1) % chunks], (LANES - 1, 1), 1),
                        (r > 0, s[r - 1][k], (1, 0), 2),
                        (r + 1 < folds, s[(r + 1) % folds][k], (7, 0), 3),
                    ):
                        if there:
                            same = same + value
                        else:
                            outer.append((pltpu.roll(value, *turn), shifted[kind]))
                    for name, value in (("down", src[down + t]), ("up", src[up + t])):
                        if name == other:
                            outer.append((value, beyond))
                        else:
                            same = same + value
                    for p in range(self.probes):
                        result = same * own[p]
                        for value, factor in outer:
                            result = result + value * factor[p]
                        to[z, p, t] = result
            return carry

        return body

    def stencil(self, ref, valid, z, emit, extra):
        chunks, folds, tiles = self.chunks, self.folds, self.tiles
        first, stop = valid

        def at(z):
            return jnp.where((z >= first) & (z < stop), z, self.zero_plane)

        down, here, there, up = at(z - 1), at(z), at(z + 1), at(z + 2)
        for p in range(self.probes):
            pair = [[ref[plane, p, t] for t in range(tiles)] for plane in (here, there)]
            for r in range(folds):
                for k in range(chunks):
                    t = r * chunks + k
                    for n, value in enumerate(pair):
                        left = value[t - 1] if k else self.from_left(value[t + chunks - 1])
                        if k + 1 < chunks:
                            right = value[t + 1]
                        else:
                            right = self.from_right(value[t + 1 - chunks])
                        if r:
                            before = value[t - chunks]
                        else:
                            before = self.from_before(value[t + tiles - chunks])
                        if r + 1 < folds:
                            after = value[t + chunks]
                        else:
                            after = self.from_after(value[t + chunks - tiles])
                        above = pair[1 - n][t] + (ref[up, p, t] if n else ref[down, p, t])
                        weight = self.coef[(z + n) * tiles + t]
                        if extra:
                            weight = weight + extra
                        sides = (left + right) + (before + after)
                        emit(z + n, p, t, (sides + above) + weight * value[t])

    def step(self, ref, to, valid, wanted, extra=0.0):
        start, stop = wanted

        def body(n, carry):
            def emit(z, p, t, result):
                to[z, p, t] = result

            self.stencil(ref, valid, jnp.minimum(start + 2 * n, stop - 2), emit, extra)
            return carry

        lax.fori_loop(0, (stop - start + 1) // 2, body, 0)

    def widen(self, ref, to, valid, at_low, at_high):
        first, stop = valid

        def move(a, b):
            for p in range(self.probes):
                for t in range(self.tiles):
                    to[b, p, t] = ref[a, p, t]

        pl.when(at_low)(lambda: move(first, first - 1))
        pl.when(at_high)(lambda: move(stop - 1, stop))

    def images(self, m, u, by_one, by_two, span, carry, other=None):
        chunks, folds, tiles = self.chunks, self.folds, self.tiles
        src = self.src

        def at(z, valid):
            return jnp.where((z >= valid[0]) & (z < valid[1]), z, self.zero_plane)

        def body(z, carry):
            carry = [list(c) for c in carry]
            down = jnp.where(z > 0, z - 1, self.zero_plane) * tiles
            up = (z + 1) * tiles
            here, kept = at(z, by_one), at(z, by_two)
            s = [src[z * tiles + t] for t in range(tiles)]
            for t in range(tiles):
                r, k = t // chunks, t % chunks
                same = self.coef[z * tiles + t] * s[t]
                moved = []
                if k:
                    same = same + s[t - 1]
                else:
                    moved.append((2, self.from_left(s[t + chunks - 1])))
                if k + 1 < chunks:
                    same = same + s[t + 1]
                else:
                    moved.append((1, self.from_right(s[t + 1 - chunks])))
                if r:
                    same = same + s[t - chunks]
                else:
                    moved.append((4, self.from_before(s[t + tiles - chunks])))
                if r + 1 < folds:
                    same = same + s[t + chunks]
                else:
                    moved.append((3, self.from_after(s[t + chunks - tiles])))
                for name, value in (("down", src[down + t]), ("up", src[up + t])):
                    if name == other:
                        moved.append((5, value))
                    else:
                        same = same + value
                scaled = s[t] * (1.0 / STEP**2)
                for p in range(self.probes):
                    value = m[here, p, t]
                    carry[p][0] = carry[p][0] + (same * value + scaled * u[kept, p, t])
                    for n, factor in moved:
                        carry[p][n] = carry[p][n] + factor * value
            return tuple(tuple(c) for c in carry)

        if isinstance(span, int):
            return body(span, carry)
        return lax.fori_loop(*span, body, carry)

    def empty_sums(self):
        nothing = jnp.zeros((8, LANES), jnp.float32)
        return ((nothing,) * 6,) * self.probes

    def moved_sums(self, sums):
        return [
            c[0]
            + (self.from_left(c[1]) + self.from_right(c[2]))
            + (self.from_before(c[3]) + self.from_after(c[4]))
            for c in sums
        ]

    def after_tangent(self, odd, even, mine, at_low, at_high):
        first, stop = mine
        by_two = (jnp.where(at_low, first - 1, first), jnp.where(at_high, stop + 1, stop))
        by_one = (jnp.where(at_low, first - 2, first), jnp.where(at_high, stop + 2, stop))
        self.step(odd, even, mine, mine, 1.0 / STEP)
        self.widen(odd, even, mine, at_low, at_high)
        self.step(even, odd, by_two, by_two)
        self.widen(even, odd, by_two, at_low, at_high)
        return by_one, by_two


def inner_kernel(
    edge, density, background_in, sites_in, log_param_in, dirs_in,
    coef, src, wide, kept, sums,
    background, sites, log_param, dirs, order, bg, site, even, odd, sems,
):
    planes, rows, columns = background.shape
    chunks, folds = columns // LANES, rows // 8
    tiles = chunks * folds
    probes = dirs.shape[0]
    copies = [
        (log_param_in, log_param),
        (dirs_in, dirs),
        (background_in, background),
        (sites_in, sites),
    ]
    copies = [pltpu.make_async_copy(a, b, sems.at[n]) for n, (a, b) in enumerate(copies)]
    for copy in copies:
        copy.start()
    steps = Steps(chunks, folds, probes, planes, coef, src)
    steps.clear(even, odd)
    nothing = jnp.zeros((8, LANES), jnp.float32)
    for t in range(tiles):
        src[planes * tiles + t] = nothing
    order[...] = cell_order(columns, chunks)
    for copy in copies:
        copy.wait()
    spread = spread_cells(dirs, log_param, folds, chunks)
    for p in range(probes):
        wide[p] = spread[p]

    def store(z, t, weight, source):
        coef[z * tiles + t] = weight
        src[z * tiles + t] = source

    weights_and_sources(
        density, spread[probes], background, sites, (0, planes), order, bg, site, store
    )
    at_low = edge[0] != 0

    def low(z):
        return jnp.where(at_low, z, 0)

    last = planes - HALO
    lax.fori_loop(low(1), last + 2, steps.first(spread[:probes], odd), 0)
    steps.step(odd, even, (low(1), last + 2), (low(2), last + 1))
    for n, (ref, z) in enumerate(((odd, last), (odd, last + 1), (even, last - 1), (even, last))):
        for p in range(probes):
            for t in range(tiles):
                kept[n, p, t] = ref[z, p, t]
    mine = (low(HALO), last)
    steps.step(even, odd, (low(2), last + 1), mine)
    by_one, by_two = steps.after_tangent(odd, even, mine, at_low, True)
    result = steps.moved_sums(steps.images(odd, even, by_one, by_two, by_one, steps.empty_sums()))
    for p in range(probes):
        sums[p] = result[p]


def outer_kernel(
    chunks, folds, edge, own_coef, own_src, own_wide, kept, own_sums, packet, out,
    coef, src, even, odd,
):
    tiles = chunks * folds
    probes = own_wide.shape[0]
    total = even.shape[0] - 1
    planes = total - 2 * HALO
    steps = Steps(chunks, folds, probes, total, coef, src)
    last = planes - HALO
    halo = planes * tiles

    def copy(source, start, target, at, count):
        def body(n, carry):
            for t in range(tiles):
                target[at + n * tiles + t] = source[start + n * tiles + t]
            return carry

        lax.fori_loop(0, count, body, 0)

    own = (last - HALO) * tiles
    copy(own_src, own, src, own, planes - last + HALO)
    copy(own_coef, own, coef, own, planes - last + HALO)
    copy(packet, probes, src, halo, 2 * HALO)
    copy(packet, probes + 2 * HALO * tiles, coef, halo, 2 * HALO - 1)
    steps.clear(even, odd)
    for p in range(probes):
        for t in range(tiles):
            odd[last, p, t] = kept[0, p, t]
            odd[last + 1, p, t] = kept[1, p, t]
            even[last - 1, p, t] = kept[2, p, t]
            even[last, p, t] = kept[3, p, t]

    at_high = edge[1] != 0

    def high(z):
        return jnp.where(at_high, z, planes)

    mine = [own_wide[p] for p in range(probes)]
    beyond = [packet[p] for p in range(probes)]
    steps.first(mine, odd, "up", beyond)(planes - 1, 0)

    @pl.when(at_high)
    def _():
        steps.first(beyond, odd, "down", mine)(planes, 0)
        lax.fori_loop(planes + 1, total - 1, steps.first(beyond, odd), 0)

    steps.step(odd, even, (last, high(total - 1)), (last + 1, high(total - 2)))
    mine = (last, high(total - HALO))
    steps.step(even, odd, (last - 1, high(total - 2)), mine)
    by_one, by_two = steps.after_tangent(odd, even, mine, True, at_high)
    start, stop = by_one
    empty = steps.empty_sums()
    inside = steps.images(odd, even, by_one, by_two, (start, planes - 1), empty)
    inside = steps.images(odd, even, by_one, by_two, planes - 1, inside, "up")
    above = [list(c) for c in empty]
    for p in range(probes):
        above[p][0] = inside[p][5]
    above = steps.images(odd, even, by_one, by_two, (planes + 1, stop), tuple(tuple(c) for c in above))
    above = steps.images(odd, even, by_one, by_two, planes, above, "down")
    inside = [x + own_sums[p] + above[p][5] for p, x in enumerate(steps.moved_sums(inside))]
    above = steps.moved_sums(above)

    added = jnp.concatenate(inside + above, axis=0) * STEP**6
    images = dot_nt(added, cell_matrix(chunks))
    mask = own_cells(folds)
    for part in range(2):
        halves = []
        for p in range(probes):
            image = jnp.where(mask, images[8 * (part * probes + p) :][:8], 0.0)
            image = jnp.sum(image, axis=0, keepdims=True)
            halves += [image[:, h * LANES : (h + 1) * LANES] for h in range(image.shape[1] // LANES)]
        halves = jnp.concatenate(halves, axis=0)

        def send(n, carry):
            out[n, part] = halves
            return carry

        lax.fori_loop(0, out.shape[0], send, 0, unroll=8)


def eliminate(gram):
    count = gram.shape[0]
    rows = lax.broadcasted_iota(jnp.int32, (count, count), 0)
    columns = lax.broadcasted_iota(jnp.int32, (count, count), 1)
    inverse = jnp.where(rows == columns, 1.0, 0.0)
    for j in range(count - 1):
        across = jnp.broadcast_to(gram[:, j : j + 1], (count, count))
        turned = 1.0 / across
        ratio = jnp.where(rows > j, across, 0.0)
        gram_row, inverse_row = (gram * turned)[j : j + 1, :], (inverse * turned)[j : j + 1, :]
        gram = gram - ratio * gram_row
        inverse = inverse - ratio * inverse_row
    diagonal = jnp.sum(jnp.where(rows == columns, gram, 0.0), axis=1, keepdims=True)
    scale = 1.0 / jnp.sqrt(diagonal)
    upper = jnp.where(columns >= rows, gram, 0.0) * scale
    return upper, inverse * scale


def float_parts(x):
    first = x.astype(jnp.bfloat16).astype(jnp.float32)
    rest = x - first
    second = rest.astype(jnp.bfloat16).astype(jnp.float32)
    return first, second, rest - second


def gram_of(parts, count):
    stacked = jnp.concatenate(list(parts) + [jnp.zeros_like(parts[0])], axis=0)
    stacked = stacked.astype(jnp.bfloat16)
    every = lax.dot_general(
        stacked, stacked, (((1,), (1,)), ((), ())), preferred_element_type=jnp.float32
    )
    tall = every[:count] + (every[count : 2 * count] + every[2 * count : 3 * count])
    return tall[:, :count] + (tall[:, count : 2 * count] + tall[:, 2 * count : 3 * count])


def times(a, parts):
    first, second, third = float_parts(a)
    left = jnp.concatenate([first, second, third, first, second, first], axis=1)
    right = jnp.concatenate([parts[0]] * 3 + [parts[1]] * 2 + [parts[2]], axis=0)
    return bf16_dot(left.astype(jnp.bfloat16), right.astype(jnp.bfloat16))


def factor_kernel(place, parts, q_out, lower_out, rows_ref, q_ref):
    groups, slabs, _, probes, cells = parts.shape
    count = groups * probes
    for g in range(groups):

        def gather(slab, carry):
            before = jnp.maximum(slab - 1, 0)
            image = parts[g, slab, 0] + jnp.where(slab > 0, parts[g, before, 1], 0.0)
            at = pl.multiple_of(slab * cells, cells)
            rows_ref[pl.ds(g * probes, probes), pl.ds(at, cells)] = image
            return carry

        lax.fori_loop(0, slabs, gather, 0, unroll=True if slabs <= 16 else 8)
    total = slabs * cells
    rows = rows_ref[...]
    parts_one = float_parts(rows)
    upper_one, inverse_one = eliminate(gram_of(parts_one, count) / total)
    basis = times(inverse_one, parts_one)
    rows_ref[...] = basis
    upper_two, inverse_two = eliminate(gram_of(float_parts(basis), count) / total)
    mine = rows_ref[:, pl.ds(pl.multiple_of(place[1] * cells, cells), cells)]
    q_ref[...] = dot_nn(inverse_two, mine)
    for g in range(groups):

        @pl.when(place[0] == g)
        def _():
            q_out[:, 0, :] = q_ref[pl.ds(g * probes, probes), :]

    r = lax.broadcasted_iota(jnp.int32, (count, count), 0)
    c = lax.broadcasted_iota(jnp.int32, (count, count), 1)
    lower_one = dot_nt(jnp.where(r == c, 1.0, 0.0), upper_one)
    lower_out[...] = dot_nt(lower_one, upper_two)


def everywhere(x):
    x = jnp.broadcast_to(jnp.sum(x, axis=1, keepdims=True), x.shape)
    for shift in (4, 2, 1):
        x = x + pltpu.roll(x, shift, 0)
    return x


def cholesky(rows, total):
    count = len(rows)
    rows = [list(row) for row in rows]
    gram = {}
    for i in range(count):
        for j in range(i + 1):
            product = sum(a * b for a, b in zip(rows[i][1:], rows[j][1:]))
            gram[i, j] = everywhere(rows[i][0] * rows[j][0] + product) * (1.0 / total)
    factor = {}
    for j in range(count):
        pivot = gram[j, j]
        turned = lax.rsqrt(pivot)
        turned = turned * (1.5 - 0.5 * pivot * turned * turned)
        factor[j, j] = pivot * turned
        rows[j] = [x * turned for x in rows[j]]
        for i in range(j + 1, count):
            factor[i, j] = gram[i, j] * turned
        for i in range(j + 1, count):
            for k in range(j + 1, i + 1):
                gram[i, k] = gram[i, k] - factor[i, j] * factor[k, j]
            rows[i] = [x - factor[i, j] * y for x, y in zip(rows[i], rows[j])]
    return factor, rows


def register_kernel(groups, slabs, probes, place, parts, q_out, lower_out, q_ref):
    halves = q_out.shape[2] // LANES
    pieces = probes * halves
    step = 2 * pieces
    sublane = lax.broadcasted_iota(jnp.int32, (8, LANES), 0)
    rows = []
    for g in range(groups):
        for p in range(probes):
            row = []
            for block in range(slabs // 8):
                for h in range(halves):
                    at = (g * slabs + 8 * block) * step + p * halves + h
                    own = parts[pl.ds(at, 8, stride=step), :]
                    if block:
                        before = parts[pl.ds(at + pieces - step, 8, stride=step), :]
                    else:
                        before = parts[pl.ds(at + pieces, 8, stride=step), :]
                        before = jnp.where(sublane == 0, 0.0, pltpu.roll(before, 1, 0))
                    row.append(own + before)
            rows.append(row)
    total = slabs * halves * LANES
    factor_one, basis = cholesky(rows, total)
    factor_two, rows = cholesky(basis, total)
    for i, row in enumerate(rows):
        for n, x in enumerate(row):
            q_ref[i, n % halves, pl.ds(8 * (n // halves), 8), :] = x
    for p in range(probes):
        for h in range(halves):
            mine = q_ref[place[0] * probes + p, h, pl.ds(place[1], 1), :]
            q_out[p, :, pl.ds(h * LANES, LANES)] = mine
    count = len(rows)
    r = lax.broadcasted_iota(jnp.int32, (8, LANES), 0)
    c = lax.broadcasted_iota(jnp.int32, (8, LANES), 1)
    lower = jnp.zeros((8, LANES), jnp.float32)
    for i in range(count):
        for j in range(i + 1):
            entry = sum(factor_one[i, k] * factor_two[k, j] for k in range(j, i + 1))
            lower = jnp.where((r == i) & (c == j), entry, lower)
    lower_out[...] = lower[:count, :count]


def shards(probe_dirs, log_param, background, site_class, trap_density):
    probes = probe_dirs.shape[0]
    cells = probe_dirs.shape[2]
    planes, rows, columns = background.shape
    slabs = lax.axis_size("space")
    groups = lax.axis_size("probe")
    at_space = lax.axis_index("space")
    vmem = pl.BlockSpec(memory_space=pltpu.VMEM)
    smem = pl.BlockSpec(memory_space=pltpu.SMEM)
    anywhere = pl.BlockSpec(memory_space=pl.ANY)
    params = pltpu.CompilerParams(vmem_limit_bytes=62 * 2**20)

    chunks, folds = columns // LANES, rows // 8
    tiles = chunks * folds
    total = planes + 2 * HALO
    tile = (8, LANES)

    def shape(*dims):
        return jax.ShapeDtypeStruct(dims + tile, jnp.float32)

    def scratch(*dims):
        return pltpu.VMEM(dims + tile, jnp.float32)

    def copies(count):
        return pltpu.SemaphoreType.DMA((count,))

    def inputs(held):
        return [
            pltpu.VMEM((held, rows, columns), jnp.float32),
            pltpu.VMEM((held, rows, columns), jnp.int32),
            pltpu.VMEM(log_param.shape, jnp.float32),
            pltpu.VMEM(probe_dirs.shape, jnp.float32),
            pltpu.VMEM((columns, columns), jnp.bfloat16),
        ]

    def rows_of(held):
        return pltpu.VMEM((chunks, held * rows, LANES), jnp.float32)

    size = probes + (4 * HALO - 1) * tiles
    packet = pl.pallas_call(
        packet_kernel,
        out_shape=shape(size),
        in_specs=[smem] + [anywhere] * 4,
        out_specs=anywhere,
        scratch_shapes=inputs(2 * HALO)
        + [rows_of(HALO), rows_of(HALO), scratch(size), copies(6), copies(4)],
        compiler_params=params,
        name="packet",
    )(trap_density, background, site_class, log_param, probe_dirs)

    down = [(i + 1, i) for i in range(slabs - 1)]
    next_packet = lax.ppermute(packet, "space", down)
    edge = jnp.stack([at_space > 0, at_space < slabs - 1]).astype(jnp.int32)
    own_coef, own_src, wide, kept, sums = pl.pallas_call(
        inner_kernel,
        out_shape=(
            shape(planes * tiles),
            shape((planes + 1) * tiles),
            shape(probes),
            shape(4, probes, tiles),
            shape(probes),
        ),
        in_specs=[smem, smem] + [anywhere] * 4,
        out_specs=(vmem,) * 5,
        scratch_shapes=inputs(planes)
        + [rows_of(planes), rows_of(planes)]
        + [scratch(planes + 1, probes, tiles)] * 2
        + [copies(4)],
        compiler_params=pltpu.CompilerParams(vmem_limit_bytes=28 * 2**20),
        cost_estimate=pl.CostEstimate(flops=10**9, bytes_accessed=2**24, transcendentals=256),
        name="inner",
    )(edge, trap_density, background, site_class, log_param, probe_dirs)

    pieces = probes * cells // LANES
    images = pl.pallas_call(
        functools.partial(outer_kernel, chunks, folds),
        out_shape=jax.ShapeDtypeStruct((groups * slabs, 2, pieces, LANES), jnp.float32),
        in_specs=[smem] + [vmem] * 6,
        out_specs=vmem,
        scratch_shapes=[
            scratch(total * tiles),
            scratch(total * tiles),
            scratch(total + 1, probes, tiles),
            scratch(total + 1, probes, tiles),
        ],
        compiler_params=pltpu.CompilerParams(vmem_limit_bytes=28 * 2**20),
        name="outer",
    )(edge, own_coef, own_src, wide, kept, sums, next_packet)

    every = lax.all_to_all(images, ("probe", "space"), split_axis=0, concat_axis=0, tiled=True)
    place = jnp.stack([lax.axis_index("probe"), at_space]).astype(jnp.int32)
    count = groups * probes
    results = (
        jax.ShapeDtypeStruct((probes, 1, cells), jnp.float32),
        jax.ShapeDtypeStruct((count, count), jnp.float32),
    )
    params = pltpu.CompilerParams(vmem_limit_bytes=28 * 2**20)
    if count <= 8 and slabs % 8 == 0:
        halves = cells // LANES
        return pl.pallas_call(
            functools.partial(register_kernel, groups, slabs, probes),
            out_shape=results,
            in_specs=[smem, vmem],
            out_specs=(vmem, vmem),
            scratch_shapes=[pltpu.VMEM((count, halves, slabs, LANES), jnp.float32)],
            compiler_params=params,
            name="factor",
        )(place, every.reshape((groups * slabs * 2 * pieces, LANES)))
    return pl.pallas_call(
        factor_kernel,
        out_shape=results,
        in_specs=[smem, vmem],
        out_specs=(vmem, vmem),
        scratch_shapes=[
            pltpu.VMEM((count, slabs * cells), jnp.float32),
            pltpu.VMEM((count, cells), jnp.float32),
        ],
        compiler_params=params,
        name="factor",
    )(place, every.reshape((groups, slabs, 2, probes, cells)))


def solution(mesh):
    placed = (
        P("probe", "space", None),
        P("space", None),
        P("space", None, None),
        P("space", None, None),
        P(),
    )
    return jax.shard_map(
        shards,
        mesh=mesh,
        in_specs=placed,
        out_specs=(P("probe", "space", None), P()),
        check_vma=False,
    )
```

```python
import functools

import jax
import jax.numpy as jnp
from jax import lax
from jax.experimental import pallas as pl
from jax.experimental.pallas import tpu as pltpu
from jax.sharding import PartitionSpec as P

PX = 64
PY = 4
REF = 8
STEP = 0.12
HALO = 3
LANES = 128
HIGHEST = lax.Precision.HIGHEST


def dot_nn(a, b):
    return lax.dot_general(
        a, b, (((1,), (0,)), ((), ())), precision=HIGHEST, preferred_element_type=jnp.float32
    )


def dot_nt(a, b):
    return lax.dot_general(
        a, b, (((1,), (1,)), ((), ())), precision=HIGHEST, preferred_element_type=jnp.float32
    )


def parts_of(x):
    first = x.astype(jnp.bfloat16)
    rest = x - first.astype(jnp.float32)
    second = rest.astype(jnp.bfloat16)
    third = (rest - second.astype(jnp.float32)).astype(jnp.bfloat16)
    return first, second, third


def bf16_dot(a, b):
    return jnp.dot(a, b, preferred_element_type=jnp.float32)


def interleave(background, sites, order, bg, site):
    count = background.shape[0]
    parts = list(parts_of(background)) + [sites.astype(jnp.bfloat16)]
    placed = bf16_dot(jnp.concatenate(parts, axis=0), order[...])
    for k in range(bg.shape[0]):
        columns = placed[:, k * LANES : (k + 1) * LANES]
        both = columns[:count] + columns[count : 2 * count]
        bg[k] = both + columns[2 * count : 3 * count]
        site[k] = columns[3 * count :]


def cell_matrix(chunks, turned=False):
    half = REF // chunks
    dims = (LANES, PX * PY) if turned else (PX * PY, LANES)
    cell = lax.broadcasted_iota(jnp.int32, dims, int(turned)) % PX
    lane = lax.broadcasted_iota(jnp.int32, dims, 1 - int(turned)) // half
    return jnp.where(cell == lane, 1.0, 0.0).astype(jnp.float32)


def own_cells(folds):
    half = REF // folds
    sublane = lax.broadcasted_iota(jnp.int32, (8, PX * PY), 0) // half
    return lax.broadcasted_iota(jnp.int32, (8, PX * PY), 1) // PX == sublane


def prolonged(coarse, folds, chunks):
    mask = own_cells(folds)
    rows = [jnp.where(mask, coarse[n : n + 1, :], 0.0) for n in range(coarse.shape[0])]
    return cell_dot(jnp.concatenate(rows, axis=0), cell_matrix(chunks))


def cell_dot(rows, matrix):
    count = rows.shape[0]
    parts = jnp.concatenate(float_parts(rows), axis=0).astype(jnp.bfloat16)
    placed = bf16_dot(parts, matrix.astype(jnp.bfloat16))
    return (placed[:count] + placed[count : 2 * count]) + placed[2 * count :]


def float_parts(x):
    first = x.astype(jnp.bfloat16).astype(jnp.float32)
    rest = x - first
    second = rest.astype(jnp.bfloat16).astype(jnp.float32)
    return first, second, rest - second


def cell_order(columns, chunks):
    x = lax.broadcasted_iota(jnp.int32, (columns, columns), 0)
    place = lax.broadcasted_iota(jnp.int32, (columns, columns), 1)
    wanted = chunks * (place % LANES) + place // LANES
    return jnp.where(x == wanted, 1.0, 0.0).astype(jnp.bfloat16)


def spread_cells(dirs, log_param, folds, chunks):
    probes = dirs.shape[0]
    coarse = [dirs[p] for p in range(probes)] + [jnp.exp(log_param[...])]
    spread = prolonged(jnp.concatenate(coarse, axis=0), folds, chunks)
    return [spread[8 * n : 8 * n + 8, :] for n in range(probes + 1)]


def weights_and_sources(density, scale, background, sites, planes, order, bg, site, store):
    first, count = planes
    rows, columns = background.shape[1:]
    chunks, folds = columns // LANES, rows // 8
    at = pl.ds(first, count)
    cells = (count * rows, columns)
    interleave(
        background[at].reshape(cells),
        sites[at].reshape(cells).astype(jnp.float32),
        order,
        bg,
        site,
    )
    for z in range(count):
        for r in range(folds):
            for k in range(chunks):
                row = pl.ds(z * rows + r, 8, stride=folds)
                kind = site[k, row, :]
                trap = jnp.full((8, LANES), density[density.shape[0] - 1])
                for n in range(density.shape[0] - 2, -1, -1):
                    trap = jnp.where(kind == float(n), density[n], trap)
                trap = trap * scale
                weight = (1.0 / STEP - 6.0) - trap
                store(first + z, r * chunks + k, weight, -STEP * trap * bg[k, row, :])


def packet_kernel(
    density, background_in, sites_in, log_param_in, dirs_in, packet,
    background, sites, log_param, dirs, order, bg, site, made, sems, out_sems,
):
    rows, columns = background.shape[1:]
    chunks, folds = columns // LANES, rows // 8
    tiles = chunks * folds
    probes = dirs.shape[0]
    pairs = [
        (log_param_in, log_param),
        (dirs_in, dirs),
        (background_in.at[pl.ds(0, 2 * HALO)], background),
        (sites_in.at[pl.ds(0, 2 * HALO)], sites),
    ]
    copies = [pltpu.make_async_copy(a, b, sems.at[n]) for n, (a, b) in enumerate(pairs)]
    for copy in copies:
        copy.start()
    order[...] = cell_order(columns, chunks)
    copies[0].wait()
    copies[1].wait()
    spread = spread_cells(dirs, log_param, folds, chunks)
    for p in range(probes):
        made[p] = spread[p]

    first_weight = probes + 2 * HALO * tiles
    ranges = {
        HALO - 1: [(0, probes + HALO * tiles), (first_weight, HALO * tiles)],
        2 * HALO - 1: [
            (probes + HALO * tiles, HALO * tiles),
            (first_weight + HALO * tiles, (HALO - 1) * tiles),
        ],
    }
    sent = []

    def store(z, t, weight, source):
        made[probes + z * tiles + t] = source
        if z < 2 * HALO - 1:
            made[probes + (2 * HALO + z) * tiles + t] = weight
        if t == tiles - 1:
            for start, length in ranges.get(z, []):
                at = pl.ds(start, length)
                copy = pltpu.make_async_copy(made.at[at], packet.at[at], out_sems.at[len(sent)])
                copy.start()
                sent.append(copy)

    copies[2].wait()
    copies[3].wait()
    weights_and_sources(
        density, spread[probes], background, sites, (0, 2 * HALO), order, bg, site, store
    )
    for copy in sent:
        copy.wait()


class Steps:
    def __init__(self, chunks, folds, probes, zero_plane, coef, src):
        self.chunks, self.folds, self.tiles = chunks, folds, chunks * folds
        self.probes, self.zero_plane = probes, zero_plane
        self.coef, self.src = coef, src
        self.lane = lax.broadcasted_iota(jnp.int32, (8, LANES), 1)
        self.sublane = lax.broadcasted_iota(jnp.int32, (8, LANES), 0)

    def clear(self, *fields):
        nothing = jnp.zeros((8, LANES), jnp.float32)
        for t in range(self.tiles):
            for field in fields:
                for p in range(self.probes):
                    field[self.zero_plane, p, t] = nothing

    def from_left(self, x):
        return jnp.where(self.lane == 0, 0.0, pltpu.roll(x, 1, 1))

    def from_right(self, x):
        return jnp.where(self.lane == LANES - 1, 0.0, pltpu.roll(x, LANES - 1, 1))

    def from_before(self, x):
        return jnp.where(self.sublane == 0, 0.0, pltpu.roll(x, 1, 0))

    def from_after(self, x):
        return jnp.where(self.sublane == 7, 0.0, pltpu.roll(x, 7, 0))

    def first(self, own, to, other=None, beyond=()):
        chunks, folds, tiles = self.chunks, self.folds, self.tiles
        src, coef = self.src, self.coef
        turns = (self.from_left, self.from_right, self.from_before, self.from_after)
        shifted = [[f(x) for x in own] for f in turns]

        def body(z, carry):
            down = jnp.where(z > 0, z - 1, self.zero_plane) * tiles
            up = (z + 1) * tiles
            s = [[src[z * tiles + r * chunks + k] for k in range(chunks)] for r in range(folds)]
            for r in range(folds):
                for k in range(chunks):
                    t = r * chunks + k
                    same = coef[z * tiles + t] * s[r][k]
                    outer = []
                    for there, value, turn, kind in (
                        (k > 0, s[r][k - 1], (1, 1), 0),
                        (k + 1 < chunks, s[r][(k + 1) % chunks], (LANES - 1, 1), 1),
                        (r > 0, s[r - 1][k], (1, 0), 2),
                        (r + 1 < folds, s[(r + 1) % folds][k], (7, 0), 3),
                    ):
                        if there:
                            same = same + value
                        else:
                            outer.append((pltpu.roll(value, *turn), shifted[kind]))
                    for name, value in (("down", src[down + t]), ("up", src[up + t])):
                        if name == other:
                            outer.append((value, beyond))
                        else:
                            same = same + value
                    for p in range(self.probes):
                        result = same * own[p]
                        for value, factor in outer:
                            result = result + value * factor[p]
                        to[z, p, t] = result
            return carry

        return body

    def stencil(self, ref, valid, z, emit, extra):
        chunks, folds, tiles = self.chunks, self.folds, self.tiles
        first, stop = valid

        def at(z):
            return jnp.where((z >= first) & (z < stop), z, self.zero_plane)

        down, here, there, up = at(z - 1), at(z), at(z + 1), at(z + 2)
        for p in range(self.probes):
            pair = [[ref[plane, p, t] for t in range(tiles)] for plane in (here, there)]
            for r in range(folds):
                for k in range(chunks):
                    t = r * chunks + k
                    for n, value in enumerate(pair):
                        left = value[t - 1] if k else self.from_left(value[t + chunks - 1])
                        if k + 1 < chunks:
                            right = value[t + 1]
                        else:
                            right = self.from_right(value[t + 1 - chunks])
                        if r:
                            before = value[t - chunks]
                        else:
                            before = self.from_before(value[t + tiles - chunks])
                        if r + 1 < folds:
                            after = value[t + chunks]
                        else:
                            after = self.from_after(value[t + chunks - tiles])
                        above = pair[1 - n][t] + (ref[up, p, t] if n else ref[down, p, t])
                        weight = self.coef[(z + n) * tiles + t]
                        if extra:
                            weight = weight + extra
                        sides = (left + right) + (before + after)
                        emit(z + n, p, t, (sides + above) + weight * value[t])

    def step(self, ref, to, valid, wanted, extra=0.0):
        start, stop = wanted

        def body(n, carry):
            def emit(z, p, t, result):
                to[z, p, t] = result

            self.stencil(ref, valid, jnp.minimum(start + 2 * n, stop - 2), emit, extra)
            return carry

        lax.fori_loop(0, (stop - start + 1) // 2, body, 0)

    def widen(self, ref, to, valid, at_low, at_high):
        first, stop = valid

        def move(a, b):
            for p in range(self.probes):
                for t in range(self.tiles):
                    to[b, p, t] = ref[a, p, t]

        pl.when(at_low)(lambda: move(first, first - 1))
        pl.when(at_high)(lambda: move(stop - 1, stop))

    def images(self, m, u, by_one, by_two, span, carry, other=None):
        chunks, folds, tiles = self.chunks, self.folds, self.tiles
        src = self.src

        def at(z, valid):
            return jnp.where((z >= valid[0]) & (z < valid[1]), z, self.zero_plane)

        def body(z, carry):
            carry = [list(c) for c in carry]
            down = jnp.where(z > 0, z - 1, self.zero_plane) * tiles
            up = (z + 1) * tiles
            here, kept = at(z, by_one), at(z, by_two)
            s = [src[z * tiles + t] for t in range(tiles)]
            for t in range(tiles):
                r, k = t // chunks, t % chunks
                same = self.coef[z * tiles + t] * s[t]
                moved = []
                if k:
                    same = same + s[t - 1]
                else:
                    moved.append((2, self.from_left(s[t + chunks - 1])))
                if k + 1 < chunks:
                    same = same + s[t + 1]
                else:
                    moved.append((1, self.from_right(s[t + 1 - chunks])))
                if r:
                    same = same + s[t - chunks]
                else:
                    moved.append((4, self.from_before(s[t + tiles - chunks])))
                if r + 1 < folds:
                    same = same + s[t + chunks]
                else:
                    moved.append((3, self.from_after(s[t + chunks - tiles])))
                for name, value in (("down", src[down + t]), ("up", src[up + t])):
                    if name == other:
                        moved.append((5, value))
                    else:
                        same = same + value
                scaled = s[t] * (1.0 / STEP**2)
                for p in range(self.probes):
                    value = m[here, p, t]
                    carry[p][0] = carry[p][0] + (same * value + scaled * u[kept, p, t])
                    for n, factor in moved:
                        carry[p][n] = carry[p][n] + factor * value
            return tuple(tuple(c) for c in carry)

        if isinstance(span, int):
            return body(span, carry)
        return lax.fori_loop(*span, body, carry)

    def empty_sums(self):
        nothing = jnp.zeros((8, LANES), jnp.float32)
        return ((nothing,) * 6,) * self.probes

    def moved_sums(self, sums):
        return [
            c[0]
            + (self.from_left(c[1]) + self.from_right(c[2]))
            + (self.from_before(c[3]) + self.from_after(c[4]))
            for c in sums
        ]

    def after_tangent(self, odd, even, mine, at_low, at_high):
        first, stop = mine
        by_two = (jnp.where(at_low, first - 1, first), jnp.where(at_high, stop + 1, stop))
        by_one = (jnp.where(at_low, first - 2, first), jnp.where(at_high, stop + 2, stop))
        self.step(odd, even, mine, mine, 1.0 / STEP)
        self.widen(odd, even, mine, at_low, at_high)
        self.step(even, odd, by_two, by_two)
        self.widen(even, odd, by_two, at_low, at_high)
        return by_one, by_two


def inner_kernel(
    edge, density, background_in, sites_in, log_param_in, dirs_in,
    coef, src, wide, kept, sums,
    background, sites, log_param, dirs, order, bg, site, even, odd, sems,
):
    planes, rows, columns = background.shape
    chunks, folds = columns // LANES, rows // 8
    tiles = chunks * folds
    probes = dirs.shape[0]
    copies = [
        (log_param_in, log_param),
        (dirs_in, dirs),
        (background_in, background),
        (sites_in, sites),
    ]
    copies = [pltpu.make_async_copy(a, b, sems.at[n]) for n, (a, b) in enumerate(copies)]
    for copy in copies:
        copy.start()
    steps = Steps(chunks, folds, probes, planes, coef, src)
    steps.clear(even, odd)
    nothing = jnp.zeros((8, LANES), jnp.float32)
    for t in range(tiles):
        src[planes * tiles + t] = nothing
    order[...] = cell_order(columns, chunks)
    for copy in copies:
        copy.wait()
    spread = spread_cells(dirs, log_param, folds, chunks)
    for p in range(probes):
        wide[p] = spread[p]

    def store(z, t, weight, source):
        coef[z * tiles + t] = weight
        src[z * tiles + t] = source

    weights_and_sources(
        density, spread[probes], background, sites, (0, planes), order, bg, site, store
    )
    at_low = edge[0] != 0

    def low(z):
        return jnp.where(at_low, z, 0)

    last = planes - HALO
    lax.fori_loop(low(1), last + 2, steps.first(spread[:probes], odd), 0)
    steps.step(odd, even, (low(1), last + 2), (low(2), last + 1))
    for n, (ref, z) in enumerate(((odd, last), (odd, last + 1), (even, last - 1), (even, last))):
        for p in range(probes):
            for t in range(tiles):
                kept[n, p, t] = ref[z, p, t]
    mine = (low(HALO), last)
    steps.step(even, odd, (low(2), last + 1), mine)
    by_one, by_two = steps.after_tangent(odd, even, mine, at_low, True)
    result = steps.moved_sums(steps.images(odd, even, by_one, by_two, by_one, steps.empty_sums()))
    for p in range(probes):
        sums[p] = result[p]


def outer_kernel(
    chunks, folds, edge, own_coef, own_src, own_wide, kept, own_sums, packet, out,
    coef, src, even, odd,
):
    tiles = chunks * folds
    probes = own_wide.shape[0]
    total = even.shape[0] - 1
    planes = total - 2 * HALO
    steps = Steps(chunks, folds, probes, total, coef, src)
    last = planes - HALO
    halo = planes * tiles

    def copy(source, start, target, at, count):
        def body(n, carry):
            for t in range(tiles):
                target[at + n * tiles + t] = source[start + n * tiles + t]
            return carry

        lax.fori_loop(0, count, body, 0)

    own = (last - HALO) * tiles
    copy(own_src, own, src, own, planes - last + HALO)
    copy(own_coef, own, coef, own, planes - last + HALO)
    copy(packet, probes, src, halo, 2 * HALO)
    copy(packet, probes + 2 * HALO * tiles, coef, halo, 2 * HALO - 1)
    steps.clear(even, odd)
    for p in range(probes):
        for t in range(tiles):
            odd[last, p, t] = kept[0, p, t]
            odd[last + 1, p, t] = kept[1, p, t]
            even[last - 1, p, t] = kept[2, p, t]
            even[last, p, t] = kept[3, p, t]

    at_high = edge[1] != 0

    def high(z):
        return jnp.where(at_high, z, planes)

    mine = [own_wide[p] for p in range(probes)]
    beyond = [packet[p] for p in range(probes)]
    steps.first(mine, odd, "up", beyond)(planes - 1, 0)

    @pl.when(at_high)
    def _():
        steps.first(beyond, odd, "down", mine)(planes, 0)
        lax.fori_loop(planes + 1, total - 1, steps.first(beyond, odd), 0)

    steps.step(odd, even, (last, high(total - 1)), (last + 1, high(total - 2)))
    mine = (last, high(total - HALO))
    steps.step(even, odd, (last - 1, high(total - 2)), mine)
    by_one, by_two = steps.after_tangent(odd, even, mine, True, at_high)
    start, stop = by_one
    empty = steps.empty_sums()
    inside = steps.images(odd, even, by_one, by_two, (start, planes - 1), empty)
    inside = steps.images(odd, even, by_one, by_two, planes - 1, inside, "up")
    above = [list(c) for c in empty]
    for p in range(probes):
        above[p][0] = inside[p][5]
    above = steps.images(odd, even, by_one, by_two, (planes + 1, stop), tuple(tuple(c) for c in above))
    above = steps.images(odd, even, by_one, by_two, planes, above, "down")
    inside = [x + own_sums[p] + above[p][5] for p, x in enumerate(steps.moved_sums(inside))]
    above = steps.moved_sums(above)

    added = jnp.concatenate(inside + above, axis=0) * STEP**6
    images = cell_dot(added, cell_matrix(chunks, True))
    mask = own_cells(folds)
    for part in range(2):
        halves = []
        for p in range(probes):
            image = jnp.where(mask, images[8 * (part * probes + p) :][:8], 0.0)
            image = jnp.sum(image, axis=0, keepdims=True)
            halves += [image[:, h * LANES : (h + 1) * LANES] for h in range(image.shape[1] // LANES)]
        halves = jnp.concatenate(halves, axis=0)

        def send(n, carry):
            out[n, part] = halves
            return carry

        lax.fori_loop(0, out.shape[0], send, 0, unroll=8)


def eliminate(gram):
    count = gram.shape[0]
    rows = lax.broadcasted_iota(jnp.int32, (count, count), 0)
    columns = lax.broadcasted_iota(jnp.int32, (count, count), 1)
    inverse = jnp.where(rows == columns, 1.0, 0.0)
    for j in range(count - 1):
        across = jnp.broadcast_to(gram[:, j : j + 1], (count, count))
        turned = 1.0 / across
        ratio = jnp.where(rows > j, across, 0.0)
        gram_row, inverse_row = (gram * turned)[j : j + 1, :], (inverse * turned)[j : j + 1, :]
        gram = gram - ratio * gram_row
        inverse = inverse - ratio * inverse_row
    diagonal = jnp.sum(jnp.where(rows == columns, gram, 0.0), axis=1, keepdims=True)
    scale = 1.0 / jnp.sqrt(diagonal)
    upper = jnp.where(columns >= rows, gram, 0.0) * scale
    return upper, inverse * scale


def gram_of(parts, count):
    stacked = jnp.concatenate(list(parts) + [jnp.zeros_like(parts[0])], axis=0)
    stacked = stacked.astype(jnp.bfloat16)
    every = lax.dot_general(
        stacked, stacked, (((1,), (1,)), ((), ())), preferred_element_type=jnp.float32
    )
    tall = every[:count] + (every[count : 2 * count] + every[2 * count : 3 * count])
    return tall[:, :count] + (tall[:, count : 2 * count] + tall[:, 2 * count : 3 * count])


def times(a, parts):
    first, second, third = float_parts(a)
    left = jnp.concatenate([first, second, third, first, second, first], axis=1)
    right = jnp.concatenate([parts[0]] * 3 + [parts[1]] * 2 + [parts[2]], axis=0)
    return bf16_dot(left.astype(jnp.bfloat16), right.astype(jnp.bfloat16))


def factor_kernel(place, parts, q_out, lower_out, rows_ref, q_ref):
    groups, slabs, _, probes, cells = parts.shape
    count = groups * probes
    for g in range(groups):

        def gather(slab, carry):
            before = jnp.maximum(slab - 1, 0)
            image = parts[g, slab, 0] + jnp.where(slab > 0, parts[g, before, 1], 0.0)
            at = pl.multiple_of(slab * cells, cells)
            rows_ref[pl.ds(g * probes, probes), pl.ds(at, cells)] = image
            return carry

        lax.fori_loop(0, slabs, gather, 0, unroll=True if slabs <= 16 else 8)
    total = slabs * cells
    rows = rows_ref[...]
    parts_one = float_parts(rows)
    upper_one, inverse_one = eliminate(gram_of(parts_one, count) / total)
    basis = times(inverse_one, parts_one)
    rows_ref[...] = basis
    upper_two, inverse_two = eliminate(gram_of(float_parts(basis), count) / total)
    mine = rows_ref[:, pl.ds(pl.multiple_of(place[1] * cells, cells), cells)]
    q_ref[...] = dot_nn(inverse_two, mine)
    for g in range(groups):

        @pl.when(place[0] == g)
        def _():
            q_out[:, 0, :] = q_ref[pl.ds(g * probes, probes), :]

    r = lax.broadcasted_iota(jnp.int32, (count, count), 0)
    c = lax.broadcasted_iota(jnp.int32, (count, count), 1)
    lower_one = dot_nt(jnp.where(r == c, 1.0, 0.0), upper_one)
    lower_out[...] = dot_nt(lower_one, upper_two)


def everywhere(x):
    x = jnp.broadcast_to(jnp.sum(x, axis=1, keepdims=True), x.shape)
    for shift in (4, 2, 1):
        x = x + pltpu.roll(x, shift, 0)
    return x


def cholesky(rows, total):
    count = len(rows)
    rows = [list(row) for row in rows]
    gram = {}
    for i in range(count):
        for j in range(i + 1):
            product = sum(a * b for a, b in zip(rows[i][1:], rows[j][1:]))
            gram[i, j] = everywhere(rows[i][0] * rows[j][0] + product) * (1.0 / total)
    factor = {}
    for j in range(count):
        pivot = gram[j, j]
        turned = lax.rsqrt(pivot)
        turned = turned * (1.5 - 0.5 * pivot * turned * turned)
        factor[j, j] = pivot * turned
        rows[j] = [x * turned for x in rows[j]]
        for i in range(j + 1, count):
            factor[i, j] = gram[i, j] * turned
        for i in range(j + 1, count):
            for k in range(j + 1, i + 1):
                gram[i, k] = gram[i, k] - factor[i, j] * factor[k, j]
            rows[i] = [x - factor[i, j] * y for x, y in zip(rows[i], rows[j])]
    return factor, rows


def register_kernel(groups, slabs, probes, place, parts, q_out, lower_out, q_ref):
    halves = q_out.shape[2] // LANES
    pieces = probes * halves
    step = 2 * pieces
    sublane = lax.broadcasted_iota(jnp.int32, (8, LANES), 0)
    rows = []
    for g in range(groups):
        for p in range(probes):
            row = []
            for block in range(slabs // 8):
                for h in range(halves):
                    at = (8 * block * groups + g) * step + p * halves + h
                    own = parts[pl.ds(at, 8, stride=groups * step), :]
                    if block:
                        before = parts[pl.ds(at + pieces - groups * step, 8, stride=groups * step), :]
                    else:
                        before = parts[pl.ds(at + pieces, 8, stride=groups * step), :]
                        before = jnp.where(sublane == 0, 0.0, pltpu.roll(before, 1, 0))
                    row.append(own + before)
            rows.append(row)
    total = slabs * halves * LANES
    factor_one, basis = cholesky(rows, total)
    factor_two, rows = cholesky(basis, total)
    for i, row in enumerate(rows):
        for n, x in enumerate(row):
            q_ref[i, n % halves, pl.ds(8 * (n // halves), 8), :] = x
    for p in range(probes):
        for h in range(halves):
            mine = q_ref[place[0] * probes + p, h, pl.ds(place[1], 1), :]
            q_out[p, :, pl.ds(h * LANES, LANES)] = mine
    count = len(rows)
    r = lax.broadcasted_iota(jnp.int32, (8, LANES), 0)
    c = lax.broadcasted_iota(jnp.int32, (8, LANES), 1)
    lower = jnp.zeros((8, LANES), jnp.float32)
    for i in range(count):
        for j in range(i + 1):
            entry = sum(factor_one[i, k] * factor_two[k, j] for k in range(j, i + 1))
            lower = jnp.where((r == i) & (c == j), entry, lower)
    lower_out[...] = lower[:count, :count]


def shards(probe_dirs, log_param, background, site_class, trap_density):
    probes = probe_dirs.shape[0]
    cells = probe_dirs.shape[2]
    planes, rows, columns = background.shape
    slabs = lax.axis_size("space")
    groups = lax.axis_size("probe")
    at_space = lax.axis_index("space")
    vmem = pl.BlockSpec(memory_space=pltpu.VMEM)
    smem = pl.BlockSpec(memory_space=pltpu.SMEM)
    anywhere = pl.BlockSpec(memory_space=pl.ANY)
    params = pltpu.CompilerParams(vmem_limit_bytes=62 * 2**20)

    chunks, folds = columns // LANES, rows // 8
    tiles = chunks * folds
    total = planes + 2 * HALO
    tile = (8, LANES)

    def shape(*dims):
        return jax.ShapeDtypeStruct(dims + tile, jnp.float32)

    def scratch(*dims):
        return pltpu.VMEM(dims + tile, jnp.float32)

    def copies(count):
        return pltpu.SemaphoreType.DMA((count,))

    def inputs(held):
        return [
            pltpu.VMEM((held, rows, columns), jnp.float32),
            pltpu.VMEM((held, rows, columns), jnp.int32),
            pltpu.VMEM(log_param.shape, jnp.float32),
            pltpu.VMEM(probe_dirs.shape, jnp.float32),
            pltpu.VMEM((columns, columns), jnp.bfloat16),
        ]

    def rows_of(held):
        return pltpu.VMEM((chunks, held * rows, LANES), jnp.float32)

    size = probes + (4 * HALO - 1) * tiles
    packet = pl.pallas_call(
        packet_kernel,
        out_shape=shape(size),
        in_specs=[smem] + [anywhere] * 4,
        out_specs=anywhere,
        scratch_shapes=inputs(2 * HALO)
        + [rows_of(2 * HALO), rows_of(2 * HALO), scratch(size), copies(4), copies(4)],
        compiler_params=params,
        name="packet",
    )(trap_density, background, site_class, log_param, probe_dirs)

    down = [(i + 1, i) for i in range(slabs - 1)]
    next_packet = lax.ppermute(packet, "space", down)
    edge = jnp.stack([at_space > 0, at_space < slabs - 1]).astype(jnp.int32)
    own_coef, own_src, wide, kept, sums = pl.pallas_call(
        inner_kernel,
        out_shape=(
            shape(planes * tiles),
            shape((planes + 1) * tiles),
            shape(probes),
            shape(4, probes, tiles),
            shape(probes),
        ),
        in_specs=[smem, smem] + [anywhere] * 4,
        out_specs=(vmem,) * 5,
        scratch_shapes=inputs(planes)
        + [rows_of(planes), rows_of(planes)]
        + [scratch(planes + 1, probes, tiles)] * 2
        + [copies(4)],
        compiler_params=pltpu.CompilerParams(vmem_limit_bytes=28 * 2**20),
        cost_estimate=pl.CostEstimate(flops=10**9, bytes_accessed=2**24, transcendentals=256),
        name="inner",
    )(edge, trap_density, background, site_class, log_param, probe_dirs)

    pieces = probes * cells // LANES
    images = pl.pallas_call(
        functools.partial(outer_kernel, chunks, folds),
        out_shape=jax.ShapeDtypeStruct((groups * slabs, 2, pieces, LANES), jnp.float32),
        in_specs=[smem] + [vmem] * 6,
        out_specs=vmem,
        scratch_shapes=[
            scratch(total * tiles),
            scratch(total * tiles),
            scratch(total + 1, probes, tiles),
            scratch(total + 1, probes, tiles),
        ],
        compiler_params=pltpu.CompilerParams(vmem_limit_bytes=28 * 2**20),
        name="outer",
    )(edge, own_coef, own_src, wide, kept, sums, next_packet)

    every = lax.all_to_all(images, ("space", "probe"), split_axis=0, concat_axis=0, tiled=True)
    place = jnp.stack([lax.axis_index("probe"), at_space]).astype(jnp.int32)
    count = groups * probes
    results = (
        jax.ShapeDtypeStruct((probes, 1, cells), jnp.float32),
        jax.ShapeDtypeStruct((count, count), jnp.float32),
    )
    params = pltpu.CompilerParams(vmem_limit_bytes=28 * 2**20)
    if count <= 8 and slabs % 8 == 0:
        halves = cells // LANES
        return pl.pallas_call(
            functools.partial(register_kernel, groups, slabs, probes),
            out_shape=results,
            in_specs=[smem, vmem],
            out_specs=(vmem, vmem),
            scratch_shapes=[pltpu.VMEM((count, halves, slabs, LANES), jnp.float32)],
            compiler_params=params,
            name="factor",
        )(place, every.reshape((groups * slabs * 2 * pieces, LANES)))
    return pl.pallas_call(
        factor_kernel,
        out_shape=results,
        in_specs=[smem, vmem],
        out_specs=(vmem, vmem),
        scratch_shapes=[
            pltpu.VMEM((count, slabs * cells), jnp.float32),
            pltpu.VMEM((count, cells), jnp.float32),
        ],
        compiler_params=params,
        name="factor",
    )(place, every.reshape((slabs, groups, 2, probes, cells)).swapaxes(0, 1))


def solution(mesh):
    placed = (
        P("probe", "space", None),
        P("space", None),
        P("space", None, None),
        P("space", None, None),
        P(),
    )
    return jax.shard_map(
        shards,
        mesh=mesh,
        in_specs=placed,
        out_specs=(P("probe", "space", None), P()),
        check_vma=False,
    )
```

```python
import functools

import jax
import jax.numpy as jnp
from jax import lax
from jax.experimental import pallas as pl
from jax.experimental.pallas import tpu as pltpu
from jax.sharding import PartitionSpec as P

PX = 64
PY = 4
REF = 8
STEP = 0.12
HALO = 3
LANES = 128
HIGHEST = lax.Precision.HIGHEST


def dot_nn(a, b):
    return lax.dot_general(
        a, b, (((1,), (0,)), ((), ())), precision=HIGHEST, preferred_element_type=jnp.float32
    )


def dot_nt(a, b):
    return lax.dot_general(
        a, b, (((1,), (1,)), ((), ())), precision=HIGHEST, preferred_element_type=jnp.float32
    )


def parts_of(x):
    first = x.astype(jnp.bfloat16)
    rest = x - first.astype(jnp.float32)
    second = rest.astype(jnp.bfloat16)
    third = (rest - second.astype(jnp.float32)).astype(jnp.bfloat16)
    return first, second, third


def bf16_dot(a, b):
    return jnp.dot(a, b, preferred_element_type=jnp.float32)


def interleave(background, sites, order, bg, site):
    count = background.shape[0]
    parts = list(parts_of(background)) + [sites.astype(jnp.bfloat16)]
    placed = bf16_dot(jnp.concatenate(parts, axis=0), order[...])
    for k in range(bg.shape[0]):
        columns = placed[:, k * LANES : (k + 1) * LANES]
        both = columns[:count] + columns[count : 2 * count]
        bg[k] = both + columns[2 * count : 3 * count]
        site[k] = columns[3 * count :]


def cell_matrix(chunks, turned=False):
    half = REF // chunks
    dims = (LANES, PX * PY) if turned else (PX * PY, LANES)
    cell = lax.broadcasted_iota(jnp.int32, dims, int(turned)) % PX
    lane = lax.broadcasted_iota(jnp.int32, dims, 1 - int(turned)) // half
    return jnp.where(cell == lane, 1.0, 0.0).astype(jnp.float32)


def own_cells(folds):
    half = REF // folds
    sublane = lax.broadcasted_iota(jnp.int32, (8, PX * PY), 0) // half
    return lax.broadcasted_iota(jnp.int32, (8, PX * PY), 1) // PX == sublane


def prolonged(coarse, folds, chunks):
    mask = own_cells(folds)
    rows = [jnp.where(mask, coarse[n : n + 1, :], 0.0) for n in range(coarse.shape[0])]
    return cell_dot(jnp.concatenate(rows, axis=0), cell_matrix(chunks))


def cell_dot(rows, matrix):
    count = rows.shape[0]
    parts = jnp.concatenate(float_parts(rows), axis=0).astype(jnp.bfloat16)
    placed = bf16_dot(parts, matrix.astype(jnp.bfloat16))
    return (placed[:count] + placed[count : 2 * count]) + placed[2 * count :]


def float_parts(x):
    first = x.astype(jnp.bfloat16).astype(jnp.float32)
    rest = x - first
    second = rest.astype(jnp.bfloat16).astype(jnp.float32)
    return first, second, rest - second


def cell_order(columns, chunks):
    x = lax.broadcasted_iota(jnp.int32, (columns, columns), 0)
    place = lax.broadcasted_iota(jnp.int32, (columns, columns), 1)
    wanted = chunks * (place % LANES) + place // LANES
    return jnp.where(x == wanted, 1.0, 0.0).astype(jnp.bfloat16)


def spread_cells(dirs, log_param, folds, chunks):
    probes = dirs.shape[0]
    coarse = [dirs[p] for p in range(probes)] + [jnp.exp(log_param[...])]
    spread = prolonged(jnp.concatenate(coarse, axis=0), folds, chunks)
    return [spread[8 * n : 8 * n + 8, :] for n in range(probes + 1)]


def weights_and_sources(density, scale, background, sites, planes, order, bg, site, store):
    first, count = planes
    rows, columns = background.shape[1:]
    chunks, folds = columns // LANES, rows // 8
    at = pl.ds(first, count)
    cells = (count * rows, columns)
    interleave(
        background[at].reshape(cells),
        sites[at].reshape(cells).astype(jnp.float32),
        order,
        bg,
        site,
    )
    for z in range(count):
        for r in range(folds):
            for k in range(chunks):
                row = pl.ds(z * rows + r, 8, stride=folds)
                kind = site[k, row, :]
                trap = jnp.full((8, LANES), density[density.shape[0] - 1])
                for n in range(density.shape[0] - 2, -1, -1):
                    trap = jnp.where(kind == float(n), density[n], trap)
                trap = trap * scale
                weight = (1.0 / STEP - 6.0) - trap
                store(first + z, r * chunks + k, weight, -STEP * trap * bg[k, row, :])


def packet_kernel(
    density, background_in, sites_in, log_param_in, dirs_in, packet,
    background, sites, log_param, dirs, order, bg, site, made, sems, out_sems,
):
    rows, columns = background.shape[1:]
    chunks, folds = columns // LANES, rows // 8
    tiles = chunks * folds
    probes = dirs.shape[0]
    pairs = [
        (log_param_in, log_param),
        (dirs_in, dirs),
        (background_in.at[pl.ds(0, 2 * HALO)], background),
        (sites_in.at[pl.ds(0, 2 * HALO)], sites),
    ]
    copies = [pltpu.make_async_copy(a, b, sems.at[n]) for n, (a, b) in enumerate(pairs)]
    for copy in copies:
        copy.start()
    order[...] = cell_order(columns, chunks)
    copies[0].wait()
    copies[1].wait()
    spread = spread_cells(dirs, log_param, folds, chunks)
    for p in range(probes):
        made[p] = spread[p]

    first_weight = probes + 2 * HALO * tiles
    ranges = {
        HALO - 1: [(0, probes + HALO * tiles), (first_weight, HALO * tiles)],
        2 * HALO - 1: [
            (probes + HALO * tiles, HALO * tiles),
            (first_weight + HALO * tiles, (HALO - 1) * tiles),
        ],
    }
    sent = []

    def store(z, t, weight, source):
        made[probes + z * tiles + t] = source
        if z < 2 * HALO - 1:
            made[probes + (2 * HALO + z) * tiles + t] = weight
        if t == tiles - 1:
            for start, length in ranges.get(z, []):
                at = pl.ds(start, length)
                copy = pltpu.make_async_copy(made.at[at], packet.at[at], out_sems.at[len(sent)])
                copy.start()
                sent.append(copy)

    copies[2].wait()
    copies[3].wait()
    weights_and_sources(
        density, spread[probes], background, sites, (0, 2 * HALO), order, bg, site, store
    )
    for copy in sent:
        copy.wait()


class Steps:
    def __init__(self, chunks, folds, probes, zero_plane, coef, src):
        self.chunks, self.folds, self.tiles = chunks, folds, chunks * folds
        self.probes, self.zero_plane = probes, zero_plane
        self.coef, self.src = coef, src
        self.lane = lax.broadcasted_iota(jnp.int32, (8, LANES), 1)
        self.sublane = lax.broadcasted_iota(jnp.int32, (8, LANES), 0)

    def clear(self, *fields):
        nothing = jnp.zeros((8, LANES), jnp.float32)
        for t in range(self.tiles):
            for field in fields:
                for p in range(self.probes):
                    field[self.zero_plane, p, t] = nothing

    def from_left(self, x):
        return jnp.where(self.lane == 0, 0.0, pltpu.roll(x, 1, 1))

    def from_right(self, x):
        return jnp.where(self.lane == LANES - 1, 0.0, pltpu.roll(x, LANES - 1, 1))

    def from_before(self, x):
        return jnp.where(self.sublane == 0, 0.0, pltpu.roll(x, 1, 0))

    def from_after(self, x):
        return jnp.where(self.sublane == 7, 0.0, pltpu.roll(x, 7, 0))

    def first(self, own, to, other=None, beyond=()):
        chunks, folds, tiles = self.chunks, self.folds, self.tiles
        src, coef = self.src, self.coef
        turns = (self.from_left, self.from_right, self.from_before, self.from_after)
        shifted = [[f(x) for x in own] for f in turns]

        def body(z, carry):
            down = jnp.where(z > 0, z - 1, self.zero_plane) * tiles
            up = (z + 1) * tiles
            s = [[src[z * tiles + r * chunks + k] for k in range(chunks)] for r in range(folds)]
            for r in range(folds):
                for k in range(chunks):
                    t = r * chunks + k
                    same = coef[z * tiles + t] * s[r][k]
                    outer = []
                    for there, value, turn, kind in (
                        (k > 0, s[r][k - 1], (1, 1), 0),
                        (k + 1 < chunks, s[r][(k + 1) % chunks], (LANES - 1, 1), 1),
                        (r > 0, s[r - 1][k], (1, 0), 2),
                        (r + 1 < folds, s[(r + 1) % folds][k], (7, 0), 3),
                    ):
                        if there:
                            same = same + value
                        else:
                            outer.append((pltpu.roll(value, *turn), shifted[kind]))
                    for name, value in (("down", src[down + t]), ("up", src[up + t])):
                        if name == other:
                            outer.append((value, beyond))
                        else:
                            same = same + value
                    for p in range(self.probes):
                        result = same * own[p]
                        for value, factor in outer:
                            result = result + value * factor[p]
                        to[z, p, t] = result
            return carry

        return body

    def stencil(self, ref, valid, z, emit, extra):
        chunks, folds, tiles = self.chunks, self.folds, self.tiles
        first, stop = valid

        def at(z):
            return jnp.where((z >= first) & (z < stop), z, self.zero_plane)

        down, here, there, up = at(z - 1), at(z), at(z + 1), at(z + 2)
        for p in range(self.probes):
            pair = [[ref[plane, p, t] for t in range(tiles)] for plane in (here, there)]
            for r in range(folds):
                for k in range(chunks):
                    t = r * chunks + k
                    for n, value in enumerate(pair):
                        left = value[t - 1] if k else self.from_left(value[t + chunks - 1])
                        if k + 1 < chunks:
                            right = value[t + 1]
                        else:
                            right = self.from_right(value[t + 1 - chunks])
                        if r:
                            before = value[t - chunks]
                        else:
                            before = self.from_before(value[t + tiles - chunks])
                        if r + 1 < folds:
                            after = value[t + chunks]
                        else:
                            after = self.from_after(value[t + chunks - tiles])
                        above = pair[1 - n][t] + (ref[up, p, t] if n else ref[down, p, t])
                        weight = self.coef[(z + n) * tiles + t]
                        if extra:
                            weight = weight + extra
                        sides = (left + right) + (before + after)
                        emit(z + n, p, t, (sides + above) + weight * value[t])

    def step(self, ref, to, valid, wanted, extra=0.0):
        start, stop = wanted

        def body(n, carry):
            def emit(z, p, t, result):
                to[z, p, t] = result

            self.stencil(ref, valid, jnp.minimum(start + 2 * n, stop - 2), emit, extra)
            return carry

        lax.fori_loop(0, (stop - start + 1) // 2, body, 0)

    def widen(self, ref, to, valid, at_low, at_high):
        first, stop = valid

        def move(a, b):
            for p in range(self.probes):
                for t in range(self.tiles):
                    to[b, p, t] = ref[a, p, t]

        pl.when(at_low)(lambda: move(first, first - 1))
        pl.when(at_high)(lambda: move(stop - 1, stop))

    def images(self, m, u, by_one, by_two, span, carry, other=None):
        chunks, folds, tiles = self.chunks, self.folds, self.tiles
        src = self.src

        def at(z, valid):
            return jnp.where((z >= valid[0]) & (z < valid[1]), z, self.zero_plane)

        def body(z, carry):
            carry = [list(c) for c in carry]
            down = jnp.where(z > 0, z - 1, self.zero_plane) * tiles
            up = (z + 1) * tiles
            here, kept = at(z, by_one), at(z, by_two)
            s = [src[z * tiles + t] for t in range(tiles)]
            for t in range(tiles):
                r, k = t // chunks, t % chunks
                same = self.coef[z * tiles + t] * s[t]
                moved = []
                if k:
                    same = same + s[t - 1]
                else:
                    moved.append((2, self.from_left(s[t + chunks - 1])))
                if k + 1 < chunks:
                    same = same + s[t + 1]
                else:
                    moved.append((1, self.from_right(s[t + 1 - chunks])))
                if r:
                    same = same + s[t - chunks]
                else:
                    moved.append((4, self.from_before(s[t + tiles - chunks])))
                if r + 1 < folds:
                    same = same + s[t + chunks]
                else:
                    moved.append((3, self.from_after(s[t + chunks - tiles])))
                for name, value in (("down", src[down + t]), ("up", src[up + t])):
                    if name == other:
                        moved.append((5, value))
                    else:
                        same = same + value
                scaled = s[t] * (1.0 / STEP**2)
                for p in range(self.probes):
                    value = m[here, p, t]
                    carry[p][0] = carry[p][0] + (same * value + scaled * u[kept, p, t])
                    for n, factor in moved:
                        carry[p][n] = carry[p][n] + factor * value
            return tuple(tuple(c) for c in carry)

        if isinstance(span, int):
            return body(span, carry)
        return lax.fori_loop(*span, body, carry)

    def empty_sums(self):
        nothing = jnp.zeros((8, LANES), jnp.float32)
        return ((nothing,) * 6,) * self.probes

    def moved_sums(self, sums):
        return [
            c[0]
            + (self.from_left(c[1]) + self.from_right(c[2]))
            + (self.from_before(c[3]) + self.from_after(c[4]))
            for c in sums
        ]

    def after_tangent(self, odd, even, mine, at_low, at_high):
        first, stop = mine
        by_two = (jnp.where(at_low, first - 1, first), jnp.where(at_high, stop + 1, stop))
        by_one = (jnp.where(at_low, first - 2, first), jnp.where(at_high, stop + 2, stop))
        self.step(odd, even, mine, mine, 1.0 / STEP)
        self.widen(odd, even, mine, at_low, at_high)
        self.step(even, odd, by_two, by_two)
        self.widen(even, odd, by_two, at_low, at_high)
        return by_one, by_two


def inner_kernel(
    edge, density, background_in, sites_in, log_param_in, dirs_in,
    coef, src, wide, kept, sums,
    background, sites, log_param, dirs, order, bg, site, even, odd, sems,
):
    planes, rows, columns = background.shape
    chunks, folds = columns // LANES, rows // 8
    tiles = chunks * folds
    probes = dirs.shape[0]
    copies = [
        (log_param_in, log_param),
        (dirs_in, dirs),
        (background_in, background),
        (sites_in, sites),
    ]
    copies = [pltpu.make_async_copy(a, b, sems.at[n]) for n, (a, b) in enumerate(copies)]
    for copy in copies:
        copy.start()
    steps = Steps(chunks, folds, probes, planes, coef, src)
    steps.clear(even, odd)
    nothing = jnp.zeros((8, LANES), jnp.float32)
    for t in range(tiles):
        src[planes * tiles + t] = nothing
    order[...] = cell_order(columns, chunks)
    for copy in copies:
        copy.wait()
    spread = spread_cells(dirs, log_param, folds, chunks)
    for p in range(probes):
        wide[p] = spread[p]

    def store(z, t, weight, source):
        coef[z * tiles + t] = weight
        src[z * tiles + t] = source

    weights_and_sources(
        density, spread[probes], background, sites, (0, planes), order, bg, site, store
    )
    at_low = edge[0] != 0

    def low(z):
        return jnp.where(at_low, z, 0)

    last = planes - HALO
    lax.fori_loop(low(1), last + 2, steps.first(spread[:probes], odd), 0)
    steps.step(odd, even, (low(1), last + 2), (low(2), last + 1))
    for n, (ref, z) in enumerate(((odd, last), (odd, last + 1), (even, last - 1), (even, last))):
        for p in range(probes):
            for t in range(tiles):
                kept[n, p, t] = ref[z, p, t]
    mine = (low(HALO), last)
    steps.step(even, odd, (low(2), last + 1), mine)
    by_one, by_two = steps.after_tangent(odd, even, mine, at_low, True)
    result = steps.moved_sums(steps.images(odd, even, by_one, by_two, by_one, steps.empty_sums()))
    for p in range(probes):
        sums[p] = result[p]


def outer_kernel(
    chunks, folds, edge, own_coef, own_src, own_wide, kept, own_sums, packet, out,
    coef, src, even, odd,
):
    tiles = chunks * folds
    probes = own_wide.shape[0]
    total = even.shape[0] - 1
    planes = total - 2 * HALO
    steps = Steps(chunks, folds, probes, total, coef, src)
    last = planes - HALO
    halo = planes * tiles

    def copy(source, start, target, at, count):
        def body(n, carry):
            for t in range(tiles):
                target[at + n * tiles + t] = source[start + n * tiles + t]
            return carry

        lax.fori_loop(0, count, body, 0)

    own = (last - HALO) * tiles
    copy(own_src, own, src, own, planes - last + HALO)
    copy(own_coef, own, coef, own, planes - last + HALO)
    copy(packet, probes, src, halo, 2 * HALO)
    copy(packet, probes + 2 * HALO * tiles, coef, halo, 2 * HALO - 1)
    steps.clear(even, odd)
    for p in range(probes):
        for t in range(tiles):
            odd[last, p, t] = kept[0, p, t]
            odd[last + 1, p, t] = kept[1, p, t]
            even[last - 1, p, t] = kept[2, p, t]
            even[last, p, t] = kept[3, p, t]

    at_high = edge[1] != 0

    def high(z):
        return jnp.where(at_high, z, planes)

    mine = [own_wide[p] for p in range(probes)]
    beyond = [packet[p] for p in range(probes)]
    steps.first(mine, odd, "up", beyond)(planes - 1, 0)

    @pl.when(at_high)
    def _():
        steps.first(beyond, odd, "down", mine)(planes, 0)
        lax.fori_loop(planes + 1, total - 1, steps.first(beyond, odd), 0)

    steps.step(odd, even, (last, high(total - 1)), (last + 1, high(total - 2)))
    mine = (last, high(total - HALO))
    steps.step(even, odd, (last - 1, high(total - 2)), mine)
    by_one, by_two = steps.after_tangent(odd, even, mine, True, at_high)
    start, stop = by_one
    empty = steps.empty_sums()
    inside = steps.images(odd, even, by_one, by_two, (start, planes - 1), empty)
    inside = steps.images(odd, even, by_one, by_two, planes - 1, inside, "up")
    above = [list(c) for c in empty]
    for p in range(probes):
        above[p][0] = inside[p][5]
    above = steps.images(odd, even, by_one, by_two, (planes + 1, stop), tuple(tuple(c) for c in above))
    above = steps.images(odd, even, by_one, by_two, planes, above, "down")
    inside = [x + own_sums[p] + above[p][5] for p, x in enumerate(steps.moved_sums(inside))]
    above = steps.moved_sums(above)

    added = jnp.concatenate(inside + above, axis=0) * STEP**6
    images = cell_dot(added, cell_matrix(chunks, True))
    mask = own_cells(folds)
    for part in range(2):
        halves = []
        for p in range(probes):
            image = jnp.where(mask, images[8 * (part * probes + p) :][:8], 0.0)
            image = jnp.sum(image, axis=0, keepdims=True)
            halves += [image[:, h * LANES : (h + 1) * LANES] for h in range(image.shape[1] // LANES)]
        halves = jnp.concatenate(halves, axis=0)

        def send(n, carry):
            out[n, part] = halves
            return carry

        lax.fori_loop(0, out.shape[0], send, 0, unroll=8)


def eliminate(gram):
    count = gram.shape[0]
    rows = lax.broadcasted_iota(jnp.int32, (count, count), 0)
    columns = lax.broadcasted_iota(jnp.int32, (count, count), 1)
    inverse = jnp.where(rows == columns, 1.0, 0.0)
    for j in range(count - 1):
        across = jnp.broadcast_to(gram[:, j : j + 1], (count, count))
        turned = 1.0 / across
        ratio = jnp.where(rows > j, across, 0.0)
        gram_row, inverse_row = (gram * turned)[j : j + 1, :], (inverse * turned)[j : j + 1, :]
        gram = gram - ratio * gram_row
        inverse = inverse - ratio * inverse_row
    diagonal = jnp.sum(jnp.where(rows == columns, gram, 0.0), axis=1, keepdims=True)
    scale = 1.0 / jnp.sqrt(diagonal)
    upper = jnp.where(columns >= rows, gram, 0.0) * scale
    return upper, inverse * scale


def gram_of(parts, count):
    stacked = jnp.concatenate(list(parts) + [jnp.zeros_like(parts[0])], axis=0)
    stacked = stacked.astype(jnp.bfloat16)
    every = lax.dot_general(
        stacked, stacked, (((1,), (1,)), ((), ())), preferred_element_type=jnp.float32
    )
    tall = every[:count] + (every[count : 2 * count] + every[2 * count : 3 * count])
    return tall[:, :count] + (tall[:, count : 2 * count] + tall[:, 2 * count : 3 * count])


def times(a, parts):
    first, second, third = float_parts(a)
    left = jnp.concatenate([first, second, third, first, second, first], axis=1)
    right = jnp.concatenate([parts[0]] * 3 + [parts[1]] * 2 + [parts[2]], axis=0)
    return bf16_dot(left.astype(jnp.bfloat16), right.astype(jnp.bfloat16))


def factor_kernel(place, parts, q_out, lower_out, rows_ref, q_ref):
    groups, slabs, _, probes, cells = parts.shape
    count = groups * probes
    for g in range(groups):

        def gather(slab, carry):
            before = jnp.maximum(slab - 1, 0)
            image = parts[g, slab, 0] + jnp.where(slab > 0, parts[g, before, 1], 0.0)
            at = pl.multiple_of(slab * cells, cells)
            rows_ref[pl.ds(g * probes, probes), pl.ds(at, cells)] = image
            return carry

        lax.fori_loop(0, slabs, gather, 0, unroll=True if slabs <= 16 else 8)
    total = slabs * cells
    rows = rows_ref[...]
    parts_one = float_parts(rows)
    upper_one, inverse_one = eliminate(gram_of(parts_one, count) / total)
    basis = times(inverse_one, parts_one)
    rows_ref[...] = basis
    upper_two, inverse_two = eliminate(gram_of(float_parts(basis), count) / total)
    mine = rows_ref[:, pl.ds(pl.multiple_of(place[1] * cells, cells), cells)]
    q_ref[...] = dot_nn(inverse_two, mine)
    for g in range(groups):

        @pl.when(place[0] == g)
        def _():
            q_out[:, 0, :] = q_ref[pl.ds(g * probes, probes), :]

    r = lax.broadcasted_iota(jnp.int32, (count, count), 0)
    c = lax.broadcasted_iota(jnp.int32, (count, count), 1)
    lower_one = dot_nt(jnp.where(r == c, 1.0, 0.0), upper_one)
    lower_out[...] = dot_nt(lower_one, upper_two)


def everywhere(x):
    x = jnp.broadcast_to(jnp.sum(x, axis=1, keepdims=True), x.shape)
    for shift in (4, 2, 1):
        x = x + pltpu.roll(x, shift, 0)
    return x


def cholesky(rows, total):
    count = len(rows)
    rows = [list(row) for row in rows]
    gram = {}
    for i in range(count):
        for j in range(i + 1):
            product = sum(a * b for a, b in zip(rows[i][1:], rows[j][1:]))
            gram[i, j] = everywhere(rows[i][0] * rows[j][0] + product) * (1.0 / total)
    factor = {}
    for j in range(count):
        pivot = gram[j, j]
        turned = lax.rsqrt(pivot)
        turned = turned * (1.5 - 0.5 * pivot * turned * turned)
        factor[j, j] = pivot * turned
        rows[j] = [x * turned for x in rows[j]]
        for i in range(j + 1, count):
            factor[i, j] = gram[i, j] * turned
        for i in range(j + 1, count):
            for k in range(j + 1, i + 1):
                gram[i, k] = gram[i, k] - factor[i, j] * factor[k, j]
            rows[i] = [x - factor[i, j] * y for x, y in zip(rows[i], rows[j])]
    return factor, rows


def register_kernel(groups, slabs, probes, place, mine, other, q_out, lower_out, q_ref):
    halves = q_out.shape[2] // LANES
    pieces = probes * halves
    step = 2 * pieces
    sublane = lax.broadcasted_iota(jnp.int32, (8, LANES), 0)
    odd = jnp.broadcast_to(place[1] % 2, (8, LANES)) == 1

    def load(at):
        at = pl.ds(at, 8, stride=step)
        one, two = mine[at, :], other[at, :]
        return jnp.where(odd, two, one), jnp.where(odd, one, two)

    rows = []
    for g in range(groups):
        for p in range(probes):
            row = []
            for h in range(halves):
                last = None
                for block in range(slabs // 16):
                    at = (g * slabs // 2 + 8 * block) * step + p * halves + h
                    even_own, odd_own = load(at)
                    even_next, odd_next = load(at + pieces)
                    before = pltpu.roll(odd_next, 1, 0)
                    first = 0.0 if last is None else last
                    last = before
                    row.append((block, 0, h, even_own + jnp.where(sublane == 0, first, before)))
                    row.append((block, 1, h, odd_own + even_next))
            rows.append(row)
    places = [x[:3] for x in rows[0]]
    rows = [[x[3] for x in row] for row in rows]
    total = slabs * halves * LANES
    factor_one, basis = cholesky(rows, total)
    factor_two, rows = cholesky(basis, total)
    for i, row in enumerate(rows):
        for (block, parity, h), x in zip(places, row):
            q_ref[i, h, pl.ds(parity * (slabs // 2) + 8 * block, 8), :] = x
    own = (place[1] % 2) * (slabs // 2) + place[1] // 2
    for p in range(probes):
        for h in range(halves):
            mine = q_ref[place[0] * probes + p, h, pl.ds(own, 1), :]
            q_out[p, :, pl.ds(h * LANES, LANES)] = mine
    count = len(rows)
    r = lax.broadcasted_iota(jnp.int32, (8, LANES), 0)
    c = lax.broadcasted_iota(jnp.int32, (8, LANES), 1)
    lower = jnp.zeros((8, LANES), jnp.float32)
    for i in range(count):
        for j in range(i + 1):
            entry = sum(factor_one[i, k] * factor_two[k, j] for k in range(j, i + 1))
            lower = jnp.where((r == i) & (c == j), entry, lower)
    lower_out[...] = lower[:count, :count]


def shards(probe_dirs, log_param, background, site_class, trap_density):
    probes = probe_dirs.shape[0]
    cells = probe_dirs.shape[2]
    planes, rows, columns = background.shape
    slabs = lax.axis_size("space")
    groups = lax.axis_size("probe")
    at_space = lax.axis_index("space")
    vmem = pl.BlockSpec(memory_space=pltpu.VMEM)
    smem = pl.BlockSpec(memory_space=pltpu.SMEM)
    anywhere = pl.BlockSpec(memory_space=pl.ANY)
    params = pltpu.CompilerParams(vmem_limit_bytes=62 * 2**20)

    chunks, folds = columns // LANES, rows // 8
    tiles = chunks * folds
    total = planes + 2 * HALO
    tile = (8, LANES)

    def shape(*dims):
        return jax.ShapeDtypeStruct(dims + tile, jnp.float32)

    def scratch(*dims):
        return pltpu.VMEM(dims + tile, jnp.float32)

    def copies(count):
        return pltpu.SemaphoreType.DMA((count,))

    def inputs(held):
        return [
            pltpu.VMEM((held, rows, columns), jnp.float32),
            pltpu.VMEM((held, rows, columns), jnp.int32),
            pltpu.VMEM(log_param.shape, jnp.float32),
            pltpu.VMEM(probe_dirs.shape, jnp.float32),
            pltpu.VMEM((columns, columns), jnp.bfloat16),
        ]

    def rows_of(held):
        return pltpu.VMEM((chunks, held * rows, LANES), jnp.float32)

    size = probes + (4 * HALO - 1) * tiles
    packet = pl.pallas_call(
        packet_kernel,
        out_shape=shape(size),
        in_specs=[smem] + [anywhere] * 4,
        out_specs=anywhere,
        scratch_shapes=inputs(2 * HALO)
        + [rows_of(2 * HALO), rows_of(2 * HALO), scratch(size), copies(4), copies(4)],
        compiler_params=params,
        name="packet",
    )(trap_density, background, site_class, log_param, probe_dirs)

    down = [(i + 1, i) for i in range(slabs - 1)]
    next_packet = lax.ppermute(packet, "space", down)
    edge = jnp.stack([at_space > 0, at_space < slabs - 1]).astype(jnp.int32)
    own_coef, own_src, wide, kept, sums = pl.pallas_call(
        inner_kernel,
        out_shape=(
            shape(planes * tiles),
            shape((planes + 1) * tiles),
            shape(probes),
            shape(4, probes, tiles),
            shape(probes),
        ),
        in_specs=[smem, smem] + [anywhere] * 4,
        out_specs=(vmem,) * 5,
        scratch_shapes=inputs(planes)
        + [rows_of(planes), rows_of(planes)]
        + [scratch(planes + 1, probes, tiles)] * 2
        + [copies(4)],
        compiler_params=pltpu.CompilerParams(vmem_limit_bytes=28 * 2**20),
        cost_estimate=pl.CostEstimate(flops=10**9, bytes_accessed=2**24, transcendentals=256),
        name="inner",
    )(edge, trap_density, background, site_class, log_param, probe_dirs)

    pieces = probes * cells // LANES
    images = pl.pallas_call(
        functools.partial(outer_kernel, chunks, folds),
        out_shape=jax.ShapeDtypeStruct((groups * slabs // 2, 2, pieces, LANES), jnp.float32),
        in_specs=[smem] + [vmem] * 6,
        out_specs=vmem,
        scratch_shapes=[
            scratch(total * tiles),
            scratch(total * tiles),
            scratch(total + 1, probes, tiles),
            scratch(total + 1, probes, tiles),
        ],
        compiler_params=pltpu.CompilerParams(vmem_limit_bytes=28 * 2**20),
        name="outer",
    )(edge, own_coef, own_src, wide, kept, sums, next_packet)

    same = [
        [g * slabs + z for g in range(groups) for z in range(parity, slabs, 2)] for parity in (0, 1)
    ]
    mine = lax.all_to_all(
        images, ("probe", "space"), split_axis=0, concat_axis=0, axis_index_groups=same, tiled=True
    )
    other = lax.ppermute(mine, "space", [(z, z ^ 1) for z in range(slabs)])
    place = jnp.stack([lax.axis_index("probe"), at_space]).astype(jnp.int32)
    count = groups * probes
    results = (
        jax.ShapeDtypeStruct((probes, 1, cells), jnp.float32),
        jax.ShapeDtypeStruct((count, count), jnp.float32),
    )
    params = pltpu.CompilerParams(vmem_limit_bytes=28 * 2**20)
    if count <= 8 and slabs % 16 == 0:
        halves = cells // LANES
        return pl.pallas_call(
            functools.partial(register_kernel, groups, slabs, probes),
            out_shape=results,
            in_specs=[smem, vmem, vmem],
            out_specs=(vmem, vmem),
            scratch_shapes=[pltpu.VMEM((count, halves, slabs, LANES), jnp.float32)],
            compiler_params=params,
            name="factor",
        )(
            place,
            mine.reshape((groups * slabs * pieces, LANES)),
            other.reshape((groups * slabs * pieces, LANES)),
        )
    odd = at_space % 2 == 1
    pairs = [jnp.where(odd, other, mine), jnp.where(odd, mine, other)]
    pairs = [x.reshape((groups, slabs // 2, 2, probes, cells)) for x in pairs]
    every = jnp.stack(pairs, axis=2).reshape((groups, slabs, 2, probes, cells))
    return pl.pallas_call(
        factor_kernel,
        out_shape=results,
        in_specs=[smem, vmem],
        out_specs=(vmem, vmem),
        scratch_shapes=[
            pltpu.VMEM((count, slabs * cells), jnp.float32),
            pltpu.VMEM((count, cells), jnp.float32),
        ],
        compiler_params=params,
        name="factor",
    )(place, every)


def solution(mesh):
    placed = (
        P("probe", "space", None),
        P("space", None),
        P("space", None, None),
        P("space", None, None),
        P(),
    )
    return jax.shard_map(
        shards,
        mesh=mesh,
        in_specs=placed,
        out_specs=(P("probe", "space", None), P()),
        check_vma=False,
    )
```

```python
import functools

import jax
import jax.numpy as jnp
from jax import lax
from jax.experimental import pallas as pl
from jax.experimental.pallas import tpu as pltpu
from jax.sharding import PartitionSpec as P

PX = 64
PY = 4
REF = 8
STEP = 0.12
HALO = 3
LANES = 128
HIGHEST = lax.Precision.HIGHEST


def dot_nn(a, b):
    return lax.dot_general(
        a, b, (((1,), (0,)), ((), ())), precision=HIGHEST, preferred_element_type=jnp.float32
    )


def dot_nt(a, b):
    return lax.dot_general(
        a, b, (((1,), (1,)), ((), ())), precision=HIGHEST, preferred_element_type=jnp.float32
    )


def parts_of(x):
    first = x.astype(jnp.bfloat16)
    rest = x - first.astype(jnp.float32)
    second = rest.astype(jnp.bfloat16)
    third = (rest - second.astype(jnp.float32)).astype(jnp.bfloat16)
    return first, second, third


def bf16_dot(a, b):
    return jnp.dot(a, b, preferred_element_type=jnp.float32)


def interleave(exact, small, order):
    parts = [part for x in exact for part in parts_of(x)] + [x.astype(jnp.bfloat16) for x in small]
    placed = bf16_dot(jnp.concatenate(parts, axis=0), order[...])
    results, at = [], 0
    for x in exact:
        count = x.shape[0]
        first, second, third = [placed[at + n * count : at + (n + 1) * count] for n in range(3)]
        results.append((first + second) + third)
        at += 3 * count
    for x in small:
        results.append(placed[at : at + x.shape[0]])
        at += x.shape[0]
    return results


def keep(placed, kept):
    for k in range(kept.shape[0]):
        kept[k] = placed[:, k * LANES : (k + 1) * LANES]


def flat(planes):
    return planes.reshape((planes.shape[0] * planes.shape[1], planes.shape[2]))


def cell_matrix(chunks, turned=False):
    half = REF // chunks
    dims = (LANES, PX * PY) if turned else (PX * PY, LANES)
    cell = lax.broadcasted_iota(jnp.int32, dims, int(turned)) % PX
    lane = lax.broadcasted_iota(jnp.int32, dims, 1 - int(turned)) // half
    return jnp.where(cell == lane, 1.0, 0.0).astype(jnp.float32)


def own_cells(folds):
    half = REF // folds
    sublane = lax.broadcasted_iota(jnp.int32, (8, PX * PY), 0) // half
    return lax.broadcasted_iota(jnp.int32, (8, PX * PY), 1) // PX == sublane


def prolonged(coarse, folds, chunks):
    mask = own_cells(folds)
    rows = [jnp.where(mask, coarse[n : n + 1, :], 0.0) for n in range(coarse.shape[0])]
    return cell_dot(jnp.concatenate(rows, axis=0), cell_matrix(chunks))


def cell_dot(rows, matrix):
    count = rows.shape[0]
    parts = jnp.concatenate(float_parts(rows), axis=0).astype(jnp.bfloat16)
    placed = bf16_dot(parts, matrix.astype(jnp.bfloat16))
    return (placed[:count] + placed[count : 2 * count]) + placed[2 * count :]


def float_parts(x):
    first = x.astype(jnp.bfloat16).astype(jnp.float32)
    rest = x - first
    second = rest.astype(jnp.bfloat16).astype(jnp.float32)
    return first, second, rest - second


def cell_order(columns, chunks):
    x = lax.broadcasted_iota(jnp.int32, (columns, columns), 0)
    place = lax.broadcasted_iota(jnp.int32, (columns, columns), 1)
    wanted = chunks * (place % LANES) + place // LANES
    return jnp.where(x == wanted, 1.0, 0.0).astype(jnp.bfloat16)


def spread_cells(dirs, log_param, folds, chunks):
    probes = dirs.shape[0]
    coarse = [dirs[p] for p in range(probes)] + [jnp.exp(log_param[...])]
    spread = prolonged(jnp.concatenate(coarse, axis=0), folds, chunks)
    return [spread[8 * n : 8 * n + 8, :] for n in range(probes + 1)]


def tile_rows(z, r, rows, folds):
    return pl.ds(z * rows + r, 8, stride=folds)


def trap_of(density, kind):
    trap = jnp.full((8, LANES), density[density.shape[0] - 1])
    for n in range(density.shape[0] - 2, -1, -1):
        trap = jnp.where(kind == float(n), density[n], trap)
    return trap


def weight_of(trap):
    return (1.0 / STEP - 6.0) - trap


def source_of(trap, background):
    return -STEP * trap * background


def packet_kernel(
    density, background_in, sites_in, log_param_in, dirs_in, packet,
    background, sites, log_param, dirs, order, bg, site, made, sems, out_sems,
):
    count, rows, columns = sites.shape
    chunks, folds = columns // LANES, rows // 8
    tiles = chunks * folds
    probes = dirs.shape[0]
    pairs = [
        (log_param_in, log_param),
        (dirs_in, dirs),
        (background_in.at[pl.ds(count - 1, 1)], background),
        (sites_in.at[pl.ds(0, count)], sites),
    ]
    copies = [pltpu.make_async_copy(a, b, sems.at[n]) for n, (a, b) in enumerate(pairs)]
    for copy in copies:
        copy.start()
    order[...] = cell_order(columns, chunks)
    copies[0].wait()
    copies[1].wait()
    spread = spread_cells(dirs, log_param, folds, chunks)
    for p in range(probes):
        made[p] = spread[p]
    copies[2].wait()
    copies[3].wait()
    placed = interleave([flat(background[...])], [flat(sites[...]).astype(jnp.float32)], order)
    keep(placed[0], bg)
    keep(placed[1], site)
    sent = []

    def send(start, stop):
        at = pl.ds(start, stop - start)
        copy = pltpu.make_async_copy(made.at[at], packet.at[at], out_sems.at[len(sent)])
        copy.start()
        sent.append(copy)

    first = probes + tiles
    middle = first + (count - 1) // 2 * tiles
    for z in range(count):
        for r in range(folds):
            for k in range(chunks):
                t = r * chunks + k
                trap = trap_of(density, site[k, tile_rows(z, r, rows, folds), :]) * spread[probes]
                if z < count - 1:
                    made[first + z * tiles + t] = trap
                else:
                    made[probes + t] = source_of(trap, bg[k, tile_rows(0, r, rows, folds), :])
        if z == (count - 1) // 2 - 1:
            send(first, middle)
        elif z == count - 2:
            send(middle, first + (count - 1) * tiles)
    send(0, first)
    for copy in sent:
        copy.wait()


class Steps:
    def __init__(self, chunks, folds, probes, zero_plane, coef, src):
        self.chunks, self.folds, self.tiles = chunks, folds, chunks * folds
        self.probes, self.zero_plane = probes, zero_plane
        self.coef, self.src = coef, src
        self.lane = lax.broadcasted_iota(jnp.int32, (8, LANES), 1)
        self.sublane = lax.broadcasted_iota(jnp.int32, (8, LANES), 0)

    def clear(self, *fields):
        nothing = jnp.zeros((8, LANES), jnp.float32)
        for t in range(self.tiles):
            for field in fields:
                for p in range(self.probes):
                    field[self.zero_plane, p, t] = nothing

    def from_left(self, x):
        return jnp.where(self.lane == 0, 0.0, pltpu.roll(x, 1, 1))

    def from_right(self, x):
        return jnp.where(self.lane == LANES - 1, 0.0, pltpu.roll(x, LANES - 1, 1))

    def from_before(self, x):
        return jnp.where(self.sublane == 0, 0.0, pltpu.roll(x, 1, 0))

    def from_after(self, x):
        return jnp.where(self.sublane == 7, 0.0, pltpu.roll(x, 7, 0))

    def first(self, own, to, other=None, beyond=()):
        chunks, folds, tiles = self.chunks, self.folds, self.tiles
        src, coef = self.src, self.coef
        turns = (self.from_left, self.from_right, self.from_before, self.from_after)
        shifted = [[f(x) for x in own] for f in turns]

        def body(z, carry):
            down = jnp.where(z > 0, z - 1, self.zero_plane) * tiles
            up = (z + 1) * tiles
            s = [[src[z * tiles + r * chunks + k] for k in range(chunks)] for r in range(folds)]
            for r in range(folds):
                for k in range(chunks):
                    t = r * chunks + k
                    same = coef[z * tiles + t] * s[r][k]
                    outer = []
                    for there, value, turn, kind in (
                        (k > 0, s[r][k - 1], (1, 1), 0),
                        (k + 1 < chunks, s[r][(k + 1) % chunks], (LANES - 1, 1), 1),
                        (r > 0, s[r - 1][k], (1, 0), 2),
                        (r + 1 < folds, s[(r + 1) % folds][k], (7, 0), 3),
                    ):
                        if there:
                            same = same + value
                        else:
                            outer.append((pltpu.roll(value, *turn), shifted[kind]))
                    for name, value in (("down", src[down + t]), ("up", src[up + t])):
                        if name == other:
                            outer.append((value, beyond))
                        else:
                            same = same + value
                    for p in range(self.probes):
                        result = same * own[p]
                        for value, factor in outer:
                            result = result + value * factor[p]
                        to[z, p, t] = result
            return carry

        return body

    def stencil(self, ref, valid, z, emit, extra):
        chunks, folds, tiles = self.chunks, self.folds, self.tiles
        first, stop = valid

        def at(z):
            return jnp.where((z >= first) & (z < stop), z, self.zero_plane)

        down, here, there, up = at(z - 1), at(z), at(z + 1), at(z + 2)
        for p in range(self.probes):
            pair = [[ref[plane, p, t] for t in range(tiles)] for plane in (here, there)]
            for r in range(folds):
                for k in range(chunks):
                    t = r * chunks + k
                    for n, value in enumerate(pair):
                        left = value[t - 1] if k else self.from_left(value[t + chunks - 1])
                        if k + 1 < chunks:
                            right = value[t + 1]
                        else:
                            right = self.from_right(value[t + 1 - chunks])
                        if r:
                            before = value[t - chunks]
                        else:
                            before = self.from_before(value[t + tiles - chunks])
                        if r + 1 < folds:
                            after = value[t + chunks]
                        else:
                            after = self.from_after(value[t + chunks - tiles])
                        above = pair[1 - n][t] + (ref[up, p, t] if n else ref[down, p, t])
                        weight = self.coef[(z + n) * tiles + t]
                        if extra:
                            weight = weight + extra
                        sides = (left + right) + (before + after)
                        emit(z + n, p, t, (sides + above) + weight * value[t])

    def step(self, ref, to, valid, wanted, extra=0.0):
        start, stop = wanted

        def body(n, carry):
            def emit(z, p, t, result):
                to[z, p, t] = result

            self.stencil(ref, valid, jnp.minimum(start + 2 * n, stop - 2), emit, extra)
            return carry

        lax.fori_loop(0, (stop - start + 1) // 2, body, 0)

    def widen(self, ref, to, valid, at_low, at_high):
        first, stop = valid

        def move(a, b):
            for p in range(self.probes):
                for t in range(self.tiles):
                    to[b, p, t] = ref[a, p, t]

        pl.when(at_low)(lambda: move(first, first - 1))
        pl.when(at_high)(lambda: move(stop - 1, stop))

    def images(self, m, u, by_one, by_two, span, carry, other=None):
        chunks, folds, tiles = self.chunks, self.folds, self.tiles
        src = self.src

        def at(z, valid):
            return jnp.where((z >= valid[0]) & (z < valid[1]), z, self.zero_plane)

        def body(z, carry):
            carry = [list(c) for c in carry]
            down = jnp.where(z > 0, z - 1, self.zero_plane) * tiles
            up = (z + 1) * tiles
            here, kept = at(z, by_one), at(z, by_two)
            s = [src[z * tiles + t] for t in range(tiles)]
            for t in range(tiles):
                r, k = t // chunks, t % chunks
                same = self.coef[z * tiles + t] * s[t]
                moved = []
                if k:
                    same = same + s[t - 1]
                else:
                    moved.append((2, self.from_left(s[t + chunks - 1])))
                if k + 1 < chunks:
                    same = same + s[t + 1]
                else:
                    moved.append((1, self.from_right(s[t + 1 - chunks])))
                if r:
                    same = same + s[t - chunks]
                else:
                    moved.append((4, self.from_before(s[t + tiles - chunks])))
                if r + 1 < folds:
                    same = same + s[t + chunks]
                else:
                    moved.append((3, self.from_after(s[t + chunks - tiles])))
                for name, value in (("down", src[down + t]), ("up", src[up + t])):
                    if name == other:
                        moved.append((5, value))
                    else:
                        same = same + value
                scaled = s[t] * (1.0 / STEP**2)
                for p in range(self.probes):
                    value = m[here, p, t]
                    carry[p][0] = carry[p][0] + (same * value + scaled * u[kept, p, t])
                    for n, factor in moved:
                        carry[p][n] = carry[p][n] + factor * value
            return tuple(tuple(c) for c in carry)

        if isinstance(span, int):
            return body(span, carry)
        return lax.fori_loop(*span, body, carry)

    def empty_sums(self):
        nothing = jnp.zeros((8, LANES), jnp.float32)
        return ((nothing,) * 6,) * self.probes

    def moved_sums(self, sums):
        return [
            c[0]
            + (self.from_left(c[1]) + self.from_right(c[2]))
            + (self.from_before(c[3]) + self.from_after(c[4]))
            for c in sums
        ]

    def after_tangent(self, odd, even, mine, at_low, at_high):
        first, stop = mine
        by_two = (jnp.where(at_low, first - 1, first), jnp.where(at_high, stop + 1, stop))
        by_one = (jnp.where(at_low, first - 2, first), jnp.where(at_high, stop + 2, stop))
        self.step(odd, even, mine, mine, 1.0 / STEP)
        self.widen(odd, even, mine, at_low, at_high)
        self.step(even, odd, by_two, by_two)
        self.widen(even, odd, by_two, at_low, at_high)
        return by_one, by_two


def inner_kernel(
    edge, density, background_in, sites_in, log_param_in, dirs_in, beyond,
    coef, src, wide, kept, sums, next_bg,
    background, sites, log_param, dirs, order, bg, far, site, even, odd, sems,
):
    planes, rows, columns = background.shape
    chunks, folds = columns // LANES, rows // 8
    tiles = chunks * folds
    probes = dirs.shape[0]
    copies = [
        (log_param_in, log_param),
        (dirs_in, dirs),
        (background_in, background),
        (sites_in, sites),
    ]
    copies = [pltpu.make_async_copy(a, b, sems.at[n]) for n, (a, b) in enumerate(copies)]
    for copy in copies:
        copy.start()
    steps = Steps(chunks, folds, probes, planes, coef, src)
    steps.clear(even, odd)
    nothing = jnp.zeros((8, LANES), jnp.float32)
    for t in range(tiles):
        src[planes * tiles + t] = nothing
    order[...] = cell_order(columns, chunks)
    for copy in copies:
        copy.wait()
    spread = spread_cells(dirs, log_param, folds, chunks)
    for p in range(probes):
        wide[p] = spread[p]

    placed = interleave(
        [flat(background[...]), flat(beyond[...])], [flat(sites[...]).astype(jnp.float32)], order
    )
    for x, scratch in zip(placed, (bg, far, site)):
        keep(x, scratch)
    for r in range(folds):
        for k in range(chunks):
            t = r * chunks + k
            for z in range(planes):
                at = tile_rows(z, r, rows, folds)
                trap = trap_of(density, site[k, at, :]) * spread[probes]
                coef[z * tiles + t] = weight_of(trap)
                src[z * tiles + t] = source_of(trap, bg[k, at, :])
            for z in range(beyond.shape[0]):
                next_bg[z * tiles + t] = far[k, tile_rows(z, r, rows, folds), :]
    at_low = edge[0] != 0

    def low(z):
        return jnp.where(at_low, z, 0)

    last = planes - HALO
    lax.fori_loop(low(1), last + 2, steps.first(spread[:probes], odd), 0)
    steps.step(odd, even, (low(1), last + 2), (low(2), last + 1))
    for n, (ref, z) in enumerate(((odd, last), (odd, last + 1), (even, last - 1), (even, last))):
        for p in range(probes):
            for t in range(tiles):
                kept[n, p, t] = ref[z, p, t]
    mine = (low(HALO), last)
    steps.step(even, odd, (low(2), last + 1), mine)
    by_one, by_two = steps.after_tangent(odd, even, mine, at_low, True)
    result = steps.moved_sums(steps.images(odd, even, by_one, by_two, by_one, steps.empty_sums()))
    for p in range(probes):
        sums[p] = result[p]


def outer_kernel(
    chunks, folds, edge, own_coef, own_src, own_wide, kept, own_sums, next_bg, packet, out,
    coef, src, even, odd,
):
    tiles = chunks * folds
    probes = own_wide.shape[0]
    total = even.shape[0] - 1
    planes = total - 2 * HALO
    steps = Steps(chunks, folds, probes, total, coef, src)
    last = planes - HALO
    halo = planes * tiles

    def copy(source, start, target, at, count):
        def body(n, carry):
            for t in range(tiles):
                target[at + n * tiles + t] = source[start + n * tiles + t]
            return carry

        lax.fori_loop(0, count, body, 0)

    own = (last - HALO) * tiles
    copy(own_src, own, src, own, planes - last + HALO)
    copy(own_coef, own, coef, own, planes - last + HALO)

    def beyond_plane(n, carry):
        for t in range(tiles):
            at = n * tiles + t
            trap = packet[probes + tiles + at]
            coef[halo + at] = weight_of(trap)
            src[halo + at] = source_of(trap, next_bg[at])
        return carry

    lax.fori_loop(0, 2 * HALO - 1, beyond_plane, 0)
    copy(packet, probes, src, (total - 1) * tiles, 1)
    steps.clear(even, odd)
    for p in range(probes):
        for t in range(tiles):
            odd[last, p, t] = kept[0, p, t]
            odd[last + 1, p, t] = kept[1, p, t]
            even[last - 1, p, t] = kept[2, p, t]
            even[last, p, t] = kept[3, p, t]

    at_high = edge[1] != 0

    def high(z):
        return jnp.where(at_high, z, planes)

    mine = [own_wide[p] for p in range(probes)]
    beyond = [packet[p] for p in range(probes)]
    steps.first(mine, odd, "up", beyond)(planes - 1, 0)

    @pl.when(at_high)
    def _():
        steps.first(beyond, odd, "down", mine)(planes, 0)
        lax.fori_loop(planes + 1, total - 1, steps.first(beyond, odd), 0)

    steps.step(odd, even, (last, high(total - 1)), (last + 1, high(total - 2)))
    mine = (last, high(total - HALO))
    steps.step(even, odd, (last - 1, high(total - 2)), mine)
    by_one, by_two = steps.after_tangent(odd, even, mine, True, at_high)
    start, stop = by_one
    empty = steps.empty_sums()
    inside = steps.images(odd, even, by_one, by_two, (start, planes - 1), empty)
    inside = steps.images(odd, even, by_one, by_two, planes - 1, inside, "up")
    above = [list(c) for c in empty]
    for p in range(probes):
        above[p][0] = inside[p][5]
    above = steps.images(odd, even, by_one, by_two, (planes + 1, stop), tuple(tuple(c) for c in above))
    above = steps.images(odd, even, by_one, by_two, planes, above, "down")
    inside = [x + own_sums[p] + above[p][5] for p, x in enumerate(steps.moved_sums(inside))]
    above = steps.moved_sums(above)

    added = jnp.concatenate(inside + above, axis=0) * STEP**6
    images = cell_dot(added, cell_matrix(chunks, True))
    mask = own_cells(folds)
    for part in range(2):
        halves = []
        for p in range(probes):
            image = jnp.where(mask, images[8 * (part * probes + p) :][:8], 0.0)
            image = jnp.sum(image, axis=0, keepdims=True)
            halves += [image[:, h * LANES : (h + 1) * LANES] for h in range(image.shape[1] // LANES)]
        halves = jnp.concatenate(halves, axis=0)

        def send(n, carry):
            out[n, part] = halves
            return carry

        lax.fori_loop(0, out.shape[0], send, 0, unroll=8)


def eliminate(gram):
    count = gram.shape[0]
    rows = lax.broadcasted_iota(jnp.int32, (count, count), 0)
    columns = lax.broadcasted_iota(jnp.int32, (count, count), 1)
    inverse = jnp.where(rows == columns, 1.0, 0.0)
    for j in range(count - 1):
        across = jnp.broadcast_to(gram[:, j : j + 1], (count, count))
        turned = 1.0 / across
        ratio = jnp.where(rows > j, across, 0.0)
        gram_row, inverse_row = (gram * turned)[j : j + 1, :], (inverse * turned)[j : j + 1, :]
        gram = gram - ratio * gram_row
        inverse = inverse - ratio * inverse_row
    diagonal = jnp.sum(jnp.where(rows == columns, gram, 0.0), axis=1, keepdims=True)
    scale = 1.0 / jnp.sqrt(diagonal)
    upper = jnp.where(columns >= rows, gram, 0.0) * scale
    return upper, inverse * scale


def gram_of(parts, count):
    stacked = jnp.concatenate(list(parts) + [jnp.zeros_like(parts[0])], axis=0)
    stacked = stacked.astype(jnp.bfloat16)
    every = lax.dot_general(
        stacked, stacked, (((1,), (1,)), ((), ())), preferred_element_type=jnp.float32
    )
    tall = every[:count] + (every[count : 2 * count] + every[2 * count : 3 * count])
    return tall[:, :count] + (tall[:, count : 2 * count] + tall[:, 2 * count : 3 * count])


def times(a, parts):
    first, second, third = float_parts(a)
    left = jnp.concatenate([first, second, third, first, second, first], axis=1)
    right = jnp.concatenate([parts[0]] * 3 + [parts[1]] * 2 + [parts[2]], axis=0)
    return bf16_dot(left.astype(jnp.bfloat16), right.astype(jnp.bfloat16))


def factor_kernel(place, parts, q_out, lower_out, rows_ref, q_ref):
    groups, slabs, _, probes, cells = parts.shape
    count = groups * probes
    for g in range(groups):

        def gather(slab, carry):
            before = jnp.maximum(slab - 1, 0)
            image = parts[g, slab, 0] + jnp.where(slab > 0, parts[g, before, 1], 0.0)
            at = pl.multiple_of(slab * cells, cells)
            rows_ref[pl.ds(g * probes, probes), pl.ds(at, cells)] = image
            return carry

        lax.fori_loop(0, slabs, gather, 0, unroll=True if slabs <= 16 else 8)
    total = slabs * cells
    rows = rows_ref[...]
    parts_one = float_parts(rows)
    upper_one, inverse_one = eliminate(gram_of(parts_one, count) / total)
    basis = times(inverse_one, parts_one)
    rows_ref[...] = basis
    upper_two, inverse_two = eliminate(gram_of(float_parts(basis), count) / total)
    mine = rows_ref[:, pl.ds(pl.multiple_of(place[1] * cells, cells), cells)]
    q_ref[...] = dot_nn(inverse_two, mine)
    for g in range(groups):

        @pl.when(place[0] == g)
        def _():
            q_out[:, 0, :] = q_ref[pl.ds(g * probes, probes), :]

    r = lax.broadcasted_iota(jnp.int32, (count, count), 0)
    c = lax.broadcasted_iota(jnp.int32, (count, count), 1)
    lower_one = dot_nt(jnp.where(r == c, 1.0, 0.0), upper_one)
    lower_out[...] = dot_nt(lower_one, upper_two)


def everywhere(x):
    x = jnp.broadcast_to(jnp.sum(x, axis=1, keepdims=True), x.shape)
    for shift in (4, 2, 1):
        x = x + pltpu.roll(x, shift, 0)
    return x


def cholesky(rows, total):
    count = len(rows)
    rows = [list(row) for row in rows]
    gram = {}
    for i in range(count):
        for j in range(i + 1):
            product = sum(a * b for a, b in zip(rows[i][1:], rows[j][1:]))
            gram[i, j] = everywhere(rows[i][0] * rows[j][0] + product) * (1.0 / total)
    factor = {}
    for j in range(count):
        pivot = gram[j, j]
        turned = lax.rsqrt(pivot)
        turned = turned * (1.5 - 0.5 * pivot * turned * turned)
        factor[j, j] = pivot * turned
        rows[j] = [x * turned for x in rows[j]]
        for i in range(j + 1, count):
            factor[i, j] = gram[i, j] * turned
        for i in range(j + 1, count):
            for k in range(j + 1, i + 1):
                gram[i, k] = gram[i, k] - factor[i, j] * factor[k, j]
            rows[i] = [x - factor[i, j] * y for x, y in zip(rows[i], rows[j])]
    return factor, rows


def register_kernel(groups, slabs, probes, place, mine, other, q_out, lower_out, q_ref):
    halves = q_out.shape[2] // LANES
    pieces = probes * halves
    step = 2 * pieces
    sublane = lax.broadcasted_iota(jnp.int32, (8, LANES), 0)
    odd = jnp.broadcast_to(place[1] % 2, (8, LANES)) == 1

    def load(at):
        at = pl.ds(at, 8, stride=step)
        one, two = mine[at, :], other[at, :]
        return jnp.where(odd, two, one), jnp.where(odd, one, two)

    rows = []
    for g in range(groups):
        for p in range(probes):
            row = []
            for h in range(halves):
                last = None
                for block in range(slabs // 16):
                    at = (g * slabs // 2 + 8 * block) * step + p * halves + h
                    even_own, odd_own = load(at)
                    even_next, odd_next = load(at + pieces)
                    before = pltpu.roll(odd_next, 1, 0)
                    first = 0.0 if last is None else last
                    last = before
                    row.append((block, 0, h, even_own + jnp.where(sublane == 0, first, before)))
                    row.append((block, 1, h, odd_own + even_next))
            rows.append(row)
    places = [x[:3] for x in rows[0]]
    rows = [[x[3] for x in row] for row in rows]
    total = slabs * halves * LANES
    factor_one, basis = cholesky(rows, total)
    factor_two, rows = cholesky(basis, total)
    for i, row in enumerate(rows):
        for (block, parity, h), x in zip(places, row):
            q_ref[i, h, pl.ds(parity * (slabs // 2) + 8 * block, 8), :] = x
    own = (place[1] % 2) * (slabs // 2) + place[1] // 2
    for p in range(probes):
        for h in range(halves):
            mine = q_ref[place[0] * probes + p, h, pl.ds(own, 1), :]
            q_out[p, :, pl.ds(h * LANES, LANES)] = mine
    count = len(rows)
    r = lax.broadcasted_iota(jnp.int32, (8, LANES), 0)
    c = lax.broadcasted_iota(jnp.int32, (8, LANES), 1)
    lower = jnp.zeros((8, LANES), jnp.float32)
    for i in range(count):
        for j in range(i + 1):
            entry = sum(factor_one[i, k] * factor_two[k, j] for k in range(j, i + 1))
            lower = jnp.where((r == i) & (c == j), entry, lower)
    lower_out[...] = lower[:count, :count]


def shards(probe_dirs, log_param, background, site_class, trap_density):
    probes = probe_dirs.shape[0]
    cells = probe_dirs.shape[2]
    planes, rows, columns = background.shape
    slabs = lax.axis_size("space")
    groups = lax.axis_size("probe")
    at_space = lax.axis_index("space")
    vmem = pl.BlockSpec(memory_space=pltpu.VMEM)
    smem = pl.BlockSpec(memory_space=pltpu.SMEM)
    anywhere = pl.BlockSpec(memory_space=pl.ANY)
    params = pltpu.CompilerParams(vmem_limit_bytes=62 * 2**20)

    chunks, folds = columns // LANES, rows // 8
    tiles = chunks * folds
    total = planes + 2 * HALO
    tile = (8, LANES)

    def shape(*dims):
        return jax.ShapeDtypeStruct(dims + tile, jnp.float32)

    def scratch(*dims):
        return pltpu.VMEM(dims + tile, jnp.float32)

    def copies(count):
        return pltpu.SemaphoreType.DMA((count,))

    def inputs(held, sites):
        return [
            pltpu.VMEM((held, rows, columns), jnp.float32),
            pltpu.VMEM((sites, rows, columns), jnp.int32),
            pltpu.VMEM(log_param.shape, jnp.float32),
            pltpu.VMEM(probe_dirs.shape, jnp.float32),
            pltpu.VMEM((columns, columns), jnp.bfloat16),
        ]

    def rows_of(held):
        return pltpu.VMEM((chunks, held * rows, LANES), jnp.float32)

    down = [(i + 1, i) for i in range(slabs - 1)]
    beyond = lax.ppermute(background[: 2 * HALO - 1], "space", down)
    size = probes + 2 * HALO * tiles
    packet = pl.pallas_call(
        packet_kernel,
        out_shape=shape(size),
        in_specs=[smem] + [anywhere] * 4,
        out_specs=anywhere,
        scratch_shapes=inputs(1, 2 * HALO)
        + [rows_of(1), rows_of(2 * HALO), scratch(size), copies(4), copies(3)],
        compiler_params=params,
        name="packet",
    )(trap_density, background, site_class, log_param, probe_dirs)
    next_packet = lax.ppermute(packet, "space", down)
    edge = jnp.stack([at_space > 0, at_space < slabs - 1]).astype(jnp.int32)
    own_coef, own_src, wide, kept, sums, next_bg = pl.pallas_call(
        inner_kernel,
        out_shape=(
            shape(planes * tiles),
            shape((planes + 1) * tiles),
            shape(probes),
            shape(4, probes, tiles),
            shape(probes),
            shape((2 * HALO - 1) * tiles),
        ),
        in_specs=[smem, smem] + [anywhere] * 4 + [vmem],
        out_specs=(vmem,) * 6,
        scratch_shapes=inputs(planes, planes)
        + [rows_of(planes), rows_of(2 * HALO - 1), rows_of(planes)]
        + [scratch(planes + 1, probes, tiles)] * 2
        + [copies(4)],
        compiler_params=pltpu.CompilerParams(vmem_limit_bytes=28 * 2**20),
        cost_estimate=pl.CostEstimate(flops=10**9, bytes_accessed=2**24, transcendentals=256),
        name="inner",
    )(edge, trap_density, background, site_class, log_param, probe_dirs, beyond)

    pieces = probes * cells // LANES
    images = pl.pallas_call(
        functools.partial(outer_kernel, chunks, folds),
        out_shape=jax.ShapeDtypeStruct((groups * slabs // 2, 2, pieces, LANES), jnp.float32),
        in_specs=[smem] + [vmem] * 7,
        out_specs=vmem,
        scratch_shapes=[
            scratch(total * tiles),
            scratch(total * tiles),
            scratch(total + 1, probes, tiles),
            scratch(total + 1, probes, tiles),
        ],
        compiler_params=pltpu.CompilerParams(vmem_limit_bytes=28 * 2**20),
        name="outer",
    )(edge, own_coef, own_src, wide, kept, sums, next_bg, next_packet)

    same = [
        [g * slabs + z for g in range(groups) for z in range(parity, slabs, 2)] for parity in (0, 1)
    ]
    mine = lax.all_to_all(
        images, ("probe", "space"), split_axis=0, concat_axis=0, axis_index_groups=same, tiled=True
    )
    other = lax.ppermute(mine, "space", [(z, z ^ 1) for z in range(slabs)])
    place = jnp.stack([lax.axis_index("probe"), at_space]).astype(jnp.int32)
    count = groups * probes
    results = (
        jax.ShapeDtypeStruct((probes, 1, cells), jnp.float32),
        jax.ShapeDtypeStruct((count, count), jnp.float32),
    )
    params = pltpu.CompilerParams(vmem_limit_bytes=28 * 2**20)
    if count <= 8 and slabs % 16 == 0:
        halves = cells // LANES
        return pl.pallas_call(
            functools.partial(register_kernel, groups, slabs, probes),
            out_shape=results,
            in_specs=[smem, vmem, vmem],
            out_specs=(vmem, vmem),
            scratch_shapes=[pltpu.VMEM((count, halves, slabs, LANES), jnp.float32)],
            compiler_params=params,
            name="factor",
        )(
            place,
            mine.reshape((groups * slabs * pieces, LANES)),
            other.reshape((groups * slabs * pieces, LANES)),
        )
    odd = at_space % 2 == 1
    pairs = [jnp.where(odd, other, mine), jnp.where(odd, mine, other)]
    pairs = [x.reshape((groups, slabs // 2, 2, probes, cells)) for x in pairs]
    every = jnp.stack(pairs, axis=2).reshape((groups, slabs, 2, probes, cells))
    return pl.pallas_call(
        factor_kernel,
        out_shape=results,
        in_specs=[smem, vmem],
        out_specs=(vmem, vmem),
        scratch_shapes=[
            pltpu.VMEM((count, slabs * cells), jnp.float32),
            pltpu.VMEM((count, cells), jnp.float32),
        ],
        compiler_params=params,
        name="factor",
    )(place, every)


def solution(mesh):
    placed = (
        P("probe", "space", None),
        P("space", None),
        P("space", None, None),
        P("space", None, None),
        P(),
    )
    return jax.shard_map(
        shards,
        mesh=mesh,
        in_specs=placed,
        out_specs=(P("probe", "space", None), P()),
        check_vma=False,
    )
```

```python
import functools

import jax
import jax.numpy as jnp
from jax import lax
from jax.experimental import pallas as pl
from jax.experimental.pallas import tpu as pltpu
from jax.sharding import PartitionSpec as P

PX = 64
PY = 4
REF = 8
STEP = 0.12
HALO = 3
LANES = 128
HIGHEST = lax.Precision.HIGHEST


def dot_nn(a, b):
    return lax.dot_general(
        a, b, (((1,), (0,)), ((), ())), precision=HIGHEST, preferred_element_type=jnp.float32
    )


def dot_nt(a, b):
    return lax.dot_general(
        a, b, (((1,), (1,)), ((), ())), precision=HIGHEST, preferred_element_type=jnp.float32
    )


def parts_of(x):
    first = x.astype(jnp.bfloat16)
    rest = x - first.astype(jnp.float32)
    second = rest.astype(jnp.bfloat16)
    third = (rest - second.astype(jnp.float32)).astype(jnp.bfloat16)
    return first, second, third


def bf16_dot(a, b):
    return jnp.dot(a, b, preferred_element_type=jnp.float32)


def interleave(exact, small, order):
    parts = [part for x in exact for part in parts_of(x)] + [x.astype(jnp.bfloat16) for x in small]
    placed = bf16_dot(jnp.concatenate(parts, axis=0), order[...])
    results, at = [], 0
    for x in exact:
        count = x.shape[0]
        first, second, third = [placed[at + n * count : at + (n + 1) * count] for n in range(3)]
        results.append((first + second) + third)
        at += 3 * count
    for x in small:
        results.append(placed[at : at + x.shape[0]])
        at += x.shape[0]
    return results


def keep(placed, kept):
    for k in range(kept.shape[0]):
        kept[k] = placed[:, k * LANES : (k + 1) * LANES]


def flat(planes):
    return planes.reshape((planes.shape[0] * planes.shape[1], planes.shape[2]))


def cell_matrix(chunks, turned=False):
    half = REF // chunks
    dims = (LANES, PX * PY) if turned else (PX * PY, LANES)
    cell = lax.broadcasted_iota(jnp.int32, dims, int(turned)) % PX
    lane = lax.broadcasted_iota(jnp.int32, dims, 1 - int(turned)) // half
    return jnp.where(cell == lane, 1.0, 0.0).astype(jnp.float32)


def own_cells(folds):
    half = REF // folds
    sublane = lax.broadcasted_iota(jnp.int32, (8, PX * PY), 0) // half
    return lax.broadcasted_iota(jnp.int32, (8, PX * PY), 1) // PX == sublane


def prolonged(coarse, folds, chunks):
    mask = own_cells(folds)
    rows = [jnp.where(mask, coarse[n : n + 1, :], 0.0) for n in range(coarse.shape[0])]
    return cell_dot(jnp.concatenate(rows, axis=0), cell_matrix(chunks))


def cell_dot(rows, matrix):
    count = rows.shape[0]
    parts = jnp.concatenate(float_parts(rows), axis=0).astype(jnp.bfloat16)
    placed = bf16_dot(parts, matrix.astype(jnp.bfloat16))
    return (placed[:count] + placed[count : 2 * count]) + placed[2 * count :]


def float_parts(x):
    first = x.astype(jnp.bfloat16).astype(jnp.float32)
    rest = x - first
    second = rest.astype(jnp.bfloat16).astype(jnp.float32)
    return first, second, rest - second


def cell_order(columns, chunks):
    x = lax.broadcasted_iota(jnp.int32, (columns, columns), 0)
    place = lax.broadcasted_iota(jnp.int32, (columns, columns), 1)
    wanted = chunks * (place % LANES) + place // LANES
    return jnp.where(x == wanted, 1.0, 0.0).astype(jnp.bfloat16)


def spread_cells(dirs, log_param, folds, chunks):
    probes = dirs.shape[0]
    coarse = [dirs[p] for p in range(probes)] + [jnp.exp(log_param[...])]
    spread = prolonged(jnp.concatenate(coarse, axis=0), folds, chunks)
    return [spread[8 * n : 8 * n + 8, :] for n in range(probes + 1)]


def tile_rows(z, r, rows, folds):
    return pl.ds(z * rows + r, 8, stride=folds)


def trap_of(density, kind):
    trap = jnp.full((8, LANES), density[density.shape[0] - 1])
    for n in range(density.shape[0] - 2, -1, -1):
        trap = jnp.where(kind == float(n), density[n], trap)
    return trap


def weight_of(trap):
    return (1.0 / STEP - 6.0) - trap


def source_of(trap, background):
    return -STEP * trap * background


def packet_kernel(
    density, background_in, sites_in, log_param_in, dirs_in, packet,
    background, sites, log_param, dirs, order, bg, site, made, sems, out_sems,
):
    count, rows, columns = sites.shape
    chunks, folds = columns // LANES, rows // 8
    tiles = chunks * folds
    probes = dirs.shape[0]
    pairs = [
        (log_param_in, log_param),
        (dirs_in, dirs),
        (background_in.at[pl.ds(count - 1, 1)], background),
        (sites_in.at[pl.ds(0, count)], sites),
    ]
    copies = [pltpu.make_async_copy(a, b, sems.at[n]) for n, (a, b) in enumerate(pairs)]
    for copy in copies:
        copy.start()
    order[...] = cell_order(columns, chunks)
    copies[0].wait()
    copies[1].wait()
    spread = spread_cells(dirs, log_param, folds, chunks)
    for p in range(probes):
        made[p] = spread[p]
    copies[2].wait()
    copies[3].wait()
    placed = interleave([flat(background[...])], [flat(sites[...]).astype(jnp.float32)], order)
    keep(placed[0], bg)
    keep(placed[1], site)
    sent = []

    def send(start, stop):
        at = pl.ds(start, stop - start)
        copy = pltpu.make_async_copy(made.at[at], packet.at[at], out_sems.at[len(sent)])
        copy.start()
        sent.append(copy)

    first = probes + tiles
    middle = first + (count - 1) // 2 * tiles
    for z in range(count):
        for r in range(folds):
            for k in range(chunks):
                t = r * chunks + k
                trap = trap_of(density, site[k, tile_rows(z, r, rows, folds), :]) * spread[probes]
                if z < count - 1:
                    made[first + z * tiles + t] = trap
                else:
                    made[probes + t] = source_of(trap, bg[k, tile_rows(0, r, rows, folds), :])
        if z == (count - 1) // 2 - 1:
            send(first, middle)
        elif z == count - 2:
            send(middle, first + (count - 1) * tiles)
    send(0, first)
    for copy in sent:
        copy.wait()


class Steps:
    def __init__(self, chunks, folds, probes, zero_plane, coef, src):
        self.chunks, self.folds, self.tiles = chunks, folds, chunks * folds
        self.probes, self.zero_plane = probes, zero_plane
        self.coef, self.src = coef, src
        self.lane = lax.broadcasted_iota(jnp.int32, (8, LANES), 1)
        self.sublane = lax.broadcasted_iota(jnp.int32, (8, LANES), 0)

    def clear(self, *fields):
        nothing = jnp.zeros((8, LANES), jnp.float32)
        for t in range(self.tiles):
            for field in fields:
                for p in range(self.probes):
                    field[self.zero_plane, p, t] = nothing

    def from_left(self, x):
        return jnp.where(self.lane == 0, 0.0, pltpu.roll(x, 1, 1))

    def from_right(self, x):
        return jnp.where(self.lane == LANES - 1, 0.0, pltpu.roll(x, LANES - 1, 1))

    def from_before(self, x):
        return jnp.where(self.sublane == 0, 0.0, pltpu.roll(x, 1, 0))

    def from_after(self, x):
        return jnp.where(self.sublane == 7, 0.0, pltpu.roll(x, 7, 0))

    def first(self, own, to, other=None, beyond=()):
        chunks, folds, tiles = self.chunks, self.folds, self.tiles
        src, coef = self.src, self.coef
        turns = (self.from_left, self.from_right, self.from_before, self.from_after)
        shifted = [[f(x) for x in own] for f in turns]

        def body(z, carry):
            down = jnp.where(z > 0, z - 1, self.zero_plane) * tiles
            up = (z + 1) * tiles
            s = [[src[z * tiles + r * chunks + k] for k in range(chunks)] for r in range(folds)]
            for r in range(folds):
                for k in range(chunks):
                    t = r * chunks + k
                    same = coef[z * tiles + t] * s[r][k]
                    outer = []
                    for there, value, turn, kind in (
                        (k > 0, s[r][k - 1], (1, 1), 0),
                        (k + 1 < chunks, s[r][(k + 1) % chunks], (LANES - 1, 1), 1),
                        (r > 0, s[r - 1][k], (1, 0), 2),
                        (r + 1 < folds, s[(r + 1) % folds][k], (7, 0), 3),
                    ):
                        if there:
                            same = same + value
                        else:
                            outer.append((pltpu.roll(value, *turn), shifted[kind]))
                    for name, value in (("down", src[down + t]), ("up", src[up + t])):
                        if name == other:
                            outer.append((value, beyond))
                        else:
                            same = same + value
                    for p in range(self.probes):
                        result = same * own[p]
                        for value, factor in outer:
                            result = result + value * factor[p]
                        to[z, p, t] = result
            return carry

        return body

    def stencil(self, ref, valid, z, emit, extra):
        chunks, folds, tiles = self.chunks, self.folds, self.tiles
        first, stop = valid

        def at(z):
            return jnp.where((z >= first) & (z < stop), z, self.zero_plane)

        down, here, there, up = at(z - 1), at(z), at(z + 1), at(z + 2)
        for p in range(self.probes):
            pair = [[ref[plane, p, t] for t in range(tiles)] for plane in (here, there)]
            for r in range(folds):
                for k in range(chunks):
                    t = r * chunks + k
                    for n, value in enumerate(pair):
                        left = value[t - 1] if k else self.from_left(value[t + chunks - 1])
                        if k + 1 < chunks:
                            right = value[t + 1]
                        else:
                            right = self.from_right(value[t + 1 - chunks])
                        if r:
                            before = value[t - chunks]
                        else:
                            before = self.from_before(value[t + tiles - chunks])
                        if r + 1 < folds:
                            after = value[t + chunks]
                        else:
                            after = self.from_after(value[t + chunks - tiles])
                        above = pair[1 - n][t] + (ref[up, p, t] if n else ref[down, p, t])
                        weight = self.coef[(z + n) * tiles + t]
                        if extra:
                            weight = weight + extra
                        sides = (left + right) + (before + after)
                        emit(z + n, p, t, (sides + above) + weight * value[t])

    def step(self, ref, to, valid, wanted, extra=0.0):
        start, stop = wanted

        def body(n, carry):
            def emit(z, p, t, result):
                to[z, p, t] = result

            self.stencil(ref, valid, jnp.minimum(start + 2 * n, stop - 2), emit, extra)
            return carry

        lax.fori_loop(0, (stop - start + 1) // 2, body, 0)

    def widen(self, ref, to, valid, at_low, at_high):
        first, stop = valid

        def move(a, b):
            for p in range(self.probes):
                for t in range(self.tiles):
                    to[b, p, t] = ref[a, p, t]

        pl.when(at_low)(lambda: move(first, first - 1))
        pl.when(at_high)(lambda: move(stop - 1, stop))

    def images(self, m, u, by_one, by_two, span, carry, other=None):
        chunks, folds, tiles = self.chunks, self.folds, self.tiles
        src = self.src

        def at(z, valid):
            return jnp.where((z >= valid[0]) & (z < valid[1]), z, self.zero_plane)

        def body(z, carry):
            carry = [list(c) for c in carry]
            down = jnp.where(z > 0, z - 1, self.zero_plane) * tiles
            up = (z + 1) * tiles
            here, kept = at(z, by_one), at(z, by_two)
            s = [src[z * tiles + t] for t in range(tiles)]
            for t in range(tiles):
                r, k = t // chunks, t % chunks
                same = self.coef[z * tiles + t] * s[t]
                moved = []
                if k:
                    same = same + s[t - 1]
                else:
                    moved.append((2, self.from_left(s[t + chunks - 1])))
                if k + 1 < chunks:
                    same = same + s[t + 1]
                else:
                    moved.append((1, self.from_right(s[t + 1 - chunks])))
                if r:
                    same = same + s[t - chunks]
                else:
                    moved.append((4, self.from_before(s[t + tiles - chunks])))
                if r + 1 < folds:
                    same = same + s[t + chunks]
                else:
                    moved.append((3, self.from_after(s[t + chunks - tiles])))
                for name, value in (("down", src[down + t]), ("up", src[up + t])):
                    if name == other:
                        moved.append((5, value))
                    else:
                        same = same + value
                scaled = s[t] * (1.0 / STEP**2)
                for p in range(self.probes):
                    value = m[here, p, t]
                    carry[p][0] = carry[p][0] + (same * value + scaled * u[kept, p, t])
                    for n, factor in moved:
                        carry[p][n] = carry[p][n] + factor * value
            return tuple(tuple(c) for c in carry)

        if isinstance(span, int):
            return body(span, carry)
        return lax.fori_loop(*span, body, carry)

    def empty_sums(self):
        nothing = jnp.zeros((8, LANES), jnp.float32)
        return ((nothing,) * 6,) * self.probes

    def moved_sums(self, sums):
        return [
            c[0]
            + (self.from_left(c[1]) + self.from_right(c[2]))
            + (self.from_before(c[3]) + self.from_after(c[4]))
            for c in sums
        ]

    def after_tangent(self, odd, even, mine, at_low, at_high):
        first, stop = mine
        by_two = (jnp.where(at_low, first - 1, first), jnp.where(at_high, stop + 1, stop))
        by_one = (jnp.where(at_low, first - 2, first), jnp.where(at_high, stop + 2, stop))
        self.step(odd, even, mine, mine, 1.0 / STEP)
        self.widen(odd, even, mine, at_low, at_high)
        self.step(even, odd, by_two, by_two)
        self.widen(even, odd, by_two, at_low, at_high)
        return by_one, by_two


def inner_kernel(
    edge, density, background_in, sites_in, log_param_in, dirs_in, beyond,
    coef, src, wide, kept, sums, next_bg,
    background, sites, log_param, dirs, order, bg, far, site, even, odd, sems,
):
    planes, rows, columns = background.shape
    chunks, folds = columns // LANES, rows // 8
    tiles = chunks * folds
    probes = dirs.shape[0]
    copies = [
        (log_param_in, log_param),
        (dirs_in, dirs),
        (background_in, background),
        (sites_in, sites),
    ]
    copies = [pltpu.make_async_copy(a, b, sems.at[n]) for n, (a, b) in enumerate(copies)]
    for copy in copies:
        copy.start()
    steps = Steps(chunks, folds, probes, planes, coef, src)
    steps.clear(even, odd)
    nothing = jnp.zeros((8, LANES), jnp.float32)
    for t in range(tiles):
        src[planes * tiles + t] = nothing
    order[...] = cell_order(columns, chunks)
    for copy in copies:
        copy.wait()
    spread = spread_cells(dirs, log_param, folds, chunks)
    for p in range(probes):
        wide[p] = spread[p]

    placed = interleave(
        [flat(background[...]), flat(beyond[...])], [flat(sites[...]).astype(jnp.float32)], order
    )
    for x, scratch in zip(placed, (bg, far, site)):
        keep(x, scratch)
    for r in range(folds):
        for k in range(chunks):
            t = r * chunks + k
            for z in range(planes):
                at = tile_rows(z, r, rows, folds)
                trap = trap_of(density, site[k, at, :]) * spread[probes]
                coef[z * tiles + t] = weight_of(trap)
                src[z * tiles + t] = source_of(trap, bg[k, at, :])
            for z in range(beyond.shape[0]):
                next_bg[z * tiles + t] = far[k, tile_rows(z, r, rows, folds), :]
    at_low = edge[0] != 0

    def low(z):
        return jnp.where(at_low, z, 0)

    last = planes - HALO
    lax.fori_loop(low(1), last + 2, steps.first(spread[:probes], odd), 0)
    steps.step(odd, even, (low(1), last + 2), (low(2), last + 1))
    for n, (ref, z) in enumerate(((odd, last), (odd, last + 1), (even, last - 1), (even, last))):
        for p in range(probes):
            for t in range(tiles):
                kept[n, p, t] = ref[z, p, t]
    mine = (low(HALO), last)
    steps.step(even, odd, (low(2), last + 1), mine)
    by_one, by_two = steps.after_tangent(odd, even, mine, at_low, True)
    result = steps.moved_sums(steps.images(odd, even, by_one, by_two, by_one, steps.empty_sums()))
    for p in range(probes):
        sums[p] = result[p]


def outer_kernel(
    chunks, folds, edge, own_coef, own_src, own_wide, kept, own_sums, next_bg, packet, out,
    coef, src, even, odd,
):
    tiles = chunks * folds
    probes = own_wide.shape[0]
    total = even.shape[0] - 1
    planes = total - 2 * HALO
    steps = Steps(chunks, folds, probes, total, coef, src)
    last = planes - HALO
    halo = planes * tiles

    def copy(source, start, target, at, count):
        def body(n, carry):
            for t in range(tiles):
                target[at + n * tiles + t] = source[start + n * tiles + t]
            return carry

        lax.fori_loop(0, count, body, 0)

    own = (last - HALO) * tiles
    copy(own_src, own, src, own, planes - last + HALO)
    copy(own_coef, own, coef, own, planes - last + HALO)

    def beyond_plane(n, carry):
        for t in range(tiles):
            at = n * tiles + t
            trap = packet[probes + tiles + at]
            coef[halo + at] = weight_of(trap)
            src[halo + at] = source_of(trap, next_bg[at])
        return carry

    lax.fori_loop(0, 2 * HALO - 1, beyond_plane, 0)
    copy(packet, probes, src, (total - 1) * tiles, 1)
    steps.clear(even, odd)
    for p in range(probes):
        for t in range(tiles):
            odd[last, p, t] = kept[0, p, t]
            odd[last + 1, p, t] = kept[1, p, t]
            even[last - 1, p, t] = kept[2, p, t]
            even[last, p, t] = kept[3, p, t]

    at_high = edge[1] != 0

    def high(z):
        return jnp.where(at_high, z, planes)

    mine = [own_wide[p] for p in range(probes)]
    beyond = [packet[p] for p in range(probes)]
    steps.first(mine, odd, "up", beyond)(planes - 1, 0)

    @pl.when(at_high)
    def _():
        steps.first(beyond, odd, "down", mine)(planes, 0)
        lax.fori_loop(planes + 1, total - 1, steps.first(beyond, odd), 0)

    steps.step(odd, even, (last, high(total - 1)), (last + 1, high(total - 2)))
    mine = (last, high(total - HALO))
    steps.step(even, odd, (last - 1, high(total - 2)), mine)
    by_one, by_two = steps.after_tangent(odd, even, mine, True, at_high)
    start, stop = by_one
    empty = steps.empty_sums()
    inside = steps.images(odd, even, by_one, by_two, (start, planes - 1), empty)
    inside = steps.images(odd, even, by_one, by_two, planes - 1, inside, "up")
    above = [list(c) for c in empty]
    for p in range(probes):
        above[p][0] = inside[p][5]
    above = steps.images(odd, even, by_one, by_two, (planes + 1, stop), tuple(tuple(c) for c in above))
    above = steps.images(odd, even, by_one, by_two, planes, above, "down")
    inside = [x + own_sums[p] + above[p][5] for p, x in enumerate(steps.moved_sums(inside))]
    above = steps.moved_sums(above)

    added = jnp.concatenate(inside + above, axis=0) * STEP**6
    images = cell_dot(added, cell_matrix(chunks, True))
    mask = own_cells(folds)
    for part in range(2):
        halves = []
        for p in range(probes):
            image = jnp.where(mask, images[8 * (part * probes + p) :][:8], 0.0)
            image = jnp.sum(image, axis=0, keepdims=True)
            halves += [image[:, h * LANES : (h + 1) * LANES] for h in range(image.shape[1] // LANES)]
        halves = jnp.concatenate(halves, axis=0)

        def send(n, carry):
            out[n, part] = halves
            return carry

        lax.fori_loop(0, out.shape[0], send, 0, unroll=8)


def eliminate(gram):
    count = gram.shape[0]
    rows = lax.broadcasted_iota(jnp.int32, (count, count), 0)
    columns = lax.broadcasted_iota(jnp.int32, (count, count), 1)
    inverse = jnp.where(rows == columns, 1.0, 0.0)
    for j in range(count - 1):
        across = jnp.broadcast_to(gram[:, j : j + 1], (count, count))
        turned = 1.0 / across
        ratio = jnp.where(rows > j, across, 0.0)
        gram_row, inverse_row = (gram * turned)[j : j + 1, :], (inverse * turned)[j : j + 1, :]
        gram = gram - ratio * gram_row
        inverse = inverse - ratio * inverse_row
    diagonal = jnp.sum(jnp.where(rows == columns, gram, 0.0), axis=1, keepdims=True)
    scale = 1.0 / jnp.sqrt(diagonal)
    upper = jnp.where(columns >= rows, gram, 0.0) * scale
    return upper, inverse * scale


def gram_of(parts, count):
    stacked = jnp.concatenate(list(parts) + [jnp.zeros_like(parts[0])], axis=0)
    stacked = stacked.astype(jnp.bfloat16)
    every = lax.dot_general(
        stacked, stacked, (((1,), (1,)), ((), ())), preferred_element_type=jnp.float32
    )
    tall = every[:count] + (every[count : 2 * count] + every[2 * count : 3 * count])
    return tall[:, :count] + (tall[:, count : 2 * count] + tall[:, 2 * count : 3 * count])


def times(a, parts):
    first, second, third = float_parts(a)
    left = jnp.concatenate([first, second, third, first, second, first], axis=1)
    right = jnp.concatenate([parts[0]] * 3 + [parts[1]] * 2 + [parts[2]], axis=0)
    return bf16_dot(left.astype(jnp.bfloat16), right.astype(jnp.bfloat16))


def factor_kernel(place, parts, q_out, lower_out, rows_ref, q_ref):
    groups, slabs, _, probes, cells = parts.shape
    count = groups * probes
    for g in range(groups):

        def gather(slab, carry):
            before = jnp.maximum(slab - 1, 0)
            image = parts[g, slab, 0] + jnp.where(slab > 0, parts[g, before, 1], 0.0)
            at = pl.multiple_of(slab * cells, cells)
            rows_ref[pl.ds(g * probes, probes), pl.ds(at, cells)] = image
            return carry

        lax.fori_loop(0, slabs, gather, 0, unroll=True if slabs <= 16 else 8)
    total = slabs * cells
    rows = rows_ref[...]
    parts_one = float_parts(rows)
    upper_one, inverse_one = eliminate(gram_of(parts_one, count) / total)
    basis = times(inverse_one, parts_one)
    rows_ref[...] = basis
    upper_two, inverse_two = eliminate(gram_of(float_parts(basis), count) / total)
    mine = rows_ref[:, pl.ds(pl.multiple_of(place[1] * cells, cells), cells)]
    q_ref[...] = dot_nn(inverse_two, mine)
    for g in range(groups):

        @pl.when(place[0] == g)
        def _():
            q_out[:, 0, :] = q_ref[pl.ds(g * probes, probes), :]

    r = lax.broadcasted_iota(jnp.int32, (count, count), 0)
    c = lax.broadcasted_iota(jnp.int32, (count, count), 1)
    lower_one = dot_nt(jnp.where(r == c, 1.0, 0.0), upper_one)
    lower_out[...] = dot_nt(lower_one, upper_two)


def everywhere(x):
    x = jnp.broadcast_to(jnp.sum(x, axis=1, keepdims=True), x.shape)
    for shift in (4, 2, 1):
        x = x + pltpu.roll(x, shift, 0)
    return x


def cholesky(rows, total):
    count = len(rows)
    rows = [list(row) for row in rows]
    gram = {}
    for i in range(count):
        for j in range(i + 1):
            product = sum(a * b for a, b in zip(rows[i][1:], rows[j][1:]))
            gram[i, j] = everywhere(rows[i][0] * rows[j][0] + product) * (1.0 / total)
    factor = {}
    for j in range(count):
        pivot = gram[j, j]
        turned = lax.rsqrt(pivot)
        turned = turned * (1.5 - 0.5 * pivot * turned * turned)
        factor[j, j] = pivot * turned
        rows[j] = [x * turned for x in rows[j]]
        for i in range(j + 1, count):
            factor[i, j] = gram[i, j] * turned
        for i in range(j + 1, count):
            for k in range(j + 1, i + 1):
                gram[i, k] = gram[i, k] - factor[i, j] * factor[k, j]
            rows[i] = [x - factor[i, j] * y for x, y in zip(rows[i], rows[j])]
    return factor, rows


def register_kernel(turns, slabs, probes, place, mine, other, q_out, lower_out, q_ref):
    groups = len(turns)
    halves = q_out.shape[2] // LANES
    pieces = probes * halves
    step = 2 * pieces
    sublane = lax.broadcasted_iota(jnp.int32, (8, LANES), 0)
    odd = jnp.broadcast_to(place[1] % 2, (8, LANES)) == 1

    def load(at):
        at = pl.ds(at, 8, stride=groups * step)
        one, two = mine[at, :], other[at, :]
        return jnp.where(odd, two, one), jnp.where(odd, one, two)

    rows = []
    for g, turn in enumerate(turns):
        for p in range(probes):
            row = []
            for h in range(halves):
                at = g * step + p * halves + h
                even_own, odd_own = load(at)
                even_next, odd_next = load(at + pieces)
                if turn:
                    even_own, odd_next = pltpu.roll(even_own, turn, 0), pltpu.roll(odd_next, turn + 1, 0)
                    odd_row = pltpu.roll(odd_own + even_next, turn, 0)
                else:
                    odd_next = pltpu.roll(odd_next, 1, 0)
                    odd_row = odd_own + even_next
                row += [even_own + jnp.where(sublane == 0, 0.0, odd_next), odd_row]
            rows.append(row)
    total = slabs * halves * LANES
    factor_one, basis = cholesky(rows, total)
    factor_two, rows = cholesky(basis, total)
    for i, row in enumerate(rows):
        for n, x in enumerate(row):
            q_ref[i, n // 2, pl.ds(n % 2 * 8, 8), :] = x
    own = (place[1] % 2) * (slabs // 2) + place[1] // 2
    for p in range(probes):
        for h in range(halves):
            mine = q_ref[place[0] * probes + p, h, pl.ds(own, 1), :]
            q_out[p, :, pl.ds(h * LANES, LANES)] = mine
    count = len(rows)
    r = lax.broadcasted_iota(jnp.int32, (8, LANES), 0)
    c = lax.broadcasted_iota(jnp.int32, (8, LANES), 1)
    lower = jnp.zeros((8, LANES), jnp.float32)
    for i in range(count):
        for j in range(i + 1):
            entry = sum(factor_one[i, k] * factor_two[k, j] for k in range(j, i + 1))
            lower = jnp.where((r == i) & (c == j), entry, lower)
    lower_out[...] = lower[:count, :count]


def shards(probe_dirs, log_param, background, site_class, trap_density):
    probes = probe_dirs.shape[0]
    cells = probe_dirs.shape[2]
    planes, rows, columns = background.shape
    slabs = lax.axis_size("space")
    groups = lax.axis_size("probe")
    at_space = lax.axis_index("space")
    vmem = pl.BlockSpec(memory_space=pltpu.VMEM)
    smem = pl.BlockSpec(memory_space=pltpu.SMEM)
    anywhere = pl.BlockSpec(memory_space=pl.ANY)
    params = pltpu.CompilerParams(vmem_limit_bytes=62 * 2**20)

    chunks, folds = columns // LANES, rows // 8
    tiles = chunks * folds
    total = planes + 2 * HALO
    tile = (8, LANES)

    def shape(*dims):
        return jax.ShapeDtypeStruct(dims + tile, jnp.float32)

    def scratch(*dims):
        return pltpu.VMEM(dims + tile, jnp.float32)

    def copies(count):
        return pltpu.SemaphoreType.DMA((count,))

    def inputs(held, sites):
        return [
            pltpu.VMEM((held, rows, columns), jnp.float32),
            pltpu.VMEM((sites, rows, columns), jnp.int32),
            pltpu.VMEM(log_param.shape, jnp.float32),
            pltpu.VMEM(probe_dirs.shape, jnp.float32),
            pltpu.VMEM((columns, columns), jnp.bfloat16),
        ]

    def rows_of(held):
        return pltpu.VMEM((chunks, held * rows, LANES), jnp.float32)

    down = [(i + 1, i) for i in range(slabs - 1)]
    beyond = lax.ppermute(background[: 2 * HALO - 1], "space", down)
    size = probes + 2 * HALO * tiles
    packet = pl.pallas_call(
        packet_kernel,
        out_shape=shape(size),
        in_specs=[smem] + [anywhere] * 4,
        out_specs=anywhere,
        scratch_shapes=inputs(1, 2 * HALO)
        + [rows_of(1), rows_of(2 * HALO), scratch(size), copies(4), copies(3)],
        compiler_params=params,
        name="packet",
    )(trap_density, background, site_class, log_param, probe_dirs)
    next_packet = lax.ppermute(packet, "space", down)
    edge = jnp.stack([at_space > 0, at_space < slabs - 1]).astype(jnp.int32)
    own_coef, own_src, wide, kept, sums, next_bg = pl.pallas_call(
        inner_kernel,
        out_shape=(
            shape(planes * tiles),
            shape((planes + 1) * tiles),
            shape(probes),
            shape(4, probes, tiles),
            shape(probes),
            shape((2 * HALO - 1) * tiles),
        ),
        in_specs=[smem, smem] + [anywhere] * 4 + [vmem],
        out_specs=(vmem,) * 6,
        scratch_shapes=inputs(planes, planes)
        + [rows_of(planes), rows_of(2 * HALO - 1), rows_of(planes)]
        + [scratch(planes + 1, probes, tiles)] * 2
        + [copies(4)],
        compiler_params=pltpu.CompilerParams(vmem_limit_bytes=28 * 2**20),
        cost_estimate=pl.CostEstimate(flops=10**9, bytes_accessed=2**24, transcendentals=256),
        name="inner",
    )(edge, trap_density, background, site_class, log_param, probe_dirs, beyond)

    pieces = probes * cells // LANES
    images = pl.pallas_call(
        functools.partial(outer_kernel, chunks, folds),
        out_shape=jax.ShapeDtypeStruct((groups * slabs // 2, 2, pieces, LANES), jnp.float32),
        in_specs=[smem] + [vmem] * 7,
        out_specs=vmem,
        scratch_shapes=[
            scratch(total * tiles),
            scratch(total * tiles),
            scratch(total + 1, probes, tiles),
            scratch(total + 1, probes, tiles),
        ],
        compiler_params=pltpu.CompilerParams(vmem_limit_bytes=28 * 2**20),
        name="outer",
    )(edge, own_coef, own_src, wide, kept, sums, next_bg, next_packet)

    half = slabs // 2
    turns = [half // 2 * (g % 2) for g in range(groups)]
    same = [
        [
            g * slabs + 2 * ((n + turns[g]) % half) + parity
            for n in range(half)
            for g in range(groups)
        ]
        for parity in (0, 1)
    ]
    mine = lax.all_to_all(
        images, ("probe", "space"), split_axis=0, concat_axis=0, axis_index_groups=same, tiled=True
    )
    other = lax.ppermute(mine, "space", [(z, z ^ 1) for z in range(slabs)])
    place = jnp.stack([lax.axis_index("probe"), at_space]).astype(jnp.int32)
    count = groups * probes
    results = (
        jax.ShapeDtypeStruct((probes, 1, cells), jnp.float32),
        jax.ShapeDtypeStruct((count, count), jnp.float32),
    )
    params = pltpu.CompilerParams(vmem_limit_bytes=28 * 2**20)
    if count <= 8 and slabs == 16:
        halves = cells // LANES
        return pl.pallas_call(
            functools.partial(register_kernel, turns, slabs, probes),
            out_shape=results,
            in_specs=[smem, vmem, vmem],
            out_specs=(vmem, vmem),
            scratch_shapes=[pltpu.VMEM((count, halves, slabs, LANES), jnp.float32)],
            compiler_params=params,
            name="factor",
        )(
            place,
            mine.reshape((groups * slabs * pieces, LANES)),
            other.reshape((groups * slabs * pieces, LANES)),
        )
    odd = at_space % 2 == 1
    pairs = [jnp.where(odd, other, mine), jnp.where(odd, mine, other)]
    pairs = [x.reshape((half, groups, 2, probes, cells)) for x in pairs]
    pairs = [
        jnp.stack([jnp.roll(x[:, g], turns[g], axis=0) for g in range(groups)]) for x in pairs
    ]
    every = jnp.stack(pairs, axis=2).reshape((groups, slabs, 2, probes, cells))
    return pl.pallas_call(
        factor_kernel,
        out_shape=results,
        in_specs=[smem, vmem],
        out_specs=(vmem, vmem),
        scratch_shapes=[
            pltpu.VMEM((count, slabs * cells), jnp.float32),
            pltpu.VMEM((count, cells), jnp.float32),
        ],
        compiler_params=params,
        name="factor",
    )(place, every)


def solution(mesh):
    placed = (
        P("probe", "space", None),
        P("space", None),
        P("space", None, None),
        P("space", None, None),
        P(),
    )
    return jax.shard_map(
        shards,
        mesh=mesh,
        in_specs=placed,
        out_specs=(P("probe", "space", None), P()),
        check_vma=False,
    )
```

```python
import functools

import jax
import jax.numpy as jnp
from jax import lax
from jax.experimental import pallas as pl
from jax.experimental.pallas import tpu as pltpu
from jax.sharding import PartitionSpec as P

PX = 64
PY = 4
REF = 8
STEP = 0.12
HALO = 3
LANES = 128
HIGHEST = lax.Precision.HIGHEST


def dot_nn(a, b):
    return lax.dot_general(
        a, b, (((1,), (0,)), ((), ())), precision=HIGHEST, preferred_element_type=jnp.float32
    )


def dot_nt(a, b):
    return lax.dot_general(
        a, b, (((1,), (1,)), ((), ())), precision=HIGHEST, preferred_element_type=jnp.float32
    )


def parts_of(x):
    first = x.astype(jnp.bfloat16)
    rest = x - first.astype(jnp.float32)
    second = rest.astype(jnp.bfloat16)
    third = (rest - second.astype(jnp.float32)).astype(jnp.bfloat16)
    return first, second, third


def bf16_dot(a, b):
    return jnp.dot(a, b, preferred_element_type=jnp.float32)


def interleave(exact, small, order):
    parts = [part for x in exact for part in parts_of(x)] + [x.astype(jnp.bfloat16) for x in small]
    placed = bf16_dot(jnp.concatenate(parts, axis=0), order[...])
    results, at = [], 0
    for x in exact:
        count = x.shape[0]
        first, second, third = [placed[at + n * count : at + (n + 1) * count] for n in range(3)]
        results.append((first + second) + third)
        at += 3 * count
    for x in small:
        results.append(placed[at : at + x.shape[0]])
        at += x.shape[0]
    return results


def keep(placed, kept):
    for k in range(kept.shape[0]):
        kept[k] = placed[:, k * LANES : (k + 1) * LANES]


def flat(planes):
    return planes.reshape((planes.shape[0] * planes.shape[1], planes.shape[2]))


def cell_matrix(chunks, turned=False):
    half = REF // chunks
    dims = (LANES, PX * PY) if turned else (PX * PY, LANES)
    cell = lax.broadcasted_iota(jnp.int32, dims, int(turned)) % PX
    lane = lax.broadcasted_iota(jnp.int32, dims, 1 - int(turned)) // half
    return jnp.where(cell == lane, 1.0, 0.0).astype(jnp.float32)


def own_cells(folds):
    half = REF // folds
    sublane = lax.broadcasted_iota(jnp.int32, (8, PX * PY), 0) // half
    return lax.broadcasted_iota(jnp.int32, (8, PX * PY), 1) // PX == sublane


def prolonged(coarse, folds, chunks):
    mask = own_cells(folds)
    rows = [jnp.where(mask, coarse[n : n + 1, :], 0.0) for n in range(coarse.shape[0])]
    return cell_dot(jnp.concatenate(rows, axis=0), cell_matrix(chunks))


def cell_dot(rows, matrix):
    count = rows.shape[0]
    parts = jnp.concatenate(float_parts(rows), axis=0).astype(jnp.bfloat16)
    placed = bf16_dot(parts, matrix.astype(jnp.bfloat16))
    return (placed[:count] + placed[count : 2 * count]) + placed[2 * count :]


def float_parts(x):
    first = x.astype(jnp.bfloat16).astype(jnp.float32)
    rest = x - first
    second = rest.astype(jnp.bfloat16).astype(jnp.float32)
    return first, second, rest - second


def cell_order(columns, chunks):
    x = lax.broadcasted_iota(jnp.int32, (columns, columns), 0)
    place = lax.broadcasted_iota(jnp.int32, (columns, columns), 1)
    wanted = chunks * (place % LANES) + place // LANES
    return jnp.where(x == wanted, 1.0, 0.0).astype(jnp.bfloat16)


def spread_cells(dirs, log_param, folds, chunks):
    probes = dirs.shape[0]
    coarse = [dirs[p] for p in range(probes)] + [jnp.exp(log_param[...])]
    spread = prolonged(jnp.concatenate(coarse, axis=0), folds, chunks)
    return [spread[8 * n : 8 * n + 8, :] for n in range(probes + 1)]


def tile_rows(z, r, rows, folds):
    return pl.ds(z * rows + r, 8, stride=folds)


def trap_of(density, kind):
    trap = jnp.full((8, LANES), density[density.shape[0] - 1])
    for n in range(density.shape[0] - 2, -1, -1):
        trap = jnp.where(kind == float(n), density[n], trap)
    return trap


def weight_of(trap):
    return (1.0 / STEP - 6.0) - trap


def source_of(trap, background):
    return -STEP * trap * background


def packet_kernel(
    density, background_in, sites_in, log_param_in, dirs_in, packet,
    background, sites, log_param, dirs, order, bg, site, made, sems, out_sems,
):
    count, rows, columns = sites.shape
    chunks, folds = columns // LANES, rows // 8
    tiles = chunks * folds
    probes = dirs.shape[0]
    pairs = [
        (log_param_in, log_param),
        (dirs_in, dirs),
        (background_in.at[pl.ds(count - 1, 1)], background),
        (sites_in.at[pl.ds(0, count)], sites),
    ]
    copies = [pltpu.make_async_copy(a, b, sems.at[n]) for n, (a, b) in enumerate(pairs)]
    for copy in copies:
        copy.start()
    order[...] = cell_order(columns, chunks)
    copies[0].wait()
    copies[1].wait()
    spread = spread_cells(dirs, log_param, folds, chunks)
    for p in range(probes):
        made[p] = spread[p]
    copies[2].wait()
    copies[3].wait()
    placed = interleave([flat(background[...])], [flat(sites[...]).astype(jnp.float32)], order)
    keep(placed[0], bg)
    keep(placed[1], site)
    sent = []

    def send(start, stop):
        at = pl.ds(start, stop - start)
        copy = pltpu.make_async_copy(made.at[at], packet.at[at], out_sems.at[len(sent)])
        copy.start()
        sent.append(copy)

    first = probes + tiles
    middle = first + (count - 1) // 2 * tiles
    for z in range(count):
        for r in range(folds):
            for k in range(chunks):
                t = r * chunks + k
                trap = trap_of(density, site[k, tile_rows(z, r, rows, folds), :]) * spread[probes]
                if z < count - 1:
                    made[first + z * tiles + t] = trap
                else:
                    made[probes + t] = source_of(trap, bg[k, tile_rows(0, r, rows, folds), :])
        if z == (count - 1) // 2 - 1:
            send(first, middle)
        elif z == count - 2:
            send(middle, first + (count - 1) * tiles)
    send(0, first)
    for copy in sent:
        copy.wait()


class Steps:
    def __init__(self, chunks, folds, probes, zero_plane, coef, src):
        self.chunks, self.folds, self.tiles = chunks, folds, chunks * folds
        self.probes, self.zero_plane = probes, zero_plane
        self.coef, self.src = coef, src
        self.lane = lax.broadcasted_iota(jnp.int32, (8, LANES), 1)
        self.sublane = lax.broadcasted_iota(jnp.int32, (8, LANES), 0)

    def rows(self, t, moved=0):
        r, k = t // self.chunks, t % self.chunks
        if r in (0, self.folds - 1):
            return pl.ds(8 + 16 * k + int(r > 0) + 2 * moved, 8, stride=2)
        return pl.ds(16 + 8 * (self.chunks * (r + 1) + k), 8)

    def load(self, field, plane, p, t, moved=0):
        return field[plane, p, self.rows(t, moved), :]

    def store(self, field, plane, p, t, value):
        field[plane, p, self.rows(t), :] = value

    def clear(self, *fields):
        nothing = jnp.zeros((8, LANES), jnp.float32)
        for t in range(self.tiles):
            for field in fields:
                for p in range(self.probes):
                    self.store(field, self.zero_plane, p, t, nothing)

    def from_left(self, x):
        return jnp.where(self.lane == 0, 0.0, pltpu.roll(x, 1, 1))

    def from_right(self, x):
        return jnp.where(self.lane == LANES - 1, 0.0, pltpu.roll(x, LANES - 1, 1))

    def from_before(self, x):
        return jnp.where(self.sublane == 0, 0.0, pltpu.roll(x, 1, 0))

    def from_after(self, x):
        return jnp.where(self.sublane == 7, 0.0, pltpu.roll(x, 7, 0))

    def first(self, own, to, other=None, beyond=()):
        chunks, folds, tiles = self.chunks, self.folds, self.tiles
        src, coef = self.src, self.coef
        turns = (self.from_left, self.from_right, self.from_before, self.from_after)
        shifted = [[f(x) for x in own] for f in turns]

        def body(z, carry):
            down = jnp.where(z > 0, z - 1, self.zero_plane) * tiles
            up = (z + 1) * tiles
            s = [[src[z * tiles + r * chunks + k] for k in range(chunks)] for r in range(folds)]
            for r in range(folds):
                for k in range(chunks):
                    t = r * chunks + k
                    same = coef[z * tiles + t] * s[r][k]
                    outer = []
                    for there, value, turn, kind in (
                        (k > 0, s[r][k - 1], (1, 1), 0),
                        (k + 1 < chunks, s[r][(k + 1) % chunks], (LANES - 1, 1), 1),
                        (r > 0, s[r - 1][k], (1, 0), 2),
                        (r + 1 < folds, s[(r + 1) % folds][k], (7, 0), 3),
                    ):
                        if there:
                            same = same + value
                        else:
                            outer.append((pltpu.roll(value, *turn), shifted[kind]))
                    for name, value in (("down", src[down + t]), ("up", src[up + t])):
                        if name == other:
                            outer.append((value, beyond))
                        else:
                            same = same + value
                    for p in range(self.probes):
                        result = same * own[p]
                        for value, factor in outer:
                            result = result + value * factor[p]
                        self.store(to, z, p, t, result)
            return carry

        return body

    def stencil(self, ref, valid, z, emit, extra):
        chunks, folds, tiles = self.chunks, self.folds, self.tiles
        first, stop = valid

        def at(z):
            return jnp.where((z >= first) & (z < stop), z, self.zero_plane)

        down, here, there, up = at(z - 1), at(z), at(z + 1), at(z + 2)
        for p in range(self.probes):
            pair = [
                [self.load(ref, plane, p, t) for t in range(tiles)] for plane in (here, there)
            ]
            for r in range(folds):
                for k in range(chunks):
                    t = r * chunks + k
                    for n, value in enumerate(pair):
                        left = value[t - 1] if k else self.from_left(value[t + chunks - 1])
                        if k + 1 < chunks:
                            right = value[t + 1]
                        else:
                            right = self.from_right(value[t + 1 - chunks])
                        if r:
                            before = value[t - chunks]
                        else:
                            before = self.load(ref, (here, there)[n], p, t + tiles - chunks, -1)
                            before = jnp.where(self.sublane == 0, 0.0, before)
                        if r + 1 < folds:
                            after = value[t + chunks]
                        else:
                            after = self.load(ref, (here, there)[n], p, t + chunks - tiles, 1)
                            after = jnp.where(self.sublane == 7, 0.0, after)
                        above = pair[1 - n][t] + self.load(ref, up if n else down, p, t)
                        weight = self.coef[(z + n) * tiles + t]
                        if extra:
                            weight = weight + extra
                        sides = (left + right) + (before + after)
                        emit(z + n, p, t, (sides + above) + weight * value[t])

    def step(self, ref, to, valid, wanted, extra=0.0):
        start, stop = wanted

        def body(n, carry):
            def emit(z, p, t, result):
                self.store(to, z, p, t, result)

            self.stencil(ref, valid, jnp.minimum(start + 2 * n, stop - 2), emit, extra)
            return carry

        lax.fori_loop(0, (stop - start + 1) // 2, body, 0)

    def widen(self, ref, to, valid, at_low, at_high):
        first, stop = valid

        def move(a, b):
            for p in range(self.probes):
                for t in range(self.tiles):
                    self.store(to, b, p, t, self.load(ref, a, p, t))

        pl.when(at_low)(lambda: move(first, first - 1))
        pl.when(at_high)(lambda: move(stop - 1, stop))

    def images(self, m, u, by_one, by_two, span, carry, other=None):
        chunks, folds, tiles = self.chunks, self.folds, self.tiles
        src = self.src

        def at(z, valid):
            return jnp.where((z >= valid[0]) & (z < valid[1]), z, self.zero_plane)

        def body(z, carry):
            carry = [list(c) for c in carry]
            down = jnp.where(z > 0, z - 1, self.zero_plane) * tiles
            up = (z + 1) * tiles
            here, kept = at(z, by_one), at(z, by_two)
            s = [src[z * tiles + t] for t in range(tiles)]
            for t in range(tiles):
                r, k = t // chunks, t % chunks
                same = self.coef[z * tiles + t] * s[t]
                moved = []
                if k:
                    same = same + s[t - 1]
                else:
                    moved.append((2, self.from_left(s[t + chunks - 1])))
                if k + 1 < chunks:
                    same = same + s[t + 1]
                else:
                    moved.append((1, self.from_right(s[t + 1 - chunks])))
                if r:
                    same = same + s[t - chunks]
                else:
                    moved.append((4, self.from_before(s[t + tiles - chunks])))
                if r + 1 < folds:
                    same = same + s[t + chunks]
                else:
                    moved.append((3, self.from_after(s[t + chunks - tiles])))
                for name, value in (("down", src[down + t]), ("up", src[up + t])):
                    if name == other:
                        moved.append((5, value))
                    else:
                        same = same + value
                scaled = s[t] * (1.0 / STEP**2)
                for p in range(self.probes):
                    value = self.load(m, here, p, t)
                    carry[p][0] = carry[p][0] + (same * value + scaled * self.load(u, kept, p, t))
                    for n, factor in moved:
                        carry[p][n] = carry[p][n] + factor * value
            return tuple(tuple(c) for c in carry)

        if isinstance(span, int):
            return body(span, carry)
        return lax.fori_loop(*span, body, carry)

    def empty_sums(self):
        nothing = jnp.zeros((8, LANES), jnp.float32)
        return ((nothing,) * 6,) * self.probes

    def moved_sums(self, sums):
        return [
            c[0]
            + (self.from_left(c[1]) + self.from_right(c[2]))
            + (self.from_before(c[3]) + self.from_after(c[4]))
            for c in sums
        ]

    def after_tangent(self, odd, even, mine, at_low, at_high):
        first, stop = mine
        by_two = (jnp.where(at_low, first - 1, first), jnp.where(at_high, stop + 1, stop))
        by_one = (jnp.where(at_low, first - 2, first), jnp.where(at_high, stop + 2, stop))
        self.step(odd, even, mine, mine, 1.0 / STEP)
        self.widen(odd, even, mine, at_low, at_high)
        self.step(even, odd, by_two, by_two)
        self.widen(even, odd, by_two, at_low, at_high)
        return by_one, by_two


def inner_kernel(
    edge, density, background_in, sites_in, log_param_in, dirs_in, beyond,
    coef, src, wide, kept, sums, next_bg,
    background, sites, log_param, dirs, order, bg, far, site, even, odd, sems,
):
    planes, rows, columns = background.shape
    chunks, folds = columns // LANES, rows // 8
    tiles = chunks * folds
    probes = dirs.shape[0]
    copies = [
        (log_param_in, log_param),
        (dirs_in, dirs),
        (background_in, background),
        (sites_in, sites),
    ]
    copies = [pltpu.make_async_copy(a, b, sems.at[n]) for n, (a, b) in enumerate(copies)]
    for copy in copies:
        copy.start()
    steps = Steps(chunks, folds, probes, planes, coef, src)
    steps.clear(even, odd)
    nothing = jnp.zeros((8, LANES), jnp.float32)
    for t in range(tiles):
        src[planes * tiles + t] = nothing
    order[...] = cell_order(columns, chunks)
    for copy in copies:
        copy.wait()
    spread = spread_cells(dirs, log_param, folds, chunks)
    for p in range(probes):
        wide[p] = spread[p]

    placed = interleave(
        [flat(background[...]), flat(beyond[...])], [flat(sites[...]).astype(jnp.float32)], order
    )
    for x, scratch in zip(placed, (bg, far, site)):
        keep(x, scratch)
    for r in range(folds):
        for k in range(chunks):
            t = r * chunks + k
            for z in range(planes):
                at = tile_rows(z, r, rows, folds)
                trap = trap_of(density, site[k, at, :]) * spread[probes]
                coef[z * tiles + t] = weight_of(trap)
                src[z * tiles + t] = source_of(trap, bg[k, at, :])
            for z in range(beyond.shape[0]):
                next_bg[z * tiles + t] = far[k, tile_rows(z, r, rows, folds), :]
    at_low = edge[0] != 0

    def low(z):
        return jnp.where(at_low, z, 0)

    last = planes - HALO
    lax.fori_loop(low(1), last + 2, steps.first(spread[:probes], odd), 0)
    steps.step(odd, even, (low(1), last + 2), (low(2), last + 1))
    for n, (ref, z) in enumerate(((odd, last), (odd, last + 1), (even, last - 1), (even, last))):
        for p in range(probes):
            for t in range(tiles):
                kept[n, p, t] = steps.load(ref, z, p, t)
    mine = (low(HALO), last)
    steps.step(even, odd, (low(2), last + 1), mine)
    by_one, by_two = steps.after_tangent(odd, even, mine, at_low, True)
    result = steps.moved_sums(steps.images(odd, even, by_one, by_two, by_one, steps.empty_sums()))
    for p in range(probes):
        sums[p] = result[p]


def outer_kernel(
    chunks, folds, edge, own_coef, own_src, own_wide, kept, own_sums, next_bg, packet, out,
    coef, src, even, odd,
):
    tiles = chunks * folds
    probes = own_wide.shape[0]
    total = even.shape[0] - 1
    planes = total - 2 * HALO
    steps = Steps(chunks, folds, probes, total, coef, src)
    last = planes - HALO
    halo = planes * tiles

    def copy(source, start, target, at, count):
        def body(n, carry):
            for t in range(tiles):
                target[at + n * tiles + t] = source[start + n * tiles + t]
            return carry

        lax.fori_loop(0, count, body, 0)

    own = (last - HALO) * tiles
    copy(own_src, own, src, own, planes - last + HALO)
    copy(own_coef, own, coef, own, planes - last + HALO)

    def beyond_plane(n, carry):
        for t in range(tiles):
            at = n * tiles + t
            trap = packet[probes + tiles + at]
            coef[halo + at] = weight_of(trap)
            src[halo + at] = source_of(trap, next_bg[at])
        return carry

    lax.fori_loop(0, 2 * HALO - 1, beyond_plane, 0)
    copy(packet, probes, src, (total - 1) * tiles, 1)
    steps.clear(even, odd)
    for p in range(probes):
        for t in range(tiles):
            steps.store(odd, last, p, t, kept[0, p, t])
            steps.store(odd, last + 1, p, t, kept[1, p, t])
            steps.store(even, last - 1, p, t, kept[2, p, t])
            steps.store(even, last, p, t, kept[3, p, t])

    at_high = edge[1] != 0

    def high(z):
        return jnp.where(at_high, z, planes)

    mine = [own_wide[p] for p in range(probes)]
    beyond = [packet[p] for p in range(probes)]
    steps.first(mine, odd, "up", beyond)(planes - 1, 0)

    @pl.when(at_high)
    def _():
        steps.first(beyond, odd, "down", mine)(planes, 0)
        lax.fori_loop(planes + 1, total - 1, steps.first(beyond, odd), 0)

    steps.step(odd, even, (last, high(total - 1)), (last + 1, high(total - 2)))
    mine = (last, high(total - HALO))
    steps.step(even, odd, (last - 1, high(total - 2)), mine)
    by_one, by_two = steps.after_tangent(odd, even, mine, True, at_high)
    start, stop = by_one
    empty = steps.empty_sums()
    inside = steps.images(odd, even, by_one, by_two, (start, planes - 1), empty)
    inside = steps.images(odd, even, by_one, by_two, planes - 1, inside, "up")
    above = [list(c) for c in empty]
    for p in range(probes):
        above[p][0] = inside[p][5]
    above = steps.images(odd, even, by_one, by_two, (planes + 1, stop), tuple(tuple(c) for c in above))
    above = steps.images(odd, even, by_one, by_two, planes, above, "down")
    inside = [x + own_sums[p] + above[p][5] for p, x in enumerate(steps.moved_sums(inside))]
    above = steps.moved_sums(above)

    added = jnp.concatenate(inside + above, axis=0) * STEP**6
    images = cell_dot(added, cell_matrix(chunks, True))
    mask = own_cells(folds)
    for part in range(2):
        halves = []
        for p in range(probes):
            image = jnp.where(mask, images[8 * (part * probes + p) :][:8], 0.0)
            image = jnp.sum(image, axis=0, keepdims=True)
            halves += [image[:, h * LANES : (h + 1) * LANES] for h in range(image.shape[1] // LANES)]
        halves = jnp.concatenate(halves, axis=0)

        def send(n, carry):
            out[n, part] = halves
            return carry

        lax.fori_loop(0, out.shape[0], send, 0, unroll=8)


def eliminate(gram):
    count = gram.shape[0]
    rows = lax.broadcasted_iota(jnp.int32, (count, count), 0)
    columns = lax.broadcasted_iota(jnp.int32, (count, count), 1)
    inverse = jnp.where(rows == columns, 1.0, 0.0)
    for j in range(count - 1):
        across = jnp.broadcast_to(gram[:, j : j + 1], (count, count))
        turned = 1.0 / across
        ratio = jnp.where(rows > j, across, 0.0)
        gram_row, inverse_row = (gram * turned)[j : j + 1, :], (inverse * turned)[j : j + 1, :]
        gram = gram - ratio * gram_row
        inverse = inverse - ratio * inverse_row
    diagonal = jnp.sum(jnp.where(rows == columns, gram, 0.0), axis=1, keepdims=True)
    scale = 1.0 / jnp.sqrt(diagonal)
    upper = jnp.where(columns >= rows, gram, 0.0) * scale
    return upper, inverse * scale


def gram_of(parts, count):
    stacked = jnp.concatenate(list(parts) + [jnp.zeros_like(parts[0])], axis=0)
    stacked = stacked.astype(jnp.bfloat16)
    every = lax.dot_general(
        stacked, stacked, (((1,), (1,)), ((), ())), preferred_element_type=jnp.float32
    )
    tall = every[:count] + (every[count : 2 * count] + every[2 * count : 3 * count])
    return tall[:, :count] + (tall[:, count : 2 * count] + tall[:, 2 * count : 3 * count])


def times(a, parts):
    first, second, third = float_parts(a)
    left = jnp.concatenate([first, second, third, first, second, first], axis=1)
    right = jnp.concatenate([parts[0]] * 3 + [parts[1]] * 2 + [parts[2]], axis=0)
    return bf16_dot(left.astype(jnp.bfloat16), right.astype(jnp.bfloat16))


def factor_kernel(place, parts, q_out, lower_out, rows_ref, q_ref):
    groups, slabs, _, probes, cells = parts.shape
    count = groups * probes
    for g in range(groups):

        def gather(slab, carry):
            before = jnp.maximum(slab - 1, 0)
            image = parts[g, slab, 0] + jnp.where(slab > 0, parts[g, before, 1], 0.0)
            at = pl.multiple_of(slab * cells, cells)
            rows_ref[pl.ds(g * probes, probes), pl.ds(at, cells)] = image
            return carry

        lax.fori_loop(0, slabs, gather, 0, unroll=True if slabs <= 16 else 8)
    total = slabs * cells
    rows = rows_ref[...]
    parts_one = float_parts(rows)
    upper_one, inverse_one = eliminate(gram_of(parts_one, count) / total)
    basis = times(inverse_one, parts_one)
    rows_ref[...] = basis
    upper_two, inverse_two = eliminate(gram_of(float_parts(basis), count) / total)
    mine = rows_ref[:, pl.ds(pl.multiple_of(place[1] * cells, cells), cells)]
    q_ref[...] = dot_nn(inverse_two, mine)
    for g in range(groups):

        @pl.when(place[0] == g)
        def _():
            q_out[:, 0, :] = q_ref[pl.ds(g * probes, probes), :]

    r = lax.broadcasted_iota(jnp.int32, (count, count), 0)
    c = lax.broadcasted_iota(jnp.int32, (count, count), 1)
    lower_one = dot_nt(jnp.where(r == c, 1.0, 0.0), upper_one)
    lower_out[...] = dot_nt(lower_one, upper_two)


def everywhere(x):
    x = jnp.broadcast_to(jnp.sum(x, axis=1, keepdims=True), x.shape)
    for shift in (4, 2, 1):
        x = x + pltpu.roll(x, shift, 0)
    return x


def cholesky(rows, total):
    count = len(rows)
    rows = [list(row) for row in rows]
    gram = {}
    for i in range(count):
        for j in range(i + 1):
            product = sum(a * b for a, b in zip(rows[i][1:], rows[j][1:]))
            gram[i, j] = everywhere(rows[i][0] * rows[j][0] + product) * (1.0 / total)
    factor = {}
    for j in range(count):
        pivot = gram[j, j]
        turned = lax.rsqrt(pivot)
        turned = turned * (1.5 - 0.5 * pivot * turned * turned)
        factor[j, j] = pivot * turned
        rows[j] = [x * turned for x in rows[j]]
        for i in range(j + 1, count):
            factor[i, j] = gram[i, j] * turned
        for i in range(j + 1, count):
            for k in range(j + 1, i + 1):
                gram[i, k] = gram[i, k] - factor[i, j] * factor[k, j]
            rows[i] = [x - factor[i, j] * y for x, y in zip(rows[i], rows[j])]
    return factor, rows


def register_kernel(groups, slabs, probes, place, mine, other, q_out, lower_out, q_ref):
    halves = q_out.shape[2] // LANES
    pieces = probes * halves
    step = 2 * pieces
    sublane = lax.broadcasted_iota(jnp.int32, (8, LANES), 0)
    odd = jnp.broadcast_to(place[1] % 2, (8, LANES)) == 1

    def load(at):
        at = pl.ds(at, 8, stride=step)
        one, two = mine[at, :], other[at, :]
        return jnp.where(odd, two, one), jnp.where(odd, one, two)

    rows = []
    for g in range(groups):
        for p in range(probes):
            row = []
            for h in range(halves):
                last = None
                for block in range(slabs // 16):
                    at = (g * slabs // 2 + 8 * block) * step + p * halves + h
                    even_own, odd_own = load(at)
                    even_next, odd_next = load(at + pieces)
                    before = pltpu.roll(odd_next, 1, 0)
                    first = 0.0 if last is None else last
                    last = before
                    row.append((block, 0, h, even_own + jnp.where(sublane == 0, first, before)))
                    row.append((block, 1, h, odd_own + even_next))
            rows.append(row)
    places = [x[:3] for x in rows[0]]
    rows = [[x[3] for x in row] for row in rows]
    total = slabs * halves * LANES
    factor_one, basis = cholesky(rows, total)
    factor_two, rows = cholesky(basis, total)
    for i, row in enumerate(rows):
        for (block, parity, h), x in zip(places, row):
            q_ref[i, h, pl.ds(parity * (slabs // 2) + 8 * block, 8), :] = x
    own = (place[1] % 2) * (slabs // 2) + place[1] // 2
    for p in range(probes):
        for h in range(halves):
            mine = q_ref[place[0] * probes + p, h, pl.ds(own, 1), :]
            q_out[p, :, pl.ds(h * LANES, LANES)] = mine
    count = len(rows)
    r = lax.broadcasted_iota(jnp.int32, (8, LANES), 0)
    c = lax.broadcasted_iota(jnp.int32, (8, LANES), 1)
    lower = jnp.zeros((8, LANES), jnp.float32)
    for i in range(count):
        for j in range(i + 1):
            entry = sum(factor_one[i, k] * factor_two[k, j] for k in range(j, i + 1))
            lower = jnp.where((r == i) & (c == j), entry, lower)
    lower_out[...] = lower[:count, :count]


def shards(probe_dirs, log_param, background, site_class, trap_density):
    probes = probe_dirs.shape[0]
    cells = probe_dirs.shape[2]
    planes, rows, columns = background.shape
    slabs = lax.axis_size("space")
    groups = lax.axis_size("probe")
    at_space = lax.axis_index("space")
    vmem = pl.BlockSpec(memory_space=pltpu.VMEM)
    smem = pl.BlockSpec(memory_space=pltpu.SMEM)
    anywhere = pl.BlockSpec(memory_space=pl.ANY)
    params = pltpu.CompilerParams(vmem_limit_bytes=62 * 2**20)

    chunks, folds = columns // LANES, rows // 8
    tiles = chunks * folds
    total = planes + 2 * HALO
    tile = (8, LANES)

    def shape(*dims):
        return jax.ShapeDtypeStruct(dims + tile, jnp.float32)

    def scratch(*dims):
        return pltpu.VMEM(dims + tile, jnp.float32)

    def field_of(planes):
        return pltpu.VMEM((planes + 1, probes, 8 * tiles + 16, LANES), jnp.float32)

    def copies(count):
        return pltpu.SemaphoreType.DMA((count,))

    def inputs(held, sites):
        return [
            pltpu.VMEM((held, rows, columns), jnp.float32),
            pltpu.VMEM((sites, rows, columns), jnp.int32),
            pltpu.VMEM(log_param.shape, jnp.float32),
            pltpu.VMEM(probe_dirs.shape, jnp.float32),
            pltpu.VMEM((columns, columns), jnp.bfloat16),
        ]

    def rows_of(held):
        return pltpu.VMEM((chunks, held * rows, LANES), jnp.float32)

    down = [(i + 1, i) for i in range(slabs - 1)]
    beyond = lax.ppermute(background[: 2 * HALO - 1], "space", down)
    size = probes + 2 * HALO * tiles
    packet = pl.pallas_call(
        packet_kernel,
        out_shape=shape(size),
        in_specs=[smem] + [anywhere] * 4,
        out_specs=anywhere,
        scratch_shapes=inputs(1, 2 * HALO)
        + [rows_of(1), rows_of(2 * HALO), scratch(size), copies(4), copies(3)],
        compiler_params=params,
        name="packet",
    )(trap_density, background, site_class, log_param, probe_dirs)
    next_packet = lax.ppermute(packet, "space", down)
    edge = jnp.stack([at_space > 0, at_space < slabs - 1]).astype(jnp.int32)
    own_coef, own_src, wide, kept, sums, next_bg = pl.pallas_call(
        inner_kernel,
        out_shape=(
            shape(planes * tiles),
            shape((planes + 1) * tiles),
            shape(probes),
            shape(4, probes, tiles),
            shape(probes),
            shape((2 * HALO - 1) * tiles),
        ),
        in_specs=[smem, smem] + [anywhere] * 4 + [vmem],
        out_specs=(vmem,) * 6,
        scratch_shapes=inputs(planes, planes)
        + [rows_of(planes), rows_of(2 * HALO - 1), rows_of(planes)]
        + [field_of(planes)] * 2
        + [copies(4)],
        compiler_params=pltpu.CompilerParams(vmem_limit_bytes=28 * 2**20),
        cost_estimate=pl.CostEstimate(flops=10**9, bytes_accessed=2**24, transcendentals=256),
        name="inner",
    )(edge, trap_density, background, site_class, log_param, probe_dirs, beyond)

    pieces = probes * cells // LANES
    images = pl.pallas_call(
        functools.partial(outer_kernel, chunks, folds),
        out_shape=jax.ShapeDtypeStruct((groups * slabs // 2, 2, pieces, LANES), jnp.float32),
        in_specs=[smem] + [vmem] * 7,
        out_specs=vmem,
        scratch_shapes=[
            scratch(total * tiles),
            scratch(total * tiles),
            field_of(total),
            field_of(total),
        ],
        compiler_params=pltpu.CompilerParams(vmem_limit_bytes=28 * 2**20),
        name="outer",
    )(edge, own_coef, own_src, wide, kept, sums, next_bg, next_packet)

    same = [
        [g * slabs + z for g in range(groups) for z in range(parity, slabs, 2)] for parity in (0, 1)
    ]
    mine = lax.all_to_all(
        images, ("probe", "space"), split_axis=0, concat_axis=0, axis_index_groups=same, tiled=True
    )
    other = lax.ppermute(mine, "space", [(z, z ^ 1) for z in range(slabs)])
    place = jnp.stack([lax.axis_index("probe"), at_space]).astype(jnp.int32)
    count = groups * probes
    results = (
        jax.ShapeDtypeStruct((probes, 1, cells), jnp.float32),
        jax.ShapeDtypeStruct((count, count), jnp.float32),
    )
    params = pltpu.CompilerParams(vmem_limit_bytes=28 * 2**20)
    if count <= 8 and slabs % 16 == 0:
        halves = cells // LANES
        return pl.pallas_call(
            functools.partial(register_kernel, groups, slabs, probes),
            out_shape=results,
            in_specs=[smem, vmem, vmem],
            out_specs=(vmem, vmem),
            scratch_shapes=[pltpu.VMEM((count, halves, slabs, LANES), jnp.float32)],
            compiler_params=params,
            name="factor",
        )(
            place,
            mine.reshape((groups * slabs * pieces, LANES)),
            other.reshape((groups * slabs * pieces, LANES)),
        )
    odd = at_space % 2 == 1
    pairs = [jnp.where(odd, other, mine), jnp.where(odd, mine, other)]
    pairs = [x.reshape((groups, slabs // 2, 2, probes, cells)) for x in pairs]
    every = jnp.stack(pairs, axis=2).reshape((groups, slabs, 2, probes, cells))
    return pl.pallas_call(
        factor_kernel,
        out_shape=results,
        in_specs=[smem, vmem],
        out_specs=(vmem, vmem),
        scratch_shapes=[
            pltpu.VMEM((count, slabs * cells), jnp.float32),
            pltpu.VMEM((count, cells), jnp.float32),
        ],
        compiler_params=params,
        name="factor",
    )(place, every)


def solution(mesh):
    placed = (
        P("probe", "space", None),
        P("space", None),
        P("space", None, None),
        P("space", None, None),
        P(),
    )
    return jax.shard_map(
        shards,
        mesh=mesh,
        in_specs=placed,
        out_specs=(P("probe", "space", None), P()),
        check_vma=False,
    )
```

```python
import functools

import jax
import jax.numpy as jnp
from jax import lax
from jax.experimental import pallas as pl
from jax.experimental.pallas import tpu as pltpu
from jax.sharding import PartitionSpec as P

PX = 64
PY = 4
REF = 8
STEP = 0.12
HALO = 3
RAW_SITES = 3
LANES = 128
HIGHEST = lax.Precision.HIGHEST


def dot_nn(a, b):
    return lax.dot_general(
        a, b, (((1,), (0,)), ((), ())), precision=HIGHEST, preferred_element_type=jnp.float32
    )


def dot_nt(a, b):
    return lax.dot_general(
        a, b, (((1,), (1,)), ((), ())), precision=HIGHEST, preferred_element_type=jnp.float32
    )


def parts_of(x):
    first = x.astype(jnp.bfloat16)
    rest = x - first.astype(jnp.float32)
    second = rest.astype(jnp.bfloat16)
    third = (rest - second.astype(jnp.float32)).astype(jnp.bfloat16)
    return first, second, third


def bf16_dot(a, b):
    return jnp.dot(a, b, preferred_element_type=jnp.float32)


def interleave(exact, small, order):
    parts = [part for x in exact for part in parts_of(x)] + [x.astype(jnp.bfloat16) for x in small]
    placed = bf16_dot(jnp.concatenate(parts, axis=0), order[...])
    results, at = [], 0
    for x in exact:
        count = x.shape[0]
        first, second, third = [placed[at + n * count : at + (n + 1) * count] for n in range(3)]
        results.append((first + second) + third)
        at += 3 * count
    for x in small:
        results.append(placed[at : at + x.shape[0]])
        at += x.shape[0]
    return results


def keep(placed, kept):
    for k in range(kept.shape[0]):
        kept[k] = placed[:, k * LANES : (k + 1) * LANES]


def flat(planes):
    return planes.reshape((planes.shape[0] * planes.shape[1], planes.shape[2]))


def cell_matrix(chunks, turned=False):
    half = REF // chunks
    dims = (LANES, PX * PY) if turned else (PX * PY, LANES)
    cell = lax.broadcasted_iota(jnp.int32, dims, int(turned)) % PX
    lane = lax.broadcasted_iota(jnp.int32, dims, 1 - int(turned)) // half
    return jnp.where(cell == lane, 1.0, 0.0).astype(jnp.float32)


def own_cells(folds):
    half = REF // folds
    sublane = lax.broadcasted_iota(jnp.int32, (8, PX * PY), 0) // half
    return lax.broadcasted_iota(jnp.int32, (8, PX * PY), 1) // PX == sublane


def prolonged(coarse, folds, chunks):
    mask = own_cells(folds)
    rows = [jnp.where(mask, coarse[n : n + 1, :], 0.0) for n in range(coarse.shape[0])]
    return cell_dot(jnp.concatenate(rows, axis=0), cell_matrix(chunks))


def cell_dot(rows, matrix):
    count = rows.shape[0]
    parts = jnp.concatenate(float_parts(rows), axis=0).astype(jnp.bfloat16)
    placed = bf16_dot(parts, matrix.astype(jnp.bfloat16))
    return (placed[:count] + placed[count : 2 * count]) + placed[2 * count :]


def float_parts(x):
    first = x.astype(jnp.bfloat16).astype(jnp.float32)
    rest = x - first
    second = rest.astype(jnp.bfloat16).astype(jnp.float32)
    return first, second, rest - second


def cell_order(columns, chunks):
    x = lax.broadcasted_iota(jnp.int32, (columns, columns), 0)
    place = lax.broadcasted_iota(jnp.int32, (columns, columns), 1)
    wanted = chunks * (place % LANES) + place // LANES
    return jnp.where(x == wanted, 1.0, 0.0).astype(jnp.bfloat16)


def spread_cells(dirs, log_param, folds, chunks):
    probes = dirs.shape[0]
    coarse = [dirs[p] for p in range(probes)] + [jnp.exp(log_param[...])]
    spread = prolonged(jnp.concatenate(coarse, axis=0), folds, chunks)
    return [spread[8 * n : 8 * n + 8, :] for n in range(probes + 1)]


def tile_rows(z, r, rows, folds):
    return pl.ds(z * rows + r, 8, stride=folds)


def trap_of(density, kind):
    trap = jnp.full((8, LANES), density[density.shape[0] - 1])
    for n in range(density.shape[0] - 2, -1, -1):
        trap = jnp.where(kind == float(n), density[n], trap)
    return trap


def weight_of(trap):
    return (1.0 / STEP - 6.0) - trap


def source_of(trap, background):
    return -STEP * trap * background


def packet_kernel(
    density, background_in, sites_in, log_param_in, dirs_in, packet,
    background, sites, log_param, dirs, order, bg, site, made, sems,
):
    count, rows, columns = sites.shape
    chunks, folds = columns // LANES, rows // 8
    tiles = chunks * folds
    probes = dirs.shape[0]
    pairs = [
        (log_param_in, log_param),
        (dirs_in, dirs),
        (background_in.at[pl.ds(2 * HALO - 1, 1)], background),
        (sites_in.at[pl.ds(2 * HALO - count, count)], sites),
    ]
    copies = [pltpu.make_async_copy(a, b, sems.at[n]) for n, (a, b) in enumerate(pairs)]
    for copy in copies:
        copy.start()
    order[...] = cell_order(columns, chunks)
    copies[0].wait()
    copies[1].wait()
    spread = spread_cells(dirs, log_param, folds, chunks)
    for p in range(probes + 1):
        made[p] = spread[p]
    copies[2].wait()
    copies[3].wait()
    placed = interleave([flat(background[...])], [flat(sites[...]).astype(jnp.float32)], order)
    keep(placed[0], bg)
    keep(placed[1], site)
    first = probes + 1 + tiles
    for z in range(count):
        for r in range(folds):
            for k in range(chunks):
                t = r * chunks + k
                trap = trap_of(density, site[k, tile_rows(z, r, rows, folds), :]) * spread[probes]
                if z < count - 1:
                    made[first + z * tiles + t] = trap
                else:
                    source = source_of(trap, bg[k, tile_rows(0, r, rows, folds), :])
                    made[probes + 1 + t] = source
    sent = pltpu.make_async_copy(made, packet, sems.at[4])
    sent.start()
    sent.wait()


class Steps:
    def __init__(self, chunks, folds, probes, zero_plane, coef, src):
        self.chunks, self.folds, self.tiles = chunks, folds, chunks * folds
        self.probes, self.zero_plane = probes, zero_plane
        self.coef, self.src = coef, src
        self.lane = lax.broadcasted_iota(jnp.int32, (8, LANES), 1)
        self.sublane = lax.broadcasted_iota(jnp.int32, (8, LANES), 0)

    def clear(self, *fields):
        nothing = jnp.zeros((8, LANES), jnp.float32)
        for t in range(self.tiles):
            for field in fields:
                for p in range(self.probes):
                    field[self.zero_plane, p, t] = nothing

    def from_left(self, x):
        return jnp.where(self.lane == 0, 0.0, pltpu.roll(x, 1, 1))

    def from_right(self, x):
        return jnp.where(self.lane == LANES - 1, 0.0, pltpu.roll(x, LANES - 1, 1))

    def from_before(self, x):
        return jnp.where(self.sublane == 0, 0.0, pltpu.roll(x, 1, 0))

    def from_after(self, x):
        return jnp.where(self.sublane == 7, 0.0, pltpu.roll(x, 7, 0))

    def first(self, own, to, other=None, beyond=()):
        chunks, folds, tiles = self.chunks, self.folds, self.tiles
        src, coef = self.src, self.coef
        turns = (self.from_left, self.from_right, self.from_before, self.from_after)
        shifted = [[f(x) for x in own] for f in turns]

        def body(z, carry):
            down = jnp.where(z > 0, z - 1, self.zero_plane) * tiles
            up = (z + 1) * tiles
            s = [[src[z * tiles + r * chunks + k] for k in range(chunks)] for r in range(folds)]
            for r in range(folds):
                for k in range(chunks):
                    t = r * chunks + k
                    same = coef[z * tiles + t] * s[r][k]
                    outer = []
                    for there, value, turn, kind in (
                        (k > 0, s[r][k - 1], (1, 1), 0),
                        (k + 1 < chunks, s[r][(k + 1) % chunks], (LANES - 1, 1), 1),
                        (r > 0, s[r - 1][k], (1, 0), 2),
                        (r + 1 < folds, s[(r + 1) % folds][k], (7, 0), 3),
                    ):
                        if there:
                            same = same + value
                        else:
                            outer.append((pltpu.roll(value, *turn), shifted[kind]))
                    for name, value in (("down", src[down + t]), ("up", src[up + t])):
                        if name == other:
                            outer.append((value, beyond))
                        else:
                            same = same + value
                    for p in range(self.probes):
                        result = same * own[p]
                        for value, factor in outer:
                            result = result + value * factor[p]
                        to[z, p, t] = result
            return carry

        return body

    def stencil(self, ref, valid, z, emit, extra):
        chunks, folds, tiles = self.chunks, self.folds, self.tiles
        first, stop = valid

        def at(z):
            return jnp.where((z >= first) & (z < stop), z, self.zero_plane)

        down, here, there, up = at(z - 1), at(z), at(z + 1), at(z + 2)
        for p in range(self.probes):
            pair = [[ref[plane, p, t] for t in range(tiles)] for plane in (here, there)]
            for r in range(folds):
                for k in range(chunks):
                    t = r * chunks + k
                    for n, value in enumerate(pair):
                        left = value[t - 1] if k else self.from_left(value[t + chunks - 1])
                        if k + 1 < chunks:
                            right = value[t + 1]
                        else:
                            right = self.from_right(value[t + 1 - chunks])
                        if r:
                            before = value[t - chunks]
                        else:
                            before = self.from_before(value[t + tiles - chunks])
                        if r + 1 < folds:
                            after = value[t + chunks]
                        else:
                            after = self.from_after(value[t + chunks - tiles])
                        above = pair[1 - n][t] + (ref[up, p, t] if n else ref[down, p, t])
                        weight = self.coef[(z + n) * tiles + t]
                        if extra:
                            weight = weight + extra
                        sides = (left + right) + (before + after)
                        emit(z + n, p, t, (sides + above) + weight * value[t])

    def step(self, ref, to, valid, wanted, extra=0.0):
        start, stop = wanted

        def body(n, carry):
            def emit(z, p, t, result):
                to[z, p, t] = result

            self.stencil(ref, valid, jnp.minimum(start + 2 * n, stop - 2), emit, extra)
            return carry

        lax.fori_loop(0, (stop - start + 1) // 2, body, 0)

    def widen(self, ref, to, valid, at_low, at_high):
        first, stop = valid

        def move(a, b):
            for p in range(self.probes):
                for t in range(self.tiles):
                    to[b, p, t] = ref[a, p, t]

        pl.when(at_low)(lambda: move(first, first - 1))
        pl.when(at_high)(lambda: move(stop - 1, stop))

    def images(self, m, u, by_one, by_two, span, carry, other=None):
        chunks, folds, tiles = self.chunks, self.folds, self.tiles
        src = self.src

        def at(z, valid):
            return jnp.where((z >= valid[0]) & (z < valid[1]), z, self.zero_plane)

        def body(z, carry):
            carry = [list(c) for c in carry]
            down = jnp.where(z > 0, z - 1, self.zero_plane) * tiles
            up = (z + 1) * tiles
            here, kept = at(z, by_one), at(z, by_two)
            s = [src[z * tiles + t] for t in range(tiles)]
            for t in range(tiles):
                r, k = t // chunks, t % chunks
                same = self.coef[z * tiles + t] * s[t]
                moved = []
                if k:
                    same = same + s[t - 1]
                else:
                    moved.append((2, self.from_left(s[t + chunks - 1])))
                if k + 1 < chunks:
                    same = same + s[t + 1]
                else:
                    moved.append((1, self.from_right(s[t + 1 - chunks])))
                if r:
                    same = same + s[t - chunks]
                else:
                    moved.append((4, self.from_before(s[t + tiles - chunks])))
                if r + 1 < folds:
                    same = same + s[t + chunks]
                else:
                    moved.append((3, self.from_after(s[t + chunks - tiles])))
                for name, value in (("down", src[down + t]), ("up", src[up + t])):
                    if name == other:
                        moved.append((5, value))
                    else:
                        same = same + value
                scaled = s[t] * (1.0 / STEP**2)
                for p in range(self.probes):
                    value = m[here, p, t]
                    carry[p][0] = carry[p][0] + (same * value + scaled * u[kept, p, t])
                    for n, factor in moved:
                        carry[p][n] = carry[p][n] + factor * value
            return tuple(tuple(c) for c in carry)

        if isinstance(span, int):
            return body(span, carry)
        return lax.fori_loop(*span, body, carry)

    def empty_sums(self):
        nothing = jnp.zeros((8, LANES), jnp.float32)
        return ((nothing,) * 6,) * self.probes

    def moved_sums(self, sums):
        return [
            c[0]
            + (self.from_left(c[1]) + self.from_right(c[2]))
            + (self.from_before(c[3]) + self.from_after(c[4]))
            for c in sums
        ]

    def after_tangent(self, odd, even, mine, at_low, at_high):
        first, stop = mine
        by_two = (jnp.where(at_low, first - 1, first), jnp.where(at_high, stop + 1, stop))
        by_one = (jnp.where(at_low, first - 2, first), jnp.where(at_high, stop + 2, stop))
        self.step(odd, even, mine, mine, 1.0 / STEP)
        self.widen(odd, even, mine, at_low, at_high)
        self.step(even, odd, by_two, by_two)
        self.widen(even, odd, by_two, at_low, at_high)
        return by_one, by_two


def inner_kernel(
    edge, density, background_in, sites_in, log_param_in, dirs_in,
    coef, src, wide, kept, sums, order,
    background, sites, log_param, dirs, bg, site, even, odd, sems,
):
    planes, rows, columns = background.shape
    chunks, folds = columns // LANES, rows // 8
    tiles = chunks * folds
    probes = dirs.shape[0]
    copies = [
        (log_param_in, log_param),
        (dirs_in, dirs),
        (background_in, background),
        (sites_in, sites),
    ]
    copies = [pltpu.make_async_copy(a, b, sems.at[n]) for n, (a, b) in enumerate(copies)]
    for copy in copies:
        copy.start()
    steps = Steps(chunks, folds, probes, planes, coef, src)
    steps.clear(even, odd)
    nothing = jnp.zeros((8, LANES), jnp.float32)
    for t in range(tiles):
        src[planes * tiles + t] = nothing
    order[...] = cell_order(columns, chunks)
    for copy in copies:
        copy.wait()
    spread = spread_cells(dirs, log_param, folds, chunks)
    for p in range(probes):
        wide[p] = spread[p]

    placed = interleave([flat(background[...])], [flat(sites[...]).astype(jnp.float32)], order)
    for x, scratch in zip(placed, (bg, site)):
        keep(x, scratch)
    for r in range(folds):
        for k in range(chunks):
            t = r * chunks + k
            for z in range(planes):
                at = tile_rows(z, r, rows, folds)
                trap = trap_of(density, site[k, at, :]) * spread[probes]
                coef[z * tiles + t] = weight_of(trap)
                src[z * tiles + t] = source_of(trap, bg[k, at, :])
    at_low = edge[0] != 0

    def low(z):
        return jnp.where(at_low, z, 0)

    last = planes - HALO
    lax.fori_loop(low(1), last + 2, steps.first(spread[:probes], odd), 0)
    steps.step(odd, even, (low(1), last + 2), (low(2), last + 1))
    for n, (ref, z) in enumerate(((odd, last), (odd, last + 1), (even, last - 1), (even, last))):
        for p in range(probes):
            for t in range(tiles):
                kept[n, p, t] = ref[z, p, t]
    mine = (low(HALO), last)
    steps.step(even, odd, (low(2), last + 1), mine)
    by_one, by_two = steps.after_tangent(odd, even, mine, at_low, True)
    result = steps.moved_sums(steps.images(odd, even, by_one, by_two, by_one, steps.empty_sums()))
    for p in range(probes):
        sums[p] = result[p]


def beyond_kernel(rows, folds, order, raw, next_bg, next_site, bg, site):
    chunks = bg.shape[0]
    tiles = chunks * folds
    count = bg.shape[1]
    placed = interleave([raw[:count, :]], [raw[count:, :]], order)
    for x, scratch, to in zip(placed, (bg, site), (next_bg, next_site)):
        keep(x, scratch)
        for z in range(to.shape[0] // tiles):
            for t in range(tiles):
                r, k = t // chunks, t % chunks
                to[z * tiles + t] = scratch[k, tile_rows(z, r, rows, folds), :]


def outer_kernel(
    chunks, folds, edge, density, own_coef, own_src, own_wide, kept, own_sums, next_bg, next_site, packet, out,
    coef, src, even, odd,
):
    tiles = chunks * folds
    probes = own_wide.shape[0]
    total = even.shape[0] - 1
    planes = total - 2 * HALO
    steps = Steps(chunks, folds, probes, total, coef, src)
    last = planes - HALO
    halo = planes * tiles

    def copy(source, start, target, at, count):
        def body(n, carry):
            for t in range(tiles):
                target[at + n * tiles + t] = source[start + n * tiles + t]
            return carry

        lax.fori_loop(0, count, body, 0)

    own = (last - HALO) * tiles
    copy(own_src, own, src, own, planes - last + HALO)
    copy(own_coef, own, coef, own, planes - last + HALO)

    raw = next_site.shape[0]
    scale = packet[probes]

    def beyond_plane(n, carry):
        for t in range(tiles):
            at = n * tiles + t
            trap = trap_of(density, next_site[at]) * scale
            coef[halo + at] = weight_of(trap)
            src[halo + at] = source_of(trap, next_bg[at])
        return carry

    def packet_plane(n, carry):
        for t in range(tiles):
            at = n * tiles + t
            trap = packet[probes + 1 + tiles + at - raw]
            coef[halo + at] = weight_of(trap)
            src[halo + at] = source_of(trap, next_bg[at])
        return carry

    lax.fori_loop(0, raw // tiles, beyond_plane, 0)
    lax.fori_loop(raw // tiles, 2 * HALO - 1, packet_plane, 0)
    copy(packet, probes + 1, src, (total - 1) * tiles, 1)
    steps.clear(even, odd)
    for p in range(probes):
        for t in range(tiles):
            odd[last, p, t] = kept[0, p, t]
            odd[last + 1, p, t] = kept[1, p, t]
            even[last - 1, p, t] = kept[2, p, t]
            even[last, p, t] = kept[3, p, t]

    at_high = edge[1] != 0

    def high(z):
        return jnp.where(at_high, z, planes)

    mine = [own_wide[p] for p in range(probes)]
    beyond = [packet[p] for p in range(probes)]
    steps.first(mine, odd, "up", beyond)(planes - 1, 0)

    @pl.when(at_high)
    def _():
        steps.first(beyond, odd, "down", mine)(planes, 0)
        lax.fori_loop(planes + 1, total - 1, steps.first(beyond, odd), 0)

    steps.step(odd, even, (last, high(total - 1)), (last + 1, high(total - 2)))
    mine = (last, high(total - HALO))
    steps.step(even, odd, (last - 1, high(total - 2)), mine)
    by_one, by_two = steps.after_tangent(odd, even, mine, True, at_high)
    start, stop = by_one
    empty = steps.empty_sums()
    inside = steps.images(odd, even, by_one, by_two, (start, planes - 1), empty)
    inside = steps.images(odd, even, by_one, by_two, planes - 1, inside, "up")
    above = [list(c) for c in empty]
    for p in range(probes):
        above[p][0] = inside[p][5]
    above = steps.images(odd, even, by_one, by_two, (planes + 1, stop), tuple(tuple(c) for c in above))
    above = steps.images(odd, even, by_one, by_two, planes, above, "down")
    inside = [x + own_sums[p] + above[p][5] for p, x in enumerate(steps.moved_sums(inside))]
    above = steps.moved_sums(above)

    added = jnp.concatenate(inside + above, axis=0) * STEP**6
    images = cell_dot(added, cell_matrix(chunks, True))
    mask = own_cells(folds)
    for part in range(2):
        halves = []
        for p in range(probes):
            image = jnp.where(mask, images[8 * (part * probes + p) :][:8], 0.0)
            image = jnp.sum(image, axis=0, keepdims=True)
            halves += [image[:, h * LANES : (h + 1) * LANES] for h in range(image.shape[1] // LANES)]
        halves = jnp.concatenate(halves, axis=0)

        def send(n, carry):
            out[n, part] = halves
            return carry

        lax.fori_loop(0, out.shape[0], send, 0, unroll=8)


def eliminate(gram):
    count = gram.shape[0]
    rows = lax.broadcasted_iota(jnp.int32, (count, count), 0)
    columns = lax.broadcasted_iota(jnp.int32, (count, count), 1)
    inverse = jnp.where(rows == columns, 1.0, 0.0)
    for j in range(count - 1):
        across = jnp.broadcast_to(gram[:, j : j + 1], (count, count))
        turned = 1.0 / across
        ratio = jnp.where(rows > j, across, 0.0)
        gram_row, inverse_row = (gram * turned)[j : j + 1, :], (inverse * turned)[j : j + 1, :]
        gram = gram - ratio * gram_row
        inverse = inverse - ratio * inverse_row
    diagonal = jnp.sum(jnp.where(rows == columns, gram, 0.0), axis=1, keepdims=True)
    scale = 1.0 / jnp.sqrt(diagonal)
    upper = jnp.where(columns >= rows, gram, 0.0) * scale
    return upper, inverse * scale


def gram_of(parts, count):
    stacked = jnp.concatenate(list(parts) + [jnp.zeros_like(parts[0])], axis=0)
    stacked = stacked.astype(jnp.bfloat16)
    every = lax.dot_general(
        stacked, stacked, (((1,), (1,)), ((), ())), preferred_element_type=jnp.float32
    )
    tall = every[:count] + (every[count : 2 * count] + every[2 * count : 3 * count])
    return tall[:, :count] + (tall[:, count : 2 * count] + tall[:, 2 * count : 3 * count])


def times(a, parts):
    first, second, third = float_parts(a)
    left = jnp.concatenate([first, second, third, first, second, first], axis=1)
    right = jnp.concatenate([parts[0]] * 3 + [parts[1]] * 2 + [parts[2]], axis=0)
    return bf16_dot(left.astype(jnp.bfloat16), right.astype(jnp.bfloat16))


def factor_kernel(place, parts, q_out, lower_out, rows_ref, q_ref):
    groups, slabs, _, probes, cells = parts.shape
    count = groups * probes
    for g in range(groups):

        def gather(slab, carry):
            before = jnp.maximum(slab - 1, 0)
            image = parts[g, slab, 0] + jnp.where(slab > 0, parts[g, before, 1], 0.0)
            at = pl.multiple_of(slab * cells, cells)
            rows_ref[pl.ds(g * probes, probes), pl.ds(at, cells)] = image
            return carry

        lax.fori_loop(0, slabs, gather, 0, unroll=True if slabs <= 16 else 8)
    total = slabs * cells
    rows = rows_ref[...]
    parts_one = float_parts(rows)
    upper_one, inverse_one = eliminate(gram_of(parts_one, count) / total)
    basis = times(inverse_one, parts_one)
    rows_ref[...] = basis
    upper_two, inverse_two = eliminate(gram_of(float_parts(basis), count) / total)
    mine = rows_ref[:, pl.ds(pl.multiple_of(place[1] * cells, cells), cells)]
    q_ref[...] = dot_nn(inverse_two, mine)
    for g in range(groups):

        @pl.when(place[0] == g)
        def _():
            q_out[:, 0, :] = q_ref[pl.ds(g * probes, probes), :]

    r = lax.broadcasted_iota(jnp.int32, (count, count), 0)
    c = lax.broadcasted_iota(jnp.int32, (count, count), 1)
    lower_one = dot_nt(jnp.where(r == c, 1.0, 0.0), upper_one)
    lower_out[...] = dot_nt(lower_one, upper_two)


def everywhere(x):
    x = jnp.broadcast_to(jnp.sum(x, axis=1, keepdims=True), x.shape)
    for shift in (4, 2, 1):
        x = x + pltpu.roll(x, shift, 0)
    return x


def cholesky(rows, total):
    count = len(rows)
    rows = [list(row) for row in rows]
    gram = {}
    for i in range(count):
        for j in range(i + 1):
            product = sum(a * b for a, b in zip(rows[i][1:], rows[j][1:]))
            gram[i, j] = everywhere(rows[i][0] * rows[j][0] + product) * (1.0 / total)
    factor = {}
    for j in range(count):
        pivot = gram[j, j]
        turned = lax.rsqrt(pivot)
        turned = turned * (1.5 - 0.5 * pivot * turned * turned)
        factor[j, j] = pivot * turned
        rows[j] = [x * turned for x in rows[j]]
        for i in range(j + 1, count):
            factor[i, j] = gram[i, j] * turned
        for i in range(j + 1, count):
            for k in range(j + 1, i + 1):
                gram[i, k] = gram[i, k] - factor[i, j] * factor[k, j]
            rows[i] = [x - factor[i, j] * y for x, y in zip(rows[i], rows[j])]
    return factor, rows


def register_kernel(groups, slabs, probes, place, mine, other, q_out, lower_out, q_ref):
    halves = q_out.shape[2] // LANES
    pieces = probes * halves
    step = 2 * pieces
    sublane = lax.broadcasted_iota(jnp.int32, (8, LANES), 0)
    odd = jnp.broadcast_to(place[1] % 2, (8, LANES)) == 1

    def load(at):
        at = pl.ds(at, 8, stride=step)
        one, two = mine[at, :], other[at, :]
        return jnp.where(odd, two, one), jnp.where(odd, one, two)

    rows = []
    for g in range(groups):
        for p in range(probes):
            row = []
            for h in range(halves):
                last = None
                for block in range(slabs // 16):
                    at = (g * slabs // 2 + 8 * block) * step + p * halves + h
                    even_own, odd_own = load(at)
                    even_next, odd_next = load(at + pieces)
                    before = pltpu.roll(odd_next, 1, 0)
                    first = 0.0 if last is None else last
                    last = before
                    row.append((block, 0, h, even_own + jnp.where(sublane == 0, first, before)))
                    row.append((block, 1, h, odd_own + even_next))
            rows.append(row)
    places = [x[:3] for x in rows[0]]
    rows = [[x[3] for x in row] for row in rows]
    total = slabs * halves * LANES
    factor_one, basis = cholesky(rows, total)
    factor_two, rows = cholesky(basis, total)
    for i, row in enumerate(rows):
        for (block, parity, h), x in zip(places, row):
            q_ref[i, h, pl.ds(parity * (slabs // 2) + 8 * block, 8), :] = x
    own = (place[1] % 2) * (slabs // 2) + place[1] // 2
    for p in range(probes):
        for h in range(halves):
            mine = q_ref[place[0] * probes + p, h, pl.ds(own, 1), :]
            q_out[p, :, pl.ds(h * LANES, LANES)] = mine
    count = len(rows)
    r = lax.broadcasted_iota(jnp.int32, (8, LANES), 0)
    c = lax.broadcasted_iota(jnp.int32, (8, LANES), 1)
    lower = jnp.zeros((8, LANES), jnp.float32)
    for i in range(count):
        for j in range(i + 1):
            entry = sum(factor_one[i, k] * factor_two[k, j] for k in range(j, i + 1))
            lower = jnp.where((r == i) & (c == j), entry, lower)
    lower_out[...] = lower[:count, :count]


def shards(probe_dirs, log_param, background, site_class, trap_density):
    probes = probe_dirs.shape[0]
    cells = probe_dirs.shape[2]
    planes, rows, columns = background.shape
    slabs = lax.axis_size("space")
    groups = lax.axis_size("probe")
    at_space = lax.axis_index("space")
    vmem = pl.BlockSpec(memory_space=pltpu.VMEM)
    smem = pl.BlockSpec(memory_space=pltpu.SMEM)
    anywhere = pl.BlockSpec(memory_space=pl.ANY)
    params = pltpu.CompilerParams(vmem_limit_bytes=62 * 2**20)

    chunks, folds = columns // LANES, rows // 8
    tiles = chunks * folds
    total = planes + 2 * HALO
    tile = (8, LANES)

    def shape(*dims):
        return jax.ShapeDtypeStruct(dims + tile, jnp.float32)

    def scratch(*dims):
        return pltpu.VMEM(dims + tile, jnp.float32)

    def copies(count):
        return pltpu.SemaphoreType.DMA((count,))

    def inputs(held, sites):
        return [
            pltpu.VMEM((held, rows, columns), jnp.float32),
            pltpu.VMEM((sites, rows, columns), jnp.int32),
            pltpu.VMEM(log_param.shape, jnp.float32),
            pltpu.VMEM(probe_dirs.shape, jnp.float32),
            pltpu.VMEM((columns, columns), jnp.bfloat16),
        ]

    def rows_of(held):
        return pltpu.VMEM((chunks, held * rows, LANES), jnp.float32)

    down = [(i + 1, i) for i in range(slabs - 1)]
    near = 2 * HALO - 1
    raw = jnp.concatenate(
        [
            background[:near].reshape((near * rows, columns)),
            site_class[:RAW_SITES].reshape((RAW_SITES * rows, columns)).astype(jnp.float32),
        ],
        axis=0,
    )
    raw = lax.ppermute(raw, "space", down)
    size = probes + 1 + (2 * HALO - RAW_SITES) * tiles
    packet = pl.pallas_call(
        packet_kernel,
        out_shape=shape(size),
        in_specs=[smem] + [anywhere] * 4,
        out_specs=anywhere,
        scratch_shapes=inputs(1, 2 * HALO - RAW_SITES)
        + [rows_of(1), rows_of(2 * HALO - RAW_SITES), scratch(size), copies(5)],
        compiler_params=params,
        name="packet",
    )(trap_density, background, site_class, log_param, probe_dirs)
    next_packet = lax.ppermute(packet, "space", down)
    edge = jnp.stack([at_space > 0, at_space < slabs - 1]).astype(jnp.int32)
    own_coef, own_src, wide, kept, sums, order = pl.pallas_call(
        inner_kernel,
        out_shape=(
            shape(planes * tiles),
            shape((planes + 1) * tiles),
            shape(probes),
            shape(4, probes, tiles),
            shape(probes),
            jax.ShapeDtypeStruct((columns, columns), jnp.bfloat16),
        ),
        in_specs=[smem, smem] + [anywhere] * 4,
        out_specs=(vmem,) * 6,
        scratch_shapes=inputs(planes, planes)[:4]
        + [rows_of(planes), rows_of(planes)]
        + [scratch(planes + 1, probes, tiles)] * 2
        + [copies(4)],
        compiler_params=pltpu.CompilerParams(vmem_limit_bytes=28 * 2**20),
        cost_estimate=pl.CostEstimate(flops=10**9, bytes_accessed=2**24, transcendentals=256),
        name="inner",
    )(edge, trap_density, background, site_class, log_param, probe_dirs)

    next_bg, next_site = pl.pallas_call(
        functools.partial(beyond_kernel, rows, folds),
        out_shape=(shape(near * tiles), shape(RAW_SITES * tiles)),
        in_specs=[vmem] * 2,
        out_specs=(vmem,) * 2,
        scratch_shapes=[rows_of(near), rows_of(RAW_SITES)],
        compiler_params=pltpu.CompilerParams(vmem_limit_bytes=28 * 2**20),
        name="beyond",
    )(order, raw)

    pieces = probes * cells // LANES
    images = pl.pallas_call(
        functools.partial(outer_kernel, chunks, folds),
        out_shape=jax.ShapeDtypeStruct((groups * slabs // 2, 2, pieces, LANES), jnp.float32),
        in_specs=[smem] * 2 + [vmem] * 8,
        out_specs=vmem,
        scratch_shapes=[
            scratch(total * tiles),
            scratch(total * tiles),
            scratch(total + 1, probes, tiles),
            scratch(total + 1, probes, tiles),
        ],
        compiler_params=pltpu.CompilerParams(vmem_limit_bytes=28 * 2**20),
        name="outer",
    )(edge, trap_density, own_coef, own_src, wide, kept, sums, next_bg, next_site, next_packet)

    same = [
        [g * slabs + z for g in range(groups) for z in range(parity, slabs, 2)] for parity in (0, 1)
    ]
    mine = lax.all_to_all(
        images, ("probe", "space"), split_axis=0, concat_axis=0, axis_index_groups=same, tiled=True
    )
    other = lax.ppermute(mine, "space", [(z, z ^ 1) for z in range(slabs)])
    place = jnp.stack([lax.axis_index("probe"), at_space]).astype(jnp.int32)
    count = groups * probes
    results = (
        jax.ShapeDtypeStruct((probes, 1, cells), jnp.float32),
        jax.ShapeDtypeStruct((count, count), jnp.float32),
    )
    params = pltpu.CompilerParams(vmem_limit_bytes=28 * 2**20)
    if count <= 8 and slabs % 16 == 0:
        halves = cells // LANES
        return pl.pallas_call(
            functools.partial(register_kernel, groups, slabs, probes),
            out_shape=results,
            in_specs=[smem, vmem, vmem],
            out_specs=(vmem, vmem),
            scratch_shapes=[pltpu.VMEM((count, halves, slabs, LANES), jnp.float32)],
            compiler_params=params,
            name="factor",
        )(
            place,
            mine.reshape((groups * slabs * pieces, LANES)),
            other.reshape((groups * slabs * pieces, LANES)),
        )
    odd = at_space % 2 == 1
    pairs = [jnp.where(odd, other, mine), jnp.where(odd, mine, other)]
    pairs = [x.reshape((groups, slabs // 2, 2, probes, cells)) for x in pairs]
    every = jnp.stack(pairs, axis=2).reshape((groups, slabs, 2, probes, cells))
    return pl.pallas_call(
        factor_kernel,
        out_shape=results,
        in_specs=[smem, vmem],
        out_specs=(vmem, vmem),
        scratch_shapes=[
            pltpu.VMEM((count, slabs * cells), jnp.float32),
            pltpu.VMEM((count, cells), jnp.float32),
        ],
        compiler_params=params,
        name="factor",
    )(place, every)


def solution(mesh):
    placed = (
        P("probe", "space", None),
        P("space", None),
        P("space", None, None),
        P("space", None, None),
        P(),
    )
    return jax.shard_map(
        shards,
        mesh=mesh,
        in_specs=placed,
        out_specs=(P("probe", "space", None), P()),
        check_vma=False,
    )
```

```python
import functools

import jax
import jax.numpy as jnp
from jax import lax
from jax.experimental import pallas as pl
from jax.experimental.pallas import tpu as pltpu
from jax.sharding import PartitionSpec as P

PX = 64
PY = 4
REF = 8
STEP = 0.12
HALO = 3
RAW_SITES = 3
LANES = 128
HIGHEST = lax.Precision.HIGHEST


def dot_nn(a, b):
    return lax.dot_general(
        a, b, (((1,), (0,)), ((), ())), precision=HIGHEST, preferred_element_type=jnp.float32
    )


def dot_nt(a, b):
    return lax.dot_general(
        a, b, (((1,), (1,)), ((), ())), precision=HIGHEST, preferred_element_type=jnp.float32
    )


def parts_of(x):
    first = x.astype(jnp.bfloat16)
    rest = x - first.astype(jnp.float32)
    second = rest.astype(jnp.bfloat16)
    third = (rest - second.astype(jnp.float32)).astype(jnp.bfloat16)
    return first, second, third


def bf16_dot(a, b):
    return jnp.dot(a, b, preferred_element_type=jnp.float32)


def interleave(exact, small, order):
    parts = [part for x in exact for part in parts_of(x)] + [x.astype(jnp.bfloat16) for x in small]
    placed = bf16_dot(jnp.concatenate(parts, axis=0), order[...])
    results, at = [], 0
    for x in exact:
        count = x.shape[0]
        first, second, third = [placed[at + n * count : at + (n + 1) * count] for n in range(3)]
        results.append((first + second) + third)
        at += 3 * count
    for x in small:
        results.append(placed[at : at + x.shape[0]])
        at += x.shape[0]
    return results


def keep(placed, kept):
    for k in range(kept.shape[0]):
        kept[k] = placed[:, k * LANES : (k + 1) * LANES]


def flat(planes):
    return planes.reshape((planes.shape[0] * planes.shape[1], planes.shape[2]))


def cell_matrix(chunks, turned=False):
    half = REF // chunks
    dims = (LANES, PX * PY) if turned else (PX * PY, LANES)
    cell = lax.broadcasted_iota(jnp.int32, dims, int(turned)) % PX
    lane = lax.broadcasted_iota(jnp.int32, dims, 1 - int(turned)) // half
    return jnp.where(cell == lane, 1.0, 0.0).astype(jnp.float32)


def own_cells(folds):
    half = REF // folds
    sublane = lax.broadcasted_iota(jnp.int32, (8, PX * PY), 0) // half
    return lax.broadcasted_iota(jnp.int32, (8, PX * PY), 1) // PX == sublane


def prolonged(coarse, folds, chunks):
    mask = own_cells(folds)
    rows = [jnp.where(mask, coarse[n : n + 1, :], 0.0) for n in range(coarse.shape[0])]
    return cell_dot(jnp.concatenate(rows, axis=0), cell_matrix(chunks))


def cell_dot(rows, matrix):
    count = rows.shape[0]
    parts = jnp.concatenate(float_parts(rows), axis=0).astype(jnp.bfloat16)
    placed = bf16_dot(parts, matrix.astype(jnp.bfloat16))
    return (placed[:count] + placed[count : 2 * count]) + placed[2 * count :]


def float_parts(x):
    first = x.astype(jnp.bfloat16).astype(jnp.float32)
    rest = x - first
    second = rest.astype(jnp.bfloat16).astype(jnp.float32)
    return first, second, rest - second


def cell_order(columns, chunks):
    x = lax.broadcasted_iota(jnp.int32, (columns, columns), 0)
    place = lax.broadcasted_iota(jnp.int32, (columns, columns), 1)
    wanted = chunks * (place % LANES) + place // LANES
    return jnp.where(x == wanted, 1.0, 0.0).astype(jnp.bfloat16)


def spread_cells(dirs, log_param, folds, chunks):
    probes = dirs.shape[0]
    coarse = [dirs[p] for p in range(probes)] + [jnp.exp(log_param[...])]
    spread = prolonged(jnp.concatenate(coarse, axis=0), folds, chunks)
    return [spread[8 * n : 8 * n + 8, :] for n in range(probes + 1)]


def tile_rows(z, r, rows, folds):
    return pl.ds(z * rows + r, 8, stride=folds)


def trap_of(density, kind):
    trap = jnp.full((8, LANES), density[density.shape[0] - 1])
    for n in range(density.shape[0] - 2, -1, -1):
        trap = jnp.where(kind == float(n), density[n], trap)
    return trap


def weight_of(trap):
    return (1.0 / STEP - 6.0) - trap


def source_of(trap, background):
    return -STEP * trap * background


def raw_kernel(background, sites, raw, held, made, sems):
    count = held.shape[0]
    near = raw.shape[0] - count
    fetch = pltpu.make_async_copy(sites.at[pl.ds(0, count)], held, sems.at[0])
    fetch.start()
    direct = pltpu.make_async_copy(
        background.at[pl.ds(0, near)], raw.at[pl.ds(0, near)], sems.at[1]
    )
    direct.start()
    fetch.wait()
    made[...] = held[...].astype(jnp.float32)
    sent = pltpu.make_async_copy(made, raw.at[pl.ds(near, count)], sems.at[2])
    sent.start()
    sent.wait()
    direct.wait()


def packet_kernel(
    density, background_in, sites_in, log_param_in, dirs_in, packet,
    background, sites, log_param, dirs, order, bg, site, made, sems,
):
    count, rows, columns = sites.shape
    chunks, folds = columns // LANES, rows // 8
    tiles = chunks * folds
    probes = dirs.shape[0]
    pairs = [
        (log_param_in, log_param),
        (dirs_in, dirs),
        (background_in.at[pl.ds(2 * HALO - 1, 1)], background),
        (sites_in.at[pl.ds(2 * HALO - count, count)], sites),
    ]
    copies = [pltpu.make_async_copy(a, b, sems.at[n]) for n, (a, b) in enumerate(pairs)]
    for copy in copies:
        copy.start()
    order[...] = cell_order(columns, chunks)
    copies[0].wait()
    copies[1].wait()
    spread = spread_cells(dirs, log_param, folds, chunks)
    for p in range(probes + 1):
        made[p] = spread[p]
    copies[2].wait()
    copies[3].wait()
    placed = interleave([flat(background[...])], [flat(sites[...]).astype(jnp.float32)], order)
    keep(placed[0], bg)
    keep(placed[1], site)
    first = probes + 1 + tiles
    for z in range(count):
        for r in range(folds):
            for k in range(chunks):
                t = r * chunks + k
                trap = trap_of(density, site[k, tile_rows(z, r, rows, folds), :]) * spread[probes]
                if z < count - 1:
                    made[first + z * tiles + t] = trap
                else:
                    source = source_of(trap, bg[k, tile_rows(0, r, rows, folds), :])
                    made[probes + 1 + t] = source
    sent = pltpu.make_async_copy(made, packet, sems.at[4])
    sent.start()
    sent.wait()


class Steps:
    def __init__(self, chunks, folds, probes, zero_plane, coef, src):
        self.chunks, self.folds, self.tiles = chunks, folds, chunks * folds
        self.probes, self.zero_plane = probes, zero_plane
        self.coef, self.src = coef, src
        self.lane = lax.broadcasted_iota(jnp.int32, (8, LANES), 1)
        self.sublane = lax.broadcasted_iota(jnp.int32, (8, LANES), 0)

    def clear(self, *fields):
        nothing = jnp.zeros((8, LANES), jnp.float32)
        for t in range(self.tiles):
            for field in fields:
                for p in range(self.probes):
                    field[self.zero_plane, p, t] = nothing

    def from_left(self, x):
        return jnp.where(self.lane == 0, 0.0, pltpu.roll(x, 1, 1))

    def from_right(self, x):
        return jnp.where(self.lane == LANES - 1, 0.0, pltpu.roll(x, LANES - 1, 1))

    def from_before(self, x):
        return jnp.where(self.sublane == 0, 0.0, pltpu.roll(x, 1, 0))

    def from_after(self, x):
        return jnp.where(self.sublane == 7, 0.0, pltpu.roll(x, 7, 0))

    def first(self, own, to, other=None, beyond=()):
        chunks, folds, tiles = self.chunks, self.folds, self.tiles
        src, coef = self.src, self.coef
        turns = (self.from_left, self.from_right, self.from_before, self.from_after)
        shifted = [[f(x) for x in own] for f in turns]

        def body(z, carry):
            down = jnp.where(z > 0, z - 1, self.zero_plane) * tiles
            up = (z + 1) * tiles
            s = [[src[z * tiles + r * chunks + k] for k in range(chunks)] for r in range(folds)]
            for r in range(folds):
                for k in range(chunks):
                    t = r * chunks + k
                    same = coef[z * tiles + t] * s[r][k]
                    outer = []
                    for there, value, turn, kind in (
                        (k > 0, s[r][k - 1], (1, 1), 0),
                        (k + 1 < chunks, s[r][(k + 1) % chunks], (LANES - 1, 1), 1),
                        (r > 0, s[r - 1][k], (1, 0), 2),
                        (r + 1 < folds, s[(r + 1) % folds][k], (7, 0), 3),
                    ):
                        if there:
                            same = same + value
                        else:
                            outer.append((pltpu.roll(value, *turn), shifted[kind]))
                    for name, value in (("down", src[down + t]), ("up", src[up + t])):
                        if name == other:
                            outer.append((value, beyond))
                        else:
                            same = same + value
                    for p in range(self.probes):
                        result = same * own[p]
                        for value, factor in outer:
                            result = result + value * factor[p]
                        to[z, p, t] = result
            return carry

        return body

    def stencil(self, ref, valid, z, emit, extra):
        chunks, folds, tiles = self.chunks, self.folds, self.tiles
        first, stop = valid

        def at(z):
            return jnp.where((z >= first) & (z < stop), z, self.zero_plane)

        down, here, there, up = at(z - 1), at(z), at(z + 1), at(z + 2)
        for p in range(self.probes):
            pair = [[ref[plane, p, t] for t in range(tiles)] for plane in (here, there)]
            for r in range(folds):
                for k in range(chunks):
                    t = r * chunks + k
                    for n, value in enumerate(pair):
                        left = value[t - 1] if k else self.from_left(value[t + chunks - 1])
                        if k + 1 < chunks:
                            right = value[t + 1]
                        else:
                            right = self.from_right(value[t + 1 - chunks])
                        if r:
                            before = value[t - chunks]
                        else:
                            before = self.from_before(value[t + tiles - chunks])
                        if r + 1 < folds:
                            after = value[t + chunks]
                        else:
                            after = self.from_after(value[t + chunks - tiles])
                        above = pair[1 - n][t] + (ref[up, p, t] if n else ref[down, p, t])
                        weight = self.coef[(z + n) * tiles + t]
                        if extra:
                            weight = weight + extra
                        sides = (left + right) + (before + after)
                        emit(z + n, p, t, (sides + above) + weight * value[t])

    def step(self, ref, to, valid, wanted, extra=0.0):
        start, stop = wanted

        def body(n, carry):
            def emit(z, p, t, result):
                to[z, p, t] = result

            self.stencil(ref, valid, jnp.minimum(start + 2 * n, stop - 2), emit, extra)
            return carry

        lax.fori_loop(0, (stop - start + 1) // 2, body, 0)

    def widen(self, ref, to, valid, at_low, at_high):
        first, stop = valid

        def move(a, b):
            for p in range(self.probes):
                for t in range(self.tiles):
                    to[b, p, t] = ref[a, p, t]

        pl.when(at_low)(lambda: move(first, first - 1))
        pl.when(at_high)(lambda: move(stop - 1, stop))

    def images(self, m, u, by_one, by_two, span, carry, other=None):
        chunks, folds, tiles = self.chunks, self.folds, self.tiles
        src = self.src

        def at(z, valid):
            return jnp.where((z >= valid[0]) & (z < valid[1]), z, self.zero_plane)

        def body(z, carry):
            carry = [list(c) for c in carry]
            down = jnp.where(z > 0, z - 1, self.zero_plane) * tiles
            up = (z + 1) * tiles
            here, kept = at(z, by_one), at(z, by_two)
            s = [src[z * tiles + t] for t in range(tiles)]
            for t in range(tiles):
                r, k = t // chunks, t % chunks
                same = self.coef[z * tiles + t] * s[t]
                moved = []
                if k:
                    same = same + s[t - 1]
                else:
                    moved.append((2, self.from_left(s[t + chunks - 1])))
                if k + 1 < chunks:
                    same = same + s[t + 1]
                else:
                    moved.append((1, self.from_right(s[t + 1 - chunks])))
                if r:
                    same = same + s[t - chunks]
                else:
                    moved.append((4, self.from_before(s[t + tiles - chunks])))
                if r + 1 < folds:
                    same = same + s[t + chunks]
                else:
                    moved.append((3, self.from_after(s[t + chunks - tiles])))
                for name, value in (("down", src[down + t]), ("up", src[up + t])):
                    if name == other:
                        moved.append((5, value))
                    else:
                        same = same + value
                scaled = s[t] * (1.0 / STEP**2)
                for p in range(self.probes):
                    value = m[here, p, t]
                    carry[p][0] = carry[p][0] + (same * value + scaled * u[kept, p, t])
                    for n, factor in moved:
                        carry[p][n] = carry[p][n] + factor * value
            return tuple(tuple(c) for c in carry)

        if isinstance(span, int):
            return body(span, carry)
        return lax.fori_loop(*span, body, carry)

    def empty_sums(self):
        nothing = jnp.zeros((8, LANES), jnp.float32)
        return ((nothing,) * 6,) * self.probes

    def moved_sums(self, sums):
        return [
            c[0]
            + (self.from_left(c[1]) + self.from_right(c[2]))
            + (self.from_before(c[3]) + self.from_after(c[4]))
            for c in sums
        ]

    def after_tangent(self, odd, even, mine, at_low, at_high):
        first, stop = mine
        by_two = (jnp.where(at_low, first - 1, first), jnp.where(at_high, stop + 1, stop))
        by_one = (jnp.where(at_low, first - 2, first), jnp.where(at_high, stop + 2, stop))
        self.step(odd, even, mine, mine, 1.0 / STEP)
        self.widen(odd, even, mine, at_low, at_high)
        self.step(even, odd, by_two, by_two)
        self.widen(even, odd, by_two, at_low, at_high)
        return by_one, by_two


def inner_kernel(
    edge, density, background_in, sites_in, log_param_in, dirs_in,
    coef, src, wide, kept, sums, order,
    background, sites, log_param, dirs, bg, site, even, odd, sems,
):
    planes, rows, columns = background.shape
    chunks, folds = columns // LANES, rows // 8
    tiles = chunks * folds
    probes = dirs.shape[0]
    copies = [
        (log_param_in, log_param),
        (dirs_in, dirs),
        (background_in, background),
        (sites_in, sites),
    ]
    copies = [pltpu.make_async_copy(a, b, sems.at[n]) for n, (a, b) in enumerate(copies)]
    for copy in copies:
        copy.start()
    steps = Steps(chunks, folds, probes, planes, coef, src)
    steps.clear(even, odd)
    nothing = jnp.zeros((8, LANES), jnp.float32)
    for t in range(tiles):
        src[planes * tiles + t] = nothing
    order[...] = cell_order(columns, chunks)
    for copy in copies:
        copy.wait()
    spread = spread_cells(dirs, log_param, folds, chunks)
    for p in range(probes):
        wide[p] = spread[p]

    placed = interleave([flat(background[...])], [flat(sites[...]).astype(jnp.float32)], order)
    for x, scratch in zip(placed, (bg, site)):
        keep(x, scratch)
    for r in range(folds):
        for k in range(chunks):
            t = r * chunks + k
            for z in range(planes):
                at = tile_rows(z, r, rows, folds)
                trap = trap_of(density, site[k, at, :]) * spread[probes]
                coef[z * tiles + t] = weight_of(trap)
                src[z * tiles + t] = source_of(trap, bg[k, at, :])
    at_low = edge[0] != 0

    def low(z):
        return jnp.where(at_low, z, 0)

    last = planes - HALO
    lax.fori_loop(low(1), last + 2, steps.first(spread[:probes], odd), 0)
    steps.step(odd, even, (low(1), last + 2), (low(2), last + 1))
    for n, (ref, z) in enumerate(((odd, last), (odd, last + 1), (even, last - 1), (even, last))):
        for p in range(probes):
            for t in range(tiles):
                kept[n, p, t] = ref[z, p, t]
    mine = (low(HALO), last)
    steps.step(even, odd, (low(2), last + 1), mine)
    by_one, by_two = steps.after_tangent(odd, even, mine, at_low, True)
    result = steps.moved_sums(steps.images(odd, even, by_one, by_two, by_one, steps.empty_sums()))
    for p in range(probes):
        sums[p] = result[p]


def beyond_kernel(rows, folds, order, raw, next_bg, next_site, bg, site):
    chunks = bg.shape[0]
    tiles = chunks * folds
    near = bg.shape[1] // rows
    placed = interleave([flat(raw[:near])], [flat(raw[near:])], order)
    for x, scratch, to in zip(placed, (bg, site), (next_bg, next_site)):
        keep(x, scratch)
        for z in range(to.shape[0] // tiles):
            for t in range(tiles):
                r, k = t // chunks, t % chunks
                to[z * tiles + t] = scratch[k, tile_rows(z, r, rows, folds), :]


def outer_kernel(
    chunks, folds, edge, density, own_coef, own_src, own_wide, kept, own_sums, next_bg, next_site, packet, out,
    coef, src, even, odd,
):
    tiles = chunks * folds
    probes = own_wide.shape[0]
    total = even.shape[0] - 1
    planes = total - 2 * HALO
    steps = Steps(chunks, folds, probes, total, coef, src)
    last = planes - HALO
    halo = planes * tiles

    def copy(source, start, target, at, count):
        def body(n, carry):
            for t in range(tiles):
                target[at + n * tiles + t] = source[start + n * tiles + t]
            return carry

        lax.fori_loop(0, count, body, 0)

    own = (last - HALO) * tiles
    copy(own_src, own, src, own, planes - last + HALO)
    copy(own_coef, own, coef, own, planes - last + HALO)

    raw = next_site.shape[0]
    scale = packet[probes]

    def beyond_plane(n, carry):
        for t in range(tiles):
            at = n * tiles + t
            trap = trap_of(density, next_site[at]) * scale
            coef[halo + at] = weight_of(trap)
            src[halo + at] = source_of(trap, next_bg[at])
        return carry

    def packet_plane(n, carry):
        for t in range(tiles):
            at = n * tiles + t
            trap = packet[probes + 1 + tiles + at - raw]
            coef[halo + at] = weight_of(trap)
            src[halo + at] = source_of(trap, next_bg[at])
        return carry

    lax.fori_loop(0, raw // tiles, beyond_plane, 0)
    lax.fori_loop(raw // tiles, 2 * HALO - 1, packet_plane, 0)
    copy(packet, probes + 1, src, (total - 1) * tiles, 1)
    steps.clear(even, odd)
    for p in range(probes):
        for t in range(tiles):
            odd[last, p, t] = kept[0, p, t]
            odd[last + 1, p, t] = kept[1, p, t]
            even[last - 1, p, t] = kept[2, p, t]
            even[last, p, t] = kept[3, p, t]

    at_high = edge[1] != 0

    def high(z):
        return jnp.where(at_high, z, planes)

    mine = [own_wide[p] for p in range(probes)]
    beyond = [packet[p] for p in range(probes)]
    steps.first(mine, odd, "up", beyond)(planes - 1, 0)

    @pl.when(at_high)
    def _():
        steps.first(beyond, odd, "down", mine)(planes, 0)
        lax.fori_loop(planes + 1, total - 1, steps.first(beyond, odd), 0)

    steps.step(odd, even, (last, high(total - 1)), (last + 1, high(total - 2)))
    mine = (last, high(total - HALO))
    steps.step(even, odd, (last - 1, high(total - 2)), mine)
    by_one, by_two = steps.after_tangent(odd, even, mine, True, at_high)
    start, stop = by_one
    empty = steps.empty_sums()
    inside = steps.images(odd, even, by_one, by_two, (start, planes - 1), empty)
    inside = steps.images(odd, even, by_one, by_two, planes - 1, inside, "up")
    above = [list(c) for c in empty]
    for p in range(probes):
        above[p][0] = inside[p][5]
    above = steps.images(odd, even, by_one, by_two, (planes + 1, stop), tuple(tuple(c) for c in above))
    above = steps.images(odd, even, by_one, by_two, planes, above, "down")
    inside = [x + own_sums[p] + above[p][5] for p, x in enumerate(steps.moved_sums(inside))]
    above = steps.moved_sums(above)

    added = jnp.concatenate(inside + above, axis=0) * STEP**6
    images = cell_dot(added, cell_matrix(chunks, True))
    mask = own_cells(folds)
    for part in range(2):
        halves = []
        for p in range(probes):
            image = jnp.where(mask, images[8 * (part * probes + p) :][:8], 0.0)
            image = jnp.sum(image, axis=0, keepdims=True)
            halves += [image[:, h * LANES : (h + 1) * LANES] for h in range(image.shape[1] // LANES)]
        halves = jnp.concatenate(halves, axis=0)

        def send(n, carry):
            out[n, part] = halves
            return carry

        lax.fori_loop(0, out.shape[0], send, 0, unroll=8)


def eliminate(gram):
    count = gram.shape[0]
    rows = lax.broadcasted_iota(jnp.int32, (count, count), 0)
    columns = lax.broadcasted_iota(jnp.int32, (count, count), 1)
    inverse = jnp.where(rows == columns, 1.0, 0.0)
    for j in range(count - 1):
        across = jnp.broadcast_to(gram[:, j : j + 1], (count, count))
        turned = 1.0 / across
        ratio = jnp.where(rows > j, across, 0.0)
        gram_row, inverse_row = (gram * turned)[j : j + 1, :], (inverse * turned)[j : j + 1, :]
        gram = gram - ratio * gram_row
        inverse = inverse - ratio * inverse_row
    diagonal = jnp.sum(jnp.where(rows == columns, gram, 0.0), axis=1, keepdims=True)
    scale = 1.0 / jnp.sqrt(diagonal)
    upper = jnp.where(columns >= rows, gram, 0.0) * scale
    return upper, inverse * scale


def gram_of(parts, count):
    stacked = jnp.concatenate(list(parts) + [jnp.zeros_like(parts[0])], axis=0)
    stacked = stacked.astype(jnp.bfloat16)
    every = lax.dot_general(
        stacked, stacked, (((1,), (1,)), ((), ())), preferred_element_type=jnp.float32
    )
    tall = every[:count] + (every[count : 2 * count] + every[2 * count : 3 * count])
    return tall[:, :count] + (tall[:, count : 2 * count] + tall[:, 2 * count : 3 * count])


def times(a, parts):
    first, second, third = float_parts(a)
    left = jnp.concatenate([first, second, third, first, second, first], axis=1)
    right = jnp.concatenate([parts[0]] * 3 + [parts[1]] * 2 + [parts[2]], axis=0)
    return bf16_dot(left.astype(jnp.bfloat16), right.astype(jnp.bfloat16))


def factor_kernel(place, parts, q_out, lower_out, rows_ref, q_ref):
    groups, slabs, _, probes, cells = parts.shape
    count = groups * probes
    for g in range(groups):

        def gather(slab, carry):
            before = jnp.maximum(slab - 1, 0)
            image = parts[g, slab, 0] + jnp.where(slab > 0, parts[g, before, 1], 0.0)
            at = pl.multiple_of(slab * cells, cells)
            rows_ref[pl.ds(g * probes, probes), pl.ds(at, cells)] = image
            return carry

        lax.fori_loop(0, slabs, gather, 0, unroll=True if slabs <= 16 else 8)
    total = slabs * cells
    rows = rows_ref[...]
    parts_one = float_parts(rows)
    upper_one, inverse_one = eliminate(gram_of(parts_one, count) / total)
    basis = times(inverse_one, parts_one)
    rows_ref[...] = basis
    upper_two, inverse_two = eliminate(gram_of(float_parts(basis), count) / total)
    mine = rows_ref[:, pl.ds(pl.multiple_of(place[1] * cells, cells), cells)]
    q_ref[...] = dot_nn(inverse_two, mine)
    for g in range(groups):

        @pl.when(place[0] == g)
        def _():
            q_out[:, 0, :] = q_ref[pl.ds(g * probes, probes), :]

    r = lax.broadcasted_iota(jnp.int32, (count, count), 0)
    c = lax.broadcasted_iota(jnp.int32, (count, count), 1)
    lower_one = dot_nt(jnp.where(r == c, 1.0, 0.0), upper_one)
    lower_out[...] = dot_nt(lower_one, upper_two)


def everywhere(x):
    x = jnp.broadcast_to(jnp.sum(x, axis=1, keepdims=True), x.shape)
    for shift in (4, 2, 1):
        x = x + pltpu.roll(x, shift, 0)
    return x


def cholesky(rows, total):
    count = len(rows)
    rows = [list(row) for row in rows]
    gram = {}
    for i in range(count):
        for j in range(i + 1):
            product = sum(a * b for a, b in zip(rows[i][1:], rows[j][1:]))
            gram[i, j] = everywhere(rows[i][0] * rows[j][0] + product) * (1.0 / total)
    factor = {}
    for j in range(count):
        pivot = gram[j, j]
        turned = lax.rsqrt(pivot)
        turned = turned * (1.5 - 0.5 * pivot * turned * turned)
        factor[j, j] = pivot * turned
        rows[j] = [x * turned for x in rows[j]]
        for i in range(j + 1, count):
            factor[i, j] = gram[i, j] * turned
        for i in range(j + 1, count):
            for k in range(j + 1, i + 1):
                gram[i, k] = gram[i, k] - factor[i, j] * factor[k, j]
            rows[i] = [x - factor[i, j] * y for x, y in zip(rows[i], rows[j])]
    return factor, rows


def register_kernel(groups, slabs, probes, place, mine, other, q_out, lower_out, q_ref):
    halves = q_out.shape[2] // LANES
    pieces = probes * halves
    step = 2 * pieces
    sublane = lax.broadcasted_iota(jnp.int32, (8, LANES), 0)
    odd = jnp.broadcast_to(place[1] % 2, (8, LANES)) == 1

    def load(at):
        at = pl.ds(at, 8, stride=step)
        one, two = mine[at, :], other[at, :]
        return jnp.where(odd, two, one), jnp.where(odd, one, two)

    rows = []
    for g in range(groups):
        for p in range(probes):
            row = []
            for h in range(halves):
                last = None
                for block in range(slabs // 16):
                    at = (g * slabs // 2 + 8 * block) * step + p * halves + h
                    even_own, odd_own = load(at)
                    even_next, odd_next = load(at + pieces)
                    before = pltpu.roll(odd_next, 1, 0)
                    first = 0.0 if last is None else last
                    last = before
                    row.append((block, 0, h, even_own + jnp.where(sublane == 0, first, before)))
                    row.append((block, 1, h, odd_own + even_next))
            rows.append(row)
    places = [x[:3] for x in rows[0]]
    rows = [[x[3] for x in row] for row in rows]
    total = slabs * halves * LANES
    factor_one, basis = cholesky(rows, total)
    factor_two, rows = cholesky(basis, total)
    for i, row in enumerate(rows):
        for (block, parity, h), x in zip(places, row):
            q_ref[i, h, pl.ds(parity * (slabs // 2) + 8 * block, 8), :] = x
    own = (place[1] % 2) * (slabs // 2) + place[1] // 2
    for p in range(probes):
        for h in range(halves):
            mine = q_ref[place[0] * probes + p, h, pl.ds(own, 1), :]
            q_out[p, :, pl.ds(h * LANES, LANES)] = mine
    count = len(rows)
    r = lax.broadcasted_iota(jnp.int32, (8, LANES), 0)
    c = lax.broadcasted_iota(jnp.int32, (8, LANES), 1)
    lower = jnp.zeros((8, LANES), jnp.float32)
    for i in range(count):
        for j in range(i + 1):
            entry = sum(factor_one[i, k] * factor_two[k, j] for k in range(j, i + 1))
            lower = jnp.where((r == i) & (c == j), entry, lower)
    lower_out[...] = lower[:count, :count]


def shards(probe_dirs, log_param, background, site_class, trap_density):
    probes = probe_dirs.shape[0]
    cells = probe_dirs.shape[2]
    planes, rows, columns = background.shape
    slabs = lax.axis_size("space")
    groups = lax.axis_size("probe")
    at_space = lax.axis_index("space")
    vmem = pl.BlockSpec(memory_space=pltpu.VMEM)
    smem = pl.BlockSpec(memory_space=pltpu.SMEM)
    anywhere = pl.BlockSpec(memory_space=pl.ANY)
    params = pltpu.CompilerParams(vmem_limit_bytes=62 * 2**20)

    chunks, folds = columns // LANES, rows // 8
    tiles = chunks * folds
    total = planes + 2 * HALO
    tile = (8, LANES)

    def shape(*dims):
        return jax.ShapeDtypeStruct(dims + tile, jnp.float32)

    def scratch(*dims):
        return pltpu.VMEM(dims + tile, jnp.float32)

    def copies(count):
        return pltpu.SemaphoreType.DMA((count,))

    def inputs(held, sites):
        return [
            pltpu.VMEM((held, rows, columns), jnp.float32),
            pltpu.VMEM((sites, rows, columns), jnp.int32),
            pltpu.VMEM(log_param.shape, jnp.float32),
            pltpu.VMEM(probe_dirs.shape, jnp.float32),
            pltpu.VMEM((columns, columns), jnp.bfloat16),
        ]

    def rows_of(held):
        return pltpu.VMEM((chunks, held * rows, LANES), jnp.float32)

    down = [(i + 1, i) for i in range(slabs - 1)]
    near = 2 * HALO - 1
    raw = pl.pallas_call(
        raw_kernel,
        out_shape=jax.ShapeDtypeStruct((near + RAW_SITES, rows, columns), jnp.float32),
        in_specs=[anywhere] * 2,
        out_specs=anywhere,
        scratch_shapes=[
            pltpu.VMEM((RAW_SITES, rows, columns), jnp.int32),
            pltpu.VMEM((RAW_SITES, rows, columns), jnp.float32),
            copies(3),
        ],
        compiler_params=params,
        name="raw",
    )(background, site_class)
    raw = lax.ppermute(raw, "space", down)
    size = probes + 1 + (2 * HALO - RAW_SITES) * tiles
    packet = pl.pallas_call(
        packet_kernel,
        out_shape=shape(size),
        in_specs=[smem] + [anywhere] * 4,
        out_specs=anywhere,
        scratch_shapes=inputs(1, 2 * HALO - RAW_SITES)
        + [rows_of(1), rows_of(2 * HALO - RAW_SITES), scratch(size), copies(5)],
        compiler_params=params,
        name="packet",
    )(trap_density, background, site_class, log_param, probe_dirs)
    next_packet = lax.ppermute(packet, "space", down)
    edge = jnp.stack([at_space > 0, at_space < slabs - 1]).astype(jnp.int32)
    own_coef, own_src, wide, kept, sums, order = pl.pallas_call(
        inner_kernel,
        out_shape=(
            shape(planes * tiles),
            shape((planes + 1) * tiles),
            shape(probes),
            shape(4, probes, tiles),
            shape(probes),
            jax.ShapeDtypeStruct((columns, columns), jnp.bfloat16),
        ),
        in_specs=[smem, smem] + [anywhere] * 4,
        out_specs=(vmem,) * 6,
        scratch_shapes=inputs(planes, planes)[:4]
        + [rows_of(planes), rows_of(planes)]
        + [scratch(planes + 1, probes, tiles)] * 2
        + [copies(4)],
        compiler_params=pltpu.CompilerParams(vmem_limit_bytes=28 * 2**20),
        cost_estimate=pl.CostEstimate(flops=10**9, bytes_accessed=2**24, transcendentals=256),
        name="inner",
    )(edge, trap_density, background, site_class, log_param, probe_dirs)

    next_bg, next_site = pl.pallas_call(
        functools.partial(beyond_kernel, rows, folds),
        out_shape=(shape(near * tiles), shape(RAW_SITES * tiles)),
        in_specs=[vmem] * 2,
        out_specs=(vmem,) * 2,
        scratch_shapes=[rows_of(near), rows_of(RAW_SITES)],
        compiler_params=pltpu.CompilerParams(vmem_limit_bytes=28 * 2**20),
        name="beyond",
    )(order, raw)

    pieces = probes * cells // LANES
    images = pl.pallas_call(
        functools.partial(outer_kernel, chunks, folds),
        out_shape=jax.ShapeDtypeStruct((groups * slabs // 2, 2, pieces, LANES), jnp.float32),
        in_specs=[smem] * 2 + [vmem] * 8,
        out_specs=vmem,
        scratch_shapes=[
            scratch(total * tiles),
            scratch(total * tiles),
            scratch(total + 1, probes, tiles),
            scratch(total + 1, probes, tiles),
        ],
        compiler_params=pltpu.CompilerParams(vmem_limit_bytes=28 * 2**20),
        name="outer",
    )(edge, trap_density, own_coef, own_src, wide, kept, sums, next_bg, next_site, next_packet)

    same = [
        [g * slabs + z for g in range(groups) for z in range(parity, slabs, 2)] for parity in (0, 1)
    ]
    mine = lax.all_to_all(
        images, ("probe", "space"), split_axis=0, concat_axis=0, axis_index_groups=same, tiled=True
    )
    other = lax.ppermute(mine, "space", [(z, z ^ 1) for z in range(slabs)])
    place = jnp.stack([lax.axis_index("probe"), at_space]).astype(jnp.int32)
    count = groups * probes
    results = (
        jax.ShapeDtypeStruct((probes, 1, cells), jnp.float32),
        jax.ShapeDtypeStruct((count, count), jnp.float32),
    )
    params = pltpu.CompilerParams(vmem_limit_bytes=28 * 2**20)
    if count <= 8 and slabs % 16 == 0:
        halves = cells // LANES
        return pl.pallas_call(
            functools.partial(register_kernel, groups, slabs, probes),
            out_shape=results,
            in_specs=[smem, vmem, vmem],
            out_specs=(vmem, vmem),
            scratch_shapes=[pltpu.VMEM((count, halves, slabs, LANES), jnp.float32)],
            compiler_params=params,
            name="factor",
        )(
            place,
            mine.reshape((groups * slabs * pieces, LANES)),
            other.reshape((groups * slabs * pieces, LANES)),
        )
    odd = at_space % 2 == 1
    pairs = [jnp.where(odd, other, mine), jnp.where(odd, mine, other)]
    pairs = [x.reshape((groups, slabs // 2, 2, probes, cells)) for x in pairs]
    every = jnp.stack(pairs, axis=2).reshape((groups, slabs, 2, probes, cells))
    return pl.pallas_call(
        factor_kernel,
        out_shape=results,
        in_specs=[smem, vmem],
        out_specs=(vmem, vmem),
        scratch_shapes=[
            pltpu.VMEM((count, slabs * cells), jnp.float32),
            pltpu.VMEM((count, cells), jnp.float32),
        ],
        compiler_params=params,
        name="factor",
    )(place, every)


def solution(mesh):
    placed = (
        P("probe", "space", None),
        P("space", None),
        P("space", None, None),
        P("space", None, None),
        P(),
    )
    return jax.shard_map(
        shards,
        mesh=mesh,
        in_specs=placed,
        out_specs=(P("probe", "space", None), P()),
        check_vma=False,
    )
```

```python
import functools

import jax
import jax.numpy as jnp
from jax import lax
from jax.experimental import pallas as pl
from jax.experimental.pallas import tpu as pltpu
from jax.sharding import PartitionSpec as P

PX = 64
PY = 4
REF = 8
STEP = 0.12
HALO = 3
RAW_SITES = 3
LANES = 128
HIGHEST = lax.Precision.HIGHEST


def dot_nn(a, b):
    return lax.dot_general(
        a, b, (((1,), (0,)), ((), ())), precision=HIGHEST, preferred_element_type=jnp.float32
    )


def dot_nt(a, b):
    return lax.dot_general(
        a, b, (((1,), (1,)), ((), ())), precision=HIGHEST, preferred_element_type=jnp.float32
    )


def parts_of(x):
    first = x.astype(jnp.bfloat16)
    rest = x - first.astype(jnp.float32)
    second = rest.astype(jnp.bfloat16)
    third = (rest - second.astype(jnp.float32)).astype(jnp.bfloat16)
    return first, second, third


def bf16_dot(a, b):
    return jnp.dot(a, b, preferred_element_type=jnp.float32)


def interleave(exact, small, order):
    parts = [part for x in exact for part in parts_of(x)] + [x.astype(jnp.bfloat16) for x in small]
    placed = bf16_dot(jnp.concatenate(parts, axis=0), order[...])
    results, at = [], 0
    for x in exact:
        count = x.shape[0]
        first, second, third = [placed[at + n * count : at + (n + 1) * count] for n in range(3)]
        results.append((first + second) + third)
        at += 3 * count
    for x in small:
        results.append(placed[at : at + x.shape[0]])
        at += x.shape[0]
    return results


def keep(placed, kept):
    for k in range(kept.shape[0]):
        kept[k] = placed[:, k * LANES : (k + 1) * LANES]


def flat(planes):
    return planes.reshape((planes.shape[0] * planes.shape[1], planes.shape[2]))


def cell_matrix(chunks, turned=False):
    half = REF // chunks
    dims = (LANES, PX * PY) if turned else (PX * PY, LANES)
    cell = lax.broadcasted_iota(jnp.int32, dims, int(turned)) % PX
    lane = lax.broadcasted_iota(jnp.int32, dims, 1 - int(turned)) // half
    return jnp.where(cell == lane, 1.0, 0.0).astype(jnp.float32)


def own_cells(folds):
    half = REF // folds
    sublane = lax.broadcasted_iota(jnp.int32, (8, PX * PY), 0) // half
    return lax.broadcasted_iota(jnp.int32, (8, PX * PY), 1) // PX == sublane


def prolonged(coarse, folds, chunks):
    mask = own_cells(folds)
    rows = [jnp.where(mask, coarse[n : n + 1, :], 0.0) for n in range(coarse.shape[0])]
    return cell_dot(jnp.concatenate(rows, axis=0), cell_matrix(chunks))


def cell_dot(rows, matrix):
    count = rows.shape[0]
    parts = jnp.concatenate(float_parts(rows), axis=0).astype(jnp.bfloat16)
    placed = bf16_dot(parts, matrix.astype(jnp.bfloat16))
    return (placed[:count] + placed[count : 2 * count]) + placed[2 * count :]


def float_parts(x):
    first = x.astype(jnp.bfloat16).astype(jnp.float32)
    rest = x - first
    second = rest.astype(jnp.bfloat16).astype(jnp.float32)
    return first, second, rest - second


def cell_order(columns, chunks):
    x = lax.broadcasted_iota(jnp.int32, (columns, columns), 0)
    place = lax.broadcasted_iota(jnp.int32, (columns, columns), 1)
    wanted = chunks * (place % LANES) + place // LANES
    return jnp.where(x == wanted, 1.0, 0.0).astype(jnp.bfloat16)


def spread_cells(dirs, log_param, folds, chunks):
    probes = dirs.shape[0]
    coarse = [dirs[p] for p in range(probes)] + [jnp.exp(log_param[...])]
    spread = prolonged(jnp.concatenate(coarse, axis=0), folds, chunks)
    return [spread[8 * n : 8 * n + 8, :] for n in range(probes + 1)]


def tile_rows(z, r, rows, folds):
    return pl.ds(z * rows + r, 8, stride=folds)


def trap_of(density, kind):
    trap = jnp.full((8, LANES), density[density.shape[0] - 1])
    for n in range(density.shape[0] - 2, -1, -1):
        trap = jnp.where(kind == float(n), density[n], trap)
    return trap


def weight_of(trap):
    return (1.0 / STEP - 6.0) - trap


def source_of(trap, background):
    return -STEP * trap * background


def raw_kernel(background, sites, raw, held, made, sems):
    count = held.shape[0]
    near = raw.shape[0] - count
    fetch = pltpu.make_async_copy(sites.at[pl.ds(0, count)], held, sems.at[0])
    fetch.start()
    first = pl.ds(0, near)
    stage = pltpu.make_async_copy(background.at[first], made.at[first], sems.at[1])
    stage.start()
    stage.wait()
    ready = pltpu.make_async_copy(made.at[first], raw.at[first], sems.at[2])
    ready.start()
    fetch.wait()
    made[near:] = held[...].astype(jnp.float32)
    rest = pl.ds(near, count)
    sent = pltpu.make_async_copy(made.at[rest], raw.at[rest], sems.at[3])
    sent.start()
    ready.wait()
    sent.wait()


def packet_kernel(
    density, background_in, sites_in, log_param_in, dirs_in, packet,
    background, sites, log_param, dirs, order, bg, site, made, sems,
):
    count, rows, columns = sites.shape
    chunks, folds = columns // LANES, rows // 8
    tiles = chunks * folds
    probes = dirs.shape[0]
    pairs = [
        (log_param_in, log_param),
        (dirs_in, dirs),
        (background_in.at[pl.ds(2 * HALO - 1, 1)], background),
        (sites_in.at[pl.ds(2 * HALO - count, count)], sites),
    ]
    copies = [pltpu.make_async_copy(a, b, sems.at[n]) for n, (a, b) in enumerate(pairs)]
    for copy in copies:
        copy.start()
    order[...] = cell_order(columns, chunks)
    copies[0].wait()
    copies[1].wait()
    spread = spread_cells(dirs, log_param, folds, chunks)
    for p in range(probes + 1):
        made[p] = spread[p]
    copies[2].wait()
    copies[3].wait()
    placed = interleave([flat(background[...])], [flat(sites[...]).astype(jnp.float32)], order)
    keep(placed[0], bg)
    keep(placed[1], site)
    first = probes + 1 + tiles
    for z in range(count):
        for r in range(folds):
            for k in range(chunks):
                t = r * chunks + k
                trap = trap_of(density, site[k, tile_rows(z, r, rows, folds), :]) * spread[probes]
                if z < count - 1:
                    made[first + z * tiles + t] = trap
                else:
                    source = source_of(trap, bg[k, tile_rows(0, r, rows, folds), :])
                    made[probes + 1 + t] = source
    sent = pltpu.make_async_copy(made, packet, sems.at[4])
    sent.start()
    sent.wait()


class Steps:
    def __init__(self, chunks, folds, probes, zero_plane, coef, src):
        self.chunks, self.folds, self.tiles = chunks, folds, chunks * folds
        self.probes, self.zero_plane = probes, zero_plane
        self.coef, self.src = coef, src
        self.lane = lax.broadcasted_iota(jnp.int32, (8, LANES), 1)
        self.sublane = lax.broadcasted_iota(jnp.int32, (8, LANES), 0)

    def clear(self, *fields):
        nothing = jnp.zeros((8, LANES), jnp.float32)
        for t in range(self.tiles):
            for field in fields:
                for p in range(self.probes):
                    field[self.zero_plane, p, t] = nothing

    def from_left(self, x):
        return jnp.where(self.lane == 0, 0.0, pltpu.roll(x, 1, 1))

    def from_right(self, x):
        return jnp.where(self.lane == LANES - 1, 0.0, pltpu.roll(x, LANES - 1, 1))

    def from_before(self, x):
        return jnp.where(self.sublane == 0, 0.0, pltpu.roll(x, 1, 0))

    def from_after(self, x):
        return jnp.where(self.sublane == 7, 0.0, pltpu.roll(x, 7, 0))

    def first(self, own, to, other=None, beyond=()):
        chunks, folds, tiles = self.chunks, self.folds, self.tiles
        src, coef = self.src, self.coef
        turns = (self.from_left, self.from_right, self.from_before, self.from_after)
        shifted = [[f(x) for x in own] for f in turns]

        def body(z, carry):
            down = jnp.where(z > 0, z - 1, self.zero_plane) * tiles
            up = (z + 1) * tiles
            s = [[src[z * tiles + r * chunks + k] for k in range(chunks)] for r in range(folds)]
            for r in range(folds):
                for k in range(chunks):
                    t = r * chunks + k
                    same = coef[z * tiles + t] * s[r][k]
                    outer = []
                    for there, value, turn, kind in (
                        (k > 0, s[r][k - 1], (1, 1), 0),
                        (k + 1 < chunks, s[r][(k + 1) % chunks], (LANES - 1, 1), 1),
                        (r > 0, s[r - 1][k], (1, 0), 2),
                        (r + 1 < folds, s[(r + 1) % folds][k], (7, 0), 3),
                    ):
                        if there:
                            same = same + value
                        else:
                            outer.append((pltpu.roll(value, *turn), shifted[kind]))
                    for name, value in (("down", src[down + t]), ("up", src[up + t])):
                        if name == other:
                            outer.append((value, beyond))
                        else:
                            same = same + value
                    for p in range(self.probes):
                        result = same * own[p]
                        for value, factor in outer:
                            result = result + value * factor[p]
                        to[z, p, t] = result
            return carry

        return body

    def stencil(self, ref, valid, z, emit, extra):
        chunks, folds, tiles = self.chunks, self.folds, self.tiles
        first, stop = valid

        def at(z):
            return jnp.where((z >= first) & (z < stop), z, self.zero_plane)

        down, here, there, up = at(z - 1), at(z), at(z + 1), at(z + 2)
        for p in range(self.probes):
            pair = [[ref[plane, p, t] for t in range(tiles)] for plane in (here, there)]
            for r in range(folds):
                for k in range(chunks):
                    t = r * chunks + k
                    for n, value in enumerate(pair):
                        left = value[t - 1] if k else self.from_left(value[t + chunks - 1])
                        if k + 1 < chunks:
                            right = value[t + 1]
                        else:
                            right = self.from_right(value[t + 1 - chunks])
                        if r:
                            before = value[t - chunks]
                        else:
                            before = self.from_before(value[t + tiles - chunks])
                        if r + 1 < folds:
                            after = value[t + chunks]
                        else:
                            after = self.from_after(value[t + chunks - tiles])
                        above = pair[1 - n][t] + (ref[up, p, t] if n else ref[down, p, t])
                        weight = self.coef[(z + n) * tiles + t]
                        if extra:
                            weight = weight + extra
                        sides = (left + right) + (before + after)
                        emit(z + n, p, t, (sides + above) + weight * value[t])

    def step(self, ref, to, valid, wanted, extra=0.0):
        start, stop = wanted

        def body(n, carry):
            def emit(z, p, t, result):
                to[z, p, t] = result

            self.stencil(ref, valid, jnp.minimum(start + 2 * n, stop - 2), emit, extra)
            return carry

        lax.fori_loop(0, (stop - start + 1) // 2, body, 0)

    def widen(self, ref, to, valid, at_low, at_high):
        first, stop = valid

        def move(a, b):
            for p in range(self.probes):
                for t in range(self.tiles):
                    to[b, p, t] = ref[a, p, t]

        pl.when(at_low)(lambda: move(first, first - 1))
        pl.when(at_high)(lambda: move(stop - 1, stop))

    def images(self, m, u, by_one, by_two, span, carry, other=None):
        chunks, folds, tiles = self.chunks, self.folds, self.tiles
        src = self.src

        def at(z, valid):
            return jnp.where((z >= valid[0]) & (z < valid[1]), z, self.zero_plane)

        def body(z, carry):
            carry = [list(c) for c in carry]
            down = jnp.where(z > 0, z - 1, self.zero_plane) * tiles
            up = (z + 1) * tiles
            here, kept = at(z, by_one), at(z, by_two)
            s = [src[z * tiles + t] for t in range(tiles)]
            for t in range(tiles):
                r, k = t // chunks, t % chunks
                same = self.coef[z * tiles + t] * s[t]
                moved = []
                if k:
                    same = same + s[t - 1]
                else:
                    moved.append((2, self.from_left(s[t + chunks - 1])))
                if k + 1 < chunks:
                    same = same + s[t + 1]
                else:
                    moved.append((1, self.from_right(s[t + 1 - chunks])))
                if r:
                    same = same + s[t - chunks]
                else:
                    moved.append((4, self.from_before(s[t + tiles - chunks])))
                if r + 1 < folds:
                    same = same + s[t + chunks]
                else:
                    moved.append((3, self.from_after(s[t + chunks - tiles])))
                for name, value in (("down", src[down + t]), ("up", src[up + t])):
                    if name == other:
                        moved.append((5, value))
                    else:
                        same = same + value
                scaled = s[t] * (1.0 / STEP**2)
                for p in range(self.probes):
                    value = m[here, p, t]
                    carry[p][0] = carry[p][0] + (same * value + scaled * u[kept, p, t])
                    for n, factor in moved:
                        carry[p][n] = carry[p][n] + factor * value
            return tuple(tuple(c) for c in carry)

        if isinstance(span, int):
            return body(span, carry)
        return lax.fori_loop(*span, body, carry)

    def empty_sums(self):
        nothing = jnp.zeros((8, LANES), jnp.float32)
        return ((nothing,) * 6,) * self.probes

    def moved_sums(self, sums):
        return [
            c[0]
            + (self.from_left(c[1]) + self.from_right(c[2]))
            + (self.from_before(c[3]) + self.from_after(c[4]))
            for c in sums
        ]

    def after_tangent(self, odd, even, mine, at_low, at_high):
        first, stop = mine
        by_two = (jnp.where(at_low, first - 1, first), jnp.where(at_high, stop + 1, stop))
        by_one = (jnp.where(at_low, first - 2, first), jnp.where(at_high, stop + 2, stop))
        self.step(odd, even, mine, mine, 1.0 / STEP)
        self.widen(odd, even, mine, at_low, at_high)
        self.step(even, odd, by_two, by_two)
        self.widen(even, odd, by_two, at_low, at_high)
        return by_one, by_two


def inner_kernel(
    edge, density, background_in, sites_in, log_param_in, dirs_in,
    coef, src, wide, kept, sums, order,
    background, sites, log_param, dirs, bg, site, even, odd, sems,
):
    planes, rows, columns = background.shape
    chunks, folds = columns // LANES, rows // 8
    tiles = chunks * folds
    probes = dirs.shape[0]
    copies = [
        (log_param_in, log_param),
        (dirs_in, dirs),
        (background_in, background),
        (sites_in, sites),
    ]
    copies = [pltpu.make_async_copy(a, b, sems.at[n]) for n, (a, b) in enumerate(copies)]
    for copy in copies:
        copy.start()
    steps = Steps(chunks, folds, probes, planes, coef, src)
    steps.clear(even, odd)
    nothing = jnp.zeros((8, LANES), jnp.float32)
    for t in range(tiles):
        src[planes * tiles + t] = nothing
    order[...] = cell_order(columns, chunks)
    for copy in copies:
        copy.wait()
    spread = spread_cells(dirs, log_param, folds, chunks)
    for p in range(probes):
        wide[p] = spread[p]

    placed = interleave([flat(background[...])], [flat(sites[...]).astype(jnp.float32)], order)
    for x, scratch in zip(placed, (bg, site)):
        keep(x, scratch)
    for r in range(folds):
        for k in range(chunks):
            t = r * chunks + k
            for z in range(planes):
                at = tile_rows(z, r, rows, folds)
                trap = trap_of(density, site[k, at, :]) * spread[probes]
                coef[z * tiles + t] = weight_of(trap)
                src[z * tiles + t] = source_of(trap, bg[k, at, :])
    at_low = edge[0] != 0

    def low(z):
        return jnp.where(at_low, z, 0)

    last = planes - HALO
    lax.fori_loop(low(1), last + 2, steps.first(spread[:probes], odd), 0)
    steps.step(odd, even, (low(1), last + 2), (low(2), last + 1))
    for n, (ref, z) in enumerate(((odd, last), (odd, last + 1), (even, last - 1), (even, last))):
        for p in range(probes):
            for t in range(tiles):
                kept[n, p, t] = ref[z, p, t]
    mine = (low(HALO), last)
    steps.step(even, odd, (low(2), last + 1), mine)
    by_one, by_two = steps.after_tangent(odd, even, mine, at_low, True)
    result = steps.moved_sums(steps.images(odd, even, by_one, by_two, by_one, steps.empty_sums()))
    for p in range(probes):
        sums[p] = result[p]


def beyond_kernel(rows, folds, order, raw, next_bg, next_site, bg, site):
    chunks = bg.shape[0]
    tiles = chunks * folds
    near = bg.shape[1] // rows
    placed = interleave([flat(raw[:near])], [flat(raw[near:])], order)
    for x, scratch, to in zip(placed, (bg, site), (next_bg, next_site)):
        keep(x, scratch)
        for z in range(to.shape[0] // tiles):
            for t in range(tiles):
                r, k = t // chunks, t % chunks
                to[z * tiles + t] = scratch[k, tile_rows(z, r, rows, folds), :]


def outer_kernel(
    chunks, folds, edge, density, own_coef, own_src, own_wide, kept, own_sums, next_bg, next_site, packet, out,
    coef, src, even, odd,
):
    tiles = chunks * folds
    probes = own_wide.shape[0]
    total = even.shape[0] - 1
    planes = total - 2 * HALO
    steps = Steps(chunks, folds, probes, total, coef, src)
    last = planes - HALO
    halo = planes * tiles

    def copy(source, start, target, at, count):
        def body(n, carry):
            for t in range(tiles):
                target[at + n * tiles + t] = source[start + n * tiles + t]
            return carry

        lax.fori_loop(0, count, body, 0)

    own = (last - HALO) * tiles
    copy(own_src, own, src, own, planes - last + HALO)
    copy(own_coef, own, coef, own, planes - last + HALO)

    raw = next_site.shape[0]
    scale = packet[probes]

    def beyond_plane(n, carry):
        for t in range(tiles):
            at = n * tiles + t
            trap = trap_of(density, next_site[at]) * scale
            coef[halo + at] = weight_of(trap)
            src[halo + at] = source_of(trap, next_bg[at])
        return carry

    def packet_plane(n, carry):
        for t in range(tiles):
            at = n * tiles + t
            trap = packet[probes + 1 + tiles + at - raw]
            coef[halo + at] = weight_of(trap)
            src[halo + at] = source_of(trap, next_bg[at])
        return carry

    lax.fori_loop(0, raw // tiles, beyond_plane, 0)
    lax.fori_loop(raw // tiles, 2 * HALO - 1, packet_plane, 0)
    copy(packet, probes + 1, src, (total - 1) * tiles, 1)
    steps.clear(even, odd)
    for p in range(probes):
        for t in range(tiles):
            odd[last, p, t] = kept[0, p, t]
            odd[last + 1, p, t] = kept[1, p, t]
            even[last - 1, p, t] = kept[2, p, t]
            even[last, p, t] = kept[3, p, t]

    at_high = edge[1] != 0

    def high(z):
        return jnp.where(at_high, z, planes)

    mine = [own_wide[p] for p in range(probes)]
    beyond = [packet[p] for p in range(probes)]
    steps.first(mine, odd, "up", beyond)(planes - 1, 0)

    @pl.when(at_high)
    def _():
        steps.first(beyond, odd, "down", mine)(planes, 0)
        lax.fori_loop(planes + 1, total - 1, steps.first(beyond, odd), 0)

    steps.step(odd, even, (last, high(total - 1)), (last + 1, high(total - 2)))
    mine = (last, high(total - HALO))
    steps.step(even, odd, (last - 1, high(total - 2)), mine)
    by_one, by_two = steps.after_tangent(odd, even, mine, True, at_high)
    start, stop = by_one
    empty = steps.empty_sums()
    inside = steps.images(odd, even, by_one, by_two, (start, planes - 1), empty)
    inside = steps.images(odd, even, by_one, by_two, planes - 1, inside, "up")
    above = [list(c) for c in empty]
    for p in range(probes):
        above[p][0] = inside[p][5]
    above = steps.images(odd, even, by_one, by_two, (planes + 1, stop), tuple(tuple(c) for c in above))
    above = steps.images(odd, even, by_one, by_two, planes, above, "down")
    inside = [x + own_sums[p] + above[p][5] for p, x in enumerate(steps.moved_sums(inside))]
    above = steps.moved_sums(above)

    added = jnp.concatenate(inside + above, axis=0) * STEP**6
    images = cell_dot(added, cell_matrix(chunks, True))
    mask = own_cells(folds)
    for part in range(2):
        halves = []
        for p in range(probes):
            image = jnp.where(mask, images[8 * (part * probes + p) :][:8], 0.0)
            image = jnp.sum(image, axis=0, keepdims=True)
            halves += [image[:, h * LANES : (h + 1) * LANES] for h in range(image.shape[1] // LANES)]
        halves = jnp.concatenate(halves, axis=0)

        def send(n, carry):
            out[n, part] = halves
            return carry

        lax.fori_loop(0, out.shape[0], send, 0, unroll=8)


def eliminate(gram):
    count = gram.shape[0]
    rows = lax.broadcasted_iota(jnp.int32, (count, count), 0)
    columns = lax.broadcasted_iota(jnp.int32, (count, count), 1)
    inverse = jnp.where(rows == columns, 1.0, 0.0)
    for j in range(count - 1):
        across = jnp.broadcast_to(gram[:, j : j + 1], (count, count))
        turned = 1.0 / across
        ratio = jnp.where(rows > j, across, 0.0)
        gram_row, inverse_row = (gram * turned)[j : j + 1, :], (inverse * turned)[j : j + 1, :]
        gram = gram - ratio * gram_row
        inverse = inverse - ratio * inverse_row
    diagonal = jnp.sum(jnp.where(rows == columns, gram, 0.0), axis=1, keepdims=True)
    scale = 1.0 / jnp.sqrt(diagonal)
    upper = jnp.where(columns >= rows, gram, 0.0) * scale
    return upper, inverse * scale


def gram_of(parts, count):
    stacked = jnp.concatenate(list(parts) + [jnp.zeros_like(parts[0])], axis=0)
    stacked = stacked.astype(jnp.bfloat16)
    every = lax.dot_general(
        stacked, stacked, (((1,), (1,)), ((), ())), preferred_element_type=jnp.float32
    )
    tall = every[:count] + (every[count : 2 * count] + every[2 * count : 3 * count])
    return tall[:, :count] + (tall[:, count : 2 * count] + tall[:, 2 * count : 3 * count])


def times(a, parts):
    first, second, third = float_parts(a)
    left = jnp.concatenate([first, second, third, first, second, first], axis=1)
    right = jnp.concatenate([parts[0]] * 3 + [parts[1]] * 2 + [parts[2]], axis=0)
    return bf16_dot(left.astype(jnp.bfloat16), right.astype(jnp.bfloat16))


def factor_kernel(place, parts, q_out, lower_out, rows_ref, q_ref):
    groups, slabs, _, probes, cells = parts.shape
    count = groups * probes
    for g in range(groups):

        def gather(slab, carry):
            before = jnp.maximum(slab - 1, 0)
            image = parts[g, slab, 0] + jnp.where(slab > 0, parts[g, before, 1], 0.0)
            at = pl.multiple_of(slab * cells, cells)
            rows_ref[pl.ds(g * probes, probes), pl.ds(at, cells)] = image
            return carry

        lax.fori_loop(0, slabs, gather, 0, unroll=True if slabs <= 16 else 8)
    total = slabs * cells
    rows = rows_ref[...]
    parts_one = float_parts(rows)
    upper_one, inverse_one = eliminate(gram_of(parts_one, count) / total)
    basis = times(inverse_one, parts_one)
    rows_ref[...] = basis
    upper_two, inverse_two = eliminate(gram_of(float_parts(basis), count) / total)
    mine = rows_ref[:, pl.ds(pl.multiple_of(place[1] * cells, cells), cells)]
    q_ref[...] = dot_nn(inverse_two, mine)
    for g in range(groups):

        @pl.when(place[0] == g)
        def _():
            q_out[:, 0, :] = q_ref[pl.ds(g * probes, probes), :]

    r = lax.broadcasted_iota(jnp.int32, (count, count), 0)
    c = lax.broadcasted_iota(jnp.int32, (count, count), 1)
    lower_one = dot_nt(jnp.where(r == c, 1.0, 0.0), upper_one)
    lower_out[...] = dot_nt(lower_one, upper_two)


def everywhere(x):
    x = jnp.broadcast_to(jnp.sum(x, axis=1, keepdims=True), x.shape)
    for shift in (4, 2, 1):
        x = x + pltpu.roll(x, shift, 0)
    return x


def cholesky(rows, total):
    count = len(rows)
    rows = [list(row) for row in rows]
    gram = {}
    for i in range(count):
        for j in range(i + 1):
            product = sum(a * b for a, b in zip(rows[i][1:], rows[j][1:]))
            gram[i, j] = everywhere(rows[i][0] * rows[j][0] + product) * (1.0 / total)
    factor = {}
    for j in range(count):
        pivot = gram[j, j]
        turned = lax.rsqrt(pivot)
        turned = turned * (1.5 - 0.5 * pivot * turned * turned)
        factor[j, j] = pivot * turned
        rows[j] = [x * turned for x in rows[j]]
        for i in range(j + 1, count):
            factor[i, j] = gram[i, j] * turned
        for i in range(j + 1, count):
            for k in range(j + 1, i + 1):
                gram[i, k] = gram[i, k] - factor[i, j] * factor[k, j]
            rows[i] = [x - factor[i, j] * y for x, y in zip(rows[i], rows[j])]
    return factor, rows


def register_kernel(groups, slabs, probes, place, mine, other, q_out, lower_out, q_ref):
    halves = q_out.shape[2] // LANES
    pieces = probes * halves
    step = 2 * pieces
    sublane = lax.broadcasted_iota(jnp.int32, (8, LANES), 0)
    odd = jnp.broadcast_to(place[1] % 2, (8, LANES)) == 1

    def load(at):
        at = pl.ds(at, 8, stride=step)
        one, two = mine[at, :], other[at, :]
        return jnp.where(odd, two, one), jnp.where(odd, one, two)

    rows = []
    for g in range(groups):
        for p in range(probes):
            row = []
            for h in range(halves):
                last = None
                for block in range(slabs // 16):
                    at = (g * slabs // 2 + 8 * block) * step + p * halves + h
                    even_own, odd_own = load(at)
                    even_next, odd_next = load(at + pieces)
                    before = pltpu.roll(odd_next, 1, 0)
                    first = 0.0 if last is None else last
                    last = before
                    row.append((block, 0, h, even_own + jnp.where(sublane == 0, first, before)))
                    row.append((block, 1, h, odd_own + even_next))
            rows.append(row)
    places = [x[:3] for x in rows[0]]
    rows = [[x[3] for x in row] for row in rows]
    total = slabs * halves * LANES
    factor_one, basis = cholesky(rows, total)
    factor_two, rows = cholesky(basis, total)
    for i, row in enumerate(rows):
        for (block, parity, h), x in zip(places, row):
            q_ref[i, h, pl.ds(parity * (slabs // 2) + 8 * block, 8), :] = x
    own = (place[1] % 2) * (slabs // 2) + place[1] // 2
    for p in range(probes):
        for h in range(halves):
            mine = q_ref[place[0] * probes + p, h, pl.ds(own, 1), :]
            q_out[p, :, pl.ds(h * LANES, LANES)] = mine
    count = len(rows)
    r = lax.broadcasted_iota(jnp.int32, (8, LANES), 0)
    c = lax.broadcasted_iota(jnp.int32, (8, LANES), 1)
    lower = jnp.zeros((8, LANES), jnp.float32)
    for i in range(count):
        for j in range(i + 1):
            entry = sum(factor_one[i, k] * factor_two[k, j] for k in range(j, i + 1))
            lower = jnp.where((r == i) & (c == j), entry, lower)
    lower_out[...] = lower[:count, :count]


def shards(probe_dirs, log_param, background, site_class, trap_density):
    probes = probe_dirs.shape[0]
    cells = probe_dirs.shape[2]
    planes, rows, columns = background.shape
    slabs = lax.axis_size("space")
    groups = lax.axis_size("probe")
    at_space = lax.axis_index("space")
    vmem = pl.BlockSpec(memory_space=pltpu.VMEM)
    smem = pl.BlockSpec(memory_space=pltpu.SMEM)
    anywhere = pl.BlockSpec(memory_space=pl.ANY)
    params = pltpu.CompilerParams(vmem_limit_bytes=62 * 2**20)

    chunks, folds = columns // LANES, rows // 8
    tiles = chunks * folds
    total = planes + 2 * HALO
    tile = (8, LANES)

    def shape(*dims):
        return jax.ShapeDtypeStruct(dims + tile, jnp.float32)

    def scratch(*dims):
        return pltpu.VMEM(dims + tile, jnp.float32)

    def copies(count):
        return pltpu.SemaphoreType.DMA((count,))

    def inputs(held, sites):
        return [
            pltpu.VMEM((held, rows, columns), jnp.float32),
            pltpu.VMEM((sites, rows, columns), jnp.int32),
            pltpu.VMEM(log_param.shape, jnp.float32),
            pltpu.VMEM(probe_dirs.shape, jnp.float32),
            pltpu.VMEM((columns, columns), jnp.bfloat16),
        ]

    def rows_of(held):
        return pltpu.VMEM((chunks, held * rows, LANES), jnp.float32)

    down = [(i + 1, i) for i in range(slabs - 1)]
    near = 2 * HALO - 1
    raw = pl.pallas_call(
        raw_kernel,
        out_shape=jax.ShapeDtypeStruct((near + RAW_SITES, rows, columns), jnp.float32),
        in_specs=[anywhere] * 2,
        out_specs=anywhere,
        scratch_shapes=[
            pltpu.VMEM((RAW_SITES, rows, columns), jnp.int32),
            pltpu.VMEM((near + RAW_SITES, rows, columns), jnp.float32),
            copies(4),
        ],
        compiler_params=params,
        name="raw",
    )(background, site_class)
    raw = lax.ppermute(raw, "space", down)
    size = probes + 1 + (2 * HALO - RAW_SITES) * tiles
    packet = pl.pallas_call(
        packet_kernel,
        out_shape=shape(size),
        in_specs=[smem] + [anywhere] * 4,
        out_specs=anywhere,
        scratch_shapes=inputs(1, 2 * HALO - RAW_SITES)
        + [rows_of(1), rows_of(2 * HALO - RAW_SITES), scratch(size), copies(5)],
        compiler_params=params,
        name="packet",
    )(trap_density, background, site_class, log_param, probe_dirs)
    next_packet = lax.ppermute(packet, "space", down)
    edge = jnp.stack([at_space > 0, at_space < slabs - 1]).astype(jnp.int32)
    own_coef, own_src, wide, kept, sums, order = pl.pallas_call(
        inner_kernel,
        out_shape=(
            shape(planes * tiles),
            shape((planes + 1) * tiles),
            shape(probes),
            shape(4, probes, tiles),
            shape(probes),
            jax.ShapeDtypeStruct((columns, columns), jnp.bfloat16),
        ),
        in_specs=[smem, smem] + [anywhere] * 4,
        out_specs=(vmem,) * 6,
        scratch_shapes=inputs(planes, planes)[:4]
        + [rows_of(planes), rows_of(planes)]
        + [scratch(planes + 1, probes, tiles)] * 2
        + [copies(4)],
        compiler_params=pltpu.CompilerParams(vmem_limit_bytes=28 * 2**20),
        cost_estimate=pl.CostEstimate(flops=10**9, bytes_accessed=2**24, transcendentals=256),
        name="inner",
    )(edge, trap_density, background, site_class, log_param, probe_dirs)

    next_bg, next_site = pl.pallas_call(
        functools.partial(beyond_kernel, rows, folds),
        out_shape=(shape(near * tiles), shape(RAW_SITES * tiles)),
        in_specs=[vmem] * 2,
        out_specs=(vmem,) * 2,
        scratch_shapes=[rows_of(near), rows_of(RAW_SITES)],
        compiler_params=pltpu.CompilerParams(vmem_limit_bytes=28 * 2**20),
        name="beyond",
    )(order, raw)

    pieces = probes * cells // LANES
    images = pl.pallas_call(
        functools.partial(outer_kernel, chunks, folds),
        out_shape=jax.ShapeDtypeStruct((groups * slabs // 2, 2, pieces, LANES), jnp.float32),
        in_specs=[smem] * 2 + [vmem] * 8,
        out_specs=vmem,
        scratch_shapes=[
            scratch(total * tiles),
            scratch(total * tiles),
            scratch(total + 1, probes, tiles),
            scratch(total + 1, probes, tiles),
        ],
        compiler_params=pltpu.CompilerParams(vmem_limit_bytes=28 * 2**20),
        name="outer",
    )(edge, trap_density, own_coef, own_src, wide, kept, sums, next_bg, next_site, next_packet)

    same = [
        [g * slabs + z for g in range(groups) for z in range(parity, slabs, 2)] for parity in (0, 1)
    ]
    mine = lax.all_to_all(
        images, ("probe", "space"), split_axis=0, concat_axis=0, axis_index_groups=same, tiled=True
    )
    other = lax.ppermute(mine, "space", [(z, z ^ 1) for z in range(slabs)])
    place = jnp.stack([lax.axis_index("probe"), at_space]).astype(jnp.int32)
    count = groups * probes
    results = (
        jax.ShapeDtypeStruct((probes, 1, cells), jnp.float32),
        jax.ShapeDtypeStruct((count, count), jnp.float32),
    )
    params = pltpu.CompilerParams(vmem_limit_bytes=28 * 2**20)
    if count <= 8 and slabs % 16 == 0:
        halves = cells // LANES
        return pl.pallas_call(
            functools.partial(register_kernel, groups, slabs, probes),
            out_shape=results,
            in_specs=[smem, vmem, vmem],
            out_specs=(vmem, vmem),
            scratch_shapes=[pltpu.VMEM((count, halves, slabs, LANES), jnp.float32)],
            compiler_params=params,
            name="factor",
        )(
            place,
            mine.reshape((groups * slabs * pieces, LANES)),
            other.reshape((groups * slabs * pieces, LANES)),
        )
    odd = at_space % 2 == 1
    pairs = [jnp.where(odd, other, mine), jnp.where(odd, mine, other)]
    pairs = [x.reshape((groups, slabs // 2, 2, probes, cells)) for x in pairs]
    every = jnp.stack(pairs, axis=2).reshape((groups, slabs, 2, probes, cells))
    return pl.pallas_call(
        factor_kernel,
        out_shape=results,
        in_specs=[smem, vmem],
        out_specs=(vmem, vmem),
        scratch_shapes=[
            pltpu.VMEM((count, slabs * cells), jnp.float32),
            pltpu.VMEM((count, cells), jnp.float32),
        ],
        compiler_params=params,
        name="factor",
    )(place, every)


def solution(mesh):
    placed = (
        P("probe", "space", None),
        P("space", None),
        P("space", None, None),
        P("space", None, None),
        P(),
    )
    return jax.shard_map(
        shards,
        mesh=mesh,
        in_specs=placed,
        out_specs=(P("probe", "space", None), P()),
        check_vma=False,
    )
```

```python
import functools

import jax
import jax.numpy as jnp
from jax import lax
from jax.experimental import pallas as pl
from jax.experimental.pallas import tpu as pltpu
from jax.sharding import PartitionSpec as P

PX = 64
PY = 4
REF = 8
STEP = 0.12
HALO = 3
LANES = 128
HIGHEST = lax.Precision.HIGHEST


def dot_nn(a, b):
    return lax.dot_general(
        a, b, (((1,), (0,)), ((), ())), precision=HIGHEST, preferred_element_type=jnp.float32
    )


def dot_nt(a, b):
    return lax.dot_general(
        a, b, (((1,), (1,)), ((), ())), precision=HIGHEST, preferred_element_type=jnp.float32
    )


def parts_of(x):
    first = x.astype(jnp.bfloat16)
    rest = x - first.astype(jnp.float32)
    second = rest.astype(jnp.bfloat16)
    third = (rest - second.astype(jnp.float32)).astype(jnp.bfloat16)
    return first, second, third


def bf16_dot(a, b):
    return jnp.dot(a, b, preferred_element_type=jnp.float32)


def interleave(exact, small, order):
    parts = [part for x in exact for part in parts_of(x)] + [x.astype(jnp.bfloat16) for x in small]
    placed = bf16_dot(jnp.concatenate(parts, axis=0), order[...])
    results, at = [], 0
    for x in exact:
        count = x.shape[0]
        first, second, third = [placed[at + n * count : at + (n + 1) * count] for n in range(3)]
        results.append((first + second) + third)
        at += 3 * count
    for x in small:
        results.append(placed[at : at + x.shape[0]])
        at += x.shape[0]
    return results


def keep(placed, kept):
    for k in range(kept.shape[0]):
        kept[k] = placed[:, k * LANES : (k + 1) * LANES]


def flat(planes):
    return planes.reshape((planes.shape[0] * planes.shape[1], planes.shape[2]))


def cell_matrix(chunks, turned=False):
    half = REF // chunks
    dims = (LANES, PX * PY) if turned else (PX * PY, LANES)
    cell = lax.broadcasted_iota(jnp.int32, dims, int(turned)) % PX
    lane = lax.broadcasted_iota(jnp.int32, dims, 1 - int(turned)) // half
    return jnp.where(cell == lane, 1.0, 0.0).astype(jnp.float32)


def own_cells(folds):
    half = REF // folds
    sublane = lax.broadcasted_iota(jnp.int32, (8, PX * PY), 0) // half
    return lax.broadcasted_iota(jnp.int32, (8, PX * PY), 1) // PX == sublane


def prolonged(coarse, folds, chunks):
    mask = own_cells(folds)
    rows = [jnp.where(mask, coarse[n : n + 1, :], 0.0) for n in range(coarse.shape[0])]
    return cell_dot(jnp.concatenate(rows, axis=0), cell_matrix(chunks))


def cell_dot(rows, matrix):
    count = rows.shape[0]
    parts = jnp.concatenate(float_parts(rows), axis=0).astype(jnp.bfloat16)
    placed = bf16_dot(parts, matrix.astype(jnp.bfloat16))
    return (placed[:count] + placed[count : 2 * count]) + placed[2 * count :]


def float_parts(x):
    first = x.astype(jnp.bfloat16).astype(jnp.float32)
    rest = x - first
    second = rest.astype(jnp.bfloat16).astype(jnp.float32)
    return first, second, rest - second


def cell_order(columns, chunks):
    x = lax.broadcasted_iota(jnp.int32, (columns, columns), 0)
    place = lax.broadcasted_iota(jnp.int32, (columns, columns), 1)
    wanted = chunks * (place % LANES) + place // LANES
    return jnp.where(x == wanted, 1.0, 0.0).astype(jnp.bfloat16)


def spread_cells(dirs, log_param, folds, chunks):
    probes = dirs.shape[0]
    coarse = [dirs[p] for p in range(probes)] + [jnp.exp(log_param[...])]
    spread = prolonged(jnp.concatenate(coarse, axis=0), folds, chunks)
    return [spread[8 * n : 8 * n + 8, :] for n in range(probes + 1)]


def tile_rows(z, r, rows, folds):
    return pl.ds(z * rows + r, 8, stride=folds)


def trap_of(density, kind):
    trap = jnp.full((8, LANES), density[density.shape[0] - 1])
    for n in range(density.shape[0] - 2, -1, -1):
        trap = jnp.where(kind == float(n), density[n], trap)
    return trap


def weight_of(trap):
    return (1.0 / STEP - 6.0) - trap


def source_of(trap, background):
    return -STEP * trap * background


def packet_kernel(
    density, background_in, sites_in, log_param_in, dirs_in, packet,
    background, sites, log_param, dirs, order, bg, site, made, sems, out_sems,
):
    count, rows, columns = sites.shape
    chunks, folds = columns // LANES, rows // 8
    tiles = chunks * folds
    probes = dirs.shape[0]
    pairs = [
        (log_param_in, log_param),
        (dirs_in, dirs),
        (background_in.at[pl.ds(count - 1, 1)], background),
        (sites_in.at[pl.ds(0, count)], sites),
    ]
    copies = [pltpu.make_async_copy(a, b, sems.at[n]) for n, (a, b) in enumerate(pairs)]
    for copy in copies:
        copy.start()
    order[...] = cell_order(columns, chunks)
    copies[0].wait()
    copies[1].wait()
    spread = spread_cells(dirs, log_param, folds, chunks)
    for p in range(probes):
        made[p] = spread[p]
    copies[2].wait()
    copies[3].wait()
    placed = interleave([flat(background[...])], [flat(sites[...]).astype(jnp.float32)], order)
    keep(placed[0], bg)
    keep(placed[1], site)
    sent = []

    def send(start, stop):
        at = pl.ds(start, stop - start)
        copy = pltpu.make_async_copy(made.at[at], packet.at[at], out_sems.at[len(sent)])
        copy.start()
        sent.append(copy)

    first = probes + tiles
    middle = first + (count - 1) // 2 * tiles
    for z in range(count):
        for r in range(folds):
            for k in range(chunks):
                t = r * chunks + k
                trap = trap_of(density, site[k, tile_rows(z, r, rows, folds), :]) * spread[probes]
                if z < count - 1:
                    made[first + z * tiles + t] = trap
                else:
                    made[probes + t] = source_of(trap, bg[k, tile_rows(0, r, rows, folds), :])
        if z == (count - 1) // 2 - 1:
            send(first, middle)
        elif z == count - 2:
            send(middle, first + (count - 1) * tiles)
    send(0, first)
    for copy in sent:
        copy.wait()


class Steps:
    def __init__(self, chunks, folds, probes, zero_plane, coef, src):
        self.chunks, self.folds, self.tiles = chunks, folds, chunks * folds
        self.probes, self.zero_plane = probes, zero_plane
        self.coef, self.src = coef, src
        self.lane = lax.broadcasted_iota(jnp.int32, (8, LANES), 1)
        self.sublane = lax.broadcasted_iota(jnp.int32, (8, LANES), 0)

    def clear(self, *fields):
        nothing = jnp.zeros((8, LANES), jnp.float32)
        for t in range(self.tiles):
            for field in fields:
                for p in range(self.probes):
                    field[self.zero_plane, p, t] = nothing

    def from_left(self, x):
        return jnp.where(self.lane == 0, 0.0, pltpu.roll(x, 1, 1))

    def from_right(self, x):
        return jnp.where(self.lane == LANES - 1, 0.0, pltpu.roll(x, LANES - 1, 1))

    def from_before(self, x):
        return jnp.where(self.sublane == 0, 0.0, pltpu.roll(x, 1, 0))

    def from_after(self, x):
        return jnp.where(self.sublane == 7, 0.0, pltpu.roll(x, 7, 0))

    def first(self, own, to, other=None, beyond=()):
        chunks, folds, tiles = self.chunks, self.folds, self.tiles
        src, coef = self.src, self.coef
        turns = (self.from_left, self.from_right, self.from_before, self.from_after)
        shifted = [[f(x) for x in own] for f in turns]

        def body(z, carry):
            down = jnp.where(z > 0, z - 1, self.zero_plane) * tiles
            up = (z + 1) * tiles
            s = [[src[z * tiles + r * chunks + k] for k in range(chunks)] for r in range(folds)]
            for r in range(folds):
                for k in range(chunks):
                    t = r * chunks + k
                    same = coef[z * tiles + t] * s[r][k]
                    outer = []
                    for there, value, turn, kind in (
                        (k > 0, s[r][k - 1], (1, 1), 0),
                        (k + 1 < chunks, s[r][(k + 1) % chunks], (LANES - 1, 1), 1),
                        (r > 0, s[r - 1][k], (1, 0), 2),
                        (r + 1 < folds, s[(r + 1) % folds][k], (7, 0), 3),
                    ):
                        if there:
                            same = same + value
                        else:
                            outer.append((pltpu.roll(value, *turn), shifted[kind]))
                    for name, value in (("down", src[down + t]), ("up", src[up + t])):
                        if name == other:
                            outer.append((value, beyond))
                        else:
                            same = same + value
                    for p in range(self.probes):
                        result = same * own[p]
                        for value, factor in outer:
                            result = result + value * factor[p]
                        to[z, p, t] = result
            return carry

        return body

    def stencil(self, ref, valid, z, emit, extra):
        chunks, folds, tiles = self.chunks, self.folds, self.tiles
        first, stop = valid

        def at(z):
            return jnp.where((z >= first) & (z < stop), z, self.zero_plane)

        down, here, there, up = at(z - 1), at(z), at(z + 1), at(z + 2)
        for p in range(self.probes):
            pair = [[ref[plane, p, t] for t in range(tiles)] for plane in (here, there)]
            for n, value in enumerate(pair):
                shared = self.corners(value)
                for r in range(folds):
                    for k in range(chunks):
                        t = r * chunks + k
                        above = pair[1 - n][t] + (ref[up, p, t] if n else ref[down, p, t])
                        weight = self.coef[(z + n) * tiles + t]
                        if extra:
                            weight = weight + extra
                        sides = shared[r, k] + shared[r + 1, k + 1]
                        emit(z + n, p, t, (sides + above) + weight * value[t])

    def corners(self, value):
        chunks, folds = self.chunks, self.folds

        def at(r, k):
            if r < 0:
                return self.from_before(value[(folds - 1) * chunks + k])
            if r == folds:
                return self.from_after(value[k])
            if k < 0:
                return self.from_left(value[r * chunks + chunks - 1])
            if k == chunks:
                return self.from_right(value[r * chunks])
            return value[r * chunks + k]

        ends = ((folds, 0), (0, chunks))
        return {
            (r, k): at(r - 1, k) + at(r, k - 1)
            for r in range(folds + 1)
            for k in range(chunks + 1)
            if (r, k) not in ends
        }

    def step(self, ref, to, valid, wanted, extra=0.0):
        start, stop = wanted

        def body(n, carry):
            def emit(z, p, t, result):
                to[z, p, t] = result

            self.stencil(ref, valid, jnp.minimum(start + 2 * n, stop - 2), emit, extra)
            return carry

        lax.fori_loop(0, (stop - start + 1) // 2, body, 0)

    def widen(self, ref, to, valid, at_low, at_high):
        first, stop = valid

        def move(a, b):
            for p in range(self.probes):
                for t in range(self.tiles):
                    to[b, p, t] = ref[a, p, t]

        pl.when(at_low)(lambda: move(first, first - 1))
        pl.when(at_high)(lambda: move(stop - 1, stop))

    def images(self, m, u, by_one, by_two, span, carry, other=None):
        chunks, folds, tiles = self.chunks, self.folds, self.tiles
        src = self.src

        def at(z, valid):
            return jnp.where((z >= valid[0]) & (z < valid[1]), z, self.zero_plane)

        def body(z, carry):
            carry = [list(c) for c in carry]
            down = jnp.where(z > 0, z - 1, self.zero_plane) * tiles
            up = (z + 1) * tiles
            here, kept = at(z, by_one), at(z, by_two)
            s = [src[z * tiles + t] for t in range(tiles)]
            for t in range(tiles):
                r, k = t // chunks, t % chunks
                same = self.coef[z * tiles + t] * s[t]
                moved = []
                if k:
                    same = same + s[t - 1]
                else:
                    moved.append((2, self.from_left(s[t + chunks - 1])))
                if k + 1 < chunks:
                    same = same + s[t + 1]
                else:
                    moved.append((1, self.from_right(s[t + 1 - chunks])))
                if r:
                    same = same + s[t - chunks]
                else:
                    moved.append((4, self.from_before(s[t + tiles - chunks])))
                if r + 1 < folds:
                    same = same + s[t + chunks]
                else:
                    moved.append((3, self.from_after(s[t + chunks - tiles])))
                for name, value in (("down", src[down + t]), ("up", src[up + t])):
                    if name == other:
                        moved.append((5, value))
                    else:
                        same = same + value
                scaled = s[t] * (1.0 / STEP**2)
                for p in range(self.probes):
                    value = m[here, p, t]
                    carry[p][0] = carry[p][0] + (same * value + scaled * u[kept, p, t])
                    for n, factor in moved:
                        carry[p][n] = carry[p][n] + factor * value
            return tuple(tuple(c) for c in carry)

        if isinstance(span, int):
            return body(span, carry)
        return lax.fori_loop(*span, body, carry)

    def empty_sums(self):
        nothing = jnp.zeros((8, LANES), jnp.float32)
        return ((nothing,) * 6,) * self.probes

    def moved_sums(self, sums):
        return [
            c[0]
            + (self.from_left(c[1]) + self.from_right(c[2]))
            + (self.from_before(c[3]) + self.from_after(c[4]))
            for c in sums
        ]

    def after_tangent(self, odd, even, mine, at_low, at_high):
        first, stop = mine
        by_two = (jnp.where(at_low, first - 1, first), jnp.where(at_high, stop + 1, stop))
        by_one = (jnp.where(at_low, first - 2, first), jnp.where(at_high, stop + 2, stop))
        self.step(odd, even, mine, mine, 1.0 / STEP)
        self.widen(odd, even, mine, at_low, at_high)
        self.step(even, odd, by_two, by_two)
        self.widen(even, odd, by_two, at_low, at_high)
        return by_one, by_two


def inner_kernel(
    edge, density, background_in, sites_in, log_param_in, dirs_in, beyond,
    coef, src, wide, kept, sums, next_bg,
    background, sites, log_param, dirs, order, bg, far, site, even, odd, sems,
):
    planes, rows, columns = background.shape
    chunks, folds = columns // LANES, rows // 8
    tiles = chunks * folds
    probes = dirs.shape[0]
    copies = [
        (log_param_in, log_param),
        (dirs_in, dirs),
        (background_in, background),
        (sites_in, sites),
    ]
    copies = [pltpu.make_async_copy(a, b, sems.at[n]) for n, (a, b) in enumerate(copies)]
    for copy in copies:
        copy.start()
    steps = Steps(chunks, folds, probes, planes, coef, src)
    steps.clear(even, odd)
    nothing = jnp.zeros((8, LANES), jnp.float32)
    for t in range(tiles):
        src[planes * tiles + t] = nothing
    order[...] = cell_order(columns, chunks)
    for copy in copies:
        copy.wait()
    spread = spread_cells(dirs, log_param, folds, chunks)
    for p in range(probes):
        wide[p] = spread[p]

    placed = interleave(
        [flat(background[...]), flat(beyond[...])], [flat(sites[...]).astype(jnp.float32)], order
    )
    for x, scratch in zip(placed, (bg, far, site)):
        keep(x, scratch)
    for r in range(folds):
        for k in range(chunks):
            t = r * chunks + k
            for z in range(planes):
                at = tile_rows(z, r, rows, folds)
                trap = trap_of(density, site[k, at, :]) * spread[probes]
                coef[z * tiles + t] = weight_of(trap)
                src[z * tiles + t] = source_of(trap, bg[k, at, :])
            for z in range(beyond.shape[0]):
                next_bg[z * tiles + t] = far[k, tile_rows(z, r, rows, folds), :]
    at_low = edge[0] != 0

    def low(z):
        return jnp.where(at_low, z, 0)

    last = planes - HALO
    lax.fori_loop(low(1), last + 2, steps.first(spread[:probes], odd), 0)
    steps.step(odd, even, (low(1), last + 2), (low(2), last + 1))
    for n, (ref, z) in enumerate(((odd, last), (odd, last + 1), (even, last - 1), (even, last))):
        for p in range(probes):
            for t in range(tiles):
                kept[n, p, t] = ref[z, p, t]
    mine = (low(HALO), last)
    steps.step(even, odd, (low(2), last + 1), mine)
    by_one, by_two = steps.after_tangent(odd, even, mine, at_low, True)
    result = steps.moved_sums(steps.images(odd, even, by_one, by_two, by_one, steps.empty_sums()))
    for p in range(probes):
        sums[p] = result[p]


def outer_kernel(
    chunks, folds, edge, own_coef, own_src, own_wide, kept, own_sums, next_bg, packet, out,
    coef, src, even, odd,
):
    tiles = chunks * folds
    probes = own_wide.shape[0]
    total = even.shape[0] - 1
    planes = total - 2 * HALO
    steps = Steps(chunks, folds, probes, total, coef, src)
    last = planes - HALO
    halo = planes * tiles

    def copy(source, start, target, at, count):
        def body(n, carry):
            for t in range(tiles):
                target[at + n * tiles + t] = source[start + n * tiles + t]
            return carry

        lax.fori_loop(0, count, body, 0)

    own = (last - HALO) * tiles
    copy(own_src, own, src, own, planes - last + HALO)
    copy(own_coef, own, coef, own, planes - last + HALO)

    def beyond_plane(n, carry):
        for t in range(tiles):
            at = n * tiles + t
            trap = packet[probes + tiles + at]
            coef[halo + at] = weight_of(trap)
            src[halo + at] = source_of(trap, next_bg[at])
        return carry

    lax.fori_loop(0, 2 * HALO - 1, beyond_plane, 0)
    copy(packet, probes, src, (total - 1) * tiles, 1)
    steps.clear(even, odd)
    for p in range(probes):
        for t in range(tiles):
            odd[last, p, t] = kept[0, p, t]
            odd[last + 1, p, t] = kept[1, p, t]
            even[last - 1, p, t] = kept[2, p, t]
            even[last, p, t] = kept[3, p, t]

    at_high = edge[1] != 0

    def high(z):
        return jnp.where(at_high, z, planes)

    mine = [own_wide[p] for p in range(probes)]
    beyond = [packet[p] for p in range(probes)]
    steps.first(mine, odd, "up", beyond)(planes - 1, 0)

    @pl.when(at_high)
    def _():
        steps.first(beyond, odd, "down", mine)(planes, 0)
        lax.fori_loop(planes + 1, total - 1, steps.first(beyond, odd), 0)

    steps.step(odd, even, (last, high(total - 1)), (last + 1, high(total - 2)))
    mine = (last, high(total - HALO))
    steps.step(even, odd, (last - 1, high(total - 2)), mine)
    by_one, by_two = steps.after_tangent(odd, even, mine, True, at_high)
    start, stop = by_one
    empty = steps.empty_sums()
    inside = steps.images(odd, even, by_one, by_two, (start, planes - 1), empty)
    inside = steps.images(odd, even, by_one, by_two, planes - 1, inside, "up")
    above = [list(c) for c in empty]
    for p in range(probes):
        above[p][0] = inside[p][5]
    above = steps.images(odd, even, by_one, by_two, (planes + 1, stop), tuple(tuple(c) for c in above))
    above = steps.images(odd, even, by_one, by_two, planes, above, "down")
    inside = [x + own_sums[p] + above[p][5] for p, x in enumerate(steps.moved_sums(inside))]
    above = steps.moved_sums(above)

    added = jnp.concatenate(inside + above, axis=0) * STEP**6
    images = cell_dot(added, cell_matrix(chunks, True))
    mask = own_cells(folds)
    for part in range(2):
        halves = []
        for p in range(probes):
            image = jnp.where(mask, images[8 * (part * probes + p) :][:8], 0.0)
            image = jnp.sum(image, axis=0, keepdims=True)
            halves += [image[:, h * LANES : (h + 1) * LANES] for h in range(image.shape[1] // LANES)]
        halves = jnp.concatenate(halves, axis=0)

        def send(n, carry):
            out[n, part] = halves
            return carry

        lax.fori_loop(0, out.shape[0], send, 0, unroll=8)


def eliminate(gram):
    count = gram.shape[0]
    rows = lax.broadcasted_iota(jnp.int32, (count, count), 0)
    columns = lax.broadcasted_iota(jnp.int32, (count, count), 1)
    inverse = jnp.where(rows == columns, 1.0, 0.0)
    for j in range(count - 1):
        across = jnp.broadcast_to(gram[:, j : j + 1], (count, count))
        turned = 1.0 / across
        ratio = jnp.where(rows > j, across, 0.0)
        gram_row, inverse_row = (gram * turned)[j : j + 1, :], (inverse * turned)[j : j + 1, :]
        gram = gram - ratio * gram_row
        inverse = inverse - ratio * inverse_row
    diagonal = jnp.sum(jnp.where(rows == columns, gram, 0.0), axis=1, keepdims=True)
    scale = 1.0 / jnp.sqrt(diagonal)
    upper = jnp.where(columns >= rows, gram, 0.0) * scale
    return upper, inverse * scale


def gram_of(parts, count):
    stacked = jnp.concatenate(list(parts) + [jnp.zeros_like(parts[0])], axis=0)
    stacked = stacked.astype(jnp.bfloat16)
    every = lax.dot_general(
        stacked, stacked, (((1,), (1,)), ((), ())), preferred_element_type=jnp.float32
    )
    tall = every[:count] + (every[count : 2 * count] + every[2 * count : 3 * count])
    return tall[:, :count] + (tall[:, count : 2 * count] + tall[:, 2 * count : 3 * count])


def times(a, parts):
    first, second, third = float_parts(a)
    left = jnp.concatenate([first, second, third, first, second, first], axis=1)
    right = jnp.concatenate([parts[0]] * 3 + [parts[1]] * 2 + [parts[2]], axis=0)
    return bf16_dot(left.astype(jnp.bfloat16), right.astype(jnp.bfloat16))


def factor_kernel(place, parts, q_out, lower_out, rows_ref, q_ref):
    groups, slabs, _, probes, cells = parts.shape
    count = groups * probes
    for g in range(groups):

        def gather(slab, carry):
            before = jnp.maximum(slab - 1, 0)
            image = parts[g, slab, 0] + jnp.where(slab > 0, parts[g, before, 1], 0.0)
            at = pl.multiple_of(slab * cells, cells)
            rows_ref[pl.ds(g * probes, probes), pl.ds(at, cells)] = image
            return carry

        lax.fori_loop(0, slabs, gather, 0, unroll=True if slabs <= 16 else 8)
    total = slabs * cells
    rows = rows_ref[...]
    parts_one = float_parts(rows)
    upper_one, inverse_one = eliminate(gram_of(parts_one, count) / total)
    basis = times(inverse_one, parts_one)
    rows_ref[...] = basis
    upper_two, inverse_two = eliminate(gram_of(float_parts(basis), count) / total)
    mine = rows_ref[:, pl.ds(pl.multiple_of(place[1] * cells, cells), cells)]
    q_ref[...] = dot_nn(inverse_two, mine)
    for g in range(groups):

        @pl.when(place[0] == g)
        def _():
            q_out[:, 0, :] = q_ref[pl.ds(g * probes, probes), :]

    r = lax.broadcasted_iota(jnp.int32, (count, count), 0)
    c = lax.broadcasted_iota(jnp.int32, (count, count), 1)
    lower_one = dot_nt(jnp.where(r == c, 1.0, 0.0), upper_one)
    lower_out[...] = dot_nt(lower_one, upper_two)


def everywhere(x):
    x = jnp.broadcast_to(jnp.sum(x, axis=1, keepdims=True), x.shape)
    for shift in (4, 2, 1):
        x = x + pltpu.roll(x, shift, 0)
    return x


def cholesky(rows, total):
    count = len(rows)
    rows = [list(row) for row in rows]
    gram = {}
    for i in range(count):
        for j in range(i + 1):
            product = sum(a * b for a, b in zip(rows[i][1:], rows[j][1:]))
            gram[i, j] = everywhere(rows[i][0] * rows[j][0] + product) * (1.0 / total)
    factor = {}
    for j in range(count):
        pivot = gram[j, j]
        turned = lax.rsqrt(pivot)
        turned = turned * (1.5 - 0.5 * pivot * turned * turned)
        factor[j, j] = pivot * turned
        rows[j] = [x * turned for x in rows[j]]
        for i in range(j + 1, count):
            factor[i, j] = gram[i, j] * turned
        for i in range(j + 1, count):
            for k in range(j + 1, i + 1):
                gram[i, k] = gram[i, k] - factor[i, j] * factor[k, j]
            rows[i] = [x - factor[i, j] * y for x, y in zip(rows[i], rows[j])]
    return factor, rows


def register_kernel(groups, slabs, probes, place, mine, other, q_out, lower_out, q_ref):
    halves = q_out.shape[2] // LANES
    pieces = probes * halves
    step = 2 * pieces
    sublane = lax.broadcasted_iota(jnp.int32, (8, LANES), 0)
    odd = jnp.broadcast_to(place[1] % 2, (8, LANES)) == 1

    def load(at):
        at = pl.ds(at, 8, stride=step)
        one, two = mine[at, :], other[at, :]
        return jnp.where(odd, two, one), jnp.where(odd, one, two)

    rows = []
    for g in range(groups):
        for p in range(probes):
            row = []
            for h in range(halves):
                last = None
                for block in range(slabs // 16):
                    at = (g * slabs // 2 + 8 * block) * step + p * halves + h
                    even_own, odd_own = load(at)
                    even_next, odd_next = load(at + pieces)
                    before = pltpu.roll(odd_next, 1, 0)
                    first = 0.0 if last is None else last
                    last = before
                    row.append((block, 0, h, even_own + jnp.where(sublane == 0, first, before)))
                    row.append((block, 1, h, odd_own + even_next))
            rows.append(row)
    places = [x[:3] for x in rows[0]]
    rows = [[x[3] for x in row] for row in rows]
    total = slabs * halves * LANES
    factor_one, basis = cholesky(rows, total)
    factor_two, rows = cholesky(basis, total)
    for i, row in enumerate(rows):
        for (block, parity, h), x in zip(places, row):
            q_ref[i, h, pl.ds(parity * (slabs // 2) + 8 * block, 8), :] = x
    own = (place[1] % 2) * (slabs // 2) + place[1] // 2
    for p in range(probes):
        for h in range(halves):
            mine = q_ref[place[0] * probes + p, h, pl.ds(own, 1), :]
            q_out[p, :, pl.ds(h * LANES, LANES)] = mine
    count = len(rows)
    r = lax.broadcasted_iota(jnp.int32, (8, LANES), 0)
    c = lax.broadcasted_iota(jnp.int32, (8, LANES), 1)
    lower = jnp.zeros((8, LANES), jnp.float32)
    for i in range(count):
        for j in range(i + 1):
            entry = sum(factor_one[i, k] * factor_two[k, j] for k in range(j, i + 1))
            lower = jnp.where((r == i) & (c == j), entry, lower)
    lower_out[...] = lower[:count, :count]


def shards(probe_dirs, log_param, background, site_class, trap_density):
    probes = probe_dirs.shape[0]
    cells = probe_dirs.shape[2]
    planes, rows, columns = background.shape
    slabs = lax.axis_size("space")
    groups = lax.axis_size("probe")
    at_space = lax.axis_index("space")
    vmem = pl.BlockSpec(memory_space=pltpu.VMEM)
    smem = pl.BlockSpec(memory_space=pltpu.SMEM)
    anywhere = pl.BlockSpec(memory_space=pl.ANY)
    params = pltpu.CompilerParams(vmem_limit_bytes=62 * 2**20)

    chunks, folds = columns // LANES, rows // 8
    tiles = chunks * folds
    total = planes + 2 * HALO
    tile = (8, LANES)

    def shape(*dims):
        return jax.ShapeDtypeStruct(dims + tile, jnp.float32)

    def scratch(*dims):
        return pltpu.VMEM(dims + tile, jnp.float32)

    def copies(count):
        return pltpu.SemaphoreType.DMA((count,))

    def inputs(held, sites):
        return [
            pltpu.VMEM((held, rows, columns), jnp.float32),
            pltpu.VMEM((sites, rows, columns), jnp.int32),
            pltpu.VMEM(log_param.shape, jnp.float32),
            pltpu.VMEM(probe_dirs.shape, jnp.float32),
            pltpu.VMEM((columns, columns), jnp.bfloat16),
        ]

    def rows_of(held):
        return pltpu.VMEM((chunks, held * rows, LANES), jnp.float32)

    down = [(i + 1, i) for i in range(slabs - 1)]
    beyond = lax.ppermute(background[: 2 * HALO - 1], "space", down)
    size = probes + 2 * HALO * tiles
    packet = pl.pallas_call(
        packet_kernel,
        out_shape=shape(size),
        in_specs=[smem] + [anywhere] * 4,
        out_specs=anywhere,
        scratch_shapes=inputs(1, 2 * HALO)
        + [rows_of(1), rows_of(2 * HALO), scratch(size), copies(4), copies(3)],
        compiler_params=params,
        name="packet",
    )(trap_density, background, site_class, log_param, probe_dirs)
    next_packet = lax.ppermute(packet, "space", down)
    edge = jnp.stack([at_space > 0, at_space < slabs - 1]).astype(jnp.int32)
    own_coef, own_src, wide, kept, sums, next_bg = pl.pallas_call(
        inner_kernel,
        out_shape=(
            shape(planes * tiles),
            shape((planes + 1) * tiles),
            shape(probes),
            shape(4, probes, tiles),
            shape(probes),
            shape((2 * HALO - 1) * tiles),
        ),
        in_specs=[smem, smem] + [anywhere] * 4 + [vmem],
        out_specs=(vmem,) * 6,
        scratch_shapes=inputs(planes, planes)
        + [rows_of(planes), rows_of(2 * HALO - 1), rows_of(planes)]
        + [scratch(planes + 1, probes, tiles)] * 2
        + [copies(4)],
        compiler_params=pltpu.CompilerParams(vmem_limit_bytes=28 * 2**20),
        cost_estimate=pl.CostEstimate(flops=10**9, bytes_accessed=2**24, transcendentals=256),
        name="inner",
    )(edge, trap_density, background, site_class, log_param, probe_dirs, beyond)

    pieces = probes * cells // LANES
    images = pl.pallas_call(
        functools.partial(outer_kernel, chunks, folds),
        out_shape=jax.ShapeDtypeStruct((groups * slabs // 2, 2, pieces, LANES), jnp.float32),
        in_specs=[smem] + [vmem] * 7,
        out_specs=vmem,
        scratch_shapes=[
            scratch(total * tiles),
            scratch(total * tiles),
            scratch(total + 1, probes, tiles),
            scratch(total + 1, probes, tiles),
        ],
        compiler_params=pltpu.CompilerParams(vmem_limit_bytes=28 * 2**20),
        name="outer",
    )(edge, own_coef, own_src, wide, kept, sums, next_bg, next_packet)

    same = [
        [g * slabs + z for g in range(groups) for z in range(parity, slabs, 2)] for parity in (0, 1)
    ]
    mine = lax.all_to_all(
        images, ("probe", "space"), split_axis=0, concat_axis=0, axis_index_groups=same, tiled=True
    )
    other = lax.ppermute(mine, "space", [(z, z ^ 1) for z in range(slabs)])
    place = jnp.stack([lax.axis_index("probe"), at_space]).astype(jnp.int32)
    count = groups * probes
    results = (
        jax.ShapeDtypeStruct((probes, 1, cells), jnp.float32),
        jax.ShapeDtypeStruct((count, count), jnp.float32),
    )
    params = pltpu.CompilerParams(vmem_limit_bytes=28 * 2**20)
    if count <= 8 and slabs % 16 == 0:
        halves = cells // LANES
        return pl.pallas_call(
            functools.partial(register_kernel, groups, slabs, probes),
            out_shape=results,
            in_specs=[smem, vmem, vmem],
            out_specs=(vmem, vmem),
            scratch_shapes=[pltpu.VMEM((count, halves, slabs, LANES), jnp.float32)],
            compiler_params=params,
            name="factor",
        )(
            place,
            mine.reshape((groups * slabs * pieces, LANES)),
            other.reshape((groups * slabs * pieces, LANES)),
        )
    odd = at_space % 2 == 1
    pairs = [jnp.where(odd, other, mine), jnp.where(odd, mine, other)]
    pairs = [x.reshape((groups, slabs // 2, 2, probes, cells)) for x in pairs]
    every = jnp.stack(pairs, axis=2).reshape((groups, slabs, 2, probes, cells))
    return pl.pallas_call(
        factor_kernel,
        out_shape=results,
        in_specs=[smem, vmem],
        out_specs=(vmem, vmem),
        scratch_shapes=[
            pltpu.VMEM((count, slabs * cells), jnp.float32),
            pltpu.VMEM((count, cells), jnp.float32),
        ],
        compiler_params=params,
        name="factor",
    )(place, every)


def solution(mesh):
    placed = (
        P("probe", "space", None),
        P("space", None),
        P("space", None, None),
        P("space", None, None),
        P(),
    )
    return jax.shard_map(
        shards,
        mesh=mesh,
        in_specs=placed,
        out_specs=(P("probe", "space", None), P()),
        check_vma=False,
    )
```

```python
import functools

import jax
import jax.numpy as jnp
from jax import lax
from jax.experimental import pallas as pl
from jax.experimental.pallas import tpu as pltpu
from jax.sharding import PartitionSpec as P

PX = 64
PY = 4
REF = 8
STEP = 0.12
HALO = 3
LANES = 128
HIGHEST = lax.Precision.HIGHEST


def dot_nn(a, b):
    return lax.dot_general(
        a, b, (((1,), (0,)), ((), ())), precision=HIGHEST, preferred_element_type=jnp.float32
    )


def dot_nt(a, b):
    return lax.dot_general(
        a, b, (((1,), (1,)), ((), ())), precision=HIGHEST, preferred_element_type=jnp.float32
    )


def parts_of(x):
    first = x.astype(jnp.bfloat16)
    rest = x - first.astype(jnp.float32)
    second = rest.astype(jnp.bfloat16)
    third = (rest - second.astype(jnp.float32)).astype(jnp.bfloat16)
    return first, second, third


def bf16_dot(a, b):
    return jnp.dot(a, b, preferred_element_type=jnp.float32)


def interleave(exact, small, order):
    parts = [part for x in exact for part in parts_of(x)] + [x.astype(jnp.bfloat16) for x in small]
    placed = bf16_dot(jnp.concatenate(parts, axis=0), order[...])
    results, at = [], 0
    for x in exact:
        count = x.shape[0]
        first, second, third = [placed[at + n * count : at + (n + 1) * count] for n in range(3)]
        results.append((first + second) + third)
        at += 3 * count
    for x in small:
        results.append(placed[at : at + x.shape[0]])
        at += x.shape[0]
    return results


def keep(placed, kept):
    for k in range(kept.shape[0]):
        kept[k] = placed[:, k * LANES : (k + 1) * LANES]


def flat(planes):
    return planes.reshape((planes.shape[0] * planes.shape[1], planes.shape[2]))


def cell_matrix(chunks, turned=False):
    half = REF // chunks
    dims = (LANES, PX * PY) if turned else (PX * PY, LANES)
    cell = lax.broadcasted_iota(jnp.int32, dims, int(turned)) % PX
    lane = lax.broadcasted_iota(jnp.int32, dims, 1 - int(turned)) // half
    return jnp.where(cell == lane, 1.0, 0.0).astype(jnp.float32)


def own_cells(folds):
    half = REF // folds
    sublane = lax.broadcasted_iota(jnp.int32, (8, PX * PY), 0) // half
    return lax.broadcasted_iota(jnp.int32, (8, PX * PY), 1) // PX == sublane


def prolonged(coarse, folds, chunks):
    mask = own_cells(folds)
    rows = [jnp.where(mask, coarse[n : n + 1, :], 0.0) for n in range(coarse.shape[0])]
    return cell_dot(jnp.concatenate(rows, axis=0), cell_matrix(chunks))


def cell_dot(rows, matrix):
    count = rows.shape[0]
    parts = jnp.concatenate(float_parts(rows), axis=0).astype(jnp.bfloat16)
    placed = bf16_dot(parts, matrix.astype(jnp.bfloat16))
    return (placed[:count] + placed[count : 2 * count]) + placed[2 * count :]


def float_parts(x):
    first = x.astype(jnp.bfloat16).astype(jnp.float32)
    rest = x - first
    second = rest.astype(jnp.bfloat16).astype(jnp.float32)
    return first, second, rest - second


def cell_order(columns, chunks):
    x = lax.broadcasted_iota(jnp.int32, (columns, columns), 0)
    place = lax.broadcasted_iota(jnp.int32, (columns, columns), 1)
    wanted = chunks * (place % LANES) + place // LANES
    return jnp.where(x == wanted, 1.0, 0.0).astype(jnp.bfloat16)


def spread_cells(dirs, log_param, folds, chunks):
    probes = dirs.shape[0]
    coarse = [dirs[p] for p in range(probes)] + [jnp.exp(log_param[...])]
    spread = prolonged(jnp.concatenate(coarse, axis=0), folds, chunks)
    return [spread[8 * n : 8 * n + 8, :] for n in range(probes + 1)]


def tile_rows(z, r, rows, folds):
    return pl.ds(z * rows + r, 8, stride=folds)


def trap_of(density, kind):
    trap = jnp.full((8, LANES), density[density.shape[0] - 1])
    for n in range(density.shape[0] - 2, -1, -1):
        trap = jnp.where(kind == float(n), density[n], trap)
    return trap


def weight_of(trap):
    return (1.0 / STEP - 6.0) - trap


def source_of(trap, background):
    return -STEP * trap * background


def packet_kernel(
    density, background_in, sites_in, log_param_in, dirs_in, packet,
    background, sites, log_param, dirs, order, bg, site, made, sems, out_sems,
):
    count, rows, columns = sites.shape
    chunks, folds = columns // LANES, rows // 8
    tiles = chunks * folds
    probes = dirs.shape[0]
    pairs = [
        (log_param_in, log_param),
        (dirs_in, dirs),
        (background_in.at[pl.ds(count - 1, 1)], background),
        (sites_in.at[pl.ds(0, count)], sites),
    ]
    copies = [pltpu.make_async_copy(a, b, sems.at[n]) for n, (a, b) in enumerate(pairs)]
    for copy in copies:
        copy.start()
    order[...] = cell_order(columns, chunks)
    copies[0].wait()
    copies[1].wait()
    spread = spread_cells(dirs, log_param, folds, chunks)
    for p in range(probes):
        made[p] = spread[p]
    copies[2].wait()
    copies[3].wait()
    placed = interleave([flat(background[...])], [flat(sites[...]).astype(jnp.float32)], order)
    keep(placed[0], bg)
    keep(placed[1], site)
    sent = []

    def send(start, stop):
        at = pl.ds(start, stop - start)
        copy = pltpu.make_async_copy(made.at[at], packet.at[at], out_sems.at[len(sent)])
        copy.start()
        sent.append(copy)

    first = probes + tiles
    middle = first + (count - 1) // 2 * tiles
    for z in range(count):
        for r in range(folds):
            for k in range(chunks):
                t = r * chunks + k
                trap = trap_of(density, site[k, tile_rows(z, r, rows, folds), :]) * spread[probes]
                if z < count - 1:
                    made[first + z * tiles + t] = trap
                else:
                    made[probes + t] = source_of(trap, bg[k, tile_rows(0, r, rows, folds), :])
        if z == (count - 1) // 2 - 1:
            send(first, middle)
        elif z == count - 2:
            send(middle, first + (count - 1) * tiles)
    send(0, first)
    for copy in sent:
        copy.wait()


class Steps:
    def __init__(self, chunks, folds, probes, zero_plane, coef, src):
        self.chunks, self.folds, self.tiles = chunks, folds, chunks * folds
        self.probes, self.zero_plane = probes, zero_plane
        self.coef, self.src = coef, src
        self.lane = lax.broadcasted_iota(jnp.int32, (8, LANES), 1)
        self.sublane = lax.broadcasted_iota(jnp.int32, (8, LANES), 0)

    def clear(self, *fields):
        nothing = jnp.zeros((8, LANES), jnp.float32)
        for t in range(self.tiles):
            for field in fields:
                for p in range(self.probes):
                    field[self.zero_plane, p, t] = nothing

    def from_left(self, x):
        return jnp.where(self.lane == 0, 0.0, pltpu.roll(x, 1, 1))

    def from_right(self, x):
        return jnp.where(self.lane == LANES - 1, 0.0, pltpu.roll(x, LANES - 1, 1))

    def from_before(self, x):
        return jnp.where(self.sublane == 0, 0.0, pltpu.roll(x, 1, 0))

    def from_after(self, x):
        return jnp.where(self.sublane == 7, 0.0, pltpu.roll(x, 7, 0))

    def first(self, own, to, other=None, beyond=()):
        chunks, folds, tiles = self.chunks, self.folds, self.tiles
        src, coef = self.src, self.coef
        turns = (self.from_left, self.from_right, self.from_before, self.from_after)
        shifted = [[f(x) for x in own] for f in turns]

        def body(z, carry):
            down = jnp.where(z > 0, z - 1, self.zero_plane) * tiles
            up = (z + 1) * tiles
            s = [[src[z * tiles + r * chunks + k] for k in range(chunks)] for r in range(folds)]
            for r in range(folds):
                for k in range(chunks):
                    t = r * chunks + k
                    same = coef[z * tiles + t] * s[r][k]
                    outer = []
                    for there, value, turn, kind in (
                        (k > 0, s[r][k - 1], (1, 1), 0),
                        (k + 1 < chunks, s[r][(k + 1) % chunks], (LANES - 1, 1), 1),
                        (r > 0, s[r - 1][k], (1, 0), 2),
                        (r + 1 < folds, s[(r + 1) % folds][k], (7, 0), 3),
                    ):
                        if there:
                            same = same + value
                        else:
                            outer.append((pltpu.roll(value, *turn), shifted[kind]))
                    for name, value in (("down", src[down + t]), ("up", src[up + t])):
                        if name == other:
                            outer.append((value, beyond))
                        else:
                            same = same + value
                    for p in range(self.probes):
                        result = same * own[p]
                        for value, factor in outer:
                            result = result + value * factor[p]
                        to[z, p, t] = result
            return carry

        return body

    def stencil(self, ref, valid, z, emit, extra):
        chunks, folds, tiles = self.chunks, self.folds, self.tiles
        first, stop = valid

        def at(z):
            return jnp.where((z >= first) & (z < stop), z, self.zero_plane)

        down, here, there, up = at(z - 1), at(z), at(z + 1), at(z + 2)
        raised = {}
        if extra:
            for n in (0, 1):
                for t in range(tiles):
                    raised[n, t] = self.coef[(z + n) * tiles + t] + extra
        for p in range(self.probes):
            pair = [[ref[plane, p, t] for t in range(tiles)] for plane in (here, there)]
            for n, value in enumerate(pair):
                shared = self.corners(value)
                for r in range(folds):
                    for k in range(chunks):
                        t = r * chunks + k
                        above = pair[1 - n][t] + (ref[up, p, t] if n else ref[down, p, t])
                        weight = raised[n, t] if extra else self.coef[(z + n) * tiles + t]
                        sides = shared[r, k] + shared[r + 1, k + 1]
                        emit(z + n, p, t, (sides + above) + weight * value[t])

    def corners(self, value):
        chunks, folds = self.chunks, self.folds

        def at(r, k):
            if r < 0:
                return self.from_before(value[(folds - 1) * chunks + k])
            if r == folds:
                return self.from_after(value[k])
            if k < 0:
                return self.from_left(value[r * chunks + chunks - 1])
            if k == chunks:
                return self.from_right(value[r * chunks])
            return value[r * chunks + k]

        ends = ((folds, 0), (0, chunks))
        return {
            (r, k): at(r - 1, k) + at(r, k - 1)
            for r in range(folds + 1)
            for k in range(chunks + 1)
            if (r, k) not in ends
        }

    def step(self, ref, to, valid, wanted, extra=0.0):
        start, stop = wanted

        def body(n, carry):
            def emit(z, p, t, result):
                to[z, p, t] = result

            self.stencil(ref, valid, jnp.minimum(start + 2 * n, stop - 2), emit, extra)
            return carry

        lax.fori_loop(0, (stop - start + 1) // 2, body, 0)

    def widen(self, ref, to, valid, at_low, at_high):
        first, stop = valid

        def move(a, b):
            for p in range(self.probes):
                for t in range(self.tiles):
                    to[b, p, t] = ref[a, p, t]

        pl.when(at_low)(lambda: move(first, first - 1))
        pl.when(at_high)(lambda: move(stop - 1, stop))

    def images(self, m, u, by_one, by_two, span, carry, other=None):
        chunks, folds, tiles = self.chunks, self.folds, self.tiles
        src = self.src

        def at(z, valid):
            return jnp.where((z >= valid[0]) & (z < valid[1]), z, self.zero_plane)

        def body(z, carry):
            carry = [list(c) for c in carry]
            down = jnp.where(z > 0, z - 1, self.zero_plane) * tiles
            up = (z + 1) * tiles
            here, kept = at(z, by_one), at(z, by_two)
            s = [src[z * tiles + t] for t in range(tiles)]
            for t in range(tiles):
                r, k = t // chunks, t % chunks
                same = self.coef[z * tiles + t] * s[t]
                moved = []
                if k:
                    same = same + s[t - 1]
                else:
                    moved.append((2, self.from_left(s[t + chunks - 1])))
                if k + 1 < chunks:
                    same = same + s[t + 1]
                else:
                    moved.append((1, self.from_right(s[t + 1 - chunks])))
                if r:
                    same = same + s[t - chunks]
                else:
                    moved.append((4, self.from_before(s[t + tiles - chunks])))
                if r + 1 < folds:
                    same = same + s[t + chunks]
                else:
                    moved.append((3, self.from_after(s[t + chunks - tiles])))
                for name, value in (("down", src[down + t]), ("up", src[up + t])):
                    if name == other:
                        moved.append((5, value))
                    else:
                        same = same + value
                scaled = s[t] * (1.0 / STEP**2)
                for p in range(self.probes):
                    value = m[here, p, t]
                    carry[p][0] = carry[p][0] + (same * value + scaled * u[kept, p, t])
                    for n, factor in moved:
                        carry[p][n] = carry[p][n] + factor * value
            return tuple(tuple(c) for c in carry)

        if isinstance(span, int):
            return body(span, carry)
        return lax.fori_loop(*span, body, carry)

    def empty_sums(self):
        nothing = jnp.zeros((8, LANES), jnp.float32)
        return ((nothing,) * 6,) * self.probes

    def moved_sums(self, sums):
        return [
            c[0]
            + (self.from_left(c[1]) + self.from_right(c[2]))
            + (self.from_before(c[3]) + self.from_after(c[4]))
            for c in sums
        ]

    def after_tangent(self, odd, even, mine, at_low, at_high):
        first, stop = mine
        by_two = (jnp.where(at_low, first - 1, first), jnp.where(at_high, stop + 1, stop))
        by_one = (jnp.where(at_low, first - 2, first), jnp.where(at_high, stop + 2, stop))
        self.step(odd, even, mine, mine, 1.0 / STEP)
        self.widen(odd, even, mine, at_low, at_high)
        self.step(even, odd, by_two, by_two)
        self.widen(even, odd, by_two, at_low, at_high)
        return by_one, by_two


def inner_kernel(
    edge, density, background_in, sites_in, log_param_in, dirs_in, beyond,
    coef, src, wide, kept, sums, next_bg,
    background, sites, log_param, dirs, order, bg, far, site, even, odd, sems,
):
    planes, rows, columns = background.shape
    chunks, folds = columns // LANES, rows // 8
    tiles = chunks * folds
    probes = dirs.shape[0]
    copies = [
        (log_param_in, log_param),
        (dirs_in, dirs),
        (background_in, background),
        (sites_in, sites),
    ]
    copies = [pltpu.make_async_copy(a, b, sems.at[n]) for n, (a, b) in enumerate(copies)]
    for copy in copies:
        copy.start()
    steps = Steps(chunks, folds, probes, planes, coef, src)
    steps.clear(even, odd)
    nothing = jnp.zeros((8, LANES), jnp.float32)
    for t in range(tiles):
        src[planes * tiles + t] = nothing
    order[...] = cell_order(columns, chunks)
    for copy in copies:
        copy.wait()
    spread = spread_cells(dirs, log_param, folds, chunks)
    for p in range(probes):
        wide[p] = spread[p]

    placed = interleave(
        [flat(background[...]), flat(beyond[...])], [flat(sites[...]).astype(jnp.float32)], order
    )
    for x, scratch in zip(placed, (bg, far, site)):
        keep(x, scratch)
    for r in range(folds):
        for k in range(chunks):
            t = r * chunks + k
            for z in range(planes):
                at = tile_rows(z, r, rows, folds)
                trap = trap_of(density, site[k, at, :]) * spread[probes]
                coef[z * tiles + t] = weight_of(trap)
                src[z * tiles + t] = source_of(trap, bg[k, at, :])
            for z in range(beyond.shape[0]):
                next_bg[z * tiles + t] = far[k, tile_rows(z, r, rows, folds), :]
    at_low = edge[0] != 0

    def low(z):
        return jnp.where(at_low, z, 0)

    last = planes - HALO
    lax.fori_loop(low(1), last + 2, steps.first(spread[:probes], odd), 0)
    steps.step(odd, even, (low(1), last + 2), (low(2), last + 1))
    for n, (ref, z) in enumerate(((odd, last), (odd, last + 1), (even, last - 1), (even, last))):
        for p in range(probes):
            for t in range(tiles):
                kept[n, p, t] = ref[z, p, t]
    mine = (low(HALO), last)
    steps.step(even, odd, (low(2), last + 1), mine)
    by_one, by_two = steps.after_tangent(odd, even, mine, at_low, True)
    result = steps.moved_sums(steps.images(odd, even, by_one, by_two, by_one, steps.empty_sums()))
    for p in range(probes):
        sums[p] = result[p]


def outer_kernel(
    chunks, folds, edge, own_coef, own_src, own_wide, kept, own_sums, next_bg, packet, out,
    coef, src, even, odd,
):
    tiles = chunks * folds
    probes = own_wide.shape[0]
    total = even.shape[0] - 1
    planes = total - 2 * HALO
    steps = Steps(chunks, folds, probes, total, coef, src)
    last = planes - HALO
    halo = planes * tiles

    def copy(source, start, target, at, count):
        def body(n, carry):
            for t in range(tiles):
                target[at + n * tiles + t] = source[start + n * tiles + t]
            return carry

        lax.fori_loop(0, count, body, 0)

    own = (last - HALO) * tiles
    copy(own_src, own, src, own, planes - last + HALO)
    copy(own_coef, own, coef, own, planes - last + HALO)

    def beyond_plane(n, carry):
        for t in range(tiles):
            at = n * tiles + t
            trap = packet[probes + tiles + at]
            coef[halo + at] = weight_of(trap)
            src[halo + at] = source_of(trap, next_bg[at])
        return carry

    lax.fori_loop(0, 2 * HALO - 1, beyond_plane, 0)
    copy(packet, probes, src, (total - 1) * tiles, 1)
    steps.clear(even, odd)
    for p in range(probes):
        for t in range(tiles):
            odd[last, p, t] = kept[0, p, t]
            odd[last + 1, p, t] = kept[1, p, t]
            even[last - 1, p, t] = kept[2, p, t]
            even[last, p, t] = kept[3, p, t]

    at_high = edge[1] != 0

    def high(z):
        return jnp.where(at_high, z, planes)

    mine = [own_wide[p] for p in range(probes)]
    beyond = [packet[p] for p in range(probes)]
    steps.first(mine, odd, "up", beyond)(planes - 1, 0)

    @pl.when(at_high)
    def _():
        steps.first(beyond, odd, "down", mine)(planes, 0)
        lax.fori_loop(planes + 1, total - 1, steps.first(beyond, odd), 0)

    steps.step(odd, even, (last, high(total - 1)), (last + 1, high(total - 2)))
    mine = (last, high(total - HALO))
    steps.step(even, odd, (last - 1, high(total - 2)), mine)
    by_one, by_two = steps.after_tangent(odd, even, mine, True, at_high)
    start, stop = by_one
    empty = steps.empty_sums()
    inside = steps.images(odd, even, by_one, by_two, (start, planes - 1), empty)
    inside = steps.images(odd, even, by_one, by_two, planes - 1, inside, "up")
    above = [list(c) for c in empty]
    for p in range(probes):
        above[p][0] = inside[p][5]
    above = steps.images(odd, even, by_one, by_two, (planes + 1, stop), tuple(tuple(c) for c in above))
    above = steps.images(odd, even, by_one, by_two, planes, above, "down")
    inside = [x + own_sums[p] + above[p][5] for p, x in enumerate(steps.moved_sums(inside))]
    above = steps.moved_sums(above)

    added = jnp.concatenate(inside + above, axis=0) * STEP**6
    images = cell_dot(added, cell_matrix(chunks, True))
    mask = own_cells(folds)
    for part in range(2):
        halves = []
        for p in range(probes):
            image = jnp.where(mask, images[8 * (part * probes + p) :][:8], 0.0)
            image = jnp.sum(image, axis=0, keepdims=True)
            halves += [image[:, h * LANES : (h + 1) * LANES] for h in range(image.shape[1] // LANES)]
        halves = jnp.concatenate(halves, axis=0)

        def send(n, carry):
            out[n, part] = halves
            return carry

        lax.fori_loop(0, out.shape[0], send, 0, unroll=8)


def eliminate(gram):
    count = gram.shape[0]
    rows = lax.broadcasted_iota(jnp.int32, (count, count), 0)
    columns = lax.broadcasted_iota(jnp.int32, (count, count), 1)
    inverse = jnp.where(rows == columns, 1.0, 0.0)
    for j in range(count - 1):
        across = jnp.broadcast_to(gram[:, j : j + 1], (count, count))
        turned = 1.0 / across
        ratio = jnp.where(rows > j, across, 0.0)
        gram_row, inverse_row = (gram * turned)[j : j + 1, :], (inverse * turned)[j : j + 1, :]
        gram = gram - ratio * gram_row
        inverse = inverse - ratio * inverse_row
    diagonal = jnp.sum(jnp.where(rows == columns, gram, 0.0), axis=1, keepdims=True)
    scale = 1.0 / jnp.sqrt(diagonal)
    upper = jnp.where(columns >= rows, gram, 0.0) * scale
    return upper, inverse * scale


def gram_of(parts, count):
    stacked = jnp.concatenate(list(parts) + [jnp.zeros_like(parts[0])], axis=0)
    stacked = stacked.astype(jnp.bfloat16)
    every = lax.dot_general(
        stacked, stacked, (((1,), (1,)), ((), ())), preferred_element_type=jnp.float32
    )
    tall = every[:count] + (every[count : 2 * count] + every[2 * count : 3 * count])
    return tall[:, :count] + (tall[:, count : 2 * count] + tall[:, 2 * count : 3 * count])


def times(a, parts):
    first, second, third = float_parts(a)
    left = jnp.concatenate([first, second, third, first, second, first], axis=1)
    right = jnp.concatenate([parts[0]] * 3 + [parts[1]] * 2 + [parts[2]], axis=0)
    return bf16_dot(left.astype(jnp.bfloat16), right.astype(jnp.bfloat16))


def factor_kernel(place, parts, q_out, lower_out, rows_ref, q_ref):
    groups, slabs, _, probes, cells = parts.shape
    count = groups * probes
    for g in range(groups):

        def gather(slab, carry):
            before = jnp.maximum(slab - 1, 0)
            image = parts[g, slab, 0] + jnp.where(slab > 0, parts[g, before, 1], 0.0)
            at = pl.multiple_of(slab * cells, cells)
            rows_ref[pl.ds(g * probes, probes), pl.ds(at, cells)] = image
            return carry

        lax.fori_loop(0, slabs, gather, 0, unroll=True if slabs <= 16 else 8)
    total = slabs * cells
    rows = rows_ref[...]
    parts_one = float_parts(rows)
    upper_one, inverse_one = eliminate(gram_of(parts_one, count) / total)
    basis = times(inverse_one, parts_one)
    rows_ref[...] = basis
    upper_two, inverse_two = eliminate(gram_of(float_parts(basis), count) / total)
    mine = rows_ref[:, pl.ds(pl.multiple_of(place[1] * cells, cells), cells)]
    q_ref[...] = dot_nn(inverse_two, mine)
    for g in range(groups):

        @pl.when(place[0] == g)
        def _():
            q_out[:, 0, :] = q_ref[pl.ds(g * probes, probes), :]

    r = lax.broadcasted_iota(jnp.int32, (count, count), 0)
    c = lax.broadcasted_iota(jnp.int32, (count, count), 1)
    lower_one = dot_nt(jnp.where(r == c, 1.0, 0.0), upper_one)
    lower_out[...] = dot_nt(lower_one, upper_two)


def everywhere(x):
    x = jnp.broadcast_to(jnp.sum(x, axis=1, keepdims=True), x.shape)
    for shift in (4, 2, 1):
        x = x + pltpu.roll(x, shift, 0)
    return x


def cholesky(rows, total):
    count = len(rows)
    rows = [list(row) for row in rows]
    gram = {}
    for i in range(count):
        for j in range(i + 1):
            product = sum(a * b for a, b in zip(rows[i][1:], rows[j][1:]))
            gram[i, j] = everywhere(rows[i][0] * rows[j][0] + product) * (1.0 / total)
    factor = {}
    for j in range(count):
        pivot = gram[j, j]
        turned = lax.rsqrt(pivot)
        turned = turned * (1.5 - 0.5 * pivot * turned * turned)
        factor[j, j] = pivot * turned
        rows[j] = [x * turned for x in rows[j]]
        for i in range(j + 1, count):
            factor[i, j] = gram[i, j] * turned
        for i in range(j + 1, count):
            for k in range(j + 1, i + 1):
                gram[i, k] = gram[i, k] - factor[i, j] * factor[k, j]
            rows[i] = [x - factor[i, j] * y for x, y in zip(rows[i], rows[j])]
    return factor, rows


def register_kernel(groups, slabs, probes, place, mine, other, q_out, lower_out, q_ref):
    halves = q_out.shape[2] // LANES
    pieces = probes * halves
    step = 2 * pieces
    sublane = lax.broadcasted_iota(jnp.int32, (8, LANES), 0)
    odd = jnp.broadcast_to(place[1] % 2, (8, LANES)) == 1

    def load(at):
        at = pl.ds(at, 8, stride=step)
        one, two = mine[at, :], other[at, :]
        return jnp.where(odd, two, one), jnp.where(odd, one, two)

    rows = []
    for g in range(groups):
        for p in range(probes):
            row = []
            for h in range(halves):
                last = None
                for block in range(slabs // 16):
                    at = (g * slabs // 2 + 8 * block) * step + p * halves + h
                    even_own, odd_own = load(at)
                    even_next, odd_next = load(at + pieces)
                    before = pltpu.roll(odd_next, 1, 0)
                    first = 0.0 if last is None else last
                    last = before
                    row.append((block, 0, h, even_own + jnp.where(sublane == 0, first, before)))
                    row.append((block, 1, h, odd_own + even_next))
            rows.append(row)
    places = [x[:3] for x in rows[0]]
    rows = [[x[3] for x in row] for row in rows]
    total = slabs * halves * LANES
    factor_one, basis = cholesky(rows, total)
    factor_two, rows = cholesky(basis, total)
    for i, row in enumerate(rows):
        for (block, parity, h), x in zip(places, row):
            q_ref[i, h, pl.ds(parity * (slabs // 2) + 8 * block, 8), :] = x
    own = (place[1] % 2) * (slabs // 2) + place[1] // 2
    for p in range(probes):
        for h in range(halves):
            mine = q_ref[place[0] * probes + p, h, pl.ds(own, 1), :]
            q_out[p, :, pl.ds(h * LANES, LANES)] = mine
    count = len(rows)
    r = lax.broadcasted_iota(jnp.int32, (8, LANES), 0)
    c = lax.broadcasted_iota(jnp.int32, (8, LANES), 1)
    lower = jnp.zeros((8, LANES), jnp.float32)
    for i in range(count):
        for j in range(i + 1):
            entry = sum(factor_one[i, k] * factor_two[k, j] for k in range(j, i + 1))
            lower = jnp.where((r == i) & (c == j), entry, lower)
    lower_out[...] = lower[:count, :count]


def shards(probe_dirs, log_param, background, site_class, trap_density):
    probes = probe_dirs.shape[0]
    cells = probe_dirs.shape[2]
    planes, rows, columns = background.shape
    slabs = lax.axis_size("space")
    groups = lax.axis_size("probe")
    at_space = lax.axis_index("space")
    vmem = pl.BlockSpec(memory_space=pltpu.VMEM)
    smem = pl.BlockSpec(memory_space=pltpu.SMEM)
    anywhere = pl.BlockSpec(memory_space=pl.ANY)
    params = pltpu.CompilerParams(vmem_limit_bytes=62 * 2**20)

    chunks, folds = columns // LANES, rows // 8
    tiles = chunks * folds
    total = planes + 2 * HALO
    tile = (8, LANES)

    def shape(*dims):
        return jax.ShapeDtypeStruct(dims + tile, jnp.float32)

    def scratch(*dims):
        return pltpu.VMEM(dims + tile, jnp.float32)

    def copies(count):
        return pltpu.SemaphoreType.DMA((count,))

    def inputs(held, sites):
        return [
            pltpu.VMEM((held, rows, columns), jnp.float32),
            pltpu.VMEM((sites, rows, columns), jnp.int32),
            pltpu.VMEM(log_param.shape, jnp.float32),
            pltpu.VMEM(probe_dirs.shape, jnp.float32),
            pltpu.VMEM((columns, columns), jnp.bfloat16),
        ]

    def rows_of(held):
        return pltpu.VMEM((chunks, held * rows, LANES), jnp.float32)

    down = [(i + 1, i) for i in range(slabs - 1)]
    beyond = lax.ppermute(background[: 2 * HALO - 1], "space", down)
    size = probes + 2 * HALO * tiles
    packet = pl.pallas_call(
        packet_kernel,
        out_shape=shape(size),
        in_specs=[smem] + [anywhere] * 4,
        out_specs=anywhere,
        scratch_shapes=inputs(1, 2 * HALO)
        + [rows_of(1), rows_of(2 * HALO), scratch(size), copies(4), copies(3)],
        compiler_params=params,
        name="packet",
    )(trap_density, background, site_class, log_param, probe_dirs)
    next_packet = lax.ppermute(packet, "space", down)
    edge = jnp.stack([at_space > 0, at_space < slabs - 1]).astype(jnp.int32)
    own_coef, own_src, wide, kept, sums, next_bg = pl.pallas_call(
        inner_kernel,
        out_shape=(
            shape(planes * tiles),
            shape((planes + 1) * tiles),
            shape(probes),
            shape(4, probes, tiles),
            shape(probes),
            shape((2 * HALO - 1) * tiles),
        ),
        in_specs=[smem, smem] + [anywhere] * 4 + [vmem],
        out_specs=(vmem,) * 6,
        scratch_shapes=inputs(planes, planes)
        + [rows_of(planes), rows_of(2 * HALO - 1), rows_of(planes)]
        + [scratch(planes + 1, probes, tiles)] * 2
        + [copies(4)],
        compiler_params=pltpu.CompilerParams(vmem_limit_bytes=28 * 2**20),
        cost_estimate=pl.CostEstimate(flops=10**9, bytes_accessed=2**24, transcendentals=256),
        name="inner",
    )(edge, trap_density, background, site_class, log_param, probe_dirs, beyond)

    pieces = probes * cells // LANES
    images = pl.pallas_call(
        functools.partial(outer_kernel, chunks, folds),
        out_shape=jax.ShapeDtypeStruct((groups * slabs // 2, 2, pieces, LANES), jnp.float32),
        in_specs=[smem] + [vmem] * 7,
        out_specs=vmem,
        scratch_shapes=[
            scratch(total * tiles),
            scratch(total * tiles),
            scratch(total + 1, probes, tiles),
            scratch(total + 1, probes, tiles),
        ],
        compiler_params=pltpu.CompilerParams(vmem_limit_bytes=28 * 2**20),
        name="outer",
    )(edge, own_coef, own_src, wide, kept, sums, next_bg, next_packet)

    same = [
        [g * slabs + z for g in range(groups) for z in range(parity, slabs, 2)] for parity in (0, 1)
    ]
    mine = lax.all_to_all(
        images, ("probe", "space"), split_axis=0, concat_axis=0, axis_index_groups=same, tiled=True
    )
    other = lax.ppermute(mine, "space", [(z, z ^ 1) for z in range(slabs)])
    place = jnp.stack([lax.axis_index("probe"), at_space]).astype(jnp.int32)
    count = groups * probes
    results = (
        jax.ShapeDtypeStruct((probes, 1, cells), jnp.float32),
        jax.ShapeDtypeStruct((count, count), jnp.float32),
    )
    params = pltpu.CompilerParams(vmem_limit_bytes=28 * 2**20)
    if count <= 8 and slabs % 16 == 0:
        halves = cells // LANES
        return pl.pallas_call(
            functools.partial(register_kernel, groups, slabs, probes),
            out_shape=results,
            in_specs=[smem, vmem, vmem],
            out_specs=(vmem, vmem),
            scratch_shapes=[pltpu.VMEM((count, halves, slabs, LANES), jnp.float32)],
            compiler_params=params,
            name="factor",
        )(
            place,
            mine.reshape((groups * slabs * pieces, LANES)),
            other.reshape((groups * slabs * pieces, LANES)),
        )
    odd = at_space % 2 == 1
    pairs = [jnp.where(odd, other, mine), jnp.where(odd, mine, other)]
    pairs = [x.reshape((groups, slabs // 2, 2, probes, cells)) for x in pairs]
    every = jnp.stack(pairs, axis=2).reshape((groups, slabs, 2, probes, cells))
    return pl.pallas_call(
        factor_kernel,
        out_shape=results,
        in_specs=[smem, vmem],
        out_specs=(vmem, vmem),
        scratch_shapes=[
            pltpu.VMEM((count, slabs * cells), jnp.float32),
            pltpu.VMEM((count, cells), jnp.float32),
        ],
        compiler_params=params,
        name="factor",
    )(place, every)


def solution(mesh):
    placed = (
        P("probe", "space", None),
        P("space", None),
        P("space", None, None),
        P("space", None, None),
        P(),
    )
    return jax.shard_map(
        shards,
        mesh=mesh,
        in_specs=placed,
        out_specs=(P("probe", "space", None), P()),
        check_vma=False,
    )
```
